32 devices in a mesh: section: 2 (over core), shard: 4 (over z), group: 4 (over y, x).
Axes of the slice: x: 2, y: 2, z: 4, core: 2. Of those that a mesh axis runs over, the one named last changes fastest.
Arguments:
- ends_in: bfloat16 [2, 8192, 1024], P('section', ('shard', 'group')), may hold values from -8 to 8
- lengths: int32 [32, 3], P(('shard', 'group')), may hold values from 1 to 128, 256 in all within a row
- norm_gain_a: float32 [2, 1024], P('section'), may hold values from 0.5 to 1.5
- norm_bias_a: float32 [2, 1024], P('section'), may hold values from -3 to 3
- w_qkv: bfloat16 [2, 1024, 3072], P('section'), may hold values from -0.1875 to 0.1875
- w_out: bfloat16 [2, 1024, 1024], P('section'), may hold values from -0.75 to 0.75
- norm_gain_f: float32 [2, 1024], P('section'), may hold values from 0.5 to 1.5
- norm_bias_f: float32 [2, 1024], P('section'), may hold values from -3 to 3
- w_gate_up: bfloat16 [2, 1024, 8192], P('section'), may hold values from -0.1875 to 0.1875
- w_down: bfloat16 [2, 4096, 1024], P('section'), may hold values from -0.09375 to 0.09375
Outputs:
- ends_out: float32 [2, 8192, 1024], P('section', ('shard', 'group'))
- grad_gain_a: float32 [2, 1024], P('section', 'shard')
- grad_bias_a: float32 [2, 1024], P('section', 'shard')
- grad_qkv: float32 [2, 1024, 3072], P('section', 'shard')
- grad_out: float32 [2, 1024, 1024], P('section', 'shard')
- grad_gain_f: float32 [2, 1024], P('section', 'shard')
- grad_bias_f: float32 [2, 1024], P('section', 'shard')
- grad_gate_up: float32 [2, 1024, 8192], P('section', 'shard')
- grad_down: float32 [2, 4096, 1024], P('section', 'shard')
The draws below stay inside these ranges and needn't reach their ends.
Inputs may be any that keep to these rules, and one draw needn't show every extreme that they name: Each row holds the lengths of the 3 windows packed one after another into one micro-batch row of 256 tokens; they sum to 256.
All inputs are finite; a program needn't handle non-finite values.
Results may differ from the reference program's by a relative error of at most 0.014.
Values may be sent and summed in bfloat16 or wider, within the bound.
A program may use at most 320 MiB of HBM per device.

```python
import math
import jax
import jax.numpy as jnp
import numpy as np
from jax import lax

D = 1024
HEADS = 16
FF = 4096
ROW = 256
WIN = 3
HD = 64
ROWS = 32
TOKENS = 8192


def raised(drawn, key, source, target, parts, factor):
    owner, partner = [(jnp.arange(drawn.shape[dim]) // (drawn.shape[dim] // parts)).reshape([-1 if axis == dim else 1 for axis in range(drawn.ndim)]) for dim in (source, target)]
    chosen = jax.random.permutation(key, parts)[partner]
    strong = (owner == chosen) | (owner == (partner + parts // 2) % parts)
    return jnp.where(strong, factor * drawn, drawn)


def levels(rng, extent, cuts, low, top_value):
    loudness = 1.0
    for axis_at, shards_of in cuts:
        steps = jax.random.uniform(jax.random.fold_in(jax.random.fold_in(rng, 6), axis_at), (shards_of,), jnp.float32, low / len(cuts), top_value / len(cuts))
        loudness = loudness * jnp.repeat(jnp.exp(steps), extent[axis_at] // shards_of).reshape((-1,) + (1,) * (len(extent) - 1 - axis_at))
    return loudness


def profile(count, total, bound, slope):
    weights = [(1 << 20) // math.isqrt(rank ** slope) + 1 for rank in range(2, count + 1)]
    spare, counts = total - bound - (count - 1), [1] * (count - 1)
    while spare > 0:
        candidates = [i for i in range(count - 1) if counts[i] < bound]
        pool, left = sum([weights[i] for i in candidates]), spare
        for i in candidates:
            more = min(bound - counts[i], max(1, left * weights[i] // pool), spare)
            counts[i] = counts[i] + more
            spare = spare - more
    return np.array([bound] + counts)


def ragged(rng, amount, total, most, slope):
    if amount == 2:
        one = jax.random.randint(rng, (), max(1, total - most), min(most, total - 1) + 1)
        return jnp.stack([one, total - one])
    sizes = jnp.asarray(profile(amount, total, most, slope), jnp.int32)
    twos = (amount - 1) // 2
    giver, sink = sizes[1:1 + 2 * twos:2], sizes[2:2 + 2 * twos:2]
    slack = jnp.minimum(giver - 1, most - sink)
    moved = jax.random.randint(jax.random.fold_in(rng, 1), (twos,), 0, 1 << 20) % (slack + 1)
    sizes = sizes.at[1:1 + 2 * twos:2].set(giver - moved).at[2:2 + 2 * twos:2].set(sink + moved)
    return sizes[jax.random.permutation(jax.random.fold_in(rng, 2), amount)]


def scatter_about(own_key, dims, scale, reach, cuts=(), held_as=jnp.bfloat16):
    factor_of = levels(own_key, dims, cuts, -0.22, 0.18) if cuts else 1.0
    values = jax.random.normal(own_key, dims, jnp.float32) * scale * factor_of
    return jnp.minimum(jnp.maximum(values, -reach), reach).astype(held_as)


def heavy_noise(rng, dims, width, bound, cuts, heavy, kind=jnp.bfloat16):
    values = width * jax.random.normal(rng, dims, jnp.float32)
    if cuts:
        values = values * levels(rng, dims, cuts, -0.22, 0.18)
    return jnp.clip(raised(values, jax.random.fold_in(rng, 3), *heavy), -bound, bound).astype(kind)


def setup_inputs(seed: int = 0) -> dict:
    splits = jax.random.split(jax.random.key(seed), 11)
    ends_in = heavy_noise(splits[0], (2, TOKENS, D), 1.0, 8.0, ((0, 2), (1, 16)), (1, 2, 16, 2.0))
    lengths = jax.vmap(lambda own: ragged(own, WIN, ROW, ROW // 2, 2))(jax.random.split(splits[1], ROWS)).reshape((ROWS, WIN)).astype(jnp.int32)
    norm_gain_a = jnp.clip(1.0 + 0.1 * jax.random.normal(splits[2], (2, D), jnp.float32), 0.5, 1.5)
    norm_bias_a = scatter_about(splits[3], (2, D), 0.5, 3.0, ((0, 2),), jnp.float32)
    w_qkv = scatter_about(splits[4], (2, D, 3 * D), D ** -0.5, 0.1875, ((0, 2),))
    w_out = scatter_about(splits[5], (2, D, D), (D // 16) ** -0.5, 0.75, ((0, 2),))
    norm_gain_f = jnp.clip(1.0 + 0.1 * jax.random.normal(splits[6], (2, D), jnp.float32), 0.5, 1.5)
    norm_bias_f = scatter_about(splits[7], (2, D), 0.5, 3.0, ((0, 2),), jnp.float32)
    w_gate_up = scatter_about(splits[8], (2, D, 2 * FF), D ** -0.5, 0.1875, ((0, 2),))
    w_down = scatter_about(splits[9], (2, FF, D), FF ** -0.5, 0.09375, ((0, 2),))
    return {"ends_in": ends_in, "lengths": lengths, "norm_gain_a": norm_gain_a, "norm_bias_a": norm_bias_a, "w_qkv": w_qkv, "w_out": w_out, "norm_gain_f": norm_gain_f, "norm_bias_f": norm_bias_f, "w_gate_up": w_gate_up, "w_down": w_down}


@jax.custom_vjp
def low(v):
    return lax.optimization_barrier(v.astype(jnp.bfloat16)).astype(jnp.float32)

@jax.custom_vjp
def low_back(v):
    return v

def low_keep(v):
    return (low(v), None)

def low_pass(kept, grad):
    return (grad,)

def back_keep(v):
    return (v, None)

def back_low(kept, grad):
    return (low(grad),)
low.defvjp(low_keep, low_pass)
low_back.defvjp(back_keep, back_low)
epsilon = 1e-05

def product(former, latter):
    return jnp.dot(former, latter, precision=lax.Precision.HIGHEST, preferred_element_type=jnp.float32)

def layout(lengths_row):
    window_ends = jnp.cumsum(lengths_row, axis=-1).astype(jnp.int32)
    token_index = jnp.arange(ROW, dtype=jnp.int32)
    passed = token_index[:, None] >= window_ends[..., None, :]
    segment = lax.optimization_barrier(jnp.sum(passed.astype(jnp.int32), axis=-1)).astype(jnp.int32)
    before = lax.optimization_barrier(jnp.sum(jnp.where(passed, lengths_row[..., None, :], 0), axis=-1)).astype(jnp.int32)
    return (segment, token_index - before)

def tables(position):
    half_size = HD // 2
    frequency = 10000.0 ** (-2.0 * jnp.arange(half_size, dtype=jnp.float32) / HD)
    angles = position.astype(jnp.float32)[..., None] * frequency
    angles = jnp.concatenate([angles, angles], axis=-1)
    return (jnp.cos(angles)[..., None, :], jnp.sin(angles)[..., None, :])

def rotate(values, cosine, sine_table):
    half_size = HD // 2
    turned = jnp.concatenate([-values[..., half_size:], values[..., :half_size]], axis=-1)
    return values * cosine + turned * sine_table

def layer_norm(values, norm_gain, norm_bias):
    average = lax.optimization_barrier(jnp.mean(values, axis=-1, keepdims=True))
    centered = values - average
    variance = lax.optimization_barrier(jnp.mean(centered * centered, axis=-1, keepdims=True))
    return centered * lax.rsqrt(variance + epsilon) * norm_gain + norm_bias

def layer_apply(hidden_in, params, same_window, cosine, sine_table):
    gain_a, bias_a, weight_qkv, weight_out, gain_f, bias_f, weight_gu, weight_down = params
    batch_rows = hidden_in.shape[0]
    normed_a = low(layer_norm(hidden_in, gain_a, bias_a)).reshape(-1, D)
    projected = low_back(product(normed_a, weight_qkv)).reshape(batch_rows, ROW, 3, HEADS, HD)
    queries = low(rotate(projected[:, :, 0], cosine, sine_table))
    key_rot = low(rotate(projected[:, :, 1], cosine, sine_table))
    values = low(projected[:, :, 2])
    scores = jnp.einsum('bqhd,bkhd->bhqk', queries, key_rot, precision=lax.Precision.HIGHEST) * HD ** (-0.5)
    scores = low_back(scores)
    scores = jnp.where(same_window[:, None], scores, -1e+30)
    attn_probs = low(jax.nn.softmax(scores, axis=-1))
    mixture = jnp.einsum('bhqk,bkhd->bqhd', attn_probs, values, precision=lax.Precision.HIGHEST)
    mixture = low(low_back(mixture)).reshape(-1, D)
    hidden_mid = hidden_in + low_back(product(mixture, weight_out)).reshape(hidden_in.shape)
    normed_f = low(layer_norm(hidden_mid, gain_f, bias_f)).reshape(-1, D)
    gate_up = low_back(product(normed_f, weight_gu))
    hidden = low(jax.nn.silu(gate_up[:, :FF]) * gate_up[:, FF:])
    return hidden_mid + low_back(product(hidden, weight_down)).reshape(hidden_in.shape)

def two_layers(inputs, params, lengths_row):
    segment, position = layout(lengths_row)
    same_window = segment[:, :, None] == segment[:, None, :]
    cosine, sine_table = tables(position)
    first_params = tuple((item[0] for item in params))
    second_params = tuple((item[1] for item in params))
    middle = low_back(low(layer_apply(inputs, first_params, same_window, cosine, sine_table)))
    return layer_apply(middle, second_params, same_window, cosine, sine_table)

def reference(ends_in, lengths, norm_gain_a, norm_bias_a, w_qkv, w_out, norm_gain_f, norm_bias_f, w_gate_up, w_down):
    inputs = ends_in[0].astype(jnp.float32).reshape(ROWS, ROW, D)
    cotangent = ends_in[1].astype(jnp.float32).reshape(ROWS, ROW, D)
    params = tuple((item.astype(jnp.float32) for item in (norm_gain_a, norm_bias_a, w_qkv, w_out, norm_gain_f, norm_bias_f, w_gate_up, w_down)))
    group_rows = math.gcd(ROWS, max(1, 4096 // ROW))

    def forward(stream, weights):

        def run_block(blocks_in):
            return two_layers(blocks_in[0], weights, blocks_in[1])
        blocks = (stream.reshape(ROWS // group_rows, group_rows, ROW, D), lengths.reshape(ROWS // group_rows, group_rows, WIN))
        return lax.map(jax.checkpoint(run_block), blocks).reshape(ROWS, ROW, D)
    output, pullback = jax.vjp(forward, inputs, params)
    grad_inputs, grads = pullback(cotangent)
    ends_out = jnp.stack([grad_inputs, output]).reshape(2, TOKENS, D)
    return (ends_out, grads[0], grads[1], grads[2], grads[3], grads[4], grads[5], grads[6], grads[7])
```

```python
import functools

import jax
import jax.numpy as jnp
from jax import lax
from jax.experimental import pallas as pl
from jax.experimental.pallas import tpu as pltpu
from jax.sharding import PartitionSpec as P

MESH = pl.DeviceIdType.MESH
F32, BF16 = jnp.float32, jnp.bfloat16
HEADS = 16
EPSILON = 1e-05


def dot(a, b):
    return jnp.dot(a, b, preferred_element_type=F32)


def dot_cols(a, b):
    return lax.dot_general(a, b, (((1,), (1,)), ((), ())), preferred_element_type=F32)


def dot_rows(a, b):
    return lax.dot_general(a, b, (((0,), (0,)), ((), ())), preferred_element_type=F32)


def in_rows(total, step, run):
    @pl.loop(0, total // step)
    def _(index):
        run(pl.ds(pl.multiple_of(index * step, step), step))


def normalized(values):
    average = jnp.mean(values, axis=-1, keepdims=True)
    centered = values - average
    variance = jnp.mean(centered * centered, axis=-1, keepdims=True)
    spread = lax.rsqrt(variance + EPSILON)
    return centered * spread, spread


def norm_back(grad, values, gain):
    unit, spread = normalized(values)
    scaled = grad * gain
    return spread * (
        scaled
        - jnp.mean(scaled, axis=-1, keepdims=True)
        - unit * jnp.mean(scaled * unit, axis=-1, keepdims=True)
    ), grad * unit


def lanes_of(shape):
    return lax.broadcasted_iota(jnp.int32, shape, len(shape) - 1)


def turn(values, half, size):
    wide = values.shape[-1]
    early = lax.rem(lanes_of(values.shape), size) < half
    return jnp.where(early, pltpu.roll(values, wide - half, 1), pltpu.roll(values, half, 1)), early


def rotated(values, cosine, sine, size):
    other, early = turn(values, size // 2, size)
    return values * cosine + jnp.where(early, -other, other) * sine


def unrotated(values, cosine, sine, size):
    other, early = turn(values * sine, size // 2, size)
    return values * cosine + jnp.where(early, other, -other)


def window_of(index, lengths_ref, row):
    windows = lengths_ref.shape[1]
    end = lengths_ref[row, 0]
    segment = (index >= end).astype(jnp.int32)
    for window in range(1, windows):
        end = end + lengths_ref[row, window]
        segment = segment + (index >= end).astype(jnp.int32)
    return segment


def same_window(lengths_ref, row, tokens):
    queries = window_of(lax.broadcasted_iota(jnp.int32, (tokens, 1), 0), lengths_ref, row)
    keys = window_of(lax.broadcasted_iota(jnp.int32, (1, tokens), 1), lengths_ref, row)
    return queries == keys


def softmax(scores, allowed):
    scores = jnp.where(allowed, scores, -1e30)
    weights = jnp.exp(scores - jnp.max(scores, axis=-1, keepdims=True))
    return weights * (1.0 / jnp.sum(weights, axis=-1, keepdims=True))


def attention_kernel(size, row_tokens, act_ref, lengths_ref, x_ref, gain_ref, bias_ref, wq_ref, wk_ref, wv_ref,
                     wo_ref, cos_ref, sin_ref, mid_ref, low_ref, qkv_ref, mix_ref):
    tokens = x_ref.shape[0]
    part = pl.program_id(0)
    block = wq_ref.shape[1]
    pair = 2 * size

    @pl.when(act_ref[0] == 1)
    def _():
        @pl.when(part == 0)
        def _():
            def begin(rows):
                values = x_ref[rows].astype(F32)
                unit, _ = normalized(values)
                low_ref[rows] = (unit * gain_ref[...] + bias_ref[...]).astype(BF16)
                mid_ref[rows] = values
            in_rows(tokens, 64, begin)

        def project(rows):
            low = low_ref[rows]
            cosine, sine = cos_ref[rows], sin_ref[rows]
            qkv_ref[0, rows] = rotated(dot(low, wq_ref[...]), cosine, sine, size).astype(BF16)
            qkv_ref[1, rows] = rotated(dot(low, wk_ref[...]), cosine, sine, size).astype(BF16)
            qkv_ref[2, rows] = dot(low, wv_ref[...]).astype(BF16)
        in_rows(tokens, row_tokens, project)

        @pl.loop(0, tokens // row_tokens)
        def _(row):
            rows = pl.ds(pl.multiple_of(row * row_tokens, row_tokens), row_tokens)
            allowed = same_window(lengths_ref, row, row_tokens)
            first = lanes_of((row_tokens, pair)) < size
            for at in range(block // pair):
                lanes = pl.ds(at * pair, pair)
                query, key, value = (qkv_ref[which, rows, lanes] for which in range(3))
                query = query * (size ** -0.5)
                results = []
                for head in range(2):
                    own = jnp.where(first if head == 0 else jnp.logical_not(first), query, jnp.zeros_like(query))
                    probs = softmax(dot_cols(own, key), allowed)
                    results.append(dot(probs.astype(BF16), value))
                mix_ref[rows, lanes] = jnp.where(first, results[0], results[1]).astype(BF16)

        def close(rows):
            mid_ref[rows] += dot(mix_ref[rows], wo_ref[...])
        in_rows(tokens, row_tokens, close)


def attention_back_kernel(size, row_tokens, act_ref, lengths_ref, grad_ref, x_ref, gain_ref, qkv_ref, wq_ref, wk_ref,
                          wv_ref, wo_ref, cos_ref, sin_ref, branch_ref, proj_ref, input_ref, input_low_ref,
                          dgain_ref, dbias_ref, gm_ref, total_ref):
    tokens = x_ref.shape[0]
    part = pl.program_id(0)
    block = wq_ref.shape[1]
    pair = 2 * size

    @pl.when(act_ref[0] == 1)
    def _():
        @pl.when(part == 0)
        def _():
            def begin(rows):
                branch_ref[rows] = grad_ref[rows].astype(BF16)
            in_rows(tokens, 64, begin)

        def mixture_grad(rows):
            gm_ref[rows] = dot_cols(branch_ref[rows], wo_ref[...]).astype(BF16)
        in_rows(tokens, row_tokens, mixture_grad)

        @pl.loop(0, tokens // row_tokens)
        def _(row):
            rows = pl.ds(pl.multiple_of(row * row_tokens, row_tokens), row_tokens)
            allowed = same_window(lengths_ref, row, row_tokens)
            first = lanes_of((row_tokens, pair)) < size
            for at in range(block // pair):
                lanes = pl.ds(at * pair, pair)
                query, key, value = (qkv_ref[which, rows, lanes] for which in range(3))
                grad_mix = gm_ref[rows, lanes]
                scaled = query * (size ** -0.5)
                results = []
                for head in range(2):
                    mine = first if head == 0 else jnp.logical_not(first)
                    probs = softmax(dot_cols(jnp.where(mine, scaled, jnp.zeros_like(scaled)), key), allowed)
                    grad_probs = dot_cols(jnp.where(mine, grad_mix, jnp.zeros_like(grad_mix)), value)
                    grad_value = dot_rows(probs.astype(BF16), grad_mix)
                    weighted = probs * grad_probs
                    grad_scores = (weighted - probs * jnp.sum(weighted, axis=-1, keepdims=True)).astype(BF16)
                    results.append((dot(grad_scores, key), dot_rows(grad_scores, query), grad_value))
                grad_query, grad_key, grad_value = (jnp.where(first, a, b) for a, b in zip(*results))
                cosine, sine = cos_ref[rows, lanes], sin_ref[rows, lanes]
                proj_ref[0, rows, lanes] = unrotated(grad_query * (size ** -0.5), cosine, sine, size).astype(BF16)
                proj_ref[1, rows, lanes] = unrotated(grad_key * (size ** -0.5), cosine, sine, size).astype(BF16)
                proj_ref[2, rows, lanes] = grad_value.astype(BF16)

        def normed_grad(rows):
            added = (
                dot_cols(proj_ref[0, rows], wq_ref[...])
                + dot_cols(proj_ref[1, rows], wk_ref[...])
                + dot_cols(proj_ref[2, rows], wv_ref[...])
            )
            total_ref[rows] = jnp.where(part == 0, added, total_ref[rows] + added)
        in_rows(tokens, row_tokens, normed_grad)

        @pl.when(part == pl.num_programs(0) - 1)
        def _():
            dgain_ref[...] = jnp.zeros_like(dgain_ref)
            dbias_ref[...] = jnp.zeros_like(dbias_ref)

            def finish(rows):
                grad = total_ref[rows]
                through, by_gain = norm_back(grad, x_ref[rows].astype(F32), gain_ref[...])
                result = grad_ref[rows] + through
                input_ref[rows] = result
                input_low_ref[rows] = result.astype(BF16)
                dgain_ref[...] += jnp.sum(by_gain, axis=0, keepdims=True)
                dbias_ref[...] += jnp.sum(grad, axis=0, keepdims=True)
            in_rows(tokens, 64, finish)


def feed_kernel(row_tokens, act_ref, mid_ref, gain_ref, bias_ref, wg_ref, wu_ref, wd_ref, out_ref, low_ref, total_ref):
    tokens = mid_ref.shape[0]
    part = pl.program_id(0)

    @pl.when(act_ref[0] == 1)
    def _():
        @pl.when(part == 0)
        def _():
            def begin(rows):
                values = mid_ref[rows]
                unit, _ = normalized(values)
                low_ref[rows] = (unit * gain_ref[...] + bias_ref[...]).astype(BF16)
                total_ref[rows] = values
            in_rows(tokens, 64, begin)

        def step(rows):
            low = low_ref[rows]
            gate = dot(low, wg_ref[...])
            up = dot(low, wu_ref[...])
            hidden = (gate / (1.0 + jnp.exp(-gate)) * up).astype(BF16)
            total_ref[rows] += dot(hidden, wd_ref[...])
        in_rows(tokens, row_tokens, step)

        @pl.when(part == pl.num_programs(0) - 1)
        def _():
            def finish(rows):
                out_ref[rows] = total_ref[rows].astype(BF16)
            in_rows(tokens, 64, finish)


def feed_both_kernel(row_tokens, act_ref, mid_ref, grad_ref, gain_ref, bias_ref, wg_ref, wu_ref, wd_ref, out_ref,
                     low_ref, hidden_ref, ggu_ref, grad_mid_ref, dgain_ref, dbias_ref, total_ref):
    tokens = mid_ref.shape[0]
    part = pl.program_id(0)

    @pl.when(act_ref[0] == 1)
    def _():
        @pl.when(part == 0)
        def _():
            def begin(rows):
                values = mid_ref[rows]
                unit, _ = normalized(values)
                low_ref[rows] = (unit * gain_ref[...] + bias_ref[...]).astype(BF16)
                out_ref[rows] = values
            in_rows(tokens, 64, begin)

        def step(rows):
            low = low_ref[rows]
            gate = dot(low, wg_ref[...])
            up = dot(low, wu_ref[...])
            sig = 1.0 / (1.0 + jnp.exp(-gate))
            silu = gate * sig
            hidden = (silu * up).astype(BF16)
            hidden_ref[rows] = hidden
            out_ref[rows] += dot(hidden, wd_ref[...])
            grad_hidden = dot_cols(grad_ref[rows], wd_ref[...])
            grad_gate = (grad_hidden * up * (sig * (1.0 + gate * (1.0 - sig)))).astype(BF16)
            grad_up = (grad_hidden * silu).astype(BF16)
            ggu_ref[0, rows] = grad_gate
            ggu_ref[1, rows] = grad_up
            added = dot_cols(grad_gate, wg_ref[...]) + dot_cols(grad_up, wu_ref[...])
            total_ref[rows] = jnp.where(part == 0, added, total_ref[rows] + added)
        in_rows(tokens, row_tokens, step)

        @pl.when(part == pl.num_programs(0) - 1)
        def _():
            dgain_ref[...] = jnp.zeros_like(dgain_ref)
            dbias_ref[...] = jnp.zeros_like(dbias_ref)

            def finish(rows):
                grad = total_ref[rows]
                through, by_gain = norm_back(grad, mid_ref[rows], gain_ref[...])
                grad_mid_ref[rows] = grad_ref[rows].astype(F32) + through
                dgain_ref[...] += jnp.sum(by_gain, axis=0, keepdims=True)
                dbias_ref[...] += jnp.sum(grad, axis=0, keepdims=True)
            in_rows(tokens, 64, finish)


def whole(shape):
    return pl.BlockSpec(shape, lambda part, *_: (0,) * len(shape))


def column(rows, wide, offset=0):
    return pl.BlockSpec((rows, wide), lambda part, act, *_: (0, (part + offset) * act[0]))


def stacked(count, rows, wide):
    return pl.BlockSpec((count, rows, wide), lambda part, act, *_: (0, 0, part * act[0]))


def lower(rows, wide):
    return pl.BlockSpec((rows, wide), lambda part, act, *_: (part * act[0], 0))


def local_call(kernel, name, grid, scalars, args, in_specs, outs, out_specs, scratch, flops, limit=56):
    return pl.pallas_call(
        kernel,
        grid_spec=pltpu.PrefetchScalarGridSpec(
            num_scalar_prefetch=len(scalars), grid=(grid,), in_specs=in_specs, out_specs=out_specs,
            scratch_shapes=scratch),
        out_shape=outs,
        name=name,
        cost_estimate=pl.CostEstimate(flops=flops, bytes_accessed=40 * 2 ** 20, transcendentals=0),
        compiler_params=pltpu.CompilerParams(
            dimension_semantics=("arbitrary",), vmem_limit_bytes=limit * 1024 * 1024),
    )(*scalars, *args)


def attention(active, lengths, x, gain, bias, w_qkv, w_out, cosine, sine, parts=4):
    tokens, features = x.shape
    row_tokens = tokens // lengths.shape[0]
    size = features // HEADS
    wide = features // parts
    return local_call(
        functools.partial(attention_kernel, size, row_tokens), "attention", parts, (active, lengths),
        (x, gain, bias, w_qkv, w_qkv, w_qkv, w_out, cosine, sine),
        [whole((tokens, features)), whole((1, features)), whole((1, features)), column(features, wide),
         column(features, wide, parts), column(features, wide, 2 * parts), lower(wide, features),
         whole((tokens, wide)), whole((tokens, wide))],
        (jax.ShapeDtypeStruct((tokens, features), F32), jax.ShapeDtypeStruct((tokens, features), BF16),
         jax.ShapeDtypeStruct((3, tokens, features), BF16), jax.ShapeDtypeStruct((tokens, features), BF16)),
        (whole((tokens, features)), whole((tokens, features)), stacked(3, tokens, wide), column(tokens, wide)),
        [], 8 * tokens * features ** 2)


def attention_back(active, lengths, grad_mid, x, gain, qkv, w_qkv, w_out, cosine, sine, parts=4):
    tokens, features = x.shape
    row_tokens = tokens // lengths.shape[0]
    size = features // HEADS
    wide = features // parts
    vector = jax.ShapeDtypeStruct((1, features), F32)
    return local_call(
        functools.partial(attention_back_kernel, size, row_tokens), "attention_back", parts, (active, lengths),
        (grad_mid, x, gain, qkv, w_qkv, w_qkv, w_qkv, w_out, cosine, sine),
        [whole((tokens, features)), whole((tokens, features)), whole((1, features)), stacked(3, tokens, wide),
         column(features, wide), column(features, wide, parts), column(features, wide, 2 * parts),
         lower(wide, features), whole((tokens, wide)), whole((tokens, wide))],
        (jax.ShapeDtypeStruct((tokens, features), BF16), jax.ShapeDtypeStruct((3, tokens, features), BF16),
         jax.ShapeDtypeStruct((tokens, features), F32), jax.ShapeDtypeStruct((tokens, features), BF16),
         vector, vector),
        (whole((tokens, features)), stacked(3, tokens, wide), whole((tokens, features)), whole((tokens, features)),
         whole((1, features)), whole((1, features))),
        [pltpu.VMEM((tokens, wide), BF16), pltpu.VMEM((tokens, features), F32)], 20 * tokens * features ** 2)


def feed(active, mid, gain, bias, w_gate_up, w_down, parts=8):
    tokens, features = mid.shape
    wide = w_down.shape[0] // parts
    return local_call(
        functools.partial(feed_kernel, tokens // 2), "feed", parts, (active,),
        (mid, gain, bias, w_gate_up, w_gate_up, w_down),
        [whole((tokens, features)), whole((1, features)), whole((1, features)), column(features, wide),
         column(features, wide, parts), lower(wide, features)],
        jax.ShapeDtypeStruct((tokens, features), BF16), whole((tokens, features)),
        [pltpu.VMEM((tokens, features), BF16), pltpu.VMEM((tokens, features), F32)],
        6 * tokens * features * w_down.shape[0])


def feed_both(active, mid, grad, gain, bias, w_gate_up, w_down, parts=8):
    tokens, features = mid.shape
    hidden = w_down.shape[0]
    wide = hidden // parts
    vector = jax.ShapeDtypeStruct((1, features), F32)
    return local_call(
        functools.partial(feed_both_kernel, tokens // 2), "feed_both", parts, (active,),
        (mid, grad, gain, bias, w_gate_up, w_gate_up, w_down),
        [whole((tokens, features)), whole((tokens, features)), whole((1, features)), whole((1, features)),
         column(features, wide), column(features, wide, parts), lower(wide, features)],
        (jax.ShapeDtypeStruct((tokens, features), F32), jax.ShapeDtypeStruct((tokens, features), BF16),
         jax.ShapeDtypeStruct((tokens, hidden), BF16), jax.ShapeDtypeStruct((2, tokens, hidden), BF16),
         jax.ShapeDtypeStruct((tokens, features), F32), vector, vector),
        (whole((tokens, features)), whole((tokens, features)), column(tokens, wide), stacked(2, tokens, wide),
         whole((tokens, features)), whole((1, features)), whole((1, features))),
        [pltpu.VMEM((tokens, features), F32)], 12 * tokens * features * hidden)


def tables(lengths, row_tokens, size, repeat):
    ends = jnp.cumsum(lengths, axis=-1)
    index = jnp.arange(row_tokens, dtype=jnp.int32)
    passed = index[:, None] >= ends[..., None, :]
    before = jnp.sum(jnp.where(passed, lengths[..., None, :], 0), axis=-1)
    position = (index - before).reshape(-1)
    frequency = 10000.0 ** (-2.0 * jnp.arange(size // 2, dtype=F32) / size)
    angles = position.astype(F32)[:, None] * frequency
    return jnp.tile(jnp.cos(angles), (1, 2 * repeat)), jnp.tile(jnp.sin(angles), (1, 2 * repeat))


def exchange_kernel(cfg, *refs):
    shards, bits, seats, unit_rows, width, section, aliased = cfg
    arrays = len(seats)
    lefts, rights = refs[:arrays], refs[arrays:2 * arrays]
    refs = refs[2 * arrays + (1 if aliased else 0):]
    out = refs[0]
    (left, right, left_sem, right_sem, own, give, landed, mine, chain, rest_send, rest_land, rest_keep, piece,
     land_send, land_recv, chain_send, chain_recv,
     rest_ssem, rest_rsem, store_sem, gather_send, gather_recv) = refs[1:]
    units = sum(seat[0] for seat in seats)
    half = unit_rows // 2
    others = bits - 1
    final_rows = unit_rows >> bits
    sec = lax.axis_index("section")
    here = lax.axis_index("shard")
    seat = lax.axis_index("group")

    def bit_of(index):
        return lax.rem(lax.div(seat, 1 << index), 2)

    def across(index):
        return (sec, here, seat + (1 - 2 * bit_of(index)) * (1 << index))

    above = (sec, jnp.minimum(here + 1, shards - 1), seat)
    below = (sec, jnp.maximum(here - 1, 0), seat)
    first = [path for path in range(2)]
    rest = [[index for index in range(bits) if index != path] for path in range(2)]
    sides = [rest[path][::-1] + [first[path]] for path in range(2)]

    def remote(source, target, send, recv, device):
        return pltpu.make_async_remote_copy(
            src_ref=source, dst_ref=target, send_sem=send, recv_sem=recv,
            device_id=device, device_id_type=MESH,
        )

    def seat_row(path, depth):
        row = bit_of(first[path]) * half
        for step in range(depth):
            row = row + bit_of(rest[path][step]) * (half >> (step + 1))
        return row

    def valid(chunk):
        return (chunk >= 0) & (chunk < units)

    def on(condition, run):
        pl.when(condition)(run)

    def by_rows(rows, run, tall=32):
        step = min(rows, tall)

        @pl.loop(0, rows // step)
        def _(index):
            run(pl.ds(pl.multiple_of(index * step, step), step))

    def shifted(part, offset):
        return pl.ds(pl.multiple_of(part.start + offset, part.size), part.size)

    def work():
        barrier = pltpu.get_barrier_semaphore()
        for index in range(bits):
            pl.semaphore_signal(barrier, inc=1, device_id=across(index), device_id_type=MESH)
        on(here < shards - 1, lambda: pl.semaphore_signal(barrier, inc=1, device_id=above, device_id_type=MESH))
        on(here > 0, lambda: pl.semaphore_signal(barrier, inc=1, device_id=below, device_id_type=MESH))
        ends = (here > 0).astype(jnp.int32) + (here < shards - 1).astype(jnp.int32)
        pl.semaphore_wait(barrier, bits + ends)

        for path in range(2):
            for way in range(2):
                @pl.loop(0, shards)
                def _(block):
                    def clear(rows):
                        chain[path, way, chain.shape[2] - 1, block, rows] = jnp.zeros((rows.size, width), BF16)
                    by_rows(half, clear)

        def loads(chunk, run):
            slot, start = lax.rem(chunk, 2), 0
            for which, (count, blocks, inner, rows) in enumerate(seats):
                def each(which=which, start=start, blocks=blocks, inner=inner, rows=rows):
                    local = chunk - start
                    row = lax.div(local, blocks)
                    block = local - row * blocks
                    outer = lax.div(block, inner)
                    column = pl.multiple_of((block - outer * inner) * (2 * width), 2 * width)
                    run(pltpu.make_async_copy(
                        rights[which].at[outer, :, pl.ds(column, 2 * width)], right.at[slot], right_sem.at[slot]))
                    for shard in range(shards):
                        offset = pl.multiple_of(shard * rows + row * unit_rows, unit_rows)
                        run(pltpu.make_async_copy(
                            lefts[which].at[:, pl.ds(offset, unit_rows)], left.at[slot, shard],
                            left_sem.at[slot, shard]))
                on((chunk >= start) & (chunk < start + count), each)
                start += count

        def first_copy(path, chunk):
            two, four = lax.rem(chunk, 2), lax.rem(chunk, 4)
            return remote(give.at[path, two], landed.at[path, four], land_send.at[path, four],
                          land_recv.at[path, four], across(first[path]))

        def opening(path, chunk):
            two = lax.rem(chunk, 2)
            away = (1 - bit_of(first[path])) * half

            @pl.loop(0, shards)
            def _(block):
                own[path, two, block] = lax.dot_general(
                    left[two, block], right[two, :, path * width:(path + 1) * width],
                    (((0,), (0,)), ((), ())), preferred_element_type=F32)

                def round_off(rows):
                    give[path, two, block, rows] = own[path, two, block, shifted(rows, away)].astype(BF16)
                by_rows(half, round_off)
            first_copy(path, chunk).start()

        def first_sum(path, chunk):
            slot, two, four = lax.rem(chunk, shards + 2), lax.rem(chunk, 2), lax.rem(chunk, 4)
            copy = first_copy(path, chunk)
            copy.wait_recv()
            copy.wait_send()
            kept = bit_of(first[path]) * half

            @pl.loop(0, shards)
            def _(block):
                def add(rows):
                    mine[path, slot, block, rows] = (
                        own[path, two, block, shifted(rows, kept)] + landed[path, four, block, rows].astype(F32)
                    ).astype(BF16)
                by_rows(half, add)

        depth = chain.shape[2] - 1

        def hop(path, way, chunk, block):
            slot = lax.rem(chunk, depth)
            ref = chain.at[path, way, slot, block]
            return remote(ref, ref, chain_send.at[path, way, slot, block],
                          chain_recv.at[path, way, slot, block], above if way == 0 else below)

        def onward(path, way, chunk):
            slot, base = lax.rem(chunk, depth), lax.rem(chunk, shards + 2)
            arrives = here > 0 if way == 0 else here < shards - 1

            @pl.loop(0, shards - 1 - here if way == 0 else here)
            def _(index):
                block = shards - 1 - index if way == 0 else index
                copy = hop(path, way, chunk, block)
                on(arrives, lambda: copy.wait_recv())
                source = jnp.where(arrives, slot, depth)

                def add(rows):
                    chain[path, way, slot, block, rows] = (
                        chain[path, way, source, block, rows].astype(F32) + mine[path, base, block, rows].astype(F32)
                    ).astype(BF16)
                by_rows(half, add)
                copy.start()

        def sent(path, way, chunk):
            @pl.loop(0, shards - 1 - here if way == 0 else here)
            def _(index):
                hop(path, way, chunk, shards - 1 - index if way == 0 else index).wait_send()

        def rest_rows(step):
            return half >> (step + 1)

        def rest_copy(path, step, chunk):
            slot = lax.rem(chunk, 4)
            rows = pl.ds(0, rest_rows(step))
            return remote(rest_send.at[path, step, slot, rows], rest_land.at[path, step, slot, rows],
                          rest_ssem.at[path, step, slot], rest_rsem.at[path, step, slot],
                          across(rest[path][step]))

        def share(path, step, chunk, total):
            slot, rows = lax.rem(chunk, 4), rest_rows(step)
            bit = bit_of(rest[path][step])

            def give(part):
                rest_send[path, step, slot, part] = total(part, (1 - bit) * rows).astype(BF16)
            by_rows(rows, give)
            rest_copy(path, step, chunk).start()

            def keep(part):
                rest_keep[path, step, slot, part] = total(part, bit * rows)
            by_rows(rows, keep)

        def last_hop(path, chunk):
            base, slot = lax.rem(chunk, shards + 2), lax.rem(chunk, depth)
            on(here > 0, lambda: hop(path, 0, chunk, here).wait_recv())
            on(here < shards - 1, lambda: hop(path, 1, chunk, here).wait_recv())
            from_below = jnp.where(here > 0, slot, depth)
            from_above = jnp.where(here < shards - 1, slot, depth)

            def total(part, offset):
                rows = shifted(part, offset)
                return (
                    mine[path, base, here, rows].astype(F32)
                    + chain[path, 0, from_below, here, rows].astype(F32)
                    + chain[path, 1, from_above, here, rows].astype(F32)
                )
            share(path, 0, chunk, total)

        def rest_sum(path, step, chunk):
            slot, rows = lax.rem(chunk, 4), rest_rows(step)
            copy = rest_copy(path, step, chunk)
            copy.wait_recv()
            copy.wait_send()

            def total(part, offset):
                part = shifted(part, offset)
                return rest_keep[path, step, slot, part] + rest_land[path, step, slot, part].astype(F32)
            if step + 1 < others:
                share(path, step + 1, chunk, total)
            else:
                def finish(part):
                    piece[path, slot, part] = total(part, 0).astype(BF16)
                by_rows(rows, finish)
                store(path, chunk).start()
                gather(path, 0, chunk).start()

        def place(path, chunk, rows, row):
            return out.at[chunk, pl.ds(pl.multiple_of(row, rows), rows), pl.ds(path * width, width)]

        def store(path, chunk):
            slot = lax.rem(chunk, 4)
            return pltpu.make_async_copy(
                piece.at[path, slot], place(path, chunk, final_rows, seat_row(path, others)),
                store_sem.at[path, slot])

        def gather(path, step, chunk):
            slot = lax.rem(chunk, 4)
            rows = final_rows << step
            target = place(path, chunk, rows, seat_row(path, others - step))
            source = piece.at[path, slot] if step == 0 else target
            return remote(source, target, gather_send.at[path, step, slot],
                          gather_recv.at[path, step, slot], across(sides[path][step]))

        def gathered(path, step, chunk):
            copy = gather(path, step, chunk)
            copy.wait_recv()
            copy.wait_send()
            if step == 0:
                store(path, chunk).wait()
            if step + 1 < bits:
                gather(path, step + 1, chunk).start()

        lag_last = shards + others + bits
        rounds = units + lag_last + 2

        loads(0, lambda copy: copy.start())

        @pl.loop(0, rounds)
        def _(turn):
            on(turn + 1 < units, lambda: loads(turn + 1, lambda copy: copy.start()))
            on(turn < units, lambda: loads(turn, lambda copy: copy.wait()))
            for path in range(2):
                on(turn < units, lambda path=path: opening(path, turn))
            for path in range(2):
                on(valid(turn - 1), lambda path=path: first_sum(path, turn - 1))
            for path in range(2):
                for way in range(2):
                    chunk = turn - 1 - (here if way == 0 else shards - 1 - here)
                    on(valid(chunk - 2), lambda path=path, way=way, chunk=chunk: sent(path, way, chunk - 2))
                    on(valid(chunk), lambda path=path, way=way, chunk=chunk: onward(path, way, chunk))
            for path in range(2):
                on(valid(turn - shards), lambda path=path: last_hop(path, turn - shards))
            for step in range(others):
                for path in range(2):
                    chunk = turn - shards - 1 - step
                    on(valid(chunk), lambda path=path, step=step, chunk=chunk: rest_sum(path, step, chunk))
            for step in range(bits):
                for path in range(2):
                    chunk = turn - shards - others - 1 - step
                    on(valid(chunk), lambda path=path, step=step, chunk=chunk: gathered(path, step, chunk))

    if section is None:
        work()
    else:
        pl.when(sec == section)(work)


def exchange(pairs, shards, group, section, collective_id, unit_width, previous=None, unit_rows_max=256,
             name="exchange"):
    bits = group.bit_length() - 1
    lefts, rights = [p[0] for p in pairs], [p[1] for p in pairs]
    tokens = lefts[0].shape[0]
    rows_of = [a.shape[1] // shards for a in lefts]
    unit_rows = min([unit_rows_max] + rows_of)
    width = unit_width // 2
    inner = [g.shape[2] // unit_width for g in rights]
    seats = tuple(
        (r // unit_rows * g.shape[0] * k, g.shape[0] * k, k, r) for r, g, k in zip(rows_of, rights, inner))
    units = sum(seat[0] for seat in seats)
    half = unit_rows // 2
    others = bits - 1
    final_rows = unit_rows >> bits
    depth = shards + 3
    dma = pltpu.SemaphoreType.DMA
    scratch = [
        pltpu.VMEM((2, shards, tokens, unit_rows), BF16),
        pltpu.VMEM((2, tokens, unit_width), BF16),
        dma((2, shards)), dma((2,)),
        pltpu.VMEM((2, 2, shards, unit_rows, width), F32),
        pltpu.VMEM((2, 2, shards, half, width), BF16),
        pltpu.VMEM((2, 4, shards, half, width), BF16),
        pltpu.VMEM((2, shards + 2, shards, half, width), BF16),
        pltpu.VMEM((2, 2, depth + 1, shards, half, width), BF16),
        pltpu.VMEM((2, others, 4, half // 2, width), BF16),
        pltpu.VMEM((2, others, 4, half // 2, width), BF16),
        pltpu.VMEM((2, others, 4, half // 2, width), F32),
        pltpu.VMEM((2, 4, final_rows, width), BF16),
        dma((2, 4)), dma((2, 4)),
        dma((2, 2, depth, shards)), dma((2, 2, depth, shards)),
        dma((2, others, 4)), dma((2, others, 4)),
        dma((2, 4)),
        dma((2, bits, 4)), dma((2, bits, 4)),
    ]
    cfg = (shards, bits, seats, unit_rows, width, section, previous is not None)
    operands = lefts + rights + ([] if previous is None else [previous])
    return pl.pallas_call(
        functools.partial(exchange_kernel, cfg),
        out_shape=jax.ShapeDtypeStruct((units, unit_rows, unit_width), BF16),
        in_specs=[pl.BlockSpec(memory_space=pl.ANY)] * len(operands),
        out_specs=pl.BlockSpec(memory_space=pl.ANY),
        scratch_shapes=scratch,
        input_output_aliases={} if previous is None else {len(operands) - 1: 0},
        name=name,
        cost_estimate=pl.CostEstimate(
            flops=2 * tokens * units * shards * unit_rows * unit_width, bytes_accessed=100 * 2 ** 20,
            transcendentals=0),
        compiler_params=pltpu.CompilerParams(
            collective_id=collective_id, has_side_effects=True, vmem_limit_bytes=56 * 1024 * 1024),
    )(*operands)


def body(
    ends_in,
    lengths,
    norm_gain_a,
    norm_bias_a,
    w_qkv,
    w_out,
    norm_gain_f,
    norm_bias_f,
    w_gate_up,
    w_down,
):
    section = lax.axis_index("section")
    shards, group = lax.axis_size("shard"), lax.axis_size("group")
    is_first = section == 0
    first, second = ((section == which).astype(jnp.int32).reshape(1) for which in range(2))
    tokens, features = ends_in.shape[1:]
    size = features // HEADS
    rows = ends_in[0]
    weight_qkv, weight_out, weight_gu, weight_down = w_qkv[0], w_out[0], w_gate_up[0], w_down[0]
    parts = 4
    cosine, sine = tables(lengths, tokens // lengths.shape[0], size, HEADS // parts)

    def attend(active, values):
        return attention(active, lengths, values, norm_gain_a, norm_bias_a, weight_qkv, weight_out, cosine, sine, parts)

    def back(active, middle, low_a, qkv, mixture, values, grad):
        result, low_f, hidden, grad_gu, grad_middle, gain_f, bias_f = feed_both(
            active, middle, grad, norm_gain_f, norm_bias_f, weight_gu, weight_down)
        branch, grad_qkv, grad_in, grad_in_low, gain_a, bias_a = attention_back(
            active, lengths, grad_middle, values, norm_gain_a, qkv, weight_qkv, weight_out, cosine, sine, parts)
        pairs = [(hidden, grad[None]), (low_f, grad_gu), (mixture, branch[None]), (low_a, grad_qkv)]
        return result, grad_in, grad_in_low, pairs, jnp.concatenate([gain_a, bias_a, gain_f, bias_f], axis=0)

    middle_0, low_0, qkv_0, mixture_0 = attend(first, rows)
    passed = feed(first, middle_0, norm_gain_f, norm_bias_f, weight_gu, weight_down)
    arrived = lax.ppermute(passed, "section", [(0, 1)])
    middle_1, low_1, qkv_1, mixture_1 = attend(second, arrived)
    result, _, returned, pairs_1, vectors_1 = back(second, middle_1, low_1, qkv_1, mixture_1, arrived, rows)
    returned = lax.ppermute(returned, "section", [(1, 0)])
    summed = exchange(pairs_1, shards, group, 1, 1, features, name="exchange_second")
    _, grad_in, _, pairs_0, vectors_0 = back(first, middle_0, low_0, qkv_0, mixture_0, rows, returned)
    summed = exchange(pairs_0, shards, group, 0, 2, features, previous=summed, name="exchange_first")
    vectors = lax.psum(jnp.where(is_first, vectors_0, vectors_1), ("shard", "group"))
    part = features // shards
    vectors = lax.dynamic_slice(vectors, (0, lax.axis_index("shard") * part), (vectors.shape[0], part))
    ends_out = jnp.where(is_first, grad_in, result)[None]
    unit_rows = summed.shape[1]

    def shaped(start, count, blocks):
        picked = summed[start:start + count].astype(F32).reshape(count // blocks, blocks, unit_rows, features)
        return jnp.transpose(picked, (0, 2, 1, 3)).reshape(1, count // blocks * unit_rows, blocks * features)

    starts, counts, blocks = [0], [], []
    for left, right in pairs_0:
        blocks.append(right.shape[0] * right.shape[2] // features)
        counts.append(left.shape[1] // shards // unit_rows * blocks[-1])
        starts.append(starts[-1] + counts[-1])
    grad_down, grad_gate_up, grad_out, grad_qkv = (shaped(*seat) for seat in zip(starts, counts, blocks))
    return (
        ends_out,
        vectors[0:1],
        vectors[1:2],
        grad_qkv,
        grad_out,
        vectors[2:3],
        vectors[3:4],
        grad_gate_up,
        grad_down,
    )


def solution(mesh):
    placed = (
        P("section", ("shard", "group"), None),
        P(("shard", "group"), None),
        P("section", None),
        P("section", None),
        P("section", None, None),
        P("section", None, None),
        P("section", None),
        P("section", None),
        P("section", None, None),
        P("section", None, None),
    )
    return jax.shard_map(
        body,
        mesh=mesh,
        in_specs=placed,
        out_specs=(
            P("section", ("shard", "group"), None),
            P("section", "shard"),
            P("section", "shard"),
            P("section", "shard", None),
            P("section", "shard", None),
            P("section", "shard"),
            P("section", "shard"),
            P("section", "shard", None),
            P("section", "shard", None),
        ),
        check_vma=False,
    )
```

```python
import functools

import jax
import jax.numpy as jnp
from jax import lax
from jax.experimental import pallas as pl
from jax.experimental.pallas import tpu as pltpu
from jax.sharding import PartitionSpec as P

MESH = pl.DeviceIdType.MESH
F32, BF16 = jnp.float32, jnp.bfloat16
HEADS = 16
EPSILON = 1e-05


def dot(a, b):
    return jnp.dot(a, b, preferred_element_type=F32)


def dot_cols(a, b):
    return lax.dot_general(a, b, (((1,), (1,)), ((), ())), preferred_element_type=F32)


def dot_rows(a, b):
    return lax.dot_general(a, b, (((0,), (0,)), ((), ())), preferred_element_type=F32)


def in_rows(total, step, run):
    @pl.loop(0, total // step)
    def _(index):
        run(pl.ds(pl.multiple_of(index * step, step), step))


def normalized(values):
    average = jnp.mean(values, axis=-1, keepdims=True)
    centered = values - average
    variance = jnp.mean(centered * centered, axis=-1, keepdims=True)
    spread = lax.rsqrt(variance + EPSILON)
    return centered * spread, spread


def norm_back(grad, values, gain):
    unit, spread = normalized(values)
    scaled = grad * gain
    return spread * (
        scaled
        - jnp.mean(scaled, axis=-1, keepdims=True)
        - unit * jnp.mean(scaled * unit, axis=-1, keepdims=True)
    ), grad * unit


def lanes_of(shape):
    return lax.broadcasted_iota(jnp.int32, shape, len(shape) - 1)


def turn(values, half, size):
    wide = values.shape[-1]
    early = lax.rem(lanes_of(values.shape), size) < half
    return jnp.where(early, pltpu.roll(values, wide - half, 1), pltpu.roll(values, half, 1)), early


def rotated(values, cosine, sine, size):
    other, early = turn(values, size // 2, size)
    return values * cosine + jnp.where(early, -other, other) * sine


def unrotated(values, cosine, sine, size):
    other, early = turn(values * sine, size // 2, size)
    return values * cosine + jnp.where(early, other, -other)


def window_of(index, lengths_ref, row):
    windows = lengths_ref.shape[1]
    end = lengths_ref[row, 0]
    segment = (index >= end).astype(jnp.int32)
    for window in range(1, windows):
        end = end + lengths_ref[row, window]
        segment = segment + (index >= end).astype(jnp.int32)
    return segment


def same_window(lengths_ref, row, tokens):
    queries = window_of(lax.broadcasted_iota(jnp.int32, (tokens, 1), 0), lengths_ref, row)
    keys = window_of(lax.broadcasted_iota(jnp.int32, (1, tokens), 1), lengths_ref, row)
    return queries == keys


def softmax(scores, allowed):
    scores = jnp.where(allowed, scores, -1e30)
    weights = jnp.exp(scores - jnp.max(scores, axis=-1, keepdims=True))
    return weights * (1.0 / jnp.sum(weights, axis=-1, keepdims=True))


def attention_kernel(size, row_tokens, act_ref, lengths_ref, x_ref, gain_ref, bias_ref, wq_ref, wk_ref, wv_ref,
                     wo_ref, cos_ref, sin_ref, mid_ref, low_ref, qkv_ref, mix_ref):
    tokens = x_ref.shape[0]
    part = pl.program_id(0)
    block = wq_ref.shape[1]
    pair = 2 * size

    @pl.when(act_ref[0] == 1)
    def _():
        @pl.when(part == 0)
        def _():
            def begin(rows):
                values = x_ref[rows].astype(F32)
                unit, _ = normalized(values)
                low_ref[rows] = (unit * gain_ref[...] + bias_ref[...]).astype(BF16)
                mid_ref[rows] = values
            in_rows(tokens, 64, begin)

        def project(rows):
            low = low_ref[rows]
            cosine, sine = cos_ref[rows], sin_ref[rows]
            qkv_ref[0, rows] = rotated(dot(low, wq_ref[...]), cosine, sine, size).astype(BF16)
            qkv_ref[1, rows] = rotated(dot(low, wk_ref[...]), cosine, sine, size).astype(BF16)
            qkv_ref[2, rows] = dot(low, wv_ref[...]).astype(BF16)
        in_rows(tokens, row_tokens, project)

        @pl.loop(0, tokens // row_tokens)
        def _(row):
            rows = pl.ds(pl.multiple_of(row * row_tokens, row_tokens), row_tokens)
            allowed = same_window(lengths_ref, row, row_tokens)
            first = lanes_of((row_tokens, pair)) < size
            for at in range(block // pair):
                lanes = pl.ds(at * pair, pair)
                query, key, value = (qkv_ref[which, rows, lanes] for which in range(3))
                query = query * (size ** -0.5)
                results = []
                for head in range(2):
                    own = jnp.where(first if head == 0 else jnp.logical_not(first), query, jnp.zeros_like(query))
                    probs = softmax(dot_cols(own, key), allowed)
                    results.append(dot(probs.astype(BF16), value))
                mix_ref[rows, lanes] = jnp.where(first, results[0], results[1]).astype(BF16)

        def close(rows):
            mid_ref[rows] += dot(mix_ref[rows], wo_ref[...])
        in_rows(tokens, row_tokens, close)


def attention_back_kernel(size, row_tokens, act_ref, lengths_ref, grad_ref, x_ref, gain_ref, qkv_ref, wq_ref, wk_ref,
                          wv_ref, wo_ref, cos_ref, sin_ref, branch_ref, proj_ref, input_ref, input_low_ref,
                          dgain_ref, dbias_ref, gm_ref, total_ref):
    tokens = x_ref.shape[0]
    part = pl.program_id(0)
    block = wq_ref.shape[1]
    pair = 2 * size

    @pl.when(act_ref[0] == 1)
    def _():
        @pl.when(part == 0)
        def _():
            def begin(rows):
                branch_ref[rows] = grad_ref[rows].astype(BF16)
            in_rows(tokens, 64, begin)

        def mixture_grad(rows):
            gm_ref[rows] = dot_cols(branch_ref[rows], wo_ref[...]).astype(BF16)
        in_rows(tokens, row_tokens, mixture_grad)

        @pl.loop(0, tokens // row_tokens)
        def _(row):
            rows = pl.ds(pl.multiple_of(row * row_tokens, row_tokens), row_tokens)
            allowed = same_window(lengths_ref, row, row_tokens)
            first = lanes_of((row_tokens, pair)) < size
            for at in range(block // pair):
                lanes = pl.ds(at * pair, pair)
                query, key, value = (qkv_ref[which, rows, lanes] for which in range(3))
                grad_mix = gm_ref[rows, lanes]
                scaled = query * (size ** -0.5)
                results = []
                for head in range(2):
                    mine = first if head == 0 else jnp.logical_not(first)
                    probs = softmax(dot_cols(jnp.where(mine, scaled, jnp.zeros_like(scaled)), key), allowed)
                    grad_probs = dot_cols(jnp.where(mine, grad_mix, jnp.zeros_like(grad_mix)), value)
                    grad_value = dot_rows(probs.astype(BF16), grad_mix)
                    weighted = probs * grad_probs
                    grad_scores = (weighted - probs * jnp.sum(weighted, axis=-1, keepdims=True)).astype(BF16)
                    results.append((dot(grad_scores, key), dot_rows(grad_scores, query), grad_value))
                grad_query, grad_key, grad_value = (jnp.where(first, a, b) for a, b in zip(*results))
                cosine, sine = cos_ref[rows, lanes], sin_ref[rows, lanes]
                proj_ref[0, rows, lanes] = unrotated(grad_query * (size ** -0.5), cosine, sine, size).astype(BF16)
                proj_ref[1, rows, lanes] = unrotated(grad_key * (size ** -0.5), cosine, sine, size).astype(BF16)
                proj_ref[2, rows, lanes] = grad_value.astype(BF16)

        def normed_grad(rows):
            added = (
                dot_cols(proj_ref[0, rows], wq_ref[...])
                + dot_cols(proj_ref[1, rows], wk_ref[...])
                + dot_cols(proj_ref[2, rows], wv_ref[...])
            )
            total_ref[rows] = jnp.where(part == 0, added, total_ref[rows] + added)
        in_rows(tokens, row_tokens, normed_grad)

        @pl.when(part == pl.num_programs(0) - 1)
        def _():
            dgain_ref[...] = jnp.zeros_like(dgain_ref)
            dbias_ref[...] = jnp.zeros_like(dbias_ref)

            def finish(rows):
                grad = total_ref[rows]
                through, by_gain = norm_back(grad, x_ref[rows].astype(F32), gain_ref[...])
                result = grad_ref[rows] + through
                input_ref[rows] = result
                input_low_ref[rows] = result.astype(BF16)
                dgain_ref[...] += jnp.sum(by_gain, axis=0, keepdims=True)
                dbias_ref[...] += jnp.sum(grad, axis=0, keepdims=True)
            in_rows(tokens, 64, finish)


def feed_kernel(row_tokens, act_ref, mid_ref, gain_ref, bias_ref, wg_ref, wu_ref, wd_ref, out_ref, low_ref, total_ref):
    tokens = mid_ref.shape[0]
    part = pl.program_id(0)

    @pl.when(act_ref[0] == 1)
    def _():
        @pl.when(part == 0)
        def _():
            def begin(rows):
                values = mid_ref[rows]
                unit, _ = normalized(values)
                low_ref[rows] = (unit * gain_ref[...] + bias_ref[...]).astype(BF16)
                total_ref[rows] = values
            in_rows(tokens, 64, begin)

        def step(rows):
            low = low_ref[rows]
            gate = dot(low, wg_ref[...])
            up = dot(low, wu_ref[...])
            hidden = (gate / (1.0 + jnp.exp(-gate)) * up).astype(BF16)
            total_ref[rows] += dot(hidden, wd_ref[...])
        in_rows(tokens, row_tokens, step)

        @pl.when(part == pl.num_programs(0) - 1)
        def _():
            def finish(rows):
                out_ref[rows] = total_ref[rows].astype(BF16)
            in_rows(tokens, 64, finish)


def feed_both_kernel(row_tokens, act_ref, mid_ref, grad_ref, gain_ref, bias_ref, wg_ref, wu_ref, wd_ref, out_ref,
                     low_ref, hidden_ref, ggu_ref, grad_mid_ref, dgain_ref, dbias_ref, total_ref):
    tokens = mid_ref.shape[0]
    part = pl.program_id(0)

    @pl.when(act_ref[0] == 1)
    def _():
        @pl.when(part == 0)
        def _():
            def begin(rows):
                values = mid_ref[rows]
                unit, _ = normalized(values)
                low_ref[rows] = (unit * gain_ref[...] + bias_ref[...]).astype(BF16)
                out_ref[rows] = values
            in_rows(tokens, 64, begin)

        def step(rows):
            low = low_ref[rows]
            gate = dot(low, wg_ref[...])
            up = dot(low, wu_ref[...])
            sig = 1.0 / (1.0 + jnp.exp(-gate))
            silu = gate * sig
            hidden = (silu * up).astype(BF16)
            hidden_ref[rows] = hidden
            out_ref[rows] += dot(hidden, wd_ref[...])
            grad_hidden = dot_cols(grad_ref[rows], wd_ref[...])
            grad_gate = (grad_hidden * up * (sig * (1.0 + gate * (1.0 - sig)))).astype(BF16)
            grad_up = (grad_hidden * silu).astype(BF16)
            ggu_ref[0, rows] = grad_gate
            ggu_ref[1, rows] = grad_up
            added = dot_cols(grad_gate, wg_ref[...]) + dot_cols(grad_up, wu_ref[...])
            total_ref[rows] = jnp.where(part == 0, added, total_ref[rows] + added)
        in_rows(tokens, row_tokens, step)

        @pl.when(part == pl.num_programs(0) - 1)
        def _():
            dgain_ref[...] = jnp.zeros_like(dgain_ref)
            dbias_ref[...] = jnp.zeros_like(dbias_ref)

            def finish(rows):
                grad = total_ref[rows]
                through, by_gain = norm_back(grad, mid_ref[rows], gain_ref[...])
                grad_mid_ref[rows] = grad_ref[rows].astype(F32) + through
                dgain_ref[...] += jnp.sum(by_gain, axis=0, keepdims=True)
                dbias_ref[...] += jnp.sum(grad, axis=0, keepdims=True)
            in_rows(tokens, 64, finish)


def whole(shape):
    return pl.BlockSpec(shape, lambda part, *_: (0,) * len(shape))


def column(rows, wide, offset=0):
    return pl.BlockSpec((rows, wide), lambda part, act, *_: (0, (part + offset) * act[0]))


def stacked(count, rows, wide):
    return pl.BlockSpec((count, rows, wide), lambda part, act, *_: (0, 0, part * act[0]))


def lower(rows, wide):
    return pl.BlockSpec((rows, wide), lambda part, act, *_: (part * act[0], 0))


def local_call(kernel, name, grid, scalars, args, in_specs, outs, out_specs, scratch, flops, limit=56):
    return pl.pallas_call(
        kernel,
        grid_spec=pltpu.PrefetchScalarGridSpec(
            num_scalar_prefetch=len(scalars), grid=(grid,), in_specs=in_specs, out_specs=out_specs,
            scratch_shapes=scratch),
        out_shape=outs,
        name=name,
        cost_estimate=pl.CostEstimate(flops=flops, bytes_accessed=40 * 2 ** 20, transcendentals=0),
        compiler_params=pltpu.CompilerParams(
            dimension_semantics=("arbitrary",), vmem_limit_bytes=limit * 1024 * 1024),
    )(*scalars, *args)


def attention(active, lengths, x, gain, bias, w_qkv, w_out, cosine, sine, parts=4):
    tokens, features = x.shape
    row_tokens = tokens // lengths.shape[0]
    size = features // HEADS
    wide = features // parts
    return local_call(
        functools.partial(attention_kernel, size, row_tokens), "attention", parts, (active, lengths),
        (x, gain, bias, w_qkv, w_qkv, w_qkv, w_out, cosine, sine),
        [whole((tokens, features)), whole((1, features)), whole((1, features)), column(features, wide),
         column(features, wide, parts), column(features, wide, 2 * parts), lower(wide, features),
         whole((tokens, wide)), whole((tokens, wide))],
        (jax.ShapeDtypeStruct((tokens, features), F32), jax.ShapeDtypeStruct((tokens, features), BF16),
         jax.ShapeDtypeStruct((3, tokens, features), BF16), jax.ShapeDtypeStruct((tokens, features), BF16)),
        (whole((tokens, features)), whole((tokens, features)), stacked(3, tokens, wide), column(tokens, wide)),
        [], 8 * tokens * features ** 2)


def attention_back(active, lengths, grad_mid, x, gain, qkv, w_qkv, w_out, cosine, sine, parts=4):
    tokens, features = x.shape
    row_tokens = tokens // lengths.shape[0]
    size = features // HEADS
    wide = features // parts
    vector = jax.ShapeDtypeStruct((1, features), F32)
    return local_call(
        functools.partial(attention_back_kernel, size, row_tokens), "attention_back", parts, (active, lengths),
        (grad_mid, x, gain, qkv, w_qkv, w_qkv, w_qkv, w_out, cosine, sine),
        [whole((tokens, features)), whole((tokens, features)), whole((1, features)), stacked(3, tokens, wide),
         column(features, wide), column(features, wide, parts), column(features, wide, 2 * parts),
         lower(wide, features), whole((tokens, wide)), whole((tokens, wide))],
        (jax.ShapeDtypeStruct((tokens, features), BF16), jax.ShapeDtypeStruct((3, tokens, features), BF16),
         jax.ShapeDtypeStruct((tokens, features), F32), jax.ShapeDtypeStruct((tokens, features), BF16),
         vector, vector),
        (whole((tokens, features)), stacked(3, tokens, wide), whole((tokens, features)), whole((tokens, features)),
         whole((1, features)), whole((1, features))),
        [pltpu.VMEM((tokens, wide), BF16), pltpu.VMEM((tokens, features), F32)], 20 * tokens * features ** 2)


def feed(active, mid, gain, bias, w_gate_up, w_down, parts=8):
    tokens, features = mid.shape
    wide = w_down.shape[0] // parts
    return local_call(
        functools.partial(feed_kernel, tokens // 2), "feed", parts, (active,),
        (mid, gain, bias, w_gate_up, w_gate_up, w_down),
        [whole((tokens, features)), whole((1, features)), whole((1, features)), column(features, wide),
         column(features, wide, parts), lower(wide, features)],
        jax.ShapeDtypeStruct((tokens, features), BF16), whole((tokens, features)),
        [pltpu.VMEM((tokens, features), BF16), pltpu.VMEM((tokens, features), F32)],
        6 * tokens * features * w_down.shape[0])


def feed_both(active, mid, grad, gain, bias, w_gate_up, w_down, parts=8):
    tokens, features = mid.shape
    hidden = w_down.shape[0]
    wide = hidden // parts
    vector = jax.ShapeDtypeStruct((1, features), F32)
    return local_call(
        functools.partial(feed_both_kernel, tokens // 2), "feed_both", parts, (active,),
        (mid, grad, gain, bias, w_gate_up, w_gate_up, w_down),
        [whole((tokens, features)), whole((tokens, features)), whole((1, features)), whole((1, features)),
         column(features, wide), column(features, wide, parts), lower(wide, features)],
        (jax.ShapeDtypeStruct((tokens, features), F32), jax.ShapeDtypeStruct((tokens, features), BF16),
         jax.ShapeDtypeStruct((tokens, hidden), BF16), jax.ShapeDtypeStruct((2, tokens, hidden), BF16),
         jax.ShapeDtypeStruct((tokens, features), F32), vector, vector),
        (whole((tokens, features)), whole((tokens, features)), column(tokens, wide), stacked(2, tokens, wide),
         whole((tokens, features)), whole((1, features)), whole((1, features))),
        [pltpu.VMEM((tokens, features), F32)], 12 * tokens * features * hidden)


def tables(lengths, row_tokens, size, repeat):
    ends = jnp.cumsum(lengths, axis=-1)
    index = jnp.arange(row_tokens, dtype=jnp.int32)
    passed = index[:, None] >= ends[..., None, :]
    before = jnp.sum(jnp.where(passed, lengths[..., None, :], 0), axis=-1)
    position = (index - before).reshape(-1)
    frequency = 10000.0 ** (-2.0 * jnp.arange(size // 2, dtype=F32) / size)
    angles = position.astype(F32)[:, None] * frequency
    return jnp.tile(jnp.cos(angles), (1, 2 * repeat)), jnp.tile(jnp.sin(angles), (1, 2 * repeat))


def exchange_kernel(cfg, *refs):
    shards, bits, seats, unit_rows, width, section, aliased = cfg
    arrays = len(seats)
    lefts, rights = refs[:arrays], refs[arrays:2 * arrays]
    vector = refs[2 * arrays]
    refs = refs[2 * arrays + 1 + (arrays + 1 if aliased else 0):]
    outs, vector_out = refs[:arrays], refs[arrays]
    (vector_land, vector_sum, vector_send, vector_recv, vector_store, left, right, left_sem, right_sem, own, give, landed, mine, chain, rest_send, rest_land, rest_keep, piece,
     land_send, land_recv, chain_send, chain_recv,
     rest_ssem, rest_rsem, store_sem, gather_send, gather_recv) = refs[arrays + 1:]
    units = sum(seat[0] for seat in seats)
    half = unit_rows // 2
    others = bits - 1
    final_rows = unit_rows >> bits
    sec = lax.axis_index("section")
    here = lax.axis_index("shard")
    seat = lax.axis_index("group")

    def bit_of(index):
        return lax.rem(lax.div(seat, 1 << index), 2)

    def across(index):
        return (sec, here, seat + (1 - 2 * bit_of(index)) * (1 << index))

    above = (sec, jnp.minimum(here + 1, shards - 1), seat)
    below = (sec, jnp.maximum(here - 1, 0), seat)
    first = [path for path in range(2)]
    rest = [[index for index in range(bits) if index != path] for path in range(2)]
    sides = [rest[path][::-1] + [first[path]] for path in range(2)]

    def remote(source, target, send, recv, device):
        return pltpu.make_async_remote_copy(
            src_ref=source, dst_ref=target, send_sem=send, recv_sem=recv,
            device_id=device, device_id_type=MESH,
        )

    def seat_row(path, depth):
        row = bit_of(first[path]) * half
        for step in range(depth):
            row = row + bit_of(rest[path][step]) * (half >> (step + 1))
        return row

    group = 1 << bits
    peers = shards * group
    me = here * group + seat
    part = vector_out.shape[1]

    def peer(step):
        index = lax.rem(me + step, peers)
        return index, (sec, lax.div(index, group), lax.rem(index, group))

    def vector_copy(index, device):
        lanes = pl.ds(pl.multiple_of(device[1] * part, part), part)
        return remote(vector.at[:, lanes], vector_land.at[me], vector_send.at[index], vector_recv.at[me], device)

    def vector_finish():
        vector_sum[...] = vector[:, pl.ds(pl.multiple_of(here * part, part), part)]

        @pl.loop(1, peers)
        def _(step):
            index, device = peer(step)
            vector_copy(index, device).wait_send()
            remote(vector_land.at[index], vector_land.at[index], vector_send.at[index], vector_recv.at[index],
                   device).wait_recv()
            vector_sum[...] += vector_land[index]
        copy = pltpu.make_async_copy(vector_sum, vector_out, vector_store)
        copy.start()
        copy.wait()

    def valid(chunk):
        return (chunk >= 0) & (chunk < units)

    def on(condition, run):
        pl.when(condition)(run)

    def by_rows(rows, run, tall=32):
        step = min(rows, tall)

        @pl.loop(0, rows // step)
        def _(index):
            run(pl.ds(pl.multiple_of(index * step, step), step))

    def shifted(part, offset):
        return pl.ds(pl.multiple_of(part.start + offset, part.size), part.size)

    def work():
        barrier = pltpu.get_barrier_semaphore()

        @pl.loop(1, peers)
        def _(step):
            pl.semaphore_signal(barrier, inc=1, device_id=peer(step)[1], device_id_type=MESH)
        pl.semaphore_wait(barrier, peers - 1)

        @pl.loop(1, peers)
        def _(step):
            vector_copy(*peer(step)).start()

        for path in range(2):
            for way in range(2):
                @pl.loop(0, shards)
                def _(block):
                    def clear(rows):
                        chain[path, way, chain.shape[2] - 1, block, rows] = jnp.zeros((rows.size, width), BF16)
                    by_rows(half, clear)

        def loads(chunk, run):
            slot, start = lax.rem(chunk, 2), 0
            for which, (count, blocks, inner, rows) in enumerate(seats):
                def each(which=which, start=start, blocks=blocks, inner=inner, rows=rows):
                    local = chunk - start
                    row = lax.div(local, blocks)
                    block = local - row * blocks
                    outer = lax.div(block, inner)
                    column = pl.multiple_of((block - outer * inner) * (2 * width), 2 * width)
                    run(pltpu.make_async_copy(
                        rights[which].at[outer, :, pl.ds(column, 2 * width)], right.at[slot], right_sem.at[slot]))
                    for shard in range(shards):
                        offset = pl.multiple_of(shard * rows + row * unit_rows, unit_rows)
                        run(pltpu.make_async_copy(
                            lefts[which].at[:, pl.ds(offset, unit_rows)], left.at[slot, shard],
                            left_sem.at[slot, shard]))
                on((chunk >= start) & (chunk < start + count), each)
                start += count

        def first_copy(path, chunk):
            two, four = lax.rem(chunk, 2), lax.rem(chunk, 4)
            return remote(give.at[path, two], landed.at[path, four], land_send.at[path, four],
                          land_recv.at[path, four], across(first[path]))

        def opening(path, chunk):
            two = lax.rem(chunk, 2)
            away = (1 - bit_of(first[path])) * half

            @pl.loop(0, shards)
            def _(block):
                own[path, two, block] = lax.dot_general(
                    left[two, block], right[two, :, path * width:(path + 1) * width],
                    (((0,), (0,)), ((), ())), preferred_element_type=F32)

                def round_off(rows):
                    give[path, two, block, rows] = own[path, two, block, shifted(rows, away)].astype(BF16)
                by_rows(half, round_off)
            first_copy(path, chunk).start()

        def first_sum(path, chunk):
            slot, two, four = lax.rem(chunk, shards + 2), lax.rem(chunk, 2), lax.rem(chunk, 4)
            copy = first_copy(path, chunk)
            copy.wait_recv()
            copy.wait_send()
            kept = bit_of(first[path]) * half

            @pl.loop(0, shards)
            def _(block):
                def add(rows):
                    mine[path, slot, block, rows] = (
                        own[path, two, block, shifted(rows, kept)] + landed[path, four, block, rows].astype(F32)
                    ).astype(BF16)
                by_rows(half, add)

        depth = chain.shape[2] - 1

        def hop(path, way, chunk, block):
            slot = lax.rem(chunk, depth)
            ref = chain.at[path, way, slot, block]
            return remote(ref, ref, chain_send.at[path, way, slot, block],
                          chain_recv.at[path, way, slot, block], above if way == 0 else below)

        def onward(path, way, chunk):
            slot, base = lax.rem(chunk, depth), lax.rem(chunk, shards + 2)
            arrives = here > 0 if way == 0 else here < shards - 1

            @pl.loop(0, shards - 1 - here if way == 0 else here)
            def _(index):
                block = shards - 1 - index if way == 0 else index
                copy = hop(path, way, chunk, block)
                on(arrives, lambda: copy.wait_recv())
                source = jnp.where(arrives, slot, depth)

                def add(rows):
                    chain[path, way, slot, block, rows] = (
                        chain[path, way, source, block, rows].astype(F32) + mine[path, base, block, rows].astype(F32)
                    ).astype(BF16)
                by_rows(half, add)
                copy.start()

        def sent(path, way, chunk):
            @pl.loop(0, shards - 1 - here if way == 0 else here)
            def _(index):
                hop(path, way, chunk, shards - 1 - index if way == 0 else index).wait_send()

        def rest_rows(step):
            return half >> (step + 1)

        def rest_copy(path, step, chunk):
            slot = lax.rem(chunk, 4)
            rows = pl.ds(0, rest_rows(step))
            return remote(rest_send.at[path, step, slot, rows], rest_land.at[path, step, slot, rows],
                          rest_ssem.at[path, step, slot], rest_rsem.at[path, step, slot],
                          across(rest[path][step]))

        def share(path, step, chunk, total):
            slot, rows = lax.rem(chunk, 4), rest_rows(step)
            bit = bit_of(rest[path][step])

            def give(part):
                rest_send[path, step, slot, part] = total(part, (1 - bit) * rows).astype(BF16)
            by_rows(rows, give)
            rest_copy(path, step, chunk).start()

            def keep(part):
                rest_keep[path, step, slot, part] = total(part, bit * rows)
            by_rows(rows, keep)

        def last_hop(path, chunk):
            base, slot = lax.rem(chunk, shards + 2), lax.rem(chunk, depth)
            on(here > 0, lambda: hop(path, 0, chunk, here).wait_recv())
            on(here < shards - 1, lambda: hop(path, 1, chunk, here).wait_recv())
            from_below = jnp.where(here > 0, slot, depth)
            from_above = jnp.where(here < shards - 1, slot, depth)

            def total(part, offset):
                rows = shifted(part, offset)
                return (
                    mine[path, base, here, rows].astype(F32)
                    + chain[path, 0, from_below, here, rows].astype(F32)
                    + chain[path, 1, from_above, here, rows].astype(F32)
                )
            share(path, 0, chunk, total)

        def rest_sum(path, step, chunk):
            slot, rows = lax.rem(chunk, 4), rest_rows(step)
            copy = rest_copy(path, step, chunk)
            copy.wait_recv()
            copy.wait_send()

            def total(part, offset):
                part = shifted(part, offset)
                return rest_keep[path, step, slot, part] + rest_land[path, step, slot, part].astype(F32)
            if step + 1 < others:
                share(path, step + 1, chunk, total)
            else:
                def finish(part):
                    piece[path, slot, part] = total(part, 0).astype(BF16)
                by_rows(rows, finish)
                spread(path, 0, chunk)

        def placed(path, chunk, rows, row, run):
            start = 0
            for which, (count, blocks, _, _) in enumerate(seats):
                def each(which=which, start=start, blocks=blocks):
                    local = chunk - start
                    outer = lax.div(local, blocks)
                    column = (local - outer * blocks) * (2 * width) + path * width
                    run(outs[which].at[
                        pl.ds(pl.multiple_of(outer * unit_rows + row, rows), rows),
                        pl.ds(pl.multiple_of(column, width), width)])
                on((chunk >= start) & (chunk < start + count), each)
                start += count

        def any_place(rows):
            return outs[0].at[pl.ds(0, rows), pl.ds(0, width)]

        def store(path, chunk, target):
            slot = lax.rem(chunk, 4)
            return pltpu.make_async_copy(piece.at[path, slot], target, store_sem.at[path, slot])

        def gather(path, step, chunk, target):
            slot = lax.rem(chunk, 4)
            source = piece.at[path, slot] if step == 0 else target
            return remote(source, target, gather_send.at[path, step, slot],
                          gather_recv.at[path, step, slot], across(sides[path][step]))

        def spread(path, step, chunk):
            def launch(target):
                if step == 0:
                    store(path, chunk, target).start()
                gather(path, step, chunk, target).start()
            placed(path, chunk, final_rows << step, seat_row(path, others - step), launch)

        def gathered(path, step, chunk):
            target = any_place(final_rows << step)
            copy = gather(path, step, chunk, target)
            copy.wait_recv()
            copy.wait_send()
            if step == 0:
                store(path, chunk, target).wait()
            if step + 1 < bits:
                spread(path, step + 1, chunk)

        lag_last = shards + others + bits
        rounds = units + lag_last + 2

        loads(0, lambda copy: copy.start())

        @pl.loop(0, rounds)
        def _(turn):
            on(turn + 1 < units, lambda: loads(turn + 1, lambda copy: copy.start()))
            on(turn < units, lambda: loads(turn, lambda copy: copy.wait()))
            for path in range(2):
                on(turn < units, lambda path=path: opening(path, turn))
            for path in range(2):
                on(valid(turn - 1), lambda path=path: first_sum(path, turn - 1))
            for path in range(2):
                for way in range(2):
                    chunk = turn - 1 - (here if way == 0 else shards - 1 - here)
                    on(valid(chunk - 2), lambda path=path, way=way, chunk=chunk: sent(path, way, chunk - 2))
                    on(valid(chunk), lambda path=path, way=way, chunk=chunk: onward(path, way, chunk))
            for path in range(2):
                on(valid(turn - shards), lambda path=path: last_hop(path, turn - shards))
            for step in range(others):
                for path in range(2):
                    chunk = turn - shards - 1 - step
                    on(valid(chunk), lambda path=path, step=step, chunk=chunk: rest_sum(path, step, chunk))
            for step in range(bits):
                for path in range(2):
                    chunk = turn - shards - others - 1 - step
                    on(valid(chunk), lambda path=path, step=step, chunk=chunk: gathered(path, step, chunk))

        vector_finish()

    if section is None:
        work()
    else:
        pl.when(sec == section)(work)


def exchange(pairs, vector, shards, group, section, collective_id, unit_width, previous=None, unit_rows_max=256,
             name="exchange"):
    bits = group.bit_length() - 1
    lefts, rights = [p[0] for p in pairs], [p[1] for p in pairs]
    tokens = lefts[0].shape[0]
    rows_of = [a.shape[1] // shards for a in lefts]
    unit_rows = min([unit_rows_max] + rows_of)
    width = unit_width // 2
    inner = [g.shape[2] // unit_width for g in rights]
    seats = tuple(
        (r // unit_rows * g.shape[0] * k, g.shape[0] * k, k, r) for r, g, k in zip(rows_of, rights, inner))
    units = sum(seat[0] for seat in seats)
    half = unit_rows // 2
    others = bits - 1
    final_rows = unit_rows >> bits
    depth = shards + 3
    dma = pltpu.SemaphoreType.DMA
    peers = shards * group
    lanes = vector.shape[1] // shards
    scratch = [
        pltpu.VMEM((peers, vector.shape[0], lanes), F32),
        pltpu.VMEM((vector.shape[0], lanes), F32),
        dma((peers,)), dma((peers,)), dma,
        pltpu.VMEM((2, shards, tokens, unit_rows), BF16),
        pltpu.VMEM((2, tokens, unit_width), BF16),
        dma((2, shards)), dma((2,)),
        pltpu.VMEM((2, 2, shards, unit_rows, width), F32),
        pltpu.VMEM((2, 2, shards, half, width), BF16),
        pltpu.VMEM((2, 4, shards, half, width), BF16),
        pltpu.VMEM((2, shards + 2, shards, half, width), BF16),
        pltpu.VMEM((2, 2, depth + 1, shards, half, width), BF16),
        pltpu.VMEM((2, others, 4, half // 2, width), BF16),
        pltpu.VMEM((2, others, 4, half // 2, width), BF16),
        pltpu.VMEM((2, others, 4, half // 2, width), F32),
        pltpu.VMEM((2, 4, final_rows, width), BF16),
        dma((2, 4)), dma((2, 4)),
        dma((2, 2, depth, shards)), dma((2, 2, depth, shards)),
        dma((2, others, 4)), dma((2, others, 4)),
        dma((2, 4)),
        dma((2, bits, 4)), dma((2, bits, 4)),
    ]
    cfg = (shards, bits, seats, unit_rows, width, section, previous is not None)
    operands = lefts + rights + [vector] + list(previous or [])
    first = 2 * len(pairs) + 1
    results = [jax.ShapeDtypeStruct((r, g.shape[0] * g.shape[2]), BF16) for r, g in zip(rows_of, rights)]
    results.append(jax.ShapeDtypeStruct((vector.shape[0], lanes), F32))
    hbm, vmem = pl.BlockSpec(memory_space=pl.ANY), pl.BlockSpec(memory_space=pltpu.VMEM)
    in_specs = [vmem if index == first - 1 else hbm for index in range(len(operands))]
    return pl.pallas_call(
        functools.partial(exchange_kernel, cfg),
        out_shape=results,
        in_specs=in_specs,
        out_specs=[hbm] * len(results),
        scratch_shapes=scratch,
        input_output_aliases={first + index: index for index in range(len(previous or []))},
        name=name,
        cost_estimate=pl.CostEstimate(
            flops=2 * tokens * units * shards * unit_rows * unit_width, bytes_accessed=100 * 2 ** 20,
            transcendentals=0),
        compiler_params=pltpu.CompilerParams(
            collective_id=collective_id, has_side_effects=True, vmem_limit_bytes=56 * 1024 * 1024),
    )(*operands)


def body(
    ends_in,
    lengths,
    norm_gain_a,
    norm_bias_a,
    w_qkv,
    w_out,
    norm_gain_f,
    norm_bias_f,
    w_gate_up,
    w_down,
):
    section = lax.axis_index("section")
    shards, group = lax.axis_size("shard"), lax.axis_size("group")
    is_first = section == 0
    first, second = ((section == which).astype(jnp.int32).reshape(1) for which in range(2))
    tokens, features = ends_in.shape[1:]
    size = features // HEADS
    rows = ends_in[0]
    weight_qkv, weight_out, weight_gu, weight_down = w_qkv[0], w_out[0], w_gate_up[0], w_down[0]
    parts = 4
    cosine, sine = tables(lengths, tokens // lengths.shape[0], size, HEADS // parts)

    def attend(active, values):
        return attention(active, lengths, values, norm_gain_a, norm_bias_a, weight_qkv, weight_out, cosine, sine, parts)

    def back(active, middle, low_a, qkv, mixture, values, grad):
        result, low_f, hidden, grad_gu, grad_middle, gain_f, bias_f = feed_both(
            active, middle, grad, norm_gain_f, norm_bias_f, weight_gu, weight_down)
        branch, grad_qkv, grad_in, grad_in_low, gain_a, bias_a = attention_back(
            active, lengths, grad_middle, values, norm_gain_a, qkv, weight_qkv, weight_out, cosine, sine, parts)
        pairs = [(hidden, grad[None]), (low_f, grad_gu), (mixture, branch[None]), (low_a, grad_qkv)]
        vectors = jnp.concatenate([gain_a, bias_a, gain_f, bias_f, jnp.zeros((4, features), F32)], axis=0)
        return result, grad_in, grad_in_low, pairs, vectors

    middle_0, low_0, qkv_0, mixture_0 = attend(first, rows)
    passed = feed(first, middle_0, norm_gain_f, norm_bias_f, weight_gu, weight_down)
    arrived = lax.ppermute(passed, "section", [(0, 1)])
    middle_1, low_1, qkv_1, mixture_1 = attend(second, arrived)
    result, _, returned, pairs_1, vectors_1 = back(second, middle_1, low_1, qkv_1, mixture_1, arrived, rows)
    returned = lax.ppermute(returned, "section", [(1, 0)])
    summed = exchange(pairs_1, vectors_1, shards, group, 1, 1, features, name="exchange_second")
    _, grad_in, _, pairs_0, vectors_0 = back(first, middle_0, low_0, qkv_0, mixture_0, rows, returned)
    summed = exchange(pairs_0, vectors_0, shards, group, 0, 2, features, previous=summed, name="exchange_first")
    ends_out = jnp.where(is_first, grad_in, result)[None]
    grad_down, grad_gate_up, grad_out, grad_qkv = (item.astype(F32)[None] for item in summed[:4])
    vectors = summed[4]
    return (
        ends_out,
        vectors[0:1],
        vectors[1:2],
        grad_qkv,
        grad_out,
        vectors[2:3],
        vectors[3:4],
        grad_gate_up,
        grad_down,
    )


def solution(mesh):
    placed = (
        P("section", ("shard", "group"), None),
        P(("shard", "group"), None),
        P("section", None),
        P("section", None),
        P("section", None, None),
        P("section", None, None),
        P("section", None),
        P("section", None),
        P("section", None, None),
        P("section", None, None),
    )
    return jax.shard_map(
        body,
        mesh=mesh,
        in_specs=placed,
        out_specs=(
            P("section", ("shard", "group"), None),
            P("section", "shard"),
            P("section", "shard"),
            P("section", "shard", None),
            P("section", "shard", None),
            P("section", "shard"),
            P("section", "shard"),
            P("section", "shard", None),
            P("section", "shard", None),
        ),
        check_vma=False,
    )
```

```python
import functools

import jax
import jax.numpy as jnp
from jax import lax
from jax.experimental import pallas as pl
from jax.experimental.pallas import tpu as pltpu
from jax.sharding import PartitionSpec as P

MESH = pl.DeviceIdType.MESH
F32, BF16 = jnp.float32, jnp.bfloat16
HEADS = 16
EPSILON = 1e-05


def dot(a, b):
    return jnp.dot(a, b, preferred_element_type=F32)


def dot_cols(a, b):
    return lax.dot_general(a, b, (((1,), (1,)), ((), ())), preferred_element_type=F32)


def dot_rows(a, b):
    return lax.dot_general(a, b, (((0,), (0,)), ((), ())), preferred_element_type=F32)


def in_rows(total, step, run):
    @pl.loop(0, total // step)
    def _(index):
        run(pl.ds(pl.multiple_of(index * step, step), step))


def normalized(values):
    average = jnp.mean(values, axis=-1, keepdims=True)
    centered = values - average
    variance = jnp.mean(centered * centered, axis=-1, keepdims=True)
    spread = lax.rsqrt(variance + EPSILON)
    return centered * spread, spread


def norm_back(grad, values, gain):
    unit, spread = normalized(values)
    scaled = grad * gain
    return spread * (
        scaled
        - jnp.mean(scaled, axis=-1, keepdims=True)
        - unit * jnp.mean(scaled * unit, axis=-1, keepdims=True)
    ), grad * unit


def lanes_of(shape):
    return lax.broadcasted_iota(jnp.int32, shape, len(shape) - 1)


def turn(values, half, size):
    wide = values.shape[-1]
    early = lax.rem(lanes_of(values.shape), size) < half
    return jnp.where(early, pltpu.roll(values, wide - half, 1), pltpu.roll(values, half, 1)), early


def rotated(values, cosine, sine, size):
    other, early = turn(values, size // 2, size)
    return values * cosine + jnp.where(early, -other, other) * sine


def unrotated(values, cosine, sine, size):
    other, early = turn(values * sine, size // 2, size)
    return values * cosine + jnp.where(early, other, -other)


def window_of(index, lengths_ref, row):
    windows = lengths_ref.shape[1]
    end = lengths_ref[row, 0]
    segment = (index >= end).astype(jnp.int32)
    for window in range(1, windows):
        end = end + lengths_ref[row, window]
        segment = segment + (index >= end).astype(jnp.int32)
    return segment


def same_window(lengths_ref, row, tokens):
    queries = window_of(lax.broadcasted_iota(jnp.int32, (tokens, 1), 0), lengths_ref, row)
    keys = window_of(lax.broadcasted_iota(jnp.int32, (1, tokens), 1), lengths_ref, row)
    return queries == keys


def softmax(scores, allowed):
    scores = jnp.where(allowed, scores, -1e30)
    weights = jnp.exp(scores - jnp.max(scores, axis=-1, keepdims=True))
    return weights * (1.0 / jnp.sum(weights, axis=-1, keepdims=True))


def attention_kernel(size, row_tokens, act_ref, lengths_ref, x_ref, gain_ref, bias_ref, wq_ref, wk_ref, wv_ref,
                     wo_ref, cos_ref, sin_ref, mid_ref, low_ref, qkv_ref, mix_ref):
    tokens = x_ref.shape[0]
    part = pl.program_id(0)
    block = wq_ref.shape[1]
    pair = 2 * size

    @pl.when(act_ref[0] == 1)
    def _():
        @pl.when(part == 0)
        def _():
            def begin(rows):
                values = x_ref[rows].astype(F32)
                unit, _ = normalized(values)
                low_ref[rows] = (unit * gain_ref[...] + bias_ref[...]).astype(BF16)
                mid_ref[rows] = values
            in_rows(tokens, 64, begin)

        for which, weight in enumerate((wq_ref, wk_ref, wv_ref)):
            projected = dot(low_ref[...], weight[...])
            for at in range(block // pair):
                lanes = slice(at * pair, (at + 1) * pair)
                values = projected[:, lanes]
                if which < 2:
                    values = rotated(values, cos_ref[...], sin_ref[...], size)
                qkv_ref[which, :, lanes] = values.astype(BF16)

        first = lanes_of((row_tokens, pair)) < size
        for row in range(tokens // row_tokens):
            rows = pl.ds(row * row_tokens, row_tokens)
            allowed = same_window(lengths_ref, row, row_tokens)
            for start in range(0, block // pair, 2):
                work = []
                for at in range(start, start + 2):
                    lanes = pl.ds(at * pair, pair)
                    query, key, value = (qkv_ref[which, rows, lanes] for which in range(3))
                    query = query * (size ** -0.5)
                    for head in range(2):
                        own = jnp.where(first if head == 0 else jnp.logical_not(first), query, jnp.zeros_like(query))
                        work.append((dot_cols(own, key), value))
                work = [(softmax(scores, allowed).astype(BF16), value) for scores, value in work]
                work = [dot(probs, value) for probs, value in work]
                for at in range(2):
                    lanes = pl.ds((start + at) * pair, pair)
                    mix_ref[rows, lanes] = jnp.where(first, work[2 * at], work[2 * at + 1]).astype(BF16)

        mid_ref[...] += dot(mix_ref[...], wo_ref[...])


def attention_back_kernel(size, row_tokens, act_ref, lengths_ref, grad_ref, x_ref, gain_ref, qkv_ref, wq_ref, wk_ref,
                          wv_ref, wo_ref, cos_ref, sin_ref, branch_ref, proj_ref, input_ref, input_low_ref,
                          dgain_ref, dbias_ref, gm_ref, total_ref):
    tokens = x_ref.shape[0]
    part = pl.program_id(0)
    block = wq_ref.shape[1]
    pair = 2 * size
    scale = size ** -0.5

    @pl.when(act_ref[0] == 1)
    def _():
        @pl.when(part == 0)
        def _():
            def begin(rows):
                branch_ref[rows] = grad_ref[rows].astype(BF16)
            in_rows(tokens, 64, begin)

        gm_ref[...] = dot_cols(branch_ref[...], wo_ref[...]).astype(BF16)
        first = lanes_of((row_tokens, pair)) < size
        for row in range(tokens // row_tokens):
            rows = pl.ds(row * row_tokens, row_tokens)
            allowed = same_window(lengths_ref, row, row_tokens)
            cosine, sine = cos_ref[rows], sin_ref[rows]
            for start in range(0, block // pair, 2):
                work = []
                for at in range(start, start + 2):
                    lanes = pl.ds(at * pair, pair)
                    query, key, value = (qkv_ref[which, rows, lanes] for which in range(3))
                    grad_mix = gm_ref[rows, lanes]
                    scaled = query * scale
                    for head in range(2):
                        mine = first if head == 0 else jnp.logical_not(first)
                        work.append((
                            query, key, grad_mix,
                            dot_cols(jnp.where(mine, scaled, jnp.zeros_like(scaled)), key),
                            dot_cols(jnp.where(mine, grad_mix, jnp.zeros_like(grad_mix)), value)))
                results = []
                for query, key, grad_mix, scores, grad_probs in work:
                    probs = softmax(scores, allowed)
                    weighted = probs * grad_probs
                    grad_scores = (weighted - probs * jnp.sum(weighted, axis=-1, keepdims=True)).astype(BF16)
                    results.append((query, key, grad_mix, grad_scores, probs.astype(BF16)))
                results = [
                    (dot(grad_scores, key), dot_rows(grad_scores, query), dot_rows(probs, grad_mix))
                    for query, key, grad_mix, grad_scores, probs in results]
                for at in range(2):
                    lanes = pl.ds((start + at) * pair, pair)
                    grad_query, grad_key, grad_value = (
                        jnp.where(first, a, b) for a, b in zip(results[2 * at], results[2 * at + 1]))
                    proj_ref[0, rows, lanes] = unrotated(grad_query * scale, cosine, sine, size).astype(BF16)
                    proj_ref[1, rows, lanes] = unrotated(grad_key * scale, cosine, sine, size).astype(BF16)
                    proj_ref[2, rows, lanes] = grad_value.astype(BF16)

        added = (
            dot_cols(proj_ref[0], wq_ref[...])
            + dot_cols(proj_ref[1], wk_ref[...])
            + dot_cols(proj_ref[2], wv_ref[...])
        )
        total_ref[...] = jnp.where(part == 0, added, total_ref[...] + added)

        @pl.when(part == pl.num_programs(0) - 1)
        def _():
            dgain_ref[...] = jnp.zeros_like(dgain_ref)
            dbias_ref[...] = jnp.zeros_like(dbias_ref)

            def finish(rows):
                grad = total_ref[rows]
                through, by_gain = norm_back(grad, x_ref[rows].astype(F32), gain_ref[...])
                result = grad_ref[rows] + through
                input_ref[rows] = result
                input_low_ref[rows] = result.astype(BF16)
                dgain_ref[...] += jnp.sum(by_gain, axis=0, keepdims=True)
                dbias_ref[...] += jnp.sum(grad, axis=0, keepdims=True)
            in_rows(tokens, 64, finish)


def feed_kernel(act_ref, mid_ref, gain_ref, bias_ref, wg_ref, wu_ref, wd_ref, out_ref, low_ref, total_ref):
    tokens = mid_ref.shape[0]
    part = pl.program_id(0)

    @pl.when(act_ref[0] == 1)
    def _():
        @pl.when(part == 0)
        def _():
            def begin(rows):
                values = mid_ref[rows]
                unit, _ = normalized(values)
                low_ref[rows] = (unit * gain_ref[...] + bias_ref[...]).astype(BF16)
                total_ref[rows] = values
            in_rows(tokens, 64, begin)

        low = low_ref[...]
        gate = dot(low, wg_ref[...])
        up = dot(low, wu_ref[...])
        hidden = (gate / (1.0 + jnp.exp(-gate)) * up).astype(BF16)
        total_ref[...] += dot(hidden, wd_ref[...])

        @pl.when(part == pl.num_programs(0) - 1)
        def _():
            def finish(rows):
                out_ref[rows] = total_ref[rows].astype(BF16)
            in_rows(tokens, 64, finish)


def feed_both_kernel(act_ref, mid_ref, grad_ref, gain_ref, bias_ref, wg_ref, wu_ref, wd_ref, out_ref,
                     low_ref, hidden_ref, ggu_ref, grad_mid_ref, dgain_ref, dbias_ref, total_ref):
    tokens = mid_ref.shape[0]
    part = pl.program_id(0)

    @pl.when(act_ref[0] == 1)
    def _():
        @pl.when(part == 0)
        def _():
            def begin(rows):
                values = mid_ref[rows]
                unit, _ = normalized(values)
                low_ref[rows] = (unit * gain_ref[...] + bias_ref[...]).astype(BF16)
                out_ref[rows] = values
            in_rows(tokens, 64, begin)

        low = low_ref[...]
        gate = dot(low, wg_ref[...])
        up = dot(low, wu_ref[...])
        grad_hidden = dot_cols(grad_ref[...], wd_ref[...])
        sig = 1.0 / (1.0 + jnp.exp(-gate))
        silu = gate * sig
        hidden_ref[...] = (silu * up).astype(BF16)
        ggu_ref[0] = (grad_hidden * up * (sig * (1.0 + gate * (1.0 - sig)))).astype(BF16)
        ggu_ref[1] = (grad_hidden * silu).astype(BF16)
        out_ref[...] += dot(hidden_ref[...], wd_ref[...])
        added = dot_cols(ggu_ref[0], wg_ref[...]) + dot_cols(ggu_ref[1], wu_ref[...])
        total_ref[...] = jnp.where(part == 0, added, total_ref[...] + added)

        @pl.when(part == pl.num_programs(0) - 1)
        def _():
            dgain_ref[...] = jnp.zeros_like(dgain_ref)
            dbias_ref[...] = jnp.zeros_like(dbias_ref)

            def finish(rows):
                grad = total_ref[rows]
                through, by_gain = norm_back(grad, mid_ref[rows], gain_ref[...])
                grad_mid_ref[rows] = grad_ref[rows].astype(F32) + through
                dgain_ref[...] += jnp.sum(by_gain, axis=0, keepdims=True)
                dbias_ref[...] += jnp.sum(grad, axis=0, keepdims=True)
            in_rows(tokens, 64, finish)


def whole(shape):
    return pl.BlockSpec(shape, lambda part, *_: (0,) * len(shape))


def column(rows, wide, offset=0):
    return pl.BlockSpec((rows, wide), lambda part, act, *_: (0, (part + offset) * act[0]))


def stacked(count, rows, wide):
    return pl.BlockSpec((count, rows, wide), lambda part, act, *_: (0, 0, part * act[0]))


def lower(rows, wide):
    return pl.BlockSpec((rows, wide), lambda part, act, *_: (part * act[0], 0))


def local_call(kernel, name, grid, scalars, args, in_specs, outs, out_specs, scratch, flops, limit=56):
    return pl.pallas_call(
        kernel,
        grid_spec=pltpu.PrefetchScalarGridSpec(
            num_scalar_prefetch=len(scalars), grid=(grid,), in_specs=in_specs, out_specs=out_specs,
            scratch_shapes=scratch),
        out_shape=outs,
        name=name,
        cost_estimate=pl.CostEstimate(flops=flops, bytes_accessed=40 * 2 ** 20, transcendentals=0),
        compiler_params=pltpu.CompilerParams(
            dimension_semantics=("arbitrary",), vmem_limit_bytes=limit * 1024 * 1024),
    )(*scalars, *args)


def attention(active, lengths, x, gain, bias, w_qkv, w_out, cosine, sine, parts=2):
    tokens, features = x.shape
    row_tokens = tokens // lengths.shape[0]
    size = features // HEADS
    wide = features // parts
    return local_call(
        functools.partial(attention_kernel, size, row_tokens), "attention", parts, (active, lengths),
        (x, gain, bias, w_qkv, w_qkv, w_qkv, w_out, cosine, sine),
        [whole((tokens, features)), whole((1, features)), whole((1, features)), column(features, wide),
         column(features, wide, parts), column(features, wide, 2 * parts), lower(wide, features),
         whole(cosine.shape), whole(sine.shape)],
        (jax.ShapeDtypeStruct((tokens, features), F32), jax.ShapeDtypeStruct((tokens, features), BF16),
         jax.ShapeDtypeStruct((3, tokens, features), BF16), jax.ShapeDtypeStruct((tokens, features), BF16)),
        (whole((tokens, features)), whole((tokens, features)), stacked(3, tokens, wide), column(tokens, wide)),
        [], 8 * tokens * features ** 2)


def attention_back(active, lengths, grad_mid, x, gain, qkv, w_qkv, w_out, cosine, sine, parts=2):
    tokens, features = x.shape
    row_tokens = tokens // lengths.shape[0]
    size = features // HEADS
    wide = features // parts
    vector = jax.ShapeDtypeStruct((1, features), F32)
    return local_call(
        functools.partial(attention_back_kernel, size, row_tokens), "attention_back", parts, (active, lengths),
        (grad_mid, x, gain, qkv, w_qkv, w_qkv, w_qkv, w_out, cosine, sine),
        [whole((tokens, features)), whole((tokens, features)), whole((1, features)), stacked(3, tokens, wide),
         column(features, wide), column(features, wide, parts), column(features, wide, 2 * parts),
         lower(wide, features), whole(cosine.shape), whole(sine.shape)],
        (jax.ShapeDtypeStruct((tokens, features), BF16), jax.ShapeDtypeStruct((3, tokens, features), BF16),
         jax.ShapeDtypeStruct((tokens, features), F32), jax.ShapeDtypeStruct((tokens, features), BF16),
         vector, vector),
        (whole((tokens, features)), stacked(3, tokens, wide), whole((tokens, features)), whole((tokens, features)),
         whole((1, features)), whole((1, features))),
        [pltpu.VMEM((tokens, wide), BF16), pltpu.VMEM((tokens, features), F32)], 20 * tokens * features ** 2)


def feed(active, mid, gain, bias, w_gate_up, w_down, parts=8):
    tokens, features = mid.shape
    wide = w_down.shape[0] // parts
    return local_call(
        feed_kernel, "feed", parts, (active,),
        (mid, gain, bias, w_gate_up, w_gate_up, w_down),
        [whole((tokens, features)), whole((1, features)), whole((1, features)), column(features, wide),
         column(features, wide, parts), lower(wide, features)],
        jax.ShapeDtypeStruct((tokens, features), BF16), whole((tokens, features)),
        [pltpu.VMEM((tokens, features), BF16), pltpu.VMEM((tokens, features), F32)],
        6 * tokens * features * w_down.shape[0])


def feed_both(active, mid, grad, gain, bias, w_gate_up, w_down, parts=8):
    tokens, features = mid.shape
    hidden = w_down.shape[0]
    wide = hidden // parts
    vector = jax.ShapeDtypeStruct((1, features), F32)
    return local_call(
        feed_both_kernel, "feed_both", parts, (active,),
        (mid, grad, gain, bias, w_gate_up, w_gate_up, w_down),
        [whole((tokens, features)), whole((tokens, features)), whole((1, features)), whole((1, features)),
         column(features, wide), column(features, wide, parts), lower(wide, features)],
        (jax.ShapeDtypeStruct((tokens, features), F32), jax.ShapeDtypeStruct((tokens, features), BF16),
         jax.ShapeDtypeStruct((tokens, hidden), BF16), jax.ShapeDtypeStruct((2, tokens, hidden), BF16),
         jax.ShapeDtypeStruct((tokens, features), F32), vector, vector),
        (whole((tokens, features)), whole((tokens, features)), column(tokens, wide), stacked(2, tokens, wide),
         whole((tokens, features)), whole((1, features)), whole((1, features))),
        [pltpu.VMEM((tokens, features), F32)], 12 * tokens * features * hidden)


def tables(lengths, row_tokens, size):
    ends = jnp.cumsum(lengths, axis=-1)
    index = jnp.arange(row_tokens, dtype=jnp.int32)
    passed = index[:, None] >= ends[..., None, :]
    before = jnp.sum(jnp.where(passed, lengths[..., None, :], 0), axis=-1)
    position = (index - before).reshape(-1)
    frequency = 10000.0 ** (-2.0 * jnp.arange(size // 2, dtype=F32) / size)
    angles = position.astype(F32)[:, None] * frequency
    return jnp.tile(jnp.cos(angles), (1, 4)), jnp.tile(jnp.sin(angles), (1, 4))


def exchange_kernel(cfg, *refs):
    shards, bits, seats, unit_rows, width, section, aliased = cfg
    arrays = len(seats)
    lefts, rights = refs[:arrays], refs[arrays:2 * arrays]
    vector = refs[2 * arrays]
    refs = refs[2 * arrays + 1 + (arrays if aliased else 0):]
    outs, vector_out = refs[:arrays], refs[arrays]
    (vector_land, vector_sum, vector_send, vector_recv, vector_store, left, right, left_sem, right_sem, own, give, landed, mine, chain, rest_send, rest_land, rest_keep, piece,
     land_send, land_recv, chain_send, chain_recv,
     rest_ssem, rest_rsem, store_sem, gather_send, gather_recv) = refs[arrays + 1:]
    units = sum(seat[0] for seat in seats)
    half = unit_rows // 2
    others = bits - 1
    final_rows = unit_rows >> bits
    sec = lax.axis_index("section")
    here = lax.axis_index("shard")
    seat = lax.axis_index("group")

    def bit_of(index):
        return lax.rem(lax.div(seat, 1 << index), 2)

    def across(index):
        return (sec, here, seat + (1 - 2 * bit_of(index)) * (1 << index))

    above = (sec, jnp.minimum(here + 1, shards - 1), seat)
    below = (sec, jnp.maximum(here - 1, 0), seat)
    first = [path for path in range(2)]
    rest = [[index for index in range(bits) if index != path] for path in range(2)]
    sides = [rest[path][::-1] + [first[path]] for path in range(2)]

    def remote(source, target, send, recv, device):
        return pltpu.make_async_remote_copy(
            src_ref=source, dst_ref=target, send_sem=send, recv_sem=recv,
            device_id=device, device_id_type=MESH,
        )

    def seat_row(path, depth):
        row = bit_of(first[path]) * half
        for step in range(depth):
            row = row + bit_of(rest[path][step]) * (half >> (step + 1))
        return row

    group = 1 << bits
    peers = shards * group
    me = here * group + seat
    part = vector_out.shape[1]

    def peer(step):
        index = lax.rem(me + step, peers)
        return index, (sec, lax.div(index, group), lax.rem(index, group))

    def vector_copy(index, device):
        lanes = pl.ds(pl.multiple_of(device[1] * part, part), part)
        return remote(vector.at[:, lanes], vector_land.at[me], vector_send.at[index], vector_recv.at[me], device)

    def vector_finish():
        vector_sum[...] = vector[:, pl.ds(pl.multiple_of(here * part, part), part)]

        @pl.loop(1, peers)
        def _(step):
            index, device = peer(step)
            vector_copy(index, device).wait_send()
            remote(vector_land.at[index], vector_land.at[index], vector_send.at[index], vector_recv.at[index],
                   device).wait_recv()
            vector_sum[...] += vector_land[index]
        copy = pltpu.make_async_copy(vector_sum, vector_out, vector_store)
        copy.start()
        copy.wait()

    def valid(chunk):
        return (chunk >= 0) & (chunk < units)

    def on(condition, run):
        pl.when(condition)(run)

    def by_rows(rows, run, tall=32):
        step = min(rows, tall)

        @pl.loop(0, rows // step)
        def _(index):
            run(pl.ds(pl.multiple_of(index * step, step), step))

    def shifted(part, offset):
        return pl.ds(pl.multiple_of(part.start + offset, part.size), part.size)

    def work():
        barrier = pltpu.get_barrier_semaphore()

        @pl.loop(1, peers)
        def _(step):
            pl.semaphore_signal(barrier, inc=1, device_id=peer(step)[1], device_id_type=MESH)
        pl.semaphore_wait(barrier, peers - 1)

        @pl.loop(1, peers)
        def _(step):
            vector_copy(*peer(step)).start()

        for path in range(2):
            for way in range(2):
                @pl.loop(0, shards)
                def _(block):
                    def clear(rows):
                        chain[path, way, chain.shape[2] - 1, block, rows] = jnp.zeros((rows.size, width), BF16)
                    by_rows(half, clear)

        def loads(chunk, run):
            slot, start = lax.rem(chunk, 2), 0
            for which, (count, blocks, inner, rows) in enumerate(seats):
                def each(which=which, start=start, blocks=blocks, inner=inner, rows=rows):
                    local = chunk - start
                    row = lax.div(local, blocks)
                    block = local - row * blocks
                    outer = lax.div(block, inner)
                    column = pl.multiple_of((block - outer * inner) * (2 * width), 2 * width)
                    run(pltpu.make_async_copy(
                        rights[which].at[outer, :, pl.ds(column, 2 * width)], right.at[slot], right_sem.at[slot]))
                    for shard in range(shards):
                        offset = pl.multiple_of(shard * rows + row * unit_rows, unit_rows)
                        run(pltpu.make_async_copy(
                            lefts[which].at[:, pl.ds(offset, unit_rows)], left.at[slot, :, shard * unit_rows:(shard + 1) * unit_rows],
                            left_sem.at[slot, shard]))
                on((chunk >= start) & (chunk < start + count), each)
                start += count

        def first_copy(path, chunk):
            two, four = lax.rem(chunk, 2), lax.rem(chunk, 4)
            return remote(give.at[path, two], landed.at[path, four], land_send.at[path, four],
                          land_recv.at[path, four], across(first[path]))

        def opening(path, chunk):
            two = lax.rem(chunk, 2)
            away = (1 - bit_of(first[path])) * half

            own[path, two] = lax.dot_general(
                left[two], right[two, :, path * width:(path + 1) * width],
                (((0,), (0,)), ((), ())), preferred_element_type=F32)

            @pl.loop(0, shards)
            def _(block):
                def round_off(rows):
                    give[path, two, block, rows] = own[path, two, shifted(rows, block * unit_rows + away)].astype(BF16)
                by_rows(half, round_off)
            first_copy(path, chunk).start()

        def first_sum(path, chunk):
            slot, two, four = lax.rem(chunk, shards + 2), lax.rem(chunk, 2), lax.rem(chunk, 4)
            copy = first_copy(path, chunk)
            copy.wait_recv()
            copy.wait_send()
            kept = bit_of(first[path]) * half

            @pl.loop(0, shards)
            def _(block):
                def add(rows):
                    mine[path, slot, block, rows] = (
                        own[path, two, shifted(rows, block * unit_rows + kept)] + landed[path, four, block, rows].astype(F32)
                    ).astype(BF16)
                by_rows(half, add)

        depth = chain.shape[2] - 1

        def hop(path, way, chunk, block):
            slot = lax.rem(chunk, depth)
            ref = chain.at[path, way, slot, block]
            return remote(ref, ref, chain_send.at[path, way, slot, block],
                          chain_recv.at[path, way, slot, block], above if way == 0 else below)

        def onward(path, way, chunk):
            slot, base = lax.rem(chunk, depth), lax.rem(chunk, shards + 2)
            arrives = here > 0 if way == 0 else here < shards - 1

            @pl.loop(0, shards - 1 - here if way == 0 else here)
            def _(index):
                block = shards - 1 - index if way == 0 else index
                copy = hop(path, way, chunk, block)
                on(arrives, lambda: copy.wait_recv())
                source = jnp.where(arrives, slot, depth)

                def add(rows):
                    chain[path, way, slot, block, rows] = (
                        chain[path, way, source, block, rows].astype(F32) + mine[path, base, block, rows].astype(F32)
                    ).astype(BF16)
                by_rows(half, add)
                copy.start()

        def sent(path, way, chunk):
            @pl.loop(0, shards - 1 - here if way == 0 else here)
            def _(index):
                hop(path, way, chunk, shards - 1 - index if way == 0 else index).wait_send()

        def rest_rows(step):
            return half >> (step + 1)

        def rest_copy(path, step, chunk):
            slot = lax.rem(chunk, 4)
            rows = pl.ds(0, rest_rows(step))
            return remote(rest_send.at[path, step, slot, rows], rest_land.at[path, step, slot, rows],
                          rest_ssem.at[path, step, slot], rest_rsem.at[path, step, slot],
                          across(rest[path][step]))

        def share(path, step, chunk, total):
            slot, rows = lax.rem(chunk, 4), rest_rows(step)
            bit = bit_of(rest[path][step])

            def give(part):
                rest_send[path, step, slot, part] = total(part, (1 - bit) * rows).astype(BF16)
            by_rows(rows, give)
            rest_copy(path, step, chunk).start()

            def keep(part):
                rest_keep[path, step, slot, part] = total(part, bit * rows)
            by_rows(rows, keep)

        def last_hop(path, chunk):
            base, slot = lax.rem(chunk, shards + 2), lax.rem(chunk, depth)
            on(here > 0, lambda: hop(path, 0, chunk, here).wait_recv())
            on(here < shards - 1, lambda: hop(path, 1, chunk, here).wait_recv())
            from_below = jnp.where(here > 0, slot, depth)
            from_above = jnp.where(here < shards - 1, slot, depth)

            def total(part, offset):
                rows = shifted(part, offset)
                return (
                    mine[path, base, here, rows].astype(F32)
                    + chain[path, 0, from_below, here, rows].astype(F32)
                    + chain[path, 1, from_above, here, rows].astype(F32)
                )
            share(path, 0, chunk, total)

        def rest_sum(path, step, chunk):
            slot, rows = lax.rem(chunk, 4), rest_rows(step)
            copy = rest_copy(path, step, chunk)
            copy.wait_recv()
            copy.wait_send()

            def total(part, offset):
                part = shifted(part, offset)
                return rest_keep[path, step, slot, part] + rest_land[path, step, slot, part].astype(F32)
            if step + 1 < others:
                share(path, step + 1, chunk, total)
            else:
                def finish(part):
                    piece[path, slot, part] = total(part, 0).astype(BF16)
                by_rows(rows, finish)
                spread(path, 0, chunk)

        def placed(path, chunk, rows, row, run):
            start = 0
            for which, (count, blocks, _, _) in enumerate(seats):
                def each(which=which, start=start, blocks=blocks):
                    local = chunk - start
                    outer = lax.div(local, blocks)
                    column = (local - outer * blocks) * (2 * width) + path * width
                    run(outs[which].at[
                        pl.ds(pl.multiple_of(outer * unit_rows + row, rows), rows),
                        pl.ds(pl.multiple_of(column, width), width)])
                on((chunk >= start) & (chunk < start + count), each)
                start += count

        def any_place(rows):
            return outs[0].at[pl.ds(0, rows), pl.ds(0, width)]

        def store(path, chunk, target):
            slot = lax.rem(chunk, 4)
            return pltpu.make_async_copy(piece.at[path, slot], target, store_sem.at[path, slot])

        def gather(path, step, chunk, target):
            slot = lax.rem(chunk, 4)
            source = piece.at[path, slot] if step == 0 else target
            return remote(source, target, gather_send.at[path, step, slot],
                          gather_recv.at[path, step, slot], across(sides[path][step]))

        def spread(path, step, chunk):
            def launch(target):
                if step == 0:
                    store(path, chunk, target).start()
                gather(path, step, chunk, target).start()
            placed(path, chunk, final_rows << step, seat_row(path, others - step), launch)

        def gathered(path, step, chunk):
            target = any_place(final_rows << step)
            copy = gather(path, step, chunk, target)
            copy.wait_recv()
            copy.wait_send()
            if step == 0:
                store(path, chunk, target).wait()
            if step + 1 < bits:
                spread(path, step + 1, chunk)

        lag_last = shards + others + bits
        rounds = units + lag_last + 2

        loads(0, lambda copy: copy.start())

        @pl.loop(0, rounds)
        def _(turn):
            on(turn + 1 < units, lambda: loads(turn + 1, lambda copy: copy.start()))
            on(turn < units, lambda: loads(turn, lambda copy: copy.wait()))
            for path in range(2):
                on(turn < units, lambda path=path: opening(path, turn))
            for path in range(2):
                on(valid(turn - 1), lambda path=path: first_sum(path, turn - 1))
            for path in range(2):
                for way in range(2):
                    chunk = turn - 1 - (here if way == 0 else shards - 1 - here)
                    on(valid(chunk - 2), lambda path=path, way=way, chunk=chunk: sent(path, way, chunk - 2))
                    on(valid(chunk), lambda path=path, way=way, chunk=chunk: onward(path, way, chunk))
            for path in range(2):
                on(valid(turn - shards), lambda path=path: last_hop(path, turn - shards))
            for step in range(others):
                for path in range(2):
                    chunk = turn - shards - 1 - step
                    on(valid(chunk), lambda path=path, step=step, chunk=chunk: rest_sum(path, step, chunk))
            for step in range(bits):
                for path in range(2):
                    chunk = turn - shards - others - 1 - step
                    on(valid(chunk), lambda path=path, step=step, chunk=chunk: gathered(path, step, chunk))

        vector_finish()

    if section is None:
        work()
    else:
        pl.when(sec == section)(work)


def exchange(pairs, vector, shards, group, section, collective_id, unit_width, previous=None, after=None, unit_rows_max=256,
             name="exchange"):
    bits = group.bit_length() - 1
    lefts, rights = [p[0] for p in pairs], [p[1] for p in pairs]
    tokens = lefts[0].shape[0]
    rows_of = [a.shape[1] // shards for a in lefts]
    unit_rows = min([unit_rows_max] + rows_of)
    width = unit_width // 2
    inner = [g.shape[2] // unit_width for g in rights]
    seats = tuple(
        (r // unit_rows * g.shape[0] * k, g.shape[0] * k, k, r) for r, g, k in zip(rows_of, rights, inner))
    units = sum(seat[0] for seat in seats)
    half = unit_rows // 2
    others = bits - 1
    final_rows = unit_rows >> bits
    depth = shards + 3
    dma = pltpu.SemaphoreType.DMA
    peers = shards * group
    lanes = vector.shape[1] // shards
    scratch = [
        pltpu.VMEM((peers, vector.shape[0], lanes), F32),
        pltpu.VMEM((vector.shape[0], lanes), F32),
        dma((peers,)), dma((peers,)), dma,
        pltpu.VMEM((2, tokens, shards * unit_rows), BF16),
        pltpu.VMEM((2, tokens, unit_width), BF16),
        dma((2, shards)), dma((2,)),
        pltpu.VMEM((2, 2, shards * unit_rows, width), F32),
        pltpu.VMEM((2, 2, shards, half, width), BF16),
        pltpu.VMEM((2, 4, shards, half, width), BF16),
        pltpu.VMEM((2, shards + 2, shards, half, width), BF16),
        pltpu.VMEM((2, 2, depth + 1, shards, half, width), BF16),
        pltpu.VMEM((2, others, 4, half // 2, width), BF16),
        pltpu.VMEM((2, others, 4, half // 2, width), BF16),
        pltpu.VMEM((2, others, 4, half // 2, width), F32),
        pltpu.VMEM((2, 4, final_rows, width), BF16),
        dma((2, 4)), dma((2, 4)),
        dma((2, 2, depth, shards)), dma((2, 2, depth, shards)),
        dma((2, others, 4)), dma((2, others, 4)),
        dma((2, 4)),
        dma((2, bits, 4)), dma((2, bits, 4)),
    ]
    cfg = (shards, bits, seats, unit_rows, width, section, previous is not None)
    if after is not None:
        vector, _ = lax.optimization_barrier((vector, after))
    operands = lefts + rights + [vector] + list(previous or [])
    first = 2 * len(pairs) + 1
    results = [jax.ShapeDtypeStruct((r, g.shape[0] * g.shape[2]), BF16) for r, g in zip(rows_of, rights)]
    results.append(jax.ShapeDtypeStruct((vector.shape[0], lanes), F32))
    hbm, vmem = pl.BlockSpec(memory_space=pl.ANY), pl.BlockSpec(memory_space=pltpu.VMEM)
    in_specs = [vmem if index == first - 1 else hbm for index in range(len(operands))]
    return pl.pallas_call(
        functools.partial(exchange_kernel, cfg),
        out_shape=results,
        in_specs=in_specs,
        out_specs=[hbm] * len(results),
        scratch_shapes=scratch,
        input_output_aliases={first + index: index for index in range(len(previous or []))},
        name=name,
        cost_estimate=pl.CostEstimate(
            flops=2 * tokens * units * shards * unit_rows * unit_width, bytes_accessed=100 * 2 ** 20,
            transcendentals=0),
        compiler_params=pltpu.CompilerParams(
            collective_id=collective_id, has_side_effects=True, vmem_limit_bytes=56 * 1024 * 1024),
    )(*operands)


def body(
    ends_in,
    lengths,
    norm_gain_a,
    norm_bias_a,
    w_qkv,
    w_out,
    norm_gain_f,
    norm_bias_f,
    w_gate_up,
    w_down,
):
    section = lax.axis_index("section")
    shards, group = lax.axis_size("shard"), lax.axis_size("group")
    is_first = section == 0
    first, second = ((section == which).astype(jnp.int32).reshape(1) for which in range(2))
    tokens, features = ends_in.shape[1:]
    size = features // HEADS
    rows = ends_in[0]
    weight_qkv, weight_out, weight_gu, weight_down = w_qkv[0], w_out[0], w_gate_up[0], w_down[0]
    cosine, sine = tables(lengths, tokens // lengths.shape[0], size)
    nothing = jnp.zeros((2, features), F32)

    def attend(active, values):
        return attention(active, lengths, values, norm_gain_a, norm_bias_a, weight_qkv, weight_out, cosine, sine)

    def feed_back(active, middle, grad):
        return feed_both(active, middle, grad, norm_gain_f, norm_bias_f, weight_gu, weight_down)

    def attend_back(grad_middle, values, gain, qkv, weight_qkv, weight_out):
        return attention_back(first, lengths, grad_middle, values, gain, qkv, weight_qkv, weight_out, cosine, sine)

    def upward(*arrays):
        return [lax.ppermute(array, "section", [(0, 1)]) for array in arrays]

    def downward(*arrays):
        return [lax.ppermute(array, "section", [(1, 0)]) for array in arrays]

    middle_0, low_0, qkv_0, mixture_0 = attend(first, rows)
    passed = feed(first, middle_0, norm_gain_f, norm_bias_f, weight_gu, weight_down)
    (arrived,) = upward(passed)
    _, later_qkv, later_out, later_gain = lax.optimization_barrier((passed, weight_qkv, weight_out, norm_gain_a))
    later_qkv, later_out, later_gain = downward(later_qkv, later_out, later_gain)
    middle_1, low_1, qkv_1, mixture_1 = attend(second, arrived)
    (qkv_there,) = downward(qkv_1)
    result, low_f, hidden, grad_gu, grad_middle, gain_f, bias_f = feed_back(second, middle_1, rows)
    (grad_middle,) = downward(grad_middle)
    feed_sums = exchange(
        [(hidden, rows[None]), (low_f, grad_gu)], jnp.concatenate([nothing, gain_f, bias_f, nothing, nothing], axis=0),
        shards, group, 1, 1, features, name="exchange_second_feed")
    branch, grad_qkv, _, returned, gain_a, bias_a = attend_back(
        grad_middle, passed, later_gain, qkv_there, later_qkv, later_out)
    branch, grad_qkv, attention_vectors = upward(branch, grad_qkv, jnp.concatenate([gain_a, bias_a], axis=0))
    _, low_f, hidden, grad_gu, grad_middle, gain_f, bias_f = feed_back(first, middle_0, returned)
    branch_0, grad_qkv_0, grad_in, _, gain_a, bias_a = attend_back(
        grad_middle, rows, norm_gain_a, qkv_0, weight_qkv, weight_out)
    attention_sums = exchange(
        [(mixture_1, branch[None]), (low_1, grad_qkv)],
        jnp.concatenate([attention_vectors, nothing, nothing, nothing], axis=0),
        shards, group, 1, 2, features, after=feed_sums[-1], name="exchange_second_attention")
    vectors = feed_sums[-1] + attention_sums[-1]
    sums = exchange(
        [(hidden, returned[None]), (low_f, grad_gu), (mixture_0, branch_0[None]), (low_0, grad_qkv_0)],
        jnp.concatenate([gain_a, bias_a, gain_f, bias_f, nothing, nothing], axis=0),
        shards, group, 0, 3, features, previous=feed_sums[:-1] + attention_sums[:-1], name="exchange_first")
    ends_out = jnp.where(is_first, grad_in, result)[None]
    grad_down, grad_gate_up, grad_out, grad_qkv = (item.astype(F32)[None] for item in sums[:4])
    vectors = jnp.where(is_first, sums[4], vectors)
    return (
        ends_out,
        vectors[0:1],
        vectors[1:2],
        grad_qkv,
        grad_out,
        vectors[2:3],
        vectors[3:4],
        grad_gate_up,
        grad_down,
    )


def solution(mesh):
    placed = (
        P("section", ("shard", "group"), None),
        P(("shard", "group"), None),
        P("section", None),
        P("section", None),
        P("section", None, None),
        P("section", None, None),
        P("section", None),
        P("section", None),
        P("section", None, None),
        P("section", None, None),
    )
    return jax.shard_map(
        body,
        mesh=mesh,
        in_specs=placed,
        out_specs=(
            P("section", ("shard", "group"), None),
            P("section", "shard"),
            P("section", "shard"),
            P("section", "shard", None),
            P("section", "shard", None),
            P("section", "shard"),
            P("section", "shard"),
            P("section", "shard", None),
            P("section", "shard", None),
        ),
        check_vma=False,
    )
```

```python
import functools

import jax
import jax.numpy as jnp
from jax import lax
from jax.experimental import pallas as pl
from jax.experimental.pallas import tpu as pltpu
from jax.sharding import PartitionSpec as P

MESH = pl.DeviceIdType.MESH
F32, BF16 = jnp.float32, jnp.bfloat16
HEADS = 16
EPSILON = 1e-05


def dot(a, b):
    return jnp.dot(a, b, preferred_element_type=F32)


def dot_cols(a, b):
    return lax.dot_general(a, b, (((1,), (1,)), ((), ())), preferred_element_type=F32)


def dot_rows(a, b):
    return lax.dot_general(a, b, (((0,), (0,)), ((), ())), preferred_element_type=F32)


def in_rows(total, step, run):
    @pl.loop(0, total // step)
    def _(index):
        run(pl.ds(pl.multiple_of(index * step, step), step))


def normalized(values):
    average = jnp.mean(values, axis=-1, keepdims=True)
    centered = values - average
    variance = jnp.mean(centered * centered, axis=-1, keepdims=True)
    spread = lax.rsqrt(variance + EPSILON)
    return centered * spread, spread


def norm_back(grad, values, gain):
    unit, spread = normalized(values)
    scaled = grad * gain
    return spread * (
        scaled
        - jnp.mean(scaled, axis=-1, keepdims=True)
        - unit * jnp.mean(scaled * unit, axis=-1, keepdims=True)
    ), grad * unit


def lanes_of(shape):
    return lax.broadcasted_iota(jnp.int32, shape, len(shape) - 1)


def turn(values, half, size):
    wide = values.shape[-1]
    early = lax.rem(lanes_of(values.shape), size) < half
    return jnp.where(early, pltpu.roll(values, wide - half, 1), pltpu.roll(values, half, 1)), early


def rotated(values, cosine, sine, size):
    other, early = turn(values, size // 2, size)
    return values * cosine + jnp.where(early, -other, other) * sine


def unrotated(values, cosine, sine, size):
    other, early = turn(values * sine, size // 2, size)
    return values * cosine + jnp.where(early, other, -other)


def window_of(index, lengths_ref, row):
    windows = lengths_ref.shape[1]
    end = lengths_ref[row, 0]
    segment = (index >= end).astype(jnp.int32)
    for window in range(1, windows):
        end = end + lengths_ref[row, window]
        segment = segment + (index >= end).astype(jnp.int32)
    return segment


def same_window(lengths_ref, row, tokens):
    queries = window_of(lax.broadcasted_iota(jnp.int32, (tokens, 1), 0), lengths_ref, row)
    keys = window_of(lax.broadcasted_iota(jnp.int32, (1, tokens), 1), lengths_ref, row)
    return queries == keys


def softmax(scores, allowed):
    scores = jnp.where(allowed, scores, -1e30)
    weights = jnp.exp(scores - jnp.max(scores, axis=-1, keepdims=True))
    return weights * (1.0 / jnp.sum(weights, axis=-1, keepdims=True))


def attention_kernel(size, row_tokens, act_ref, lengths_ref, x_ref, gain_ref, bias_ref, wq_ref, wk_ref, wv_ref,
                     wo_ref, cos_ref, sin_ref, mid_ref, low_ref, qkv_ref, mix_ref):
    tokens = x_ref.shape[0]
    part = pl.program_id(0)
    block = wq_ref.shape[1]
    pair = 2 * size

    @pl.when(act_ref[0] == 1)
    def _():
        @pl.when(part == 0)
        def _():
            def begin(rows):
                values = x_ref[rows].astype(F32)
                unit, _ = normalized(values)
                low_ref[rows] = (unit * gain_ref[...] + bias_ref[...]).astype(BF16)
                mid_ref[rows] = values
            in_rows(tokens, 64, begin)

        for which, weight in enumerate((wq_ref, wk_ref, wv_ref)):
            projected = dot(low_ref[...], weight[...])
            for at in range(block // pair):
                lanes = slice(at * pair, (at + 1) * pair)
                values = projected[:, lanes]
                if which < 2:
                    values = rotated(values, cos_ref[...], sin_ref[...], size)
                qkv_ref[which, :, lanes] = values.astype(BF16)

        first = lanes_of((row_tokens, pair)) < size
        for row in range(tokens // row_tokens):
            rows = pl.ds(row * row_tokens, row_tokens)
            allowed = same_window(lengths_ref, row, row_tokens)
            for start in range(0, block // pair, 2):
                work = []
                for at in range(start, start + 2):
                    lanes = pl.ds(at * pair, pair)
                    query, key, value = (qkv_ref[which, rows, lanes] for which in range(3))
                    query = query * (size ** -0.5)
                    for head in range(2):
                        own = jnp.where(first if head == 0 else jnp.logical_not(first), query, jnp.zeros_like(query))
                        work.append((dot_cols(own, key), value))
                work = [(softmax(scores, allowed).astype(BF16), value) for scores, value in work]
                work = [dot(probs, value) for probs, value in work]
                for at in range(2):
                    lanes = pl.ds((start + at) * pair, pair)
                    mix_ref[rows, lanes] = jnp.where(first, work[2 * at], work[2 * at + 1]).astype(BF16)

        mid_ref[...] += dot(mix_ref[...], wo_ref[...])


def attention_back_kernel(size, row_tokens, act_ref, lengths_ref, grad_ref, x_ref, gain_ref, qkv_ref, wq_ref, wk_ref,
                          wv_ref, wo_ref, cos_ref, sin_ref, branch_ref, proj_ref, input_ref, input_low_ref,
                          dgain_ref, dbias_ref, gm_ref, total_ref):
    tokens = x_ref.shape[0]
    part = pl.program_id(0)
    block = wq_ref.shape[1]
    pair = 2 * size
    scale = size ** -0.5

    @pl.when(act_ref[0] == 1)
    def _():
        @pl.when(part == 0)
        def _():
            def begin(rows):
                branch_ref[rows] = grad_ref[rows].astype(BF16)
            in_rows(tokens, 64, begin)

        gm_ref[...] = dot_cols(branch_ref[...], wo_ref[...]).astype(BF16)
        first = lanes_of((row_tokens, pair)) < size
        for row in range(tokens // row_tokens):
            rows = pl.ds(row * row_tokens, row_tokens)
            allowed = same_window(lengths_ref, row, row_tokens)
            cosine, sine = cos_ref[rows], sin_ref[rows]
            for start in range(0, block // pair, 2):
                work = []
                for at in range(start, start + 2):
                    lanes = pl.ds(at * pair, pair)
                    query, key, value = (qkv_ref[which, rows, lanes] for which in range(3))
                    grad_mix = gm_ref[rows, lanes]
                    scaled = query * scale
                    for head in range(2):
                        mine = first if head == 0 else jnp.logical_not(first)
                        work.append((
                            query, key, grad_mix,
                            dot_cols(jnp.where(mine, scaled, jnp.zeros_like(scaled)), key),
                            dot_cols(jnp.where(mine, grad_mix, jnp.zeros_like(grad_mix)), value)))
                results = []
                for query, key, grad_mix, scores, grad_probs in work:
                    probs = softmax(scores, allowed)
                    weighted = probs * grad_probs
                    grad_scores = (weighted - probs * jnp.sum(weighted, axis=-1, keepdims=True)).astype(BF16)
                    results.append((query, key, grad_mix, grad_scores, probs.astype(BF16)))
                results = [
                    (dot(grad_scores, key), dot_rows(grad_scores, query), dot_rows(probs, grad_mix))
                    for query, key, grad_mix, grad_scores, probs in results]
                for at in range(2):
                    lanes = pl.ds((start + at) * pair, pair)
                    grad_query, grad_key, grad_value = (
                        jnp.where(first, a, b) for a, b in zip(results[2 * at], results[2 * at + 1]))
                    proj_ref[0, rows, lanes] = unrotated(grad_query * scale, cosine, sine, size).astype(BF16)
                    proj_ref[1, rows, lanes] = unrotated(grad_key * scale, cosine, sine, size).astype(BF16)
                    proj_ref[2, rows, lanes] = grad_value.astype(BF16)

        added = (
            dot_cols(proj_ref[0], wq_ref[...])
            + dot_cols(proj_ref[1], wk_ref[...])
            + dot_cols(proj_ref[2], wv_ref[...])
        )
        total_ref[...] = jnp.where(part == 0, added, total_ref[...] + added)

        @pl.when(part == pl.num_programs(0) - 1)
        def _():
            dgain_ref[...] = jnp.zeros_like(dgain_ref)
            dbias_ref[...] = jnp.zeros_like(dbias_ref)

            def finish(rows):
                grad = total_ref[rows]
                through, by_gain = norm_back(grad, x_ref[rows].astype(F32), gain_ref[...])
                result = grad_ref[rows] + through
                input_ref[rows] = result
                input_low_ref[rows] = result.astype(BF16)
                dgain_ref[...] += jnp.sum(by_gain, axis=0, keepdims=True)
                dbias_ref[...] += jnp.sum(grad, axis=0, keepdims=True)
            in_rows(tokens, 64, finish)


def feed_kernel(act_ref, mid_ref, gain_ref, bias_ref, wg_ref, wu_ref, wd_ref, out_ref, low_ref, total_ref):
    tokens = mid_ref.shape[0]
    part = pl.program_id(0)

    @pl.when(act_ref[0] == 1)
    def _():
        @pl.when(part == 0)
        def _():
            def begin(rows):
                values = mid_ref[rows]
                unit, _ = normalized(values)
                low_ref[rows] = (unit * gain_ref[...] + bias_ref[...]).astype(BF16)
                total_ref[rows] = values
            in_rows(tokens, 64, begin)

        low = low_ref[...]
        gate = dot(low, wg_ref[...])
        up = dot(low, wu_ref[...])
        hidden = (gate / (1.0 + jnp.exp(-gate)) * up).astype(BF16)
        total_ref[...] += dot(hidden, wd_ref[...])

        @pl.when(part == pl.num_programs(0) - 1)
        def _():
            def finish(rows):
                out_ref[rows] = total_ref[rows].astype(BF16)
            in_rows(tokens, 64, finish)


def feed_both_kernel(act_ref, mid_ref, grad_ref, gain_ref, bias_ref, wg_ref, wu_ref, wd_ref, out_ref,
                     low_ref, hidden_ref, ggu_ref, grad_mid_ref, dgain_ref, dbias_ref, total_ref):
    tokens = mid_ref.shape[0]
    part = pl.program_id(0)

    @pl.when(act_ref[0] == 1)
    def _():
        @pl.when(part == 0)
        def _():
            def begin(rows):
                values = mid_ref[rows]
                unit, _ = normalized(values)
                low_ref[rows] = (unit * gain_ref[...] + bias_ref[...]).astype(BF16)
                out_ref[rows] = values
            in_rows(tokens, 64, begin)

        low = low_ref[...]
        gate = dot(low, wg_ref[...])
        up = dot(low, wu_ref[...])
        grad_hidden = dot_cols(grad_ref[...], wd_ref[...])
        sig = 1.0 / (1.0 + jnp.exp(-gate))
        silu = gate * sig
        hidden_ref[...] = (silu * up).astype(BF16)
        ggu_ref[0] = (grad_hidden * up * (sig * (1.0 + gate * (1.0 - sig)))).astype(BF16)
        ggu_ref[1] = (grad_hidden * silu).astype(BF16)
        out_ref[...] += dot(hidden_ref[...], wd_ref[...])
        added = dot_cols(ggu_ref[0], wg_ref[...]) + dot_cols(ggu_ref[1], wu_ref[...])
        total_ref[...] = jnp.where(part == 0, added, total_ref[...] + added)

        @pl.when(part == pl.num_programs(0) - 1)
        def _():
            dgain_ref[...] = jnp.zeros_like(dgain_ref)
            dbias_ref[...] = jnp.zeros_like(dbias_ref)

            def finish(rows):
                grad = total_ref[rows]
                through, by_gain = norm_back(grad, mid_ref[rows], gain_ref[...])
                grad_mid_ref[rows] = grad_ref[rows].astype(F32) + through
                dgain_ref[...] += jnp.sum(by_gain, axis=0, keepdims=True)
                dbias_ref[...] += jnp.sum(grad, axis=0, keepdims=True)
            in_rows(tokens, 64, finish)


def whole(shape):
    return pl.BlockSpec(shape, lambda part, *_: (0,) * len(shape))


def column(rows, wide, offset=0):
    return pl.BlockSpec((rows, wide), lambda part, act, *_: (0, (part + offset) * act[0]))


def stacked(count, rows, wide):
    return pl.BlockSpec((count, rows, wide), lambda part, act, *_: (0, 0, part * act[0]))


def lower(rows, wide):
    return pl.BlockSpec((rows, wide), lambda part, act, *_: (part * act[0], 0))


def local_call(kernel, name, grid, scalars, args, in_specs, outs, out_specs, scratch, flops, limit=56):
    return pl.pallas_call(
        kernel,
        grid_spec=pltpu.PrefetchScalarGridSpec(
            num_scalar_prefetch=len(scalars), grid=(grid,), in_specs=in_specs, out_specs=out_specs,
            scratch_shapes=scratch),
        out_shape=outs,
        name=name,
        cost_estimate=pl.CostEstimate(flops=flops, bytes_accessed=40 * 2 ** 20, transcendentals=0),
        compiler_params=pltpu.CompilerParams(
            dimension_semantics=("arbitrary",), vmem_limit_bytes=limit * 1024 * 1024),
    )(*scalars, *args)


def attention(active, lengths, x, gain, bias, w_qkv, w_out, cosine, sine, parts=2):
    tokens, features = x.shape
    row_tokens = tokens // lengths.shape[0]
    size = features // HEADS
    wide = features // parts
    return local_call(
        functools.partial(attention_kernel, size, row_tokens), "attention", parts, (active, lengths),
        (x, gain, bias, w_qkv, w_qkv, w_qkv, w_out, cosine, sine),
        [whole((tokens, features)), whole((1, features)), whole((1, features)), column(features, wide),
         column(features, wide, parts), column(features, wide, 2 * parts), lower(wide, features),
         whole(cosine.shape), whole(sine.shape)],
        (jax.ShapeDtypeStruct((tokens, features), F32), jax.ShapeDtypeStruct((tokens, features), BF16),
         jax.ShapeDtypeStruct((3, tokens, features), BF16), jax.ShapeDtypeStruct((tokens, features), BF16)),
        (whole((tokens, features)), whole((tokens, features)), stacked(3, tokens, wide), column(tokens, wide)),
        [], 8 * tokens * features ** 2)


def attention_back(active, lengths, grad_mid, x, gain, qkv, w_qkv, w_out, cosine, sine, parts=2):
    tokens, features = x.shape
    row_tokens = tokens // lengths.shape[0]
    size = features // HEADS
    wide = features // parts
    vector = jax.ShapeDtypeStruct((1, features), F32)
    return local_call(
        functools.partial(attention_back_kernel, size, row_tokens), "attention_back", parts, (active, lengths),
        (grad_mid, x, gain, qkv, w_qkv, w_qkv, w_qkv, w_out, cosine, sine),
        [whole((tokens, features)), whole((tokens, features)), whole((1, features)), stacked(3, tokens, wide),
         column(features, wide), column(features, wide, parts), column(features, wide, 2 * parts),
         lower(wide, features), whole(cosine.shape), whole(sine.shape)],
        (jax.ShapeDtypeStruct((tokens, features), BF16), jax.ShapeDtypeStruct((3, tokens, features), BF16),
         jax.ShapeDtypeStruct((tokens, features), F32), jax.ShapeDtypeStruct((tokens, features), BF16),
         vector, vector),
        (whole((tokens, features)), stacked(3, tokens, wide), whole((tokens, features)), whole((tokens, features)),
         whole((1, features)), whole((1, features))),
        [pltpu.VMEM((tokens, wide), BF16), pltpu.VMEM((tokens, features), F32)], 20 * tokens * features ** 2)


def feed(active, mid, gain, bias, w_gate_up, w_down, parts=8):
    tokens, features = mid.shape
    wide = w_down.shape[0] // parts
    return local_call(
        feed_kernel, "feed", parts, (active,),
        (mid, gain, bias, w_gate_up, w_gate_up, w_down),
        [whole((tokens, features)), whole((1, features)), whole((1, features)), column(features, wide),
         column(features, wide, parts), lower(wide, features)],
        jax.ShapeDtypeStruct((tokens, features), BF16), whole((tokens, features)),
        [pltpu.VMEM((tokens, features), BF16), pltpu.VMEM((tokens, features), F32)],
        6 * tokens * features * w_down.shape[0])


def feed_both(active, mid, grad, gain, bias, w_gate_up, w_down, parts=8):
    tokens, features = mid.shape
    hidden = w_down.shape[0]
    wide = hidden // parts
    vector = jax.ShapeDtypeStruct((1, features), F32)
    return local_call(
        feed_both_kernel, "feed_both", parts, (active,),
        (mid, grad, gain, bias, w_gate_up, w_gate_up, w_down),
        [whole((tokens, features)), whole((tokens, features)), whole((1, features)), whole((1, features)),
         column(features, wide), column(features, wide, parts), lower(wide, features)],
        (jax.ShapeDtypeStruct((tokens, features), F32), jax.ShapeDtypeStruct((tokens, features), BF16),
         jax.ShapeDtypeStruct((tokens, hidden), BF16), jax.ShapeDtypeStruct((2, tokens, hidden), BF16),
         jax.ShapeDtypeStruct((tokens, features), F32), vector, vector),
        (whole((tokens, features)), whole((tokens, features)), column(tokens, wide), stacked(2, tokens, wide),
         whole((tokens, features)), whole((1, features)), whole((1, features))),
        [pltpu.VMEM((tokens, features), F32)], 12 * tokens * features * hidden)


def tables(lengths, row_tokens, size):
    index = jnp.arange(row_tokens, dtype=jnp.int32)[None]
    end, before = 0, 0
    for window in range(lengths.shape[1]):
        length = lengths[:, window:window + 1]
        end = end + length
        before = before + jnp.where(index >= end, length, 0)
    position = (index - before).astype(F32).reshape(-1, 1)
    half = jnp.arange(2 * size, dtype=jnp.int32) % (size // 2)
    frequency = 10000.0 ** (-2.0 * half.astype(F32) / size)
    angles = position * frequency
    return jnp.cos(angles), jnp.sin(angles)


def exchange_kernel(cfg, *refs):
    shards, bits, seats, unit_rows, width, section, aliased = cfg
    arrays = len(seats)
    lefts, rights = refs[:arrays], refs[arrays:2 * arrays]
    vector = refs[2 * arrays]
    refs = refs[2 * arrays + 1 + (arrays + 1 if aliased else 0):]
    outs, vector_out = refs[:arrays], refs[arrays]
    (vector_land, vector_sum, vector_send, vector_recv, vector_store, left, right, left_sem, right_sem, own, give, landed, mine, chain, rest_send, rest_land, rest_keep, piece,
     land_send, land_recv, chain_send, chain_recv,
     rest_ssem, rest_rsem, store_sem, gather_send, gather_recv) = refs[arrays + 1:]
    units = sum(seat[0] for seat in seats)
    half = unit_rows // 2
    others = bits - 1
    final_rows = unit_rows >> bits
    sec = lax.axis_index("section")
    here = lax.axis_index("shard")
    seat = lax.axis_index("group")

    def bit_of(index):
        return lax.rem(lax.div(seat, 1 << index), 2)

    def across(index):
        return (sec, here, seat + (1 - 2 * bit_of(index)) * (1 << index))

    above = (sec, jnp.minimum(here + 1, shards - 1), seat)
    below = (sec, jnp.maximum(here - 1, 0), seat)
    first = [path for path in range(2)]
    rest = [[index for index in range(bits) if index != path] for path in range(2)]
    sides = [rest[path][::-1] + [first[path]] for path in range(2)]

    def remote(source, target, send, recv, device):
        return pltpu.make_async_remote_copy(
            src_ref=source, dst_ref=target, send_sem=send, recv_sem=recv,
            device_id=device, device_id_type=MESH,
        )

    def seat_row(path, depth):
        row = bit_of(first[path]) * half
        for step in range(depth):
            row = row + bit_of(rest[path][step]) * (half >> (step + 1))
        return row

    group = 1 << bits
    peers = shards * group
    me = here * group + seat
    part = vector_out.shape[1]

    def peer(step):
        index = lax.rem(me + step, peers)
        return index, (sec, lax.div(index, group), lax.rem(index, group))

    def vector_copy(index, device):
        lanes = pl.ds(pl.multiple_of(device[1] * part, part), part)
        return remote(vector.at[:, lanes], vector_land.at[me], vector_send.at[index], vector_recv.at[me], device)

    def vector_finish():
        vector_sum[...] = vector[:, pl.ds(pl.multiple_of(here * part, part), part)]

        @pl.loop(1, peers)
        def _(step):
            index, device = peer(step)
            vector_copy(index, device).wait_send()
            remote(vector_land.at[index], vector_land.at[index], vector_send.at[index], vector_recv.at[index],
                   device).wait_recv()
            vector_sum[...] += vector_land[index]
        copy = pltpu.make_async_copy(vector_sum, vector_out, vector_store)
        copy.start()
        copy.wait()

    def valid(chunk):
        return (chunk >= 0) & (chunk < units)

    def on(condition, run):
        pl.when(condition)(run)

    def by_rows(rows, run, tall=32):
        step = min(rows, tall)

        @pl.loop(0, rows // step)
        def _(index):
            run(pl.ds(pl.multiple_of(index * step, step), step))

    def shifted(part, offset):
        return pl.ds(pl.multiple_of(part.start + offset, part.size), part.size)

    def work():
        barrier = pltpu.get_barrier_semaphore()

        @pl.loop(1, peers)
        def _(step):
            pl.semaphore_signal(barrier, inc=1, device_id=peer(step)[1], device_id_type=MESH)
        pl.semaphore_wait(barrier, peers - 1)

        @pl.loop(1, peers)
        def _(step):
            vector_copy(*peer(step)).start()

        for path in range(2):
            for way in range(2):
                @pl.loop(0, shards)
                def _(block):
                    def clear(rows):
                        chain[path, way, chain.shape[2] - 1, block, rows] = jnp.zeros((rows.size, width), BF16)
                    by_rows(half, clear)

        def loads(chunk, run):
            slot, start = lax.rem(chunk, 2), 0
            for which, (count, blocks, inner, rows) in enumerate(seats):
                def each(which=which, start=start, blocks=blocks, inner=inner, rows=rows):
                    local = chunk - start
                    row = lax.div(local, blocks)
                    block = local - row * blocks
                    outer = lax.div(block, inner)
                    column = pl.multiple_of((block - outer * inner) * (2 * width), 2 * width)
                    run(pltpu.make_async_copy(
                        rights[which].at[outer, :, pl.ds(column, 2 * width)], right.at[slot], right_sem.at[slot]))
                    for shard in range(shards):
                        offset = pl.multiple_of(shard * rows + row * unit_rows, unit_rows)
                        run(pltpu.make_async_copy(
                            lefts[which].at[:, pl.ds(offset, unit_rows)], left.at[slot, :, shard * unit_rows:(shard + 1) * unit_rows],
                            left_sem.at[slot, shard]))
                on((chunk >= start) & (chunk < start + count), each)
                start += count

        def first_copy(path, chunk):
            two, four = lax.rem(chunk, 2), lax.rem(chunk, 4)
            return remote(give.at[path, two], landed.at[path, four], land_send.at[path, four],
                          land_recv.at[path, four], across(first[path]))

        def opening(path, chunk):
            two = lax.rem(chunk, 2)
            away = (1 - bit_of(first[path])) * half

            own[path, two] = lax.dot_general(
                left[two], right[two, :, path * width:(path + 1) * width],
                (((0,), (0,)), ((), ())), preferred_element_type=F32)

            @pl.loop(0, shards)
            def _(block):
                def round_off(rows):
                    give[path, two, block, rows] = own[path, two, shifted(rows, block * unit_rows + away)].astype(BF16)
                by_rows(half, round_off)
            first_copy(path, chunk).start()

        def first_sum(path, chunk):
            slot, two, four = lax.rem(chunk, shards + 2), lax.rem(chunk, 2), lax.rem(chunk, 4)
            copy = first_copy(path, chunk)
            copy.wait_recv()
            copy.wait_send()
            kept = bit_of(first[path]) * half

            @pl.loop(0, shards)
            def _(block):
                def add(rows):
                    mine[path, slot, block, rows] = (
                        own[path, two, shifted(rows, block * unit_rows + kept)] + landed[path, four, block, rows].astype(F32)
                    ).astype(BF16)
                by_rows(half, add)

        depth = chain.shape[2] - 1

        def hop(path, way, chunk, block):
            slot = lax.rem(chunk, depth)
            ref = chain.at[path, way, slot, block]
            return remote(ref, ref, chain_send.at[path, way, slot, block],
                          chain_recv.at[path, way, slot, block], above if way == 0 else below)

        def onward(path, way, chunk):
            slot, base = lax.rem(chunk, depth), lax.rem(chunk, shards + 2)
            arrives = here > 0 if way == 0 else here < shards - 1

            @pl.loop(0, shards - 1 - here if way == 0 else here)
            def _(index):
                block = shards - 1 - index if way == 0 else index
                copy = hop(path, way, chunk, block)
                on(arrives, lambda: copy.wait_recv())
                source = jnp.where(arrives, slot, depth)

                def add(rows):
                    chain[path, way, slot, block, rows] = (
                        chain[path, way, source, block, rows].astype(F32) + mine[path, base, block, rows].astype(F32)
                    ).astype(BF16)
                by_rows(half, add)
                copy.start()

        def sent(path, way, chunk):
            @pl.loop(0, shards - 1 - here if way == 0 else here)
            def _(index):
                hop(path, way, chunk, shards - 1 - index if way == 0 else index).wait_send()

        def rest_rows(step):
            return half >> (step + 1)

        def rest_copy(path, step, chunk):
            slot = lax.rem(chunk, 4)
            rows = pl.ds(0, rest_rows(step))
            return remote(rest_send.at[path, step, slot, rows], rest_land.at[path, step, slot, rows],
                          rest_ssem.at[path, step, slot], rest_rsem.at[path, step, slot],
                          across(rest[path][step]))

        def share(path, step, chunk, total):
            slot, rows = lax.rem(chunk, 4), rest_rows(step)
            bit = bit_of(rest[path][step])

            def give(part):
                rest_send[path, step, slot, part] = total(part, (1 - bit) * rows).astype(BF16)
            by_rows(rows, give)
            rest_copy(path, step, chunk).start()

            def keep(part):
                rest_keep[path, step, slot, part] = total(part, bit * rows)
            by_rows(rows, keep)

        def last_hop(path, chunk):
            base, slot = lax.rem(chunk, shards + 2), lax.rem(chunk, depth)
            on(here > 0, lambda: hop(path, 0, chunk, here).wait_recv())
            on(here < shards - 1, lambda: hop(path, 1, chunk, here).wait_recv())
            from_below = jnp.where(here > 0, slot, depth)
            from_above = jnp.where(here < shards - 1, slot, depth)

            def total(part, offset):
                rows = shifted(part, offset)
                return (
                    mine[path, base, here, rows].astype(F32)
                    + chain[path, 0, from_below, here, rows].astype(F32)
                    + chain[path, 1, from_above, here, rows].astype(F32)
                )
            share(path, 0, chunk, total)

        def rest_sum(path, step, chunk):
            slot, rows = lax.rem(chunk, 4), rest_rows(step)
            copy = rest_copy(path, step, chunk)
            copy.wait_recv()
            copy.wait_send()

            def total(part, offset):
                part = shifted(part, offset)
                return rest_keep[path, step, slot, part] + rest_land[path, step, slot, part].astype(F32)
            if step + 1 < others:
                share(path, step + 1, chunk, total)
            else:
                def finish(part):
                    piece[path, slot, part] = total(part, 0).astype(BF16)
                by_rows(rows, finish)
                spread(path, 0, chunk)

        def placed(path, chunk, rows, row, run):
            start = 0
            for which, (count, blocks, _, _) in enumerate(seats):
                def each(which=which, start=start, blocks=blocks):
                    local = chunk - start
                    outer = lax.div(local, blocks)
                    column = (local - outer * blocks) * (2 * width) + path * width
                    run(outs[which].at[
                        pl.ds(pl.multiple_of(outer * unit_rows + row, rows), rows),
                        pl.ds(pl.multiple_of(column, width), width)])
                on((chunk >= start) & (chunk < start + count), each)
                start += count

        def any_place(rows):
            return outs[0].at[pl.ds(0, rows), pl.ds(0, width)]

        def store(path, chunk, target):
            slot = lax.rem(chunk, 4)
            return pltpu.make_async_copy(piece.at[path, slot], target, store_sem.at[path, slot])

        def gather(path, step, chunk, target):
            slot = lax.rem(chunk, 4)
            source = piece.at[path, slot] if step == 0 else target
            return remote(source, target, gather_send.at[path, step, slot],
                          gather_recv.at[path, step, slot], across(sides[path][step]))

        def spread(path, step, chunk):
            def launch(target):
                if step == 0:
                    store(path, chunk, target).start()
                gather(path, step, chunk, target).start()
            placed(path, chunk, final_rows << step, seat_row(path, others - step), launch)

        def gathered(path, step, chunk):
            target = any_place(final_rows << step)
            copy = gather(path, step, chunk, target)
            copy.wait_recv()
            copy.wait_send()
            if step == 0:
                store(path, chunk, target).wait()
            if step + 1 < bits:
                spread(path, step + 1, chunk)

        lag_last = shards + others + bits
        rounds = units + lag_last + 2

        loads(0, lambda copy: copy.start())

        @pl.loop(0, rounds)
        def _(turn):
            on(turn + 1 < units, lambda: loads(turn + 1, lambda copy: copy.start()))
            on(turn < units, lambda: loads(turn, lambda copy: copy.wait()))
            for path in range(2):
                on(turn < units, lambda path=path: opening(path, turn))
            for path in range(2):
                on(valid(turn - 1), lambda path=path: first_sum(path, turn - 1))
            for path in range(2):
                for way in range(2):
                    chunk = turn - 1 - (here if way == 0 else shards - 1 - here)
                    on(valid(chunk - 2), lambda path=path, way=way, chunk=chunk: sent(path, way, chunk - 2))
                    on(valid(chunk), lambda path=path, way=way, chunk=chunk: onward(path, way, chunk))
            for path in range(2):
                on(valid(turn - shards), lambda path=path: last_hop(path, turn - shards))
            for step in range(others):
                for path in range(2):
                    chunk = turn - shards - 1 - step
                    on(valid(chunk), lambda path=path, step=step, chunk=chunk: rest_sum(path, step, chunk))
            for step in range(bits):
                for path in range(2):
                    chunk = turn - shards - others - 1 - step
                    on(valid(chunk), lambda path=path, step=step, chunk=chunk: gathered(path, step, chunk))

        vector_finish()

    if section is None:
        work()
    else:
        pl.when(sec == section)(work)


def exchange(pairs, vector, shards, group, section, collective_id, unit_width, previous=None, after=None, unit_rows_max=256,
             name="exchange"):
    bits = group.bit_length() - 1
    lefts, rights = [p[0] for p in pairs], [p[1] for p in pairs]
    tokens = lefts[0].shape[0]
    rows_of = [a.shape[1] // shards for a in lefts]
    unit_rows = min([unit_rows_max] + rows_of)
    width = unit_width // 2
    inner = [g.shape[2] // unit_width for g in rights]
    seats = tuple(
        (r // unit_rows * g.shape[0] * k, g.shape[0] * k, k, r) for r, g, k in zip(rows_of, rights, inner))
    units = sum(seat[0] for seat in seats)
    half = unit_rows // 2
    others = bits - 1
    final_rows = unit_rows >> bits
    depth = shards + 3
    dma = pltpu.SemaphoreType.DMA
    peers = shards * group
    lanes = vector.shape[1] // shards
    scratch = [
        pltpu.VMEM((peers, vector.shape[0], lanes), F32),
        pltpu.VMEM((vector.shape[0], lanes), F32),
        dma((peers,)), dma((peers,)), dma,
        pltpu.VMEM((2, tokens, shards * unit_rows), BF16),
        pltpu.VMEM((2, tokens, unit_width), BF16),
        dma((2, shards)), dma((2,)),
        pltpu.VMEM((2, 2, shards * unit_rows, width), F32),
        pltpu.VMEM((2, 2, shards, half, width), BF16),
        pltpu.VMEM((2, 4, shards, half, width), BF16),
        pltpu.VMEM((2, shards + 2, shards, half, width), BF16),
        pltpu.VMEM((2, 2, depth + 1, shards, half, width), BF16),
        pltpu.VMEM((2, others, 4, half // 2, width), BF16),
        pltpu.VMEM((2, others, 4, half // 2, width), BF16),
        pltpu.VMEM((2, others, 4, half // 2, width), F32),
        pltpu.VMEM((2, 4, final_rows, width), BF16),
        dma((2, 4)), dma((2, 4)),
        dma((2, 2, depth, shards)), dma((2, 2, depth, shards)),
        dma((2, others, 4)), dma((2, others, 4)),
        dma((2, 4)),
        dma((2, bits, 4)), dma((2, bits, 4)),
    ]
    cfg = (shards, bits, seats, unit_rows, width, section, previous is not None)
    if after is not None:
        vector, _ = lax.optimization_barrier((vector, after))
    operands = lefts + rights + [vector] + list(previous or [])
    first = 2 * len(pairs) + 1
    results = [jax.ShapeDtypeStruct((r, g.shape[0] * g.shape[2]), BF16) for r, g in zip(rows_of, rights)]
    results.append(jax.ShapeDtypeStruct((vector.shape[0], lanes), F32))
    hbm, vmem = pl.BlockSpec(memory_space=pl.ANY), pl.BlockSpec(memory_space=pltpu.VMEM)
    in_specs = [vmem if index == first - 1 else hbm for index in range(len(operands))]
    return pl.pallas_call(
        functools.partial(exchange_kernel, cfg),
        out_shape=results,
        in_specs=in_specs,
        out_specs=[hbm] * len(results),
        scratch_shapes=scratch,
        input_output_aliases={first + index: index for index in range(len(previous or []))},
        name=name,
        cost_estimate=pl.CostEstimate(
            flops=2 * tokens * units * shards * unit_rows * unit_width, bytes_accessed=100 * 2 ** 20,
            transcendentals=0),
        compiler_params=pltpu.CompilerParams(
            collective_id=collective_id, has_side_effects=True, vmem_limit_bytes=56 * 1024 * 1024),
    )(*operands)


def body(
    ends_in,
    lengths,
    norm_gain_a,
    norm_bias_a,
    w_qkv,
    w_out,
    norm_gain_f,
    norm_bias_f,
    w_gate_up,
    w_down,
):
    section = lax.axis_index("section")
    shards, group = lax.axis_size("shard"), lax.axis_size("group")
    is_first = section == 0
    first, second = ((section == which).astype(jnp.int32).reshape(1) for which in range(2))
    tokens, features = ends_in.shape[1:]
    size = features // HEADS
    rows = ends_in[0]
    weight_qkv, weight_out, weight_gu, weight_down = w_qkv[0], w_out[0], w_gate_up[0], w_down[0]
    cosine, sine = tables(lengths, tokens // lengths.shape[0], size)
    nothing = jnp.zeros((4, features), F32)

    def attend(active, values):
        return attention(active, lengths, values, norm_gain_a, norm_bias_a, weight_qkv, weight_out, cosine, sine)

    def back(active, middle, low_a, qkv, mixture, values, grad):
        result, low_f, hidden, grad_gu, grad_middle, gain_f, bias_f = feed_both(
            active, middle, grad, norm_gain_f, norm_bias_f, weight_gu, weight_down)
        branch, grad_qkv, grad_in, grad_in_low, gain_a, bias_a = attention_back(
            active, lengths, grad_middle, values, norm_gain_a, qkv, weight_qkv, weight_out, cosine, sine)
        pairs = [(low_f, grad_gu), (hidden, grad[None]), (mixture, branch[None]), (low_a, grad_qkv)]
        return result, grad_in, grad_in_low, pairs, jnp.concatenate([gain_a, bias_a, gain_f, bias_f, nothing], axis=0)

    middle_0, low_0, qkv_0, mixture_0 = attend(first, rows)
    passed = feed(first, middle_0, norm_gain_f, norm_bias_f, weight_gu, weight_down)
    arrived = lax.ppermute(passed, "section", [(0, 1)])
    middle_1, low_1, qkv_1, mixture_1 = attend(second, arrived)
    result, _, returned, pairs_1, vectors_1 = back(second, middle_1, low_1, qkv_1, mixture_1, arrived, rows)
    returned = lax.ppermute(returned, "section", [(1, 0)])
    sums = exchange(pairs_1, vectors_1, shards, group, 1, 1, features // 2, name="exchange_second")
    _, grad_in, _, pairs_0, vectors_0 = back(first, middle_0, low_0, qkv_0, mixture_0, rows, returned)
    sums = exchange(pairs_0, vectors_0, shards, group, 0, 2, features // 2, previous=sums, name="exchange_first")
    ends_out = jnp.where(is_first, grad_in, result)[None]
    grad_gate_up, grad_down, grad_out, grad_qkv = (item.astype(F32)[None] for item in sums[:4])
    vectors = sums[4]
    return (
        ends_out,
        vectors[0:1],
        vectors[1:2],
        grad_qkv,
        grad_out,
        vectors[2:3],
        vectors[3:4],
        grad_gate_up,
        grad_down,
    )


def solution(mesh):
    placed = (
        P("section", ("shard", "group"), None),
        P(("shard", "group"), None),
        P("section", None),
        P("section", None),
        P("section", None, None),
        P("section", None, None),
        P("section", None),
        P("section", None),
        P("section", None, None),
        P("section", None, None),
    )
    return jax.shard_map(
        body,
        mesh=mesh,
        in_specs=placed,
        out_specs=(
            P("section", ("shard", "group"), None),
            P("section", "shard"),
            P("section", "shard"),
            P("section", "shard", None),
            P("section", "shard", None),
            P("section", "shard"),
            P("section", "shard"),
            P("section", "shard", None),
            P("section", "shard", None),
        ),
        check_vma=False,
    )
```

```python
import functools

import jax
import jax.numpy as jnp
from jax import lax
from jax.experimental import pallas as pl
from jax.experimental.pallas import tpu as pltpu
from jax.sharding import PartitionSpec as P

MESH = pl.DeviceIdType.MESH
F32, BF16 = jnp.float32, jnp.bfloat16
HEADS = 16
EPSILON = 1e-05


def dot(a, b):
    return jnp.dot(a, b, preferred_element_type=F32)


def dot_cols(a, b):
    return lax.dot_general(a, b, (((1,), (1,)), ((), ())), preferred_element_type=F32)


def dot_rows(a, b):
    return lax.dot_general(a, b, (((0,), (0,)), ((), ())), preferred_element_type=F32)


def in_rows(total, step, run):
    @pl.loop(0, total // step)
    def _(index):
        run(pl.ds(pl.multiple_of(index * step, step), step))


def normalized(values):
    average = jnp.mean(values, axis=-1, keepdims=True)
    centered = values - average
    variance = jnp.mean(centered * centered, axis=-1, keepdims=True)
    spread = lax.rsqrt(variance + EPSILON)
    return centered * spread, spread


def norm_back(grad, values, gain):
    unit, spread = normalized(values)
    scaled = grad * gain
    return spread * (
        scaled
        - jnp.mean(scaled, axis=-1, keepdims=True)
        - unit * jnp.mean(scaled * unit, axis=-1, keepdims=True)
    ), grad * unit


def lanes_of(shape):
    return lax.broadcasted_iota(jnp.int32, shape, len(shape) - 1)


def turn(values, half, size):
    wide = values.shape[-1]
    early = lax.rem(lanes_of(values.shape), size) < half
    return jnp.where(early, pltpu.roll(values, wide - half, 1), pltpu.roll(values, half, 1)), early


def rotated(values, cosine, sine, size):
    other, early = turn(values, size // 2, size)
    return values * cosine + jnp.where(early, -other, other) * sine


def unrotated(values, cosine, sine, size):
    other, early = turn(values * sine, size // 2, size)
    return values * cosine + jnp.where(early, other, -other)


def window_of(index, lengths_ref, row):
    windows = lengths_ref.shape[1]
    end = lengths_ref[row, 0]
    segment = (index >= end).astype(jnp.int32)
    for window in range(1, windows):
        end = end + lengths_ref[row, window]
        segment = segment + (index >= end).astype(jnp.int32)
    return segment


def same_window(lengths_ref, row, tokens):
    queries = window_of(lax.broadcasted_iota(jnp.int32, (tokens, 1), 0), lengths_ref, row)
    keys = window_of(lax.broadcasted_iota(jnp.int32, (1, tokens), 1), lengths_ref, row)
    return queries == keys


def softmax(scores, allowed):
    scores = jnp.where(allowed, scores, -1e30)
    weights = jnp.exp(scores - jnp.max(scores, axis=-1, keepdims=True))
    return weights * (1.0 / jnp.sum(weights, axis=-1, keepdims=True))


def attention_kernel(size, row_tokens, act_ref, lengths_ref, x_ref, gain_ref, bias_ref, gain_f_ref, bias_f_ref,
                     wq_ref, wk_ref, wv_ref, wo_ref, cos_ref, sin_ref, mid_ref, lefts_ref, qkv_ref, mix_ref):
    tokens = x_ref.shape[0]
    part = pl.program_id(0)
    block = wq_ref.shape[1]
    pair = 2 * size

    @pl.when(act_ref[0] == 1)
    def _():
        @pl.when(part == 0)
        def _():
            def begin(rows):
                values = x_ref[rows].astype(F32)
                unit, _ = normalized(values)
                lefts_ref[0, rows] = (unit * gain_ref[...] + bias_ref[...]).astype(BF16)
                mid_ref[rows] = values
            in_rows(tokens, 64, begin)

        for which, weight in enumerate((wq_ref, wk_ref, wv_ref)):
            projected = dot(lefts_ref[0], weight[...])
            for at in range(block // pair):
                lanes = slice(at * pair, (at + 1) * pair)
                values = projected[:, lanes]
                if which < 2:
                    values = rotated(values, cos_ref[...], sin_ref[...], size)
                qkv_ref[which, :, lanes] = values.astype(BF16)

        first = lanes_of((row_tokens, pair)) < size
        for row in range(tokens // row_tokens):
            rows = pl.ds(row * row_tokens, row_tokens)
            allowed = same_window(lengths_ref, row, row_tokens)
            for start in range(0, block // pair, 2):
                work = []
                for at in range(start, start + 2):
                    lanes = pl.ds(at * pair, pair)
                    query, key, value = (qkv_ref[which, rows, lanes] for which in range(3))
                    query = query * (size ** -0.5)
                    for head in range(2):
                        own = jnp.where(first if head == 0 else jnp.logical_not(first), query, jnp.zeros_like(query))
                        work.append((dot_cols(own, key), value))
                work = [(softmax(scores, allowed).astype(BF16), value) for scores, value in work]
                work = [dot(probs, value) for probs, value in work]
                for at in range(2):
                    lanes = pl.ds((start + at) * pair, pair)
                    mix_ref[rows, lanes] = jnp.where(first, work[2 * at], work[2 * at + 1]).astype(BF16)

        mixture = mix_ref[...]
        lefts_ref[1, :, pl.ds(pl.multiple_of(part * block, block), block)] = mixture
        mid_ref[...] += dot(mixture, wo_ref[...])

        @pl.when(part == pl.num_programs(0) - 1)
        def _():
            def close(rows):
                unit, _ = normalized(mid_ref[rows])
                lefts_ref[2, rows] = (unit * gain_f_ref[...] + bias_f_ref[...]).astype(BF16)
            in_rows(tokens, 64, close)


def attention_back_kernel(size, row_tokens, act_ref, lengths_ref, grad_ref, x_ref, gain_ref, qkv_ref, wq_ref, wk_ref,
                          wv_ref, wo_ref, cos_ref, sin_ref, branch_ref, proj_ref, input_ref, input_low_ref,
                          dgain_ref, dbias_ref, gm_ref, total_ref):
    tokens = x_ref.shape[0]
    part = pl.program_id(0)
    block = wq_ref.shape[1]
    pair = 2 * size
    scale = size ** -0.5

    @pl.when(act_ref[0] == 1)
    def _():
        @pl.when(part == 0)
        def _():
            def begin(rows):
                branch_ref[rows] = grad_ref[rows].astype(BF16)
            in_rows(tokens, 64, begin)

        gm_ref[...] = dot_cols(branch_ref[...], wo_ref[...]).astype(BF16)
        first = lanes_of((row_tokens, pair)) < size
        for row in range(tokens // row_tokens):
            rows = pl.ds(row * row_tokens, row_tokens)
            allowed = same_window(lengths_ref, row, row_tokens)
            cosine, sine = cos_ref[rows], sin_ref[rows]
            for start in range(0, block // pair, 2):
                work = []
                for at in range(start, start + 2):
                    lanes = pl.ds(at * pair, pair)
                    query, key, value = (qkv_ref[which, rows, lanes] for which in range(3))
                    grad_mix = gm_ref[rows, lanes]
                    scaled = query * scale
                    for head in range(2):
                        mine = first if head == 0 else jnp.logical_not(first)
                        work.append((
                            query, key, grad_mix,
                            dot_cols(jnp.where(mine, scaled, jnp.zeros_like(scaled)), key),
                            dot_cols(jnp.where(mine, grad_mix, jnp.zeros_like(grad_mix)), value)))
                results = []
                for query, key, grad_mix, scores, grad_probs in work:
                    probs = softmax(scores, allowed)
                    weighted = probs * grad_probs
                    grad_scores = (weighted - probs * jnp.sum(weighted, axis=-1, keepdims=True)).astype(BF16)
                    results.append((query, key, grad_mix, grad_scores, probs.astype(BF16)))
                results = [
                    (dot(grad_scores, key), dot_rows(grad_scores, query), dot_rows(probs, grad_mix))
                    for query, key, grad_mix, grad_scores, probs in results]
                for at in range(2):
                    lanes = pl.ds((start + at) * pair, pair)
                    grad_query, grad_key, grad_value = (
                        jnp.where(first, a, b) for a, b in zip(results[2 * at], results[2 * at + 1]))
                    proj_ref[0, rows, lanes] = unrotated(grad_query * scale, cosine, sine, size).astype(BF16)
                    proj_ref[1, rows, lanes] = unrotated(grad_key * scale, cosine, sine, size).astype(BF16)
                    proj_ref[2, rows, lanes] = grad_value.astype(BF16)

        added = (
            dot_cols(proj_ref[0], wq_ref[...])
            + dot_cols(proj_ref[1], wk_ref[...])
            + dot_cols(proj_ref[2], wv_ref[...])
        )
        total_ref[...] = jnp.where(part == 0, added, total_ref[...] + added)

        @pl.when(part == pl.num_programs(0) - 1)
        def _():
            dgain_ref[...] = jnp.zeros_like(dgain_ref)
            dbias_ref[...] = jnp.zeros_like(dbias_ref)

            def finish(rows):
                grad = total_ref[rows]
                through, by_gain = norm_back(grad, x_ref[rows].astype(F32), gain_ref[...])
                result = grad_ref[rows] + through
                input_ref[rows] = result
                input_low_ref[rows] = result.astype(BF16)
                dgain_ref[...] += jnp.sum(by_gain, axis=0, keepdims=True)
                dbias_ref[...] += jnp.sum(grad, axis=0, keepdims=True)
            in_rows(tokens, 64, finish)


def feed_kernel(unit_rows, act_ref, mid_ref, low_ref, wg_ref, wu_ref, wd_ref, out_ref, half_ref, total_ref):
    part = pl.program_id(0)

    @pl.when(act_ref[0] == 1)
    def _():
        @pl.when(part == 0)
        def _():
            total_ref[...] = mid_ref[...]

        low = low_ref[0]
        gate = dot(low, wg_ref[...])
        up = dot(low, wu_ref[...])
        hidden = (gate / (1.0 + jnp.exp(-gate)) * up).astype(BF16)
        for at in range(half_ref.shape[1] // unit_rows):
            rows = [hidden[:, (2 * at + side) * unit_rows:(2 * at + side + 1) * unit_rows] for side in range(2)]
            half_ref[:, at * unit_rows:(at + 1) * unit_rows] = jnp.where(act_ref[1] == 0, rows[0], rows[1])
        total_ref[...] += dot(hidden, wd_ref[...])

        @pl.when(part == pl.num_programs(0) - 1)
        def _():
            out_ref[...] = total_ref[...].astype(BF16)


def feed_both_kernel(act_ref, mid_ref, low_ref, grad_ref, gain_ref, wg_ref, wu_ref, wd_ref, out_ref,
                     hidden_ref, ggu_ref, grad_mid_ref, dgain_ref, dbias_ref, total_ref):
    tokens = mid_ref.shape[0]
    part = pl.program_id(0)

    @pl.when(act_ref[0] == 1)
    def _():
        @pl.when(part == 0)
        def _():
            out_ref[...] = mid_ref[...]

        low = low_ref[0]
        gate = dot(low, wg_ref[...])
        up = dot(low, wu_ref[...])
        grad_hidden = dot_cols(grad_ref[...], wd_ref[...])
        sig = 1.0 / (1.0 + jnp.exp(-gate))
        silu = gate * sig
        hidden_ref[...] = (silu * up).astype(BF16)
        ggu_ref[0] = (grad_hidden * up * (sig * (1.0 + gate * (1.0 - sig)))).astype(BF16)
        ggu_ref[1] = (grad_hidden * silu).astype(BF16)
        out_ref[...] += dot(hidden_ref[...], wd_ref[...])
        added = dot_cols(ggu_ref[0], wg_ref[...]) + dot_cols(ggu_ref[1], wu_ref[...])
        total_ref[...] = jnp.where(part == 0, added, total_ref[...] + added)

        @pl.when(part == pl.num_programs(0) - 1)
        def _():
            dgain_ref[...] = jnp.zeros_like(dgain_ref)
            dbias_ref[...] = jnp.zeros_like(dbias_ref)

            def finish(rows):
                grad = total_ref[rows]
                through, by_gain = norm_back(grad, mid_ref[rows], gain_ref[...])
                grad_mid_ref[rows] = grad_ref[rows].astype(F32) + through
                dgain_ref[...] += jnp.sum(by_gain, axis=0, keepdims=True)
                dbias_ref[...] += jnp.sum(grad, axis=0, keepdims=True)
            in_rows(tokens, 64, finish)


def whole(shape):
    return pl.BlockSpec(shape, lambda part, *_: (0,) * len(shape))


def column(rows, wide, offset=0):
    return pl.BlockSpec((rows, wide), lambda part, act, *_: (0, (part + offset) * act[0]))


def stacked(count, rows, wide):
    return pl.BlockSpec((count, rows, wide), lambda part, act, *_: (0, 0, part * act[0]))


def lower(rows, wide):
    return pl.BlockSpec((rows, wide), lambda part, act, *_: (part * act[0], 0))


def local_call(kernel, name, grid, scalars, args, in_specs, outs, out_specs, scratch, flops, limit=56):
    return pl.pallas_call(
        kernel,
        grid_spec=pltpu.PrefetchScalarGridSpec(
            num_scalar_prefetch=len(scalars), grid=(grid,), in_specs=in_specs, out_specs=out_specs,
            scratch_shapes=scratch),
        out_shape=outs,
        name=name,
        cost_estimate=pl.CostEstimate(flops=flops, bytes_accessed=40 * 2 ** 20, transcendentals=0),
        compiler_params=pltpu.CompilerParams(
            dimension_semantics=("arbitrary",), vmem_limit_bytes=limit * 1024 * 1024),
    )(*scalars, *args)


def attention(active, lengths, x, gain, bias, gain_f, bias_f, w_qkv, w_out, cosine, sine, parts=2):
    tokens, features = x.shape
    row_tokens = tokens // lengths.shape[0]
    size = features // HEADS
    wide = features // parts
    stack = jax.ShapeDtypeStruct((3, tokens, features), BF16)
    return local_call(
        functools.partial(attention_kernel, size, row_tokens), "attention", parts, (active, lengths),
        (x, gain, bias, gain_f, bias_f, w_qkv, w_qkv, w_qkv, w_out, cosine, sine),
        [whole((tokens, features))] + [whole((1, features))] * 4 + [column(features, wide),
         column(features, wide, parts), column(features, wide, 2 * parts), lower(wide, features),
         whole(cosine.shape), whole(sine.shape)],
        (jax.ShapeDtypeStruct((tokens, features), F32), stack, stack),
        (whole((tokens, features)), whole(stack.shape), stacked(3, tokens, wide)),
        [pltpu.VMEM((tokens, wide), BF16)], 8 * tokens * features ** 2)


def attention_back(active, lengths, grad_mid, x, gain, qkv, w_qkv, w_out, cosine, sine, parts=2):
    tokens, features = x.shape
    row_tokens = tokens // lengths.shape[0]
    size = features // HEADS
    wide = features // parts
    vector = jax.ShapeDtypeStruct((1, features), F32)
    return local_call(
        functools.partial(attention_back_kernel, size, row_tokens), "attention_back", parts, (active, lengths),
        (grad_mid, x, gain, qkv, w_qkv, w_qkv, w_qkv, w_out, cosine, sine),
        [whole((tokens, features)), whole((tokens, features)), whole((1, features)), stacked(3, tokens, wide),
         column(features, wide), column(features, wide, parts), column(features, wide, 2 * parts),
         lower(wide, features), whole(cosine.shape), whole(sine.shape)],
        (jax.ShapeDtypeStruct((tokens, features), BF16), jax.ShapeDtypeStruct((3, tokens, features), BF16),
         jax.ShapeDtypeStruct((tokens, features), F32), jax.ShapeDtypeStruct((tokens, features), BF16),
         vector, vector),
        (whole((tokens, features)), stacked(3, tokens, wide), whole((tokens, features)), whole((tokens, features)),
         whole((1, features)), whole((1, features))),
        [pltpu.VMEM((tokens, wide), BF16), pltpu.VMEM((tokens, features), F32)], 20 * tokens * features ** 2)


def third(tokens, features):
    return pl.BlockSpec((1, tokens, features), lambda part, *_: (2, 0, 0))


def feed(active, mid, lefts, w_gate_up, w_down, unit_rows, parts=8):
    tokens, features = mid.shape
    wide = w_down.shape[0] // parts
    return local_call(
        functools.partial(feed_kernel, unit_rows), "feed", parts, (active,),
        (mid, lefts, w_gate_up, w_gate_up, w_down),
        [whole((tokens, features)), third(tokens, features), column(features, wide), column(features, wide, parts),
         lower(wide, features)],
        (jax.ShapeDtypeStruct((tokens, features), BF16), jax.ShapeDtypeStruct((tokens, w_down.shape[0] // 2), BF16)),
        (whole((tokens, features)), column(tokens, wide // 2)),
        [pltpu.VMEM((tokens, features), F32)], 6 * tokens * features * w_down.shape[0])


def feed_both(active, mid, lefts, grad, gain, w_gate_up, w_down, parts=8):
    tokens, features = mid.shape
    hidden = w_down.shape[0]
    wide = hidden // parts
    vector = jax.ShapeDtypeStruct((1, features), F32)
    return local_call(
        feed_both_kernel, "feed_both", parts, (active,),
        (mid, lefts, grad, gain, w_gate_up, w_gate_up, w_down),
        [whole((tokens, features)), third(tokens, features), whole((tokens, features)), whole((1, features)),
         column(features, wide), column(features, wide, parts), lower(wide, features)],
        (jax.ShapeDtypeStruct((tokens, features), F32), jax.ShapeDtypeStruct((tokens, hidden), BF16),
         jax.ShapeDtypeStruct((2, tokens, hidden), BF16), jax.ShapeDtypeStruct((tokens, features), F32),
         vector, vector),
        (whole((tokens, features)), column(tokens, wide), stacked(2, tokens, wide),
         whole((tokens, features)), whole((1, features)), whole((1, features))),
        [pltpu.VMEM((tokens, features), F32)], 12 * tokens * features * hidden)


def tables(lengths, row_tokens, size):
    index = jnp.arange(row_tokens, dtype=jnp.int32)[None]
    end, before = 0, 0
    for window in range(lengths.shape[1]):
        length = lengths[:, window:window + 1]
        end = end + length
        before = before + jnp.where(index >= end, length, 0)
    position = (index - before).astype(F32).reshape(-1, 1)
    half = jnp.arange(2 * size, dtype=jnp.int32) % (size // 2)
    frequency = 10000.0 ** (-2.0 * half.astype(F32) / size)
    angles = position * frequency
    return jnp.cos(angles), jnp.sin(angles)


def exchange_kernel(cfg, *refs):
    shards, bits, seats, unit_rows, width, section, aliased, late, layers = cfg
    arrays = len(seats)
    refs = list(refs)

    def take(count):
        taken = refs[:count]
        del refs[:count]
        return taken

    lefts, rights = take(arrays), take(arrays)
    left_others, right_others = take(arrays - (1 if late else 0)), take(1)
    lefts = [ref if at is None else ref.at[at] for ref, at in zip(lefts, layers)]
    left_others = [ref if at is None else ref.at[at] for ref, at in zip(left_others, layers)]
    (vector,) = take(1)
    take(arrays + 1 if aliased else 0)
    outs, (vector_out,) = take(arrays), take(1)
    if late:
        left_others = left_others + take(1)
    (vector_land, vector_sum, vector_send, vector_recv, vector_store, left, right, left_sem, right_sem, other_sem,
     right_send, right_recv, late_send, late_recv, mine, side_land, side, side_send, side_recv, chain_a, chain_b,
     chain_send, chain_recv, rest_send, rest_land, rest_keep, rest_ssem, rest_rsem, piece, store_sem, gather_send,
     gather_recv) = refs
    units = sum(seat[0] for seat in seats)
    by_column = units - seats[-1][0]
    others = bits - 1
    final_rows = unit_rows >> others
    tokens = left.shape[1] // 2
    chains = (chain_a, chain_b)
    chain_rows = (final_rows, unit_rows)
    depth = chain_a.shape[1] - 1
    ring = mine.shape[1]
    sec = lax.axis_index("section")
    here = lax.axis_index("shard")
    seat = lax.axis_index("group")
    group = 1 << bits
    peers = shards * group
    me = here * group + seat
    part = vector_out.shape[1]

    def bit_of(index):
        return lax.rem(lax.div(seat, 1 << index), 2)

    def across(index):
        return (sec, here, seat + (1 - 2 * bit_of(index)) * (1 << index))

    above = (sec, jnp.minimum(here + 1, shards - 1), seat)
    below = (sec, jnp.maximum(here - 1, 0), seat)
    half = bit_of(0)

    def remote(source, target, send, recv, device):
        return pltpu.make_async_remote_copy(
            src_ref=source, dst_ref=target, send_sem=send, recv_sem=recv,
            device_id=device, device_id_type=MESH,
        )

    def aligned(start, size):
        return pl.ds(pl.multiple_of(start, size), size)

    def peer(step):
        index = lax.rem(me + step, peers)
        return index, (sec, lax.div(index, group), lax.rem(index, group))

    def vector_copy(index, device):
        return remote(vector.at[:, aligned(device[1] * part, part)], vector_land.at[me], vector_send.at[index],
                      vector_recv.at[me], device)

    def vector_finish():
        vector_sum[...] = vector[:, aligned(here * part, part)]

        @pl.loop(1, peers)
        def _(step):
            index, device = peer(step)
            vector_copy(index, device).wait_send()
            remote(vector_land.at[index], vector_land.at[index], vector_send.at[index], vector_recv.at[index],
                   device).wait_recv()
            vector_sum[...] += vector_land[index]
        copy = pltpu.make_async_copy(vector_sum, vector_out, vector_store)
        copy.start()
        copy.wait()

    def valid(chunk):
        return (chunk >= 0) & (chunk < units)

    def on(condition, run):
        pl.when(condition)(run)

    def by_rows(rows, run, tall=64):
        step = min(rows, tall)

        @pl.loop(0, rows // step)
        def _(index):
            run(aligned(index * step, step))

    def shifted(rows, offset):
        return aligned(rows.start + offset, rows.size)

    pace = min(by_column // seats[-1][0], 2)
    lead = by_column - pace * seats[-1][0]

    def seat_of(chunk):
        behind = jnp.maximum(chunk - lead, 0)
        period = lax.div(behind, pace + 1)
        step = behind - period * (pace + 1)
        last = (chunk >= lead) & (step == 0)
        return last, jnp.where(last, period, jnp.where(chunk < lead, chunk, lead + period * pace + step - 1))

    def each_array(chunk, run):
        last, index = seat_of(chunk)
        start = 0
        for which, (count, blocks, _, _) in enumerate(seats):
            begin = 0 if split_rows(which) else start

            def launch(which=which, begin=begin, blocks=blocks):
                local = index - begin
                row = lax.div(local, blocks)
                run(which, row, local - row * blocks)
            here_it_is = last if split_rows(which) else jnp.logical_not(last) & (index >= start) & (index < start + count)
            on((chunk < units) & here_it_is, launch)
            start += count

    def split_rows(which):
        return which == arrays - 1

    def right_columns(which, block, bit):
        inner = seats[which][2]
        if split_rows(which):
            return 0, aligned(block * (2 * width), 2 * width)
        outer = lax.div(block, inner)
        return outer, aligned((block - outer * inner) * (4 * width) + bit * (2 * width), 2 * width)

    def loads(chunk, run):
        two, four = lax.rem(chunk, 2), lax.rem(chunk, 5)

        def each(which, row, block):
            rows = seats[which][3]
            outer, columns = right_columns(which, block, half)
            run(pltpu.make_async_copy(
                rights[which].at[outer, :, columns], right.at[four, :tokens], right_sem.at[four]))
            if split_rows(which):
                run(pltpu.make_async_copy(
                    right_others[0].at[:, columns], right.at[four, tokens:], other_sem.at[four]))
            for shard in range(shards):
                if split_rows(which):
                    offsets = (shard * rows + (2 * row + half) * unit_rows, shard * (rows // 2) + row * unit_rows)
                else:
                    offsets = (shard * rows + row * unit_rows,) * 2
                for which_side, source in enumerate((lefts[which], left_others[which])):
                    run(pltpu.make_async_copy(
                        source.at[:, aligned(offsets[which_side], unit_rows)],
                        left.at[two, which_side * tokens:(which_side + 1) * tokens,
                                shard * unit_rows:(shard + 1) * unit_rows],
                        left_sem.at[two, which_side, shard]))
        each_array(chunk, each)

    def right_copy(chunk, source):
        four = lax.rem(chunk, 5)
        return remote(source, right.at[four, tokens:], right_send.at[four], right_recv.at[four], across(0))

    def send_right(chunk):
        def each(which, row, block):
            if not split_rows(which):
                outer, columns = right_columns(which, block, 1 - half)
                right_copy(chunk, rights[which].at[outer, :, columns]).start()
        each_array(chunk, each)

    late_rows = seats[-1][3] // (2 * unit_rows)

    def late_copy(row, shard):
        source = aligned(shard * seats[-1][3] + (2 * row + 1 - half) * unit_rows, unit_rows)
        target = aligned(shard * (seats[-1][3] // 2) + row * unit_rows, unit_rows)
        return remote(lefts[-1].at[:, source], left_others[-1].at[:, target], late_send.at[row, shard],
                      late_recv.at[row, shard], across(0))

    def late_turn(turn):
        begin = 0
        for row in range(late_rows):
            need = max(lead + row * seats[-1][1] * (pace + 1) - 1, 0)
            at_once = -(-shards // max(need - begin, 1))
            for index in range(at_once):
                shard = (turn - begin) * at_once + index
                on((turn >= begin) & (shard < shards), lambda row=row, shard=shard: late_copy(row, shard).start())

            def finish(row=row):
                @pl.loop(0, shards)
                def _(shard):
                    late_copy(row, shard).wait_send()
                    late_copy(row, shard).wait_recv()
            on(turn == need, finish)
            begin = need

    def multiply(chunk):
        two, four, slot = lax.rem(chunk, 2), lax.rem(chunk, 5), lax.rem(chunk, ring)
        loads(chunk, lambda copy: copy.wait())

        def arrived():
            copy = right_copy(chunk, right.at[four, tokens:])
            copy.wait_recv()
            copy.wait_send()
        on(jnp.logical_not(seat_of(chunk)[0]), arrived)
        result = lax.dot_general(left[two], right[four], (((0,), (0,)), ((), ())), preferred_element_type=F32)
        for shard in range(shards):
            for path in range(2):
                mine[path, slot, shard] = result[
                    shard * unit_rows:(shard + 1) * unit_rows, path * width:(path + 1) * width].astype(BF16)

    def side_copy(step, chunk):
        slot, four = lax.rem(chunk, ring), lax.rem(chunk, 4)
        rows = unit_rows >> (step + 1)
        away = aligned((1 - bit_of(step + 1)) * rows, rows)
        source = mine.at[0, slot, :, away] if step == 0 else side.at[step - 1, slot, :, away]
        return remote(source, side_land.at[step, four, :, :rows], side_send.at[step, four], side_recv.at[step, four],
                      across(step + 1))

    def side_sum(step, chunk):
        slot, four = lax.rem(chunk, ring), lax.rem(chunk, 4)
        rows = unit_rows >> (step + 1)
        kept = bit_of(step + 1) * rows
        copy = side_copy(step, chunk)
        copy.wait_recv()
        copy.wait_send()

        @pl.loop(0, shards)
        def _(shard):
            def add(part):
                source = mine[0, slot, shard, shifted(part, kept)] if step == 0 else side[
                    step - 1, slot, shard, shifted(part, kept)]
                side[step, slot, shard, part] = (
                    source.astype(F32) + side_land[step, four, shard, part].astype(F32)).astype(BF16)
            by_rows(rows, add)
        if step + 1 < others:
            side_copy(step + 1, chunk).start()

    def base(path, slot, shard, rows):
        return (side[others - 1, slot, shard, rows] if path == 0 else mine[1, slot, shard, rows]).astype(F32)

    def hop(path, way, chunk, shard):
        slot = lax.rem(chunk, depth)
        ref = chains[path].at[way, slot, shard]
        return remote(ref, ref, chain_send.at[path, way, slot, shard], chain_recv.at[path, way, slot, shard],
                      above if way == 0 else below)

    def onward(path, way, chunk):
        slot, from_base = lax.rem(chunk, depth), lax.rem(chunk, ring)
        arrives = here > 0 if way == 0 else here < shards - 1

        @pl.loop(0, shards - 1 - here if way == 0 else here)
        def _(index):
            shard = shards - 1 - index if way == 0 else index
            copy = hop(path, way, chunk, shard)
            on(arrives, lambda: copy.wait_recv())
            source = jnp.where(arrives, slot, depth)

            def add(rows):
                chains[path][way, slot, shard, rows] = (
                    chains[path][way, source, shard, rows].astype(F32) + base(path, from_base, shard, rows)
                ).astype(BF16)
            by_rows(chain_rows[path], add)
            copy.start()

    def sent(path, way, chunk):
        @pl.loop(0, shards - 1 - here if way == 0 else here)
        def _(index):
            hop(path, way, chunk, shards - 1 - index if way == 0 else index).wait_send()

    def last_hop(path, chunk):
        from_base, slot = lax.rem(chunk, ring), lax.rem(chunk, depth)
        on(here > 0, lambda: hop(path, 0, chunk, here).wait_recv())
        on(here < shards - 1, lambda: hop(path, 1, chunk, here).wait_recv())
        from_below = jnp.where(here > 0, slot, depth)
        from_above = jnp.where(here < shards - 1, slot, depth)

        def total(rows, offset):
            rows = shifted(rows, offset)
            return (
                base(path, from_base, here, rows)
                + chains[path][0, from_below, here, rows].astype(F32)
                + chains[path][1, from_above, here, rows].astype(F32)
            )
        if path == 0:
            finish(path, chunk, total)
        else:
            share(0, chunk, total)

    def rest_copy(step, chunk):
        slot, rows = lax.rem(chunk, 4), pl.ds(0, unit_rows >> (step + 1))
        return remote(rest_send.at[step, slot, rows], rest_land.at[step, slot, rows], rest_ssem.at[step, slot],
                      rest_rsem.at[step, slot], across(step + 1))

    def share(step, chunk, total):
        slot, rows = lax.rem(chunk, 4), unit_rows >> (step + 1)
        bit = bit_of(step + 1)

        def give(part):
            rest_send[step, slot, part] = total(part, (1 - bit) * rows).astype(BF16)
        by_rows(rows, give)
        rest_copy(step, chunk).start()

        def keep(part):
            rest_keep[step, slot, part] = total(part, bit * rows)
        by_rows(rows, keep)

    def rest_sum(step, chunk):
        slot = lax.rem(chunk, 4)
        copy = rest_copy(step, chunk)
        copy.wait_recv()
        copy.wait_send()

        def total(part, offset):
            part = shifted(part, offset)
            return rest_keep[step, slot, part] + rest_land[step, slot, part].astype(F32)
        if step + 1 < others:
            share(step + 1, chunk, total)
        else:
            finish(1, chunk, total)

    def finish(path, chunk, total):
        def put(part):
            piece[path, lax.rem(chunk, 4), part] = total(part, 0).astype(BF16)
        by_rows(final_rows, put)
        spread(path, 0, chunk)

    def place(which, row, block, path, bit, offset, rows):
        if split_rows(which):
            row0, column = (2 * row + bit) * unit_rows, block * (2 * width) + path * width
        else:
            row0, column = row * unit_rows, block * (4 * width) + bit * (2 * width) + path * width
        return outs[which].at[aligned(row0 + offset, rows), aligned(column, width)]

    def seat_row(steps):
        row = 0
        for step in range(steps):
            row = row + bit_of(step + 1) * (unit_rows >> (step + 1))
        return row

    def store(path, chunk, target):
        slot = lax.rem(chunk, 4)
        return pltpu.make_async_copy(piece.at[path, slot], target, store_sem.at[path, slot])

    def gather(path, step, other, chunk, target):
        slot = lax.rem(chunk, 4)
        source = piece.at[path, slot] if step == 0 else target
        return remote(source, target, gather_send.at[path, step, other, slot], gather_recv.at[path, step, other, slot],
                      across(0 if step == 0 else bits - step))

    def spread(path, step, chunk):
        steps = others - max(step - 1, 0)
        rows = unit_rows >> steps

        def each(which, row, block):
            for other in range(1 if step == 0 else 2):
                bit = half if other == 0 else 1 - half
                target = place(which, row, block, path, bit, seat_row(steps), rows)
                if step == 0:
                    store(path, chunk, target).start()
                gather(path, step, other, chunk, target).start()
        each_array(chunk, each)

    def gathered(path, step, chunk):
        rows = unit_rows >> (others - max(step - 1, 0))
        target = outs[0].at[pl.ds(0, rows), pl.ds(0, width)]
        for other in range(1 if step == 0 else 2):
            copy = gather(path, step, other, chunk, target)
            copy.wait_recv()
            copy.wait_send()
        if step == 0:
            store(path, chunk, target).wait()
        if step + 1 < bits:
            spread(path, step + 1, chunk)

    def work():
        barrier = pltpu.get_barrier_semaphore()

        @pl.loop(1, peers)
        def _(step):
            pl.semaphore_signal(barrier, inc=1, device_id=peer(step)[1], device_id_type=MESH)
        pl.semaphore_wait(barrier, peers - 1)
        send_right(0)
        loads(0, lambda copy: copy.start())

        @pl.loop(1, peers)
        def _(step):
            vector_copy(*peer(step)).start()

        for path in range(2):
            for way in range(2):
                @pl.loop(0, shards)
                def _(shard):
                    def clear(rows):
                        chains[path][way, depth, shard, rows] = jnp.zeros((rows.size, width), BF16)
                    by_rows(chain_rows[path], clear)

        line = shards - 1

        @pl.loop(0, units + line + others + bits + 2)
        def _(turn):
            on(turn + 1 < units, lambda: send_right(turn + 1))
            if late:
                late_turn(turn)
            on(turn + 1 < units, lambda: loads(turn + 1, lambda copy: copy.start()))

            def opening():
                multiply(turn)
                side_copy(0, turn).start()
            on(turn < units, opening)
            for step in range(others):
                on(valid(turn - 1 - step), lambda step=step: side_sum(step, turn - 1 - step))
            for path in range(2):
                for way in range(2):
                    chunk = turn - (others if path == 0 else 0) - (here if way == 0 else line - here)
                    on(valid(chunk - 2), lambda path=path, way=way, chunk=chunk: sent(path, way, chunk - 2))
                    on(valid(chunk), lambda path=path, way=way, chunk=chunk: onward(path, way, chunk))
            on(valid(turn - line), lambda: last_hop(1, turn - line))
            on(valid(turn - line - others), lambda: last_hop(0, turn - line - others))
            for step in range(others):
                on(valid(turn - line - 1 - step), lambda step=step: rest_sum(step, turn - line - 1 - step))
            for step in range(bits):
                for path in range(2):
                    chunk = turn - line - others - 1 - step
                    on(valid(chunk), lambda path=path, step=step, chunk=chunk: gathered(path, step, chunk))

        vector_finish()

    if section is None:
        work()
    else:
        pl.when(sec == section)(work)


def exchange(pairs, vector, shards, group, section, collective_id, unit_width, previous=None, unit_rows_max=256,
             name="exchange"):
    bits = group.bit_length() - 1
    arrays = len(pairs)
    lefts, rights = [pair[0][0] for pair in pairs], [pair[1] for pair in pairs]
    layers = tuple(pair[0][1] for pair in pairs)
    left_others = [pair[2] for pair in pairs]
    late = left_others[-1] is None
    if late:
        left_others = left_others[:-1]
    tokens = lefts[0].shape[-2]
    rows_of = [left.shape[-1] // shards for left in lefts]
    unit_rows = min([unit_rows_max] + rows_of[:-1])
    width = unit_width // 4
    seats = []
    for index, (rows, right) in enumerate(zip(rows_of, rights)):
        tall, wide = (2 * unit_rows, 2 * width) if index == arrays - 1 else (unit_rows, 4 * width)
        inner = right.shape[2] // wide
        seats.append((rows // tall * right.shape[0] * inner, right.shape[0] * inner, inner, rows))
    units = sum(seat[0] for seat in seats)
    others = bits - 1
    final_rows = unit_rows >> others
    depth, ring = shards + 3, shards + 2
    late_rows = rows_of[-1] // (2 * unit_rows)
    peers, lanes = shards * group, vector.shape[1] // shards
    dma = pltpu.SemaphoreType.DMA
    scratch = [
        pltpu.VMEM((peers, vector.shape[0], lanes), F32),
        pltpu.VMEM((vector.shape[0], lanes), F32),
        dma((peers,)), dma((peers,)), dma,
        pltpu.VMEM((2, 2 * tokens, shards * unit_rows), BF16),
        pltpu.VMEM((5, 2 * tokens, 2 * width), BF16),
        dma((2, 2, shards)), dma((5,)), dma((5,)),
        dma((5,)), dma((5,)),
        dma((late_rows, shards)), dma((late_rows, shards)),
        pltpu.VMEM((2, ring, shards, unit_rows, width), BF16),
        pltpu.VMEM((others, 4, shards, unit_rows // 2, width), BF16),
        pltpu.VMEM((others, ring, shards, unit_rows // 2, width), BF16),
        dma((others, 4)), dma((others, 4)),
        pltpu.VMEM((2, depth + 1, shards, final_rows, width), BF16),
        pltpu.VMEM((2, depth + 1, shards, unit_rows, width), BF16),
        dma((2, 2, depth, shards)), dma((2, 2, depth, shards)),
        pltpu.VMEM((others, 4, unit_rows // 2, width), BF16),
        pltpu.VMEM((others, 4, unit_rows // 2, width), BF16),
        pltpu.VMEM((others, 4, unit_rows // 2, width), F32),
        dma((others, 4)), dma((others, 4)),
        pltpu.VMEM((2, 4, final_rows, width), BF16),
        dma((2, 4)),
        dma((2, bits, 2, 4)), dma((2, bits, 2, 4)),
    ]
    cfg = (shards, bits, tuple(seats), unit_rows, width, section, previous is not None, late, layers)
    operands = lefts + rights + left_others + [pairs[-1][3], vector] + list(previous or [])
    first = len(operands) - len(previous or [])
    results = [jax.ShapeDtypeStruct((r, g.shape[0] * g.shape[2]), BF16) for r, g in zip(rows_of, rights)]
    results.append(jax.ShapeDtypeStruct((vector.shape[0], lanes), F32))
    if late:
        results.append(jax.ShapeDtypeStruct((tokens, lefts[-1].shape[-1] // 2), BF16))
    hbm, vmem = pl.BlockSpec(memory_space=pl.ANY), pl.BlockSpec(memory_space=pltpu.VMEM)
    in_specs = [vmem if index == first - 1 else hbm for index in range(len(operands))]
    return pl.pallas_call(
        functools.partial(exchange_kernel, cfg),
        out_shape=results,
        in_specs=in_specs,
        out_specs=[hbm] * len(results),
        scratch_shapes=scratch,
        input_output_aliases={first + index: index for index in range(len(previous or []))},
        name=name,
        cost_estimate=pl.CostEstimate(
            flops=4 * tokens * units * shards * unit_rows * 2 * width, bytes_accessed=100 * 2 ** 20,
            transcendentals=0),
        compiler_params=pltpu.CompilerParams(
            collective_id=collective_id, has_side_effects=True, vmem_limit_bytes=56 * 1024 * 1024),
    )(*operands)[:arrays + 1]


UNIT_WIDTH = 512


def body(
    ends_in,
    lengths,
    norm_gain_a,
    norm_bias_a,
    w_qkv,
    w_out,
    norm_gain_f,
    norm_bias_f,
    w_gate_up,
    w_down,
):
    section = lax.axis_index("section")
    shards, group = lax.axis_size("shard"), lax.axis_size("group")
    is_first = section == 0
    first, second = ((section == which).astype(jnp.int32).reshape(1) for which in range(2))
    tokens, features = ends_in.shape[1:]
    size = features // HEADS
    rows = ends_in[0]
    weight_qkv, weight_out, weight_gu, weight_down = w_qkv[0], w_out[0], w_gate_up[0], w_down[0]
    cosine, sine = tables(lengths, tokens // lengths.shape[0], size)
    nothing = jnp.zeros((4, features), F32)
    unit_rows = min(256, features // shards)
    partner_bit = (1 - lax.axis_index("group") % 2).astype(jnp.int32).reshape(1)

    def beside(which, array):
        pairs = [(which * group + index, which * group + (index ^ 1)) for index in range(group)]
        return lax.ppermute(array, ("section", "group"), pairs)

    def attend(active, values):
        return attention(active, lengths, values, norm_gain_a, norm_bias_a, norm_gain_f, norm_bias_f, weight_qkv,
                         weight_out, cosine, sine)

    def back(active, middle, lefts, qkv, values, grad):
        result, hidden, grad_gu, grad_middle, gain_f, bias_f = feed_both(
            active, middle, lefts, grad, norm_gain_f, weight_gu, weight_down)
        branch, grad_qkv, grad_in, grad_in_low, gain_a, bias_a = attention_back(
            active, lengths, grad_middle, values, norm_gain_a, qkv, weight_qkv, weight_out, cosine, sine)
        vectors = jnp.concatenate([gain_a, bias_a, gain_f, bias_f, nothing], axis=0)
        return result, grad_in, grad_in_low, hidden, (grad_gu, branch[None], grad_qkv, grad[None]), vectors

    def sum_all(which, lefts, lefts_beside, hidden, hidden_beside, rights, right_beside, vectors, **more):
        pairs = [((lefts, at), right, lefts_beside) for at, right in zip((2, 1, 0), rights)]
        pairs.append(((hidden, None), rights[3], hidden_beside, right_beside))
        return exchange(pairs, vectors, shards, group, which, which + 1, UNIT_WIDTH * features // 1024, **more)

    rows_beside = beside(1, rows)
    middle_0, lefts_0, qkv_0 = attend(first, rows)
    passed, hidden_half_0 = feed(
        jnp.concatenate([first, partner_bit]), middle_0, lefts_0, weight_gu, weight_down, unit_rows)
    arrived = lax.ppermute(passed, "section", [(0, 1)])
    lefts_beside_0, hidden_beside_0 = beside(0, lefts_0), beside(0, hidden_half_0)
    middle_1, lefts_1, qkv_1 = attend(second, arrived)
    lefts_beside_1 = beside(1, lefts_1)
    result, _, returned, hidden_1, rights_1, vectors_1 = back(second, middle_1, lefts_1, qkv_1, arrived, rows)
    returned = lax.ppermute(returned, "section", [(1, 0)])
    sums = sum_all(1, lefts_1, lefts_beside_1, hidden_1, None, rights_1, rows_beside, vectors_1,
                   name="exchange_second")
    returned, _, lefts_beside_0, hidden_beside_0 = lax.optimization_barrier(
        (returned, sums[4], lefts_beside_0, hidden_beside_0))
    returned_beside = beside(0, returned)
    _, grad_in, _, hidden_0, rights_0, vectors_0 = back(first, middle_0, lefts_0, qkv_0, rows, returned)
    sums = sum_all(0, lefts_0, lefts_beside_0, hidden_0, hidden_beside_0, rights_0, returned_beside, vectors_0,
                   previous=sums, name="exchange_first")
    ends_out = jnp.where(is_first, grad_in, result)[None]
    grad_gate_up, grad_out, grad_qkv, grad_down = (item.astype(F32)[None] for item in sums[:4])
    vectors = sums[4]
    return (
        ends_out,
        vectors[0:1],
        vectors[1:2],
        grad_qkv,
        grad_out,
        vectors[2:3],
        vectors[3:4],
        grad_gate_up,
        grad_down,
    )


def solution(mesh):
    placed = (
        P("section", ("shard", "group"), None),
        P(("shard", "group"), None),
        P("section", None),
        P("section", None),
        P("section", None, None),
        P("section", None, None),
        P("section", None),
        P("section", None),
        P("section", None, None),
        P("section", None, None),
    )
    return jax.shard_map(
        body,
        mesh=mesh,
        in_specs=placed,
        out_specs=(
            P("section", ("shard", "group"), None),
            P("section", "shard"),
            P("section", "shard"),
            P("section", "shard", None),
            P("section", "shard", None),
            P("section", "shard"),
            P("section", "shard"),
            P("section", "shard", None),
            P("section", "shard", None),
        ),
        check_vma=False,
    )
```

```python
import functools

import jax
import jax.numpy as jnp
from jax import lax
from jax.experimental import pallas as pl
from jax.experimental.pallas import tpu as pltpu
from jax.sharding import PartitionSpec as P

MESH = pl.DeviceIdType.MESH
F32, BF16 = jnp.float32, jnp.bfloat16
HEADS = 16
EPSILON = 1e-05


def dot(a, b):
    return jnp.dot(a, b, preferred_element_type=F32)


def dot_cols(a, b):
    return lax.dot_general(a, b, (((1,), (1,)), ((), ())), preferred_element_type=F32)


def dot_rows(a, b):
    return lax.dot_general(a, b, (((0,), (0,)), ((), ())), preferred_element_type=F32)


def in_rows(total, step, run):
    @pl.loop(0, total // step)
    def _(index):
        run(pl.ds(pl.multiple_of(index * step, step), step))


def normalized(values):
    average = jnp.mean(values, axis=-1, keepdims=True)
    centered = values - average
    variance = jnp.mean(centered * centered, axis=-1, keepdims=True)
    spread = lax.rsqrt(variance + EPSILON)
    return centered * spread, spread


def norm_back(grad, values, gain):
    unit, spread = normalized(values)
    scaled = grad * gain
    return spread * (
        scaled
        - jnp.mean(scaled, axis=-1, keepdims=True)
        - unit * jnp.mean(scaled * unit, axis=-1, keepdims=True)
    ), grad * unit


def lanes_of(shape):
    return lax.broadcasted_iota(jnp.int32, shape, len(shape) - 1)


def turn(values, half, size):
    wide = values.shape[-1]
    early = lax.rem(lanes_of(values.shape), size) < half
    return jnp.where(early, pltpu.roll(values, wide - half, 1), pltpu.roll(values, half, 1)), early


def rotated(values, cosine, sine, size):
    other, early = turn(values, size // 2, size)
    return values * cosine + jnp.where(early, -other, other) * sine


def unrotated(values, cosine, sine, size):
    other, early = turn(values * sine, size // 2, size)
    return values * cosine + jnp.where(early, other, -other)


def window_of(index, lengths_ref, row):
    windows = lengths_ref.shape[1]
    end = lengths_ref[row, 0]
    segment = (index >= end).astype(jnp.int32)
    for window in range(1, windows):
        end = end + lengths_ref[row, window]
        segment = segment + (index >= end).astype(jnp.int32)
    return segment


def same_window(lengths_ref, row, tokens):
    queries = window_of(lax.broadcasted_iota(jnp.int32, (tokens, 1), 0), lengths_ref, row)
    keys = window_of(lax.broadcasted_iota(jnp.int32, (1, tokens), 1), lengths_ref, row)
    return queries == keys


def softmax(scores, allowed):
    scores = jnp.where(allowed, scores, -1e30)
    weights = jnp.exp(scores - jnp.max(scores, axis=-1, keepdims=True))
    return weights * (1.0 / jnp.sum(weights, axis=-1, keepdims=True))


def attention_kernel(size, row_tokens, act_ref, lengths_ref, x_ref, gain_ref, bias_ref, gain_f_ref, bias_f_ref,
                     wq_ref, wk_ref, wv_ref, wo_ref, cos_ref, sin_ref, mid_ref, lefts_ref, qkv_ref, mix_ref):
    tokens = x_ref.shape[0]
    part = pl.program_id(0)
    block = wq_ref.shape[1]
    pair = 2 * size

    @pl.when(act_ref[0] == 1)
    def _():
        @pl.when(part == 0)
        def _():
            def begin(rows):
                values = x_ref[rows].astype(F32)
                unit, _ = normalized(values)
                lefts_ref[0, rows] = (unit * gain_ref[...] + bias_ref[...]).astype(BF16)
                mid_ref[rows] = values
            in_rows(tokens, 64, begin)

        for which, weight in enumerate((wq_ref, wk_ref, wv_ref)):
            projected = dot(lefts_ref[0], weight[...])
            for at in range(block // pair):
                lanes = slice(at * pair, (at + 1) * pair)
                values = projected[:, lanes]
                if which < 2:
                    values = rotated(values, cos_ref[...], sin_ref[...], size)
                qkv_ref[which, :, lanes] = values.astype(BF16)

        first = lanes_of((row_tokens, pair)) < size
        for row in range(tokens // row_tokens):
            rows = pl.ds(row * row_tokens, row_tokens)
            allowed = same_window(lengths_ref, row, row_tokens)
            for start in range(0, block // pair, 2):
                work = []
                for at in range(start, start + 2):
                    lanes = pl.ds(at * pair, pair)
                    query, key, value = (qkv_ref[which, rows, lanes] for which in range(3))
                    query = query * (size ** -0.5)
                    for head in range(2):
                        own = jnp.where(first if head == 0 else jnp.logical_not(first), query, jnp.zeros_like(query))
                        work.append((dot_cols(own, key), value))
                work = [(softmax(scores, allowed).astype(BF16), value) for scores, value in work]
                work = [dot(probs, value) for probs, value in work]
                for at in range(2):
                    lanes = pl.ds((start + at) * pair, pair)
                    mix_ref[rows, lanes] = jnp.where(first, work[2 * at], work[2 * at + 1]).astype(BF16)

        mixture = mix_ref[...]
        lefts_ref[1, :, pl.ds(pl.multiple_of(part * block, block), block)] = mixture
        mid_ref[...] += dot(mixture, wo_ref[...])

        @pl.when(part == pl.num_programs(0) - 1)
        def _():
            def close(rows):
                unit, _ = normalized(mid_ref[rows])
                lefts_ref[2, rows] = (unit * gain_f_ref[...] + bias_f_ref[...]).astype(BF16)
            in_rows(tokens, 64, close)


def attention_back_kernel(size, row_tokens, act_ref, lengths_ref, grad_ref, x_ref, gain_ref, qkv_ref, wq_ref, wk_ref,
                          wv_ref, wo_ref, cos_ref, sin_ref, branch_ref, proj_ref, input_ref, input_low_ref,
                          dgain_ref, dbias_ref, gm_ref, total_ref):
    tokens = x_ref.shape[0]
    part = pl.program_id(0)
    block = wq_ref.shape[1]
    pair = 2 * size
    scale = size ** -0.5

    @pl.when(act_ref[0] == 1)
    def _():
        @pl.when(part == 0)
        def _():
            def begin(rows):
                branch_ref[rows] = grad_ref[rows].astype(BF16)
            in_rows(tokens, 64, begin)

        gm_ref[...] = dot_cols(branch_ref[...], wo_ref[...]).astype(BF16)
        first = lanes_of((row_tokens, pair)) < size
        for row in range(tokens // row_tokens):
            rows = pl.ds(row * row_tokens, row_tokens)
            allowed = same_window(lengths_ref, row, row_tokens)
            cosine, sine = cos_ref[rows], sin_ref[rows]
            for start in range(0, block // pair, 2):
                work = []
                for at in range(start, start + 2):
                    lanes = pl.ds(at * pair, pair)
                    query, key, value = (qkv_ref[which, rows, lanes] for which in range(3))
                    grad_mix = gm_ref[rows, lanes]
                    scaled = query * scale
                    for head in range(2):
                        mine = first if head == 0 else jnp.logical_not(first)
                        work.append((
                            query, key, grad_mix,
                            dot_cols(jnp.where(mine, scaled, jnp.zeros_like(scaled)), key),
                            dot_cols(jnp.where(mine, grad_mix, jnp.zeros_like(grad_mix)), value)))
                results = []
                for query, key, grad_mix, scores, grad_probs in work:
                    probs = softmax(scores, allowed)
                    weighted = probs * grad_probs
                    grad_scores = (weighted - probs * jnp.sum(weighted, axis=-1, keepdims=True)).astype(BF16)
                    results.append((query, key, grad_mix, grad_scores, probs.astype(BF16)))
                results = [
                    (dot(grad_scores, key), dot_rows(grad_scores, query), dot_rows(probs, grad_mix))
                    for query, key, grad_mix, grad_scores, probs in results]
                for at in range(2):
                    lanes = pl.ds((start + at) * pair, pair)
                    grad_query, grad_key, grad_value = (
                        jnp.where(first, a, b) for a, b in zip(results[2 * at], results[2 * at + 1]))
                    proj_ref[0, rows, lanes] = unrotated(grad_query * scale, cosine, sine, size).astype(BF16)
                    proj_ref[1, rows, lanes] = unrotated(grad_key * scale, cosine, sine, size).astype(BF16)
                    proj_ref[2, rows, lanes] = grad_value.astype(BF16)

        added = (
            dot_cols(proj_ref[0], wq_ref[...])
            + dot_cols(proj_ref[1], wk_ref[...])
            + dot_cols(proj_ref[2], wv_ref[...])
        )
        total_ref[...] = jnp.where(part == 0, added, total_ref[...] + added)

        @pl.when(part == pl.num_programs(0) - 1)
        def _():
            dgain_ref[...] = jnp.zeros_like(dgain_ref)
            dbias_ref[...] = jnp.zeros_like(dbias_ref)

            def finish(rows):
                grad = total_ref[rows]
                through, by_gain = norm_back(grad, x_ref[rows].astype(F32), gain_ref[...])
                result = grad_ref[rows] + through
                input_ref[rows] = result
                input_low_ref[rows] = result.astype(BF16)
                dgain_ref[...] += jnp.sum(by_gain, axis=0, keepdims=True)
                dbias_ref[...] += jnp.sum(grad, axis=0, keepdims=True)
            in_rows(tokens, 64, finish)


def feed_kernel(unit_rows, act_ref, mid_ref, low_ref, wg_ref, wu_ref, wd_ref, out_ref, half_ref, total_ref):
    part = pl.program_id(0)

    @pl.when(act_ref[0] == 1)
    def _():
        @pl.when(part == 0)
        def _():
            total_ref[...] = mid_ref[...]

        low = low_ref[0]
        gate = dot(low, wg_ref[...])
        up = dot(low, wu_ref[...])
        hidden = (gate / (1.0 + jnp.exp(-gate)) * up).astype(BF16)
        for at in range(half_ref.shape[1] // unit_rows):
            rows = [hidden[:, (2 * at + side) * unit_rows:(2 * at + side + 1) * unit_rows] for side in range(2)]
            half_ref[:, at * unit_rows:(at + 1) * unit_rows] = jnp.where(act_ref[1] == 0, rows[0], rows[1])
        total_ref[...] += dot(hidden, wd_ref[...])

        @pl.when(part == pl.num_programs(0) - 1)
        def _():
            out_ref[...] = total_ref[...].astype(BF16)


def feed_both_kernel(act_ref, mid_ref, low_ref, grad_ref, gain_ref, wg_ref, wu_ref, wd_ref, out_ref,
                     hidden_ref, ggu_ref, grad_mid_ref, dgain_ref, dbias_ref, total_ref):
    tokens = mid_ref.shape[0]
    part = pl.program_id(0)

    @pl.when(act_ref[0] == 1)
    def _():
        @pl.when(part == 0)
        def _():
            out_ref[...] = mid_ref[...]

        low = low_ref[0]
        gate = dot(low, wg_ref[...])
        up = dot(low, wu_ref[...])
        grad_hidden = dot_cols(grad_ref[...], wd_ref[...])
        sig = 1.0 / (1.0 + jnp.exp(-gate))
        silu = gate * sig
        hidden_ref[...] = (silu * up).astype(BF16)
        ggu_ref[0] = (grad_hidden * up * (sig * (1.0 + gate * (1.0 - sig)))).astype(BF16)
        ggu_ref[1] = (grad_hidden * silu).astype(BF16)
        out_ref[...] += dot(hidden_ref[...], wd_ref[...])
        added = dot_cols(ggu_ref[0], wg_ref[...]) + dot_cols(ggu_ref[1], wu_ref[...])
        total_ref[...] = jnp.where(part == 0, added, total_ref[...] + added)

        @pl.when(part == pl.num_programs(0) - 1)
        def _():
            dgain_ref[...] = jnp.zeros_like(dgain_ref)
            dbias_ref[...] = jnp.zeros_like(dbias_ref)

            def finish(rows):
                grad = total_ref[rows]
                through, by_gain = norm_back(grad, mid_ref[rows], gain_ref[...])
                grad_mid_ref[rows] = grad_ref[rows].astype(F32) + through
                dgain_ref[...] += jnp.sum(by_gain, axis=0, keepdims=True)
                dbias_ref[...] += jnp.sum(grad, axis=0, keepdims=True)
            in_rows(tokens, 64, finish)


def whole(shape):
    return pl.BlockSpec(shape, lambda part, *_: (0,) * len(shape))


def column(rows, wide, offset=0):
    return pl.BlockSpec((rows, wide), lambda part, act, *_: (0, (part + offset) * act[0]))


def stacked(count, rows, wide):
    return pl.BlockSpec((count, rows, wide), lambda part, act, *_: (0, 0, part * act[0]))


def lower(rows, wide):
    return pl.BlockSpec((rows, wide), lambda part, act, *_: (part * act[0], 0))


def local_call(kernel, name, grid, scalars, args, in_specs, outs, out_specs, scratch, flops, limit=56):
    return pl.pallas_call(
        kernel,
        grid_spec=pltpu.PrefetchScalarGridSpec(
            num_scalar_prefetch=len(scalars), grid=(grid,), in_specs=in_specs, out_specs=out_specs,
            scratch_shapes=scratch),
        out_shape=outs,
        name=name,
        cost_estimate=pl.CostEstimate(flops=flops, bytes_accessed=40 * 2 ** 20, transcendentals=0),
        compiler_params=pltpu.CompilerParams(
            dimension_semantics=("arbitrary",), vmem_limit_bytes=limit * 1024 * 1024),
    )(*scalars, *args)


def attention(active, lengths, x, gain, bias, gain_f, bias_f, w_qkv, w_out, cosine, sine, parts=2):
    tokens, features = x.shape
    row_tokens = tokens // lengths.shape[0]
    size = features // HEADS
    wide = features // parts
    stack = jax.ShapeDtypeStruct((3, tokens, features), BF16)
    return local_call(
        functools.partial(attention_kernel, size, row_tokens), "attention", parts, (active, lengths),
        (x, gain, bias, gain_f, bias_f, w_qkv, w_qkv, w_qkv, w_out, cosine, sine),
        [whole((tokens, features))] + [whole((1, features))] * 4 + [column(features, wide),
         column(features, wide, parts), column(features, wide, 2 * parts), lower(wide, features),
         whole(cosine.shape), whole(sine.shape)],
        (jax.ShapeDtypeStruct((tokens, features), F32), stack, stack),
        (whole((tokens, features)), whole(stack.shape), stacked(3, tokens, wide)),
        [pltpu.VMEM((tokens, wide), BF16)], 8 * tokens * features ** 2)


def attention_back(active, lengths, grad_mid, x, gain, qkv, w_qkv, w_out, cosine, sine, parts=2):
    tokens, features = x.shape
    row_tokens = tokens // lengths.shape[0]
    size = features // HEADS
    wide = features // parts
    vector = jax.ShapeDtypeStruct((1, features), F32)
    return local_call(
        functools.partial(attention_back_kernel, size, row_tokens), "attention_back", parts, (active, lengths),
        (grad_mid, x, gain, qkv, w_qkv, w_qkv, w_qkv, w_out, cosine, sine),
        [whole((tokens, features)), whole((tokens, features)), whole((1, features)), stacked(3, tokens, wide),
         column(features, wide), column(features, wide, parts), column(features, wide, 2 * parts),
         lower(wide, features), whole(cosine.shape), whole(sine.shape)],
        (jax.ShapeDtypeStruct((tokens, features), BF16), jax.ShapeDtypeStruct((3, tokens, features), BF16),
         jax.ShapeDtypeStruct((tokens, features), F32), jax.ShapeDtypeStruct((tokens, features), BF16),
         vector, vector),
        (whole((tokens, features)), stacked(3, tokens, wide), whole((tokens, features)), whole((tokens, features)),
         whole((1, features)), whole((1, features))),
        [pltpu.VMEM((tokens, wide), BF16), pltpu.VMEM((tokens, features), F32)], 20 * tokens * features ** 2)


def third(tokens, features):
    return pl.BlockSpec((1, tokens, features), lambda part, *_: (2, 0, 0))


def feed(active, mid, lefts, w_gate_up, w_down, unit_rows, parts=8):
    tokens, features = mid.shape
    wide = w_down.shape[0] // parts
    return local_call(
        functools.partial(feed_kernel, unit_rows), "feed", parts, (active,),
        (mid, lefts, w_gate_up, w_gate_up, w_down),
        [whole((tokens, features)), third(tokens, features), column(features, wide), column(features, wide, parts),
         lower(wide, features)],
        (jax.ShapeDtypeStruct((tokens, features), BF16), jax.ShapeDtypeStruct((tokens, w_down.shape[0] // 2), BF16)),
        (whole((tokens, features)), column(tokens, wide // 2)),
        [pltpu.VMEM((tokens, features), F32)], 6 * tokens * features * w_down.shape[0])


def feed_both(active, mid, lefts, grad, gain, w_gate_up, w_down, parts=8):
    tokens, features = mid.shape
    hidden = w_down.shape[0]
    wide = hidden // parts
    vector = jax.ShapeDtypeStruct((1, features), F32)
    return local_call(
        feed_both_kernel, "feed_both", parts, (active,),
        (mid, lefts, grad, gain, w_gate_up, w_gate_up, w_down),
        [whole((tokens, features)), third(tokens, features), whole((tokens, features)), whole((1, features)),
         column(features, wide), column(features, wide, parts), lower(wide, features)],
        (jax.ShapeDtypeStruct((tokens, features), F32), jax.ShapeDtypeStruct((tokens, hidden), BF16),
         jax.ShapeDtypeStruct((2, tokens, hidden), BF16), jax.ShapeDtypeStruct((tokens, features), F32),
         vector, vector),
        (whole((tokens, features)), column(tokens, wide), stacked(2, tokens, wide),
         whole((tokens, features)), whole((1, features)), whole((1, features))),
        [pltpu.VMEM((tokens, features), F32)], 12 * tokens * features * hidden)


def tables(lengths, row_tokens, size):
    index = jnp.arange(row_tokens, dtype=jnp.int32)[None]
    end, before = 0, 0
    for window in range(lengths.shape[1]):
        length = lengths[:, window:window + 1]
        end = end + length
        before = before + jnp.where(index >= end, length, 0)
    position = (index - before).astype(F32).reshape(-1, 1)
    half = jnp.arange(2 * size, dtype=jnp.int32) % (size // 2)
    frequency = 10000.0 ** (-2.0 * half.astype(F32) / size)
    angles = position * frequency
    return jnp.cos(angles), jnp.sin(angles)


def exchange_kernel(cfg, *refs):
    shards, bits, seats, unit_rows, width, section, aliased, late, layers, lag = cfg
    arrays = len(seats)
    refs = list(refs)

    def take(count):
        taken = refs[:count]
        del refs[:count]
        return taken

    lefts, rights = take(arrays), take(arrays)
    left_others, right_others = take(arrays - (1 if late else 0)), take(1)
    lefts = [ref if at is None else ref.at[at] for ref, at in zip(lefts, layers)]
    left_others = [ref if at is None else ref.at[at] for ref, at in zip(left_others, layers)]
    (vector,) = take(1)
    take(arrays + 1 if aliased else 0)
    outs, (vector_out,) = take(arrays), take(1)
    if late:
        left_others = left_others + take(1)
    (vector_land, vector_sum, vector_send, vector_recv, vector_store, left, right, left_sem, right_sem, other_sem,
     right_send, right_recv, late_send, late_recv, mine, side_land, side, side_send, side_recv, chain_a, chain_b,
     chain_send, chain_recv, rest_send, rest_land, rest_keep, rest_ssem, rest_rsem, piece, store_sem, gather_send,
     gather_recv) = refs
    units = sum(seat[0] for seat in seats)
    by_column = units - seats[-1][0]
    others = bits - 1
    final_rows = unit_rows >> others
    tokens = left.shape[1] // 2
    chains = (chain_a, chain_b)
    chain_rows = (final_rows, unit_rows)
    depth = chain_a.shape[1] - 1
    ring = mine.shape[1]
    slots, right_slots = piece.shape[1], right.shape[0]
    sec = lax.axis_index("section")
    here = lax.axis_index("shard")
    seat = lax.axis_index("group")
    group = 1 << bits
    peers = shards * group
    me = here * group + seat
    part = vector_out.shape[1]

    def bit_of(index):
        return lax.rem(lax.div(seat, 1 << index), 2)

    def across(index):
        return (sec, here, seat + (1 - 2 * bit_of(index)) * (1 << index))

    above = (sec, jnp.minimum(here + 1, shards - 1), seat)
    below = (sec, jnp.maximum(here - 1, 0), seat)
    half = bit_of(0)

    def remote(source, target, send, recv, device):
        return pltpu.make_async_remote_copy(
            src_ref=source, dst_ref=target, send_sem=send, recv_sem=recv,
            device_id=device, device_id_type=MESH,
        )

    def aligned(start, size):
        return pl.ds(pl.multiple_of(start, size), size)

    def peer(step):
        index = lax.rem(me + step, peers)
        return index, (sec, lax.div(index, group), lax.rem(index, group))

    def vector_copy(index, device):
        return remote(vector.at[:, aligned(device[1] * part, part)], vector_land.at[me], vector_send.at[index],
                      vector_recv.at[me], device)

    def vector_finish():
        vector_sum[...] = vector[:, aligned(here * part, part)]

        @pl.loop(1, peers)
        def _(step):
            index, device = peer(step)
            vector_copy(index, device).wait_send()
            remote(vector_land.at[index], vector_land.at[index], vector_send.at[index], vector_recv.at[index],
                   device).wait_recv()
            vector_sum[...] += vector_land[index]
        copy = pltpu.make_async_copy(vector_sum, vector_out, vector_store)
        copy.start()
        copy.wait()

    def valid(chunk):
        return (chunk >= 0) & (chunk < units)

    def on(condition, run):
        pl.when(condition)(run)

    def by_rows(rows, run, tall=64):
        step = min(rows, tall)

        @pl.loop(0, rows // step)
        def _(index):
            run(aligned(index * step, step))

    def shifted(rows, offset):
        return aligned(rows.start + offset, rows.size)

    pace = min(by_column // seats[-1][0], 2)
    lead = by_column - pace * seats[-1][0]

    def seat_of(chunk):
        behind = jnp.maximum(chunk - lead, 0)
        period = lax.div(behind, pace + 1)
        step = behind - period * (pace + 1)
        last = (chunk >= lead) & (step == 0)
        return last, jnp.where(last, period, jnp.where(chunk < lead, chunk, lead + period * pace + step - 1))

    def each_array(chunk, run):
        last, index = seat_of(chunk)
        start = 0
        for which, (count, blocks, _, _) in enumerate(seats):
            begin = 0 if split_rows(which) else start

            def launch(which=which, begin=begin, blocks=blocks):
                local = index - begin
                row = lax.div(local, blocks)
                run(which, row, local - row * blocks)
            here_it_is = last if split_rows(which) else jnp.logical_not(last) & (index >= start) & (index < start + count)
            on((chunk < units) & here_it_is, launch)
            start += count

    def split_rows(which):
        return which == arrays - 1

    def right_columns(which, block, bit):
        inner = seats[which][2]
        if split_rows(which):
            return 0, aligned(block * (2 * width), 2 * width)
        outer = lax.div(block, inner)
        return outer, aligned((block - outer * inner) * (4 * width) + bit * (2 * width), 2 * width)

    def loads(chunk, run):
        slot = lax.rem(chunk, right_slots)

        def each(which, row, block):
            outer, columns = right_columns(which, block, half)
            run(pltpu.make_async_copy(
                rights[which].at[outer, :, columns], right.at[slot, :tokens], right_sem.at[slot]))
            if split_rows(which):
                run(pltpu.make_async_copy(
                    right_others[0].at[:, columns], right.at[slot, tokens:], other_sem.at[slot]))
        each_array(chunk, each)

    def load_left(chunk):
        def each(which, row, block):
            rows = seats[which][3]
            kind = int(split_rows(which))
            copies = []
            for shard in range(shards):
                if split_rows(which):
                    offsets = (shard * rows + (2 * row + half) * unit_rows, shard * (rows // 2) + row * unit_rows)
                else:
                    offsets = (shard * rows + row * unit_rows,) * 2
                for side, source in enumerate((lefts[which], left_others[which])):
                    copies.append(pltpu.make_async_copy(
                        source.at[:, aligned(offsets[side], unit_rows)],
                        left.at[kind, side * tokens:(side + 1) * tokens, shard * unit_rows:(shard + 1) * unit_rows],
                        left_sem.at[kind, side, shard]))

            def fetch():
                for copy in copies:
                    copy.start()
                for copy in copies:
                    copy.wait()
            on(block == 0, fetch)
        each_array(chunk, each)

    def right_copy(chunk, source):
        four = lax.rem(chunk, right_slots)
        return remote(source, right.at[four, tokens:], right_send.at[four], right_recv.at[four], across(0))

    def send_right(chunk):
        def each(which, row, block):
            if not split_rows(which):
                outer, columns = right_columns(which, block, 1 - half)
                right_copy(chunk, rights[which].at[outer, :, columns]).start()
        each_array(chunk, each)

    late_rows = seats[-1][3] // (2 * unit_rows)

    def late_copy(row, shard):
        source = aligned(shard * seats[-1][3] + (2 * row + 1 - half) * unit_rows, unit_rows)
        target = aligned(shard * (seats[-1][3] // 2) + row * unit_rows, unit_rows)
        return remote(lefts[-1].at[:, source], left_others[-1].at[:, target], late_send.at[row, shard],
                      late_recv.at[row, shard], across(0))

    def late_turn(turn):
        begin = 0
        for row in range(late_rows):
            need = max(lead + row * seats[-1][1] * (pace + 1) - 1, 0)
            at_once = -(-shards // max(need - begin, 1))
            for index in range(at_once):
                shard = (turn - begin) * at_once + index
                on((turn >= begin) & (shard < shards), lambda row=row, shard=shard: late_copy(row, shard).start())

            def finish(row=row):
                @pl.loop(0, shards)
                def _(shard):
                    late_copy(row, shard).wait_send()
                    late_copy(row, shard).wait_recv()
            on(turn == need, finish)
            begin = need

    def multiply(chunk):
        four, slot = lax.rem(chunk, right_slots), lax.rem(chunk, ring)
        load_left(chunk)
        loads(chunk, lambda copy: copy.wait())
        last = seat_of(chunk)[0]

        def arrived():
            copy = right_copy(chunk, right.at[four, tokens:])
            copy.wait_recv()
            copy.wait_send()
        on(jnp.logical_not(last), arrived)
        result = lax.dot_general(left[last.astype(jnp.int32)], right[four], (((0,), (0,)), ((), ())), preferred_element_type=F32)
        for shard in range(shards):
            for path in range(2):
                mine[path, slot, shard] = result[
                    shard * unit_rows:(shard + 1) * unit_rows, path * width:(path + 1) * width].astype(BF16)

    def side_copy(step, chunk):
        slot, four = lax.rem(chunk, ring), lax.rem(chunk, slots)
        rows = unit_rows >> (step + 1)
        away = aligned((1 - bit_of(step + 1)) * rows, rows)
        source = mine.at[0, slot, :, away] if step == 0 else side.at[step - 1, slot, :, away]
        return remote(source, side_land.at[step, four, :, :rows], side_send.at[step, four], side_recv.at[step, four],
                      across(step + 1))

    def side_sum(step, chunk):
        slot, four = lax.rem(chunk, ring), lax.rem(chunk, slots)
        rows = unit_rows >> (step + 1)
        kept = bit_of(step + 1) * rows
        copy = side_copy(step, chunk)
        copy.wait_recv()
        copy.wait_send()

        @pl.loop(0, shards)
        def _(shard):
            def add(part):
                source = mine[0, slot, shard, shifted(part, kept)] if step == 0 else side[
                    step - 1, slot, shard, shifted(part, kept)]
                side[step, slot, shard, part] = (
                    source.astype(F32) + side_land[step, four, shard, part].astype(F32)).astype(BF16)
            by_rows(rows, add)
        if step + 1 < others:
            side_copy(step + 1, chunk).start()

    def base(path, slot, shard, rows):
        return (side[others - 1, slot, shard, rows] if path == 0 else mine[1, slot, shard, rows]).astype(F32)

    def hop(path, way, chunk, shard):
        slot = lax.rem(chunk, depth)
        ref = chains[path].at[way, slot, shard]
        return remote(ref, ref, chain_send.at[path, way, slot, shard], chain_recv.at[path, way, slot, shard],
                      above if way == 0 else below)

    def onward(path, way, chunk):
        slot, from_base = lax.rem(chunk, depth), lax.rem(chunk, ring)
        arrives = here > 0 if way == 0 else here < shards - 1

        @pl.loop(0, shards - 1 - here if way == 0 else here)
        def _(index):
            shard = shards - 1 - index if way == 0 else index
            copy = hop(path, way, chunk, shard)
            on(arrives, lambda: copy.wait_recv())
            source = jnp.where(arrives, slot, depth)

            def add(rows):
                chains[path][way, slot, shard, rows] = (
                    chains[path][way, source, shard, rows].astype(F32) + base(path, from_base, shard, rows)
                ).astype(BF16)
            by_rows(chain_rows[path], add)
            copy.start()

    def sent(path, way, chunk):
        @pl.loop(0, shards - 1 - here if way == 0 else here)
        def _(index):
            hop(path, way, chunk, shards - 1 - index if way == 0 else index).wait_send()

    def last_hop(path, chunk):
        from_base, slot = lax.rem(chunk, ring), lax.rem(chunk, depth)
        on(here > 0, lambda: hop(path, 0, chunk, here).wait_recv())
        on(here < shards - 1, lambda: hop(path, 1, chunk, here).wait_recv())
        from_below = jnp.where(here > 0, slot, depth)
        from_above = jnp.where(here < shards - 1, slot, depth)

        def total(rows, offset):
            rows = shifted(rows, offset)
            return (
                base(path, from_base, here, rows)
                + chains[path][0, from_below, here, rows].astype(F32)
                + chains[path][1, from_above, here, rows].astype(F32)
            )
        if path == 0:
            finish(path, chunk, total)
        else:
            share(0, chunk, total)

    def rest_copy(step, chunk):
        slot, rows = lax.rem(chunk, slots), pl.ds(0, unit_rows >> (step + 1))
        return remote(rest_send.at[step, slot, rows], rest_land.at[step, slot, rows], rest_ssem.at[step, slot],
                      rest_rsem.at[step, slot], across(step + 1))

    def share(step, chunk, total):
        slot, rows = lax.rem(chunk, slots), unit_rows >> (step + 1)
        bit = bit_of(step + 1)

        def give(part):
            rest_send[step, slot, part] = total(part, (1 - bit) * rows).astype(BF16)
        by_rows(rows, give)
        rest_copy(step, chunk).start()

        def keep(part):
            rest_keep[step, slot, part] = total(part, bit * rows)
        by_rows(rows, keep)

    def rest_sum(step, chunk):
        slot = lax.rem(chunk, slots)
        copy = rest_copy(step, chunk)
        copy.wait_recv()
        copy.wait_send()

        def total(part, offset):
            part = shifted(part, offset)
            return rest_keep[step, slot, part] + rest_land[step, slot, part].astype(F32)
        if step + 1 < others:
            share(step + 1, chunk, total)
        else:
            finish(1, chunk, total)

    def finish(path, chunk, total):
        def put(part):
            piece[path, lax.rem(chunk, slots), part] = total(part, 0).astype(BF16)
        by_rows(final_rows, put)
        spread(path, 0, chunk)

    def place(which, row, block, path, bit, offset, rows):
        if split_rows(which):
            row0, column = (2 * row + bit) * unit_rows, block * (2 * width) + path * width
        else:
            row0, column = row * unit_rows, block * (4 * width) + bit * (2 * width) + path * width
        return outs[which].at[aligned(row0 + offset, rows), aligned(column, width)]

    def seat_row(steps):
        row = 0
        for step in range(steps):
            row = row + bit_of(step + 1) * (unit_rows >> (step + 1))
        return row

    def store(path, chunk, target):
        slot = lax.rem(chunk, slots)
        return pltpu.make_async_copy(piece.at[path, slot], target, store_sem.at[path, slot])

    def gather(path, step, other, chunk, target):
        slot = lax.rem(chunk, slots)
        source = piece.at[path, slot] if step == 0 else target
        return remote(source, target, gather_send.at[path, step, other, slot], gather_recv.at[path, step, other, slot],
                      across(0 if step == 0 else bits - step))

    def spread(path, step, chunk):
        steps = others - max(step - 1, 0)
        rows = unit_rows >> steps

        def each(which, row, block):
            for other in range(1 if step == 0 else 2):
                bit = half if other == 0 else 1 - half
                target = place(which, row, block, path, bit, seat_row(steps), rows)
                if step == 0:
                    store(path, chunk, target).start()
                gather(path, step, other, chunk, target).start()
        each_array(chunk, each)

    def gathered(path, step, chunk):
        rows = unit_rows >> (others - max(step - 1, 0))
        target = outs[0].at[pl.ds(0, rows), pl.ds(0, width)]
        for other in range(1 if step == 0 else 2):
            copy = gather(path, step, other, chunk, target)
            copy.wait_recv()
            copy.wait_send()
        if step == 0:
            store(path, chunk, target).wait()
        if step + 1 < bits:
            spread(path, step + 1, chunk)

    def work():
        barrier = pltpu.get_barrier_semaphore()

        @pl.loop(1, peers)
        def _(step):
            pl.semaphore_signal(barrier, inc=1, device_id=peer(step)[1], device_id_type=MESH)
        pl.semaphore_wait(barrier, peers - 1)
        for chunk in range(lag):
            send_right(chunk)
        loads(0, lambda copy: copy.start())

        @pl.loop(1, peers)
        def _(step):
            vector_copy(*peer(step)).start()

        for path in range(2):
            for way in range(2):
                @pl.loop(0, shards)
                def _(shard):
                    def clear(rows):
                        chains[path][way, depth, shard, rows] = jnp.zeros((rows.size, width), BF16)
                    by_rows(chain_rows[path], clear)

        line = shards - 1

        @pl.loop(0, units + lag * (line + others + bits) + 2)
        def _(turn):
            on(turn + lag < units, lambda: send_right(turn + lag))
            if late:
                late_turn(turn)
            on(turn + 1 < units, lambda: loads(turn + 1, lambda copy: copy.start()))

            def opening():
                multiply(turn)
                side_copy(0, turn).start()
            on(turn < units, opening)
            for step in range(others):
                chunk = turn - lag * (1 + step)
                on(valid(chunk), lambda step=step, chunk=chunk: side_sum(step, chunk))
            for path in range(2):
                for way in range(2):
                    chunk = turn - lag * ((others if path == 0 else 0) + (here if way == 0 else line - here))
                    on(valid(chunk - 2), lambda path=path, way=way, chunk=chunk: sent(path, way, chunk - 2))
                    on(valid(chunk), lambda path=path, way=way, chunk=chunk: onward(path, way, chunk))
            on(valid(turn - lag * line), lambda: last_hop(1, turn - lag * line))
            on(valid(turn - lag * (line + others)), lambda: last_hop(0, turn - lag * (line + others)))
            for step in range(others):
                chunk = turn - lag * (line + 1 + step)
                on(valid(chunk), lambda step=step, chunk=chunk: rest_sum(step, chunk))
            for step in range(bits):
                for path in range(2):
                    chunk = turn - lag * (line + others + 1 + step)
                    on(valid(chunk), lambda path=path, step=step, chunk=chunk: gathered(path, step, chunk))

        vector_finish()

    if section is None:
        work()
    else:
        pl.when(sec == section)(work)


def exchange(pairs, vector, shards, group, section, collective_id, unit_width, previous=None, lag=2, unit_rows_max=256,
             name="exchange"):
    bits = group.bit_length() - 1
    arrays = len(pairs)
    lefts, rights = [pair[0][0] for pair in pairs], [pair[1] for pair in pairs]
    layers = tuple(pair[0][1] for pair in pairs)
    left_others = [pair[2] for pair in pairs]
    late = left_others[-1] is None
    if late:
        left_others = left_others[:-1]
    tokens = lefts[0].shape[-2]
    rows_of = [left.shape[-1] // shards for left in lefts]
    unit_rows = min([unit_rows_max] + rows_of[:-1])
    width = unit_width // 4
    seats = []
    for index, (rows, right) in enumerate(zip(rows_of, rights)):
        tall, wide = (2 * unit_rows, 2 * width) if index == arrays - 1 else (unit_rows, 4 * width)
        inner = right.shape[2] // wide
        seats.append((rows // tall * right.shape[0] * inner, right.shape[0] * inner, inner, rows))
    units = sum(seat[0] for seat in seats)
    others = bits - 1
    final_rows = unit_rows >> others
    slots, right_slots = 2 * lag + 2, 2 * lag + 3
    depth, ring = lag * shards + 3, lag * (shards - 1) + 2
    late_rows = rows_of[-1] // (2 * unit_rows)
    peers, lanes = shards * group, vector.shape[1] // shards
    dma = pltpu.SemaphoreType.DMA
    scratch = [
        pltpu.VMEM((peers, vector.shape[0], lanes), F32),
        pltpu.VMEM((vector.shape[0], lanes), F32),
        dma((peers,)), dma((peers,)), dma,
        pltpu.VMEM((2, 2 * tokens, shards * unit_rows), BF16),
        pltpu.VMEM((right_slots, 2 * tokens, 2 * width), BF16),
        dma((2, 2, shards)), dma((right_slots,)), dma((right_slots,)),
        dma((right_slots,)), dma((right_slots,)),
        dma((late_rows, shards)), dma((late_rows, shards)),
        pltpu.VMEM((2, ring, shards, unit_rows, width), BF16),
        pltpu.VMEM((others, slots, shards, unit_rows // 2, width), BF16),
        pltpu.VMEM((others, ring, shards, unit_rows // 2, width), BF16),
        dma((others, slots)), dma((others, slots)),
        pltpu.VMEM((2, depth + 1, shards, final_rows, width), BF16),
        pltpu.VMEM((2, depth + 1, shards, unit_rows, width), BF16),
        dma((2, 2, depth, shards)), dma((2, 2, depth, shards)),
        pltpu.VMEM((others, slots, unit_rows // 2, width), BF16),
        pltpu.VMEM((others, slots, unit_rows // 2, width), BF16),
        pltpu.VMEM((others, slots, unit_rows // 2, width), F32),
        dma((others, slots)), dma((others, slots)),
        pltpu.VMEM((2, slots, final_rows, width), BF16),
        dma((2, slots)),
        dma((2, bits, 2, slots)), dma((2, bits, 2, slots)),
    ]
    cfg = (shards, bits, tuple(seats), unit_rows, width, section, previous is not None, late, layers, lag)
    operands = lefts + rights + left_others + [pairs[-1][3], vector] + list(previous or [])
    first = len(operands) - len(previous or [])
    results = [jax.ShapeDtypeStruct((r, g.shape[0] * g.shape[2]), BF16) for r, g in zip(rows_of, rights)]
    results.append(jax.ShapeDtypeStruct((vector.shape[0], lanes), F32))
    if late:
        results.append(jax.ShapeDtypeStruct((tokens, lefts[-1].shape[-1] // 2), BF16))
    hbm, vmem = pl.BlockSpec(memory_space=pl.ANY), pl.BlockSpec(memory_space=pltpu.VMEM)
    in_specs = [vmem if index == first - 1 else hbm for index in range(len(operands))]
    return pl.pallas_call(
        functools.partial(exchange_kernel, cfg),
        out_shape=results,
        in_specs=in_specs,
        out_specs=[hbm] * len(results),
        scratch_shapes=scratch,
        input_output_aliases={first + index: index for index in range(len(previous or []))},
        name=name,
        cost_estimate=pl.CostEstimate(
            flops=4 * tokens * units * shards * unit_rows * 2 * width, bytes_accessed=100 * 2 ** 20,
            transcendentals=0),
        compiler_params=pltpu.CompilerParams(
            collective_id=collective_id, has_side_effects=True, vmem_limit_bytes=56 * 1024 * 1024),
    )(*operands)[:arrays + 1]


UNIT_WIDTH = 512


def body(
    ends_in,
    lengths,
    norm_gain_a,
    norm_bias_a,
    w_qkv,
    w_out,
    norm_gain_f,
    norm_bias_f,
    w_gate_up,
    w_down,
):
    section = lax.axis_index("section")
    shards, group = lax.axis_size("shard"), lax.axis_size("group")
    is_first = section == 0
    first, second = ((section == which).astype(jnp.int32).reshape(1) for which in range(2))
    tokens, features = ends_in.shape[1:]
    size = features // HEADS
    rows = ends_in[0]
    weight_qkv, weight_out, weight_gu, weight_down = w_qkv[0], w_out[0], w_gate_up[0], w_down[0]
    cosine, sine = tables(lengths, tokens // lengths.shape[0], size)
    nothing = jnp.zeros((4, features), F32)
    unit_rows = min(256, features // shards)
    partner_bit = (1 - lax.axis_index("group") % 2).astype(jnp.int32).reshape(1)

    def beside(which, array):
        pairs = [(which * group + index, which * group + (index ^ 1)) for index in range(group)]
        return lax.ppermute(array, ("section", "group"), pairs)

    def attend(active, values):
        return attention(active, lengths, values, norm_gain_a, norm_bias_a, norm_gain_f, norm_bias_f, weight_qkv,
                         weight_out, cosine, sine)

    def back(active, middle, lefts, qkv, values, grad):
        result, hidden, grad_gu, grad_middle, gain_f, bias_f = feed_both(
            active, middle, lefts, grad, norm_gain_f, weight_gu, weight_down)
        branch, grad_qkv, grad_in, grad_in_low, gain_a, bias_a = attention_back(
            active, lengths, grad_middle, values, norm_gain_a, qkv, weight_qkv, weight_out, cosine, sine)
        vectors = jnp.concatenate([gain_a, bias_a, gain_f, bias_f, nothing], axis=0)
        return result, grad_in, grad_in_low, hidden, (grad_gu, branch[None], grad_qkv, grad[None]), vectors

    def sum_all(which, lefts, lefts_beside, hidden, hidden_beside, rights, right_beside, vectors, **more):
        pairs = [((lefts, at), right, lefts_beside) for at, right in zip((2, 1, 0), rights)]
        pairs.append(((hidden, None), rights[3], hidden_beside, right_beside))
        return exchange(pairs, vectors, shards, group, which, which + 1, UNIT_WIDTH * features // 1024, **more)

    rows_beside = beside(1, rows)
    middle_0, lefts_0, qkv_0 = attend(first, rows)
    passed, hidden_half_0 = feed(
        jnp.concatenate([first, partner_bit]), middle_0, lefts_0, weight_gu, weight_down, unit_rows)
    arrived = lax.ppermute(passed, "section", [(0, 1)])
    lefts_beside_0, hidden_beside_0 = beside(0, lefts_0), beside(0, hidden_half_0)
    middle_1, lefts_1, qkv_1 = attend(second, arrived)
    lefts_beside_1 = beside(1, lefts_1)
    result, _, returned, hidden_1, rights_1, vectors_1 = back(second, middle_1, lefts_1, qkv_1, arrived, rows)
    returned = lax.ppermute(returned, "section", [(1, 0)])
    sums = sum_all(1, lefts_1, lefts_beside_1, hidden_1, None, rights_1, rows_beside, vectors_1,
                   name="exchange_second", lag=1)
    returned, _, lefts_beside_0, hidden_beside_0 = lax.optimization_barrier(
        (returned, sums[4], lefts_beside_0, hidden_beside_0))
    returned_beside = beside(0, returned)
    _, grad_in, _, hidden_0, rights_0, vectors_0 = back(first, middle_0, lefts_0, qkv_0, rows, returned)
    sums = sum_all(0, lefts_0, lefts_beside_0, hidden_0, hidden_beside_0, rights_0, returned_beside, vectors_0,
                   previous=sums, name="exchange_first", lag=2)
    ends_out = jnp.where(is_first, grad_in, result)[None]
    grad_gate_up, grad_out, grad_qkv, grad_down = (item.astype(F32)[None] for item in sums[:4])
    vectors = sums[4]
    return (
        ends_out,
        vectors[0:1],
        vectors[1:2],
        grad_qkv,
        grad_out,
        vectors[2:3],
        vectors[3:4],
        grad_gate_up,
        grad_down,
    )


def solution(mesh):
    placed = (
        P("section", ("shard", "group"), None),
        P(("shard", "group"), None),
        P("section", None),
        P("section", None),
        P("section", None, None),
        P("section", None, None),
        P("section", None),
        P("section", None),
        P("section", None, None),
        P("section", None, None),
    )
    return jax.shard_map(
        body,
        mesh=mesh,
        in_specs=placed,
        out_specs=(
            P("section", ("shard", "group"), None),
            P("section", "shard"),
            P("section", "shard"),
            P("section", "shard", None),
            P("section", "shard", None),
            P("section", "shard"),
            P("section", "shard"),
            P("section", "shard", None),
            P("section", "shard", None),
        ),
        check_vma=False,
    )
```

```python
import functools

import jax
import jax.numpy as jnp
from jax import lax
from jax.experimental import pallas as pl
from jax.experimental.pallas import tpu as pltpu
from jax.sharding import PartitionSpec as P

MESH = pl.DeviceIdType.MESH
F32, BF16 = jnp.float32, jnp.bfloat16
HEADS = 16
EPSILON = 1e-05


def dot(a, b):
    return jnp.dot(a, b, preferred_element_type=F32)


def dot_cols(a, b):
    return lax.dot_general(a, b, (((1,), (1,)), ((), ())), preferred_element_type=F32)


def dot_rows(a, b):
    return lax.dot_general(a, b, (((0,), (0,)), ((), ())), preferred_element_type=F32)


def in_rows(total, step, run):
    @pl.loop(0, total // step)
    def _(index):
        run(pl.ds(pl.multiple_of(index * step, step), step))


def normalized(values):
    average = jnp.mean(values, axis=-1, keepdims=True)
    centered = values - average
    variance = jnp.mean(centered * centered, axis=-1, keepdims=True)
    spread = lax.rsqrt(variance + EPSILON)
    return centered * spread, spread


def norm_back(grad, values, gain):
    unit, spread = normalized(values)
    scaled = grad * gain
    return spread * (
        scaled
        - jnp.mean(scaled, axis=-1, keepdims=True)
        - unit * jnp.mean(scaled * unit, axis=-1, keepdims=True)
    ), grad * unit


def lanes_of(shape):
    return lax.broadcasted_iota(jnp.int32, shape, len(shape) - 1)


def turn(values, half, size):
    wide = values.shape[-1]
    early = lax.rem(lanes_of(values.shape), size) < half
    return jnp.where(early, pltpu.roll(values, wide - half, 1), pltpu.roll(values, half, 1)), early


def rotated(values, cosine, sine, size):
    other, early = turn(values, size // 2, size)
    return values * cosine + jnp.where(early, -other, other) * sine


def unrotated(values, cosine, sine, size):
    other, early = turn(values * sine, size // 2, size)
    return values * cosine + jnp.where(early, other, -other)


def window_of(index, lengths_ref, row):
    windows = lengths_ref.shape[1]
    end = lengths_ref[row, 0]
    segment = (index >= end).astype(jnp.int32)
    for window in range(1, windows):
        end = end + lengths_ref[row, window]
        segment = segment + (index >= end).astype(jnp.int32)
    return segment


def same_window(lengths_ref, row, tokens):
    queries = window_of(lax.broadcasted_iota(jnp.int32, (tokens, 1), 0), lengths_ref, row)
    keys = window_of(lax.broadcasted_iota(jnp.int32, (1, tokens), 1), lengths_ref, row)
    return queries == keys


def softmax(scores, allowed):
    scores = jnp.where(allowed, scores, -1e30)
    weights = jnp.exp(scores - jnp.max(scores, axis=-1, keepdims=True))
    return weights * (1.0 / jnp.sum(weights, axis=-1, keepdims=True))


def attention_kernel(size, row_tokens, act_ref, lengths_ref, x_ref, gain_ref, bias_ref, gain_f_ref, bias_f_ref,
                     wq_ref, wk_ref, wv_ref, wo_ref, cos_ref, sin_ref, mid_ref, lefts_ref, qkv_ref, mix_ref):
    tokens = x_ref.shape[0]
    part = pl.program_id(0)
    block = wq_ref.shape[1]
    pair = 2 * size

    @pl.when(act_ref[0] == 1)
    def _():
        @pl.when(part == 0)
        def _():
            def begin(rows):
                values = x_ref[rows].astype(F32)
                unit, _ = normalized(values)
                lefts_ref[0, rows] = (unit * gain_ref[...] + bias_ref[...]).astype(BF16)
                mid_ref[rows] = values
            in_rows(tokens, 64, begin)

        for which, weight in enumerate((wq_ref, wk_ref, wv_ref)):
            projected = dot(lefts_ref[0], weight[...])
            for at in range(block // pair):
                lanes = slice(at * pair, (at + 1) * pair)
                values = projected[:, lanes]
                if which < 2:
                    values = rotated(values, cos_ref[...], sin_ref[...], size)
                qkv_ref[which, :, lanes] = values.astype(BF16)

        first = lanes_of((row_tokens, pair)) < size
        @pl.loop(0, tokens // row_tokens)
        def _(row):
            rows = pl.ds(pl.multiple_of(row * row_tokens, row_tokens), row_tokens)
            allowed = same_window(lengths_ref, row, row_tokens)
            for start in range(0, block // pair, 2):
                work = []
                for at in range(start, start + 2):
                    lanes = pl.ds(at * pair, pair)
                    query, key, value = (qkv_ref[which, rows, lanes] for which in range(3))
                    query = query * (size ** -0.5)
                    for head in range(2):
                        own = jnp.where(first if head == 0 else jnp.logical_not(first), query, jnp.zeros_like(query))
                        work.append((dot_cols(own, key), value))
                work = [(softmax(scores, allowed).astype(BF16), value) for scores, value in work]
                work = [dot(probs, value) for probs, value in work]
                for at in range(2):
                    lanes = pl.ds((start + at) * pair, pair)
                    mix_ref[rows, lanes] = jnp.where(first, work[2 * at], work[2 * at + 1]).astype(BF16)

        mixture = mix_ref[...]
        lefts_ref[1, :, pl.ds(pl.multiple_of(part * block, block), block)] = mixture
        mid_ref[...] += dot(mixture, wo_ref[...])

        @pl.when(part == pl.num_programs(0) - 1)
        def _():
            def close(rows):
                unit, _ = normalized(mid_ref[rows])
                lefts_ref[2, rows] = (unit * gain_f_ref[...] + bias_f_ref[...]).astype(BF16)
            in_rows(tokens, 64, close)


def attention_back_kernel(size, row_tokens, parts, act_ref, lengths_ref, grad_in, x_in, qkv_in, wqkv_in, wo_in, cos_in,
                          sin_in, branch_out, proj_out, input_out, input_low_out, vectors_out, grad_ref, x_ref, qkv_ref,
                          wqkv_ref, wo_ref, cos_ref, sin_ref, branch_ref, proj_ref, input_low_ref, vectors_ref, gm_ref,
                          total_ref, load_sem, part_sem, store_sem):
    tokens, features = x_ref.shape
    block = features // parts
    pair = 2 * size
    scale = size ** -0.5
    copy = pltpu.make_async_copy

    def work():
        loads = [
            copy(source, target, load_sem.at[index]) for index, (source, target) in enumerate(
                ((grad_in, grad_ref), (cos_in, cos_ref), (sin_in, sin_ref), (x_in, x_ref)))]
        part_loads = []
        for part in range(parts):
            lanes = pl.ds(part * block, block)
            part_loads.append([copy(wo_in.at[lanes], wo_ref.at[lanes], part_sem.at[part, 0]),
                               copy(qkv_in.at[:, :, lanes], qkv_ref.at[:, :, lanes], part_sem.at[part, 1])] + [
                copy(wqkv_in.at[:, pl.ds(which * features + part * block, block)],
                     wqkv_ref.at[:, pl.ds(which * features + part * block, block)], part_sem.at[part, 2 + which])
                for which in range(3)])
        for item in loads[:1] + part_loads[0][:2] + loads[1:3] + part_loads[0][2:] + loads[3:]:
            item.start()
        for items in part_loads[1:]:
            for item in items:
                item.start()
        loads[0].wait()

        def begin(rows):
            branch_ref[rows] = grad_ref[rows].astype(BF16)
        in_rows(tokens, 64, begin)
        branch_store = copy(branch_ref, branch_out, store_sem.at[0])
        branch_store.start()
        stores = [branch_store]
        for part in range(parts):
            columns = slice(part * block, (part + 1) * block)
            part_loads[part][0].wait()
            gm_ref[...] = dot_cols(branch_ref[...], wo_ref[columns]).astype(BF16)
            part_loads[part][1].wait()
            if part == 0:
                loads[1].wait()
                loads[2].wait()
            first = lanes_of((row_tokens, pair)) < size
            @pl.loop(0, tokens // row_tokens)
            def _(row):
                rows = pl.ds(pl.multiple_of(row * row_tokens, row_tokens), row_tokens)
                allowed = same_window(lengths_ref, row, row_tokens)
                cosine, sine = cos_ref[rows], sin_ref[rows]
                for start in range(0, block // pair, 2):
                    work = []
                    for at in range(start, start + 2):
                        lanes = pl.ds(part * block + at * pair, pair)
                        query, key, value = (qkv_ref[which, rows, lanes] for which in range(3))
                        grad_mix = gm_ref[rows, pl.ds(at * pair, pair)]
                        scaled = query * scale
                        for head in range(2):
                            mine = first if head == 0 else jnp.logical_not(first)
                            work.append((
                                query, key, grad_mix,
                                dot_cols(jnp.where(mine, scaled, jnp.zeros_like(scaled)), key),
                                dot_cols(jnp.where(mine, grad_mix, jnp.zeros_like(grad_mix)), value)))
                    results = []
                    for query, key, grad_mix, scores, grad_probs in work:
                        probs = softmax(scores, allowed)
                        weighted = probs * grad_probs
                        grad_scores = (weighted - probs * jnp.sum(weighted, axis=-1, keepdims=True)).astype(BF16)
                        results.append((query, key, grad_mix, grad_scores, probs.astype(BF16)))
                    results = [
                        (dot(grad_scores, key), dot_rows(grad_scores, query), dot_rows(probs, grad_mix))
                        for query, key, grad_mix, grad_scores, probs in results]
                    for at in range(2):
                        lanes = pl.ds(part * block + (start + at) * pair, pair)
                        grad_query, grad_key, grad_value = (
                            jnp.where(first, a, b) for a, b in zip(results[2 * at], results[2 * at + 1]))
                        proj_ref[0, rows, lanes] = unrotated(grad_query * scale, cosine, sine, size).astype(BF16)
                        proj_ref[1, rows, lanes] = unrotated(grad_key * scale, cosine, sine, size).astype(BF16)
                        proj_ref[2, rows, lanes] = grad_value.astype(BF16)
            lanes = pl.ds(part * block, block)
            stores.append(copy(proj_ref.at[:, :, lanes], proj_out.at[:, :, lanes], store_sem.at[1 + part]))
            stores[-1].start()
            added = 0.0
            for which in range(3):
                part_loads[part][2 + which].wait()
                weights = wqkv_ref[:, which * features + part * block:which * features + (part + 1) * block]
                added = added + dot_cols(proj_ref[which, :, columns], weights)
            total_ref[...] = added if part == 0 else total_ref[...] + added
        loads[3].wait()
        vectors_ref[...] = jnp.zeros_like(vectors_ref)

        def finish(rows):
            grad = total_ref[rows]
            through, by_gain = norm_back(grad, x_ref[rows].astype(F32), grad_ref[tokens:tokens + 1])
            result = grad_ref[rows] + through
            total_ref[rows] = result
            input_low_ref[rows] = result.astype(BF16)
            vectors_ref[0:1] += jnp.sum(by_gain, axis=0, keepdims=True)
            vectors_ref[1:2] += jnp.sum(grad, axis=0, keepdims=True)
        in_rows(tokens, 64, finish)
        for index, (source, target) in enumerate(
                ((input_low_ref, input_low_out), (total_ref, input_out), (vectors_ref, vectors_out))):
            stores.append(copy(source, target, store_sem.at[1 + parts + index]))
            stores[-1].start()
        for item in stores:
            item.wait()

    pl.when(act_ref[0] == 1)(work)


def places():
    section, shard, seat = (lax.axis_index(name) for name in ("section", "shard", "group"))
    stride = 2 - section
    bit = lax.rem(lax.div(seat, stride), 2)
    return section, bit, (section, shard, seat + (1 - 2 * bit) * stride), (1 - section, shard, seat)


def remote(source, target, sems, index, device):
    return pltpu.make_async_remote_copy(
        src_ref=source, dst_ref=target, send_sem=sems.at[0, index], recv_sem=sems.at[1, index], device_id=device,
        device_id_type=pl.DeviceIdType.MESH)


def meet(*devices):
    barrier = pltpu.get_barrier_semaphore()
    for device in devices:
        pl.semaphore_signal(barrier, inc=1, device_id=device, device_id_type=pl.DeviceIdType.MESH)
    pl.semaphore_wait(barrier, len(devices))


def feed_kernel(unit_rows, mid_ref, low_ref, wg_ref, wu_ref, wd_ref, lefts_ref, rows_ref, out_ref, half_ref,
                arrived_ref, lefts_land, rows_land, total_ref, sems):
    part = pl.program_id(0)
    section, bit, beside, above = places()
    lefts_copy = remote(lefts_ref.at[0:2], lefts_land, sems, 0, beside)
    rows_copy = remote(rows_ref, rows_land, sems, 0, beside)
    out_copy = remote(out_ref, arrived_ref, sems, 1, above)

    @pl.when(part == 0)
    def _():
        meet(beside, above)
        pl.when(section == 0)(lefts_copy.start)
        pl.when(section == 1)(rows_copy.start)

    @pl.when(section == 0)
    def _():
        @pl.when(part == 0)
        def _():
            total_ref[...] = mid_ref[...]

        low = low_ref[0]
        gate = dot(low, wg_ref[...])
        up = dot(low, wu_ref[...])
        hidden = (gate / (1.0 + jnp.exp(-gate)) * up).astype(BF16)
        for at in range(half_ref.shape[1] // unit_rows):
            rows = [hidden[:, (2 * at + side) * unit_rows:(2 * at + side + 1) * unit_rows] for side in range(2)]
            half_ref[:, at * unit_rows:(at + 1) * unit_rows] = jnp.where(bit == 0, rows[1], rows[0])
        total_ref[...] += dot(hidden, wd_ref[...])

    @pl.when(part == pl.num_programs(0) - 1)
    def _():
        @pl.when(section == 0)
        def _():
            out_ref[...] = total_ref[...].astype(BF16)
            out_copy.start()
            out_copy.wait_send()
            lefts_copy.wait()

        @pl.when(section == 1)
        def _():
            out_copy.wait_recv()
            rows_copy.wait()


def feed_both_kernel(active, mid_ref, low_ref, grad_ref, gain_ref, gain_a_ref, wg_ref, wu_ref, wd_ref, *refs):
    sends, refs = refs[:6 if active else 1], refs[6 if active else 1:]
    out_ref, hidden_ref, ggu_ref, grad_mid_ref, vectors_ref = refs[:5]
    lands = refs[5:5 + (6 if active else 1)]
    total_ref, sems = refs[-2:]
    tokens = mid_ref.shape[0]
    part = pl.program_id(0)
    section, _, beside, other = places()
    pieces = 4
    step = tokens // pieces
    if active:
        lefts_ref, qkv_ref, wqkv_ref, wo_ref, lefts_first, hidden_first = sends
        lefts_land, qkv_land, wqkv_land, wo_land, hidden_land, grad_land = lands
        working = [
            remote(lefts_ref, lefts_land, sems, 0, beside), remote(qkv_ref, qkv_land, sems, 1, other),
            remote(wqkv_ref, wqkv_land, sems, 2, other), remote(wo_ref, wo_land, sems, 3, other)]
        waiting = [
            remote(lefts_first.at[2], lefts_land.at[2], sems, 4, beside),
            remote(hidden_first, hidden_land, sems, 5, beside)]

        def grad_copy(piece):
            rows = pl.ds(piece * step, step + (8 if piece == pieces - 1 else 0))
            return remote(grad_mid_ref.at[rows], grad_land.at[rows], sems, 6 + piece, other)
    else:
        working = [remote(sends[0], lands[0], sems, 0, beside)]

    @pl.when(part == 0)
    def _():
        if active:
            meet(beside, other)

            @pl.when(section != active)
            def _():
                for copy in waiting:
                    copy.start()

        @pl.when(section == active)
        def _():
            if not active:
                meet(beside)
            for copy in working:
                copy.start()

    @pl.when(section == active)
    def _():
        @pl.when(part == 0)
        def _():
            out_ref[...] = mid_ref[...]

        low = low_ref[0]
        gate = dot(low, wg_ref[...])
        up = dot(low, wu_ref[...])
        grad_hidden = dot_cols(grad_ref[...], wd_ref[...])
        sig = 1.0 / (1.0 + jnp.exp(-gate))
        silu = gate * sig
        hidden_ref[...] = (silu * up).astype(BF16)
        ggu_ref[0] = (grad_hidden * up * (sig * (1.0 + gate * (1.0 - sig)))).astype(BF16)
        ggu_ref[1] = (grad_hidden * silu).astype(BF16)
        out_ref[...] += dot(hidden_ref[...], wd_ref[...])
        added = dot_cols(ggu_ref[0], wg_ref[...]) + dot_cols(ggu_ref[1], wu_ref[...])
        total_ref[...] = jnp.where(part == 0, added, total_ref[...] + added)

    @pl.when(part == pl.num_programs(0) - 1)
    def _():
        @pl.when(section == active)
        def _():
            vectors_ref[...] = jnp.zeros_like(vectors_ref)
            grad_mid_ref[pl.ds(tokens, 8)] = jnp.broadcast_to(gain_a_ref[...], (8, gain_a_ref.shape[1]))

            def finish(rows):
                grad = total_ref[rows]
                through, by_gain = norm_back(grad, mid_ref[rows], gain_ref[...])
                grad_mid_ref[rows] = grad_ref[rows].astype(F32) + through
                vectors_ref[2:3] += jnp.sum(by_gain, axis=0, keepdims=True)
                vectors_ref[3:4] += jnp.sum(grad, axis=0, keepdims=True)
            for piece in range(pieces):
                for at in range(2):
                    finish(pl.ds(piece * step + at * (step // 2), step // 2))
                if active:
                    grad_copy(piece).start()
            if active:
                for piece in range(pieces):
                    grad_copy(piece).wait_send()
                for copy in working[1:]:
                    copy.wait_send()
            working[0].wait()

        if active:
            @pl.when(section != active)
            def _():
                for piece in range(pieces):
                    grad_copy(piece).wait_recv()
                for copy in working[1:]:
                    copy.wait_recv()
                for copy in waiting:
                    copy.wait()


def whole(shape):
    return pl.BlockSpec(shape, lambda part, *_: (0,) * len(shape))


def column(rows, wide, offset=0):
    return pl.BlockSpec((rows, wide), lambda part, *act: (0, (part + offset) * (act[0][0] if act else 1)))


def stacked(count, rows, wide):
    return pl.BlockSpec((count, rows, wide), lambda part, *act: (0, 0, part * (act[0][0] if act else 1)))


def lower(rows, wide):
    return pl.BlockSpec((rows, wide), lambda part, *act: (part * (act[0][0] if act else 1), 0))


def local_call(kernel, name, grid, scalars, args, in_specs, outs, out_specs, scratch, flops, limit=56):
    return pl.pallas_call(
        kernel,
        grid_spec=pltpu.PrefetchScalarGridSpec(
            num_scalar_prefetch=len(scalars), grid=(grid,), in_specs=in_specs, out_specs=out_specs,
            scratch_shapes=scratch),
        out_shape=outs,
        name=name,
        cost_estimate=pl.CostEstimate(flops=flops, bytes_accessed=40 * 2 ** 20, transcendentals=0),
        compiler_params=pltpu.CompilerParams(
            dimension_semantics=("arbitrary",), vmem_limit_bytes=limit * 1024 * 1024),
    )(*scalars, *args)


def attention(active, lengths, x, gain, bias, gain_f, bias_f, w_qkv, w_out, cosine, sine, parts=2):
    tokens, features = x.shape
    row_tokens = tokens // lengths.shape[0]
    size = features // HEADS
    wide = features // parts
    stack = jax.ShapeDtypeStruct((3, tokens, features), BF16)
    return local_call(
        functools.partial(attention_kernel, size, row_tokens), "attention", parts, (active, lengths),
        (x, gain, bias, gain_f, bias_f, w_qkv, w_qkv, w_qkv, w_out, cosine, sine),
        [whole((tokens, features))] + [whole((1, features))] * 4 + [column(features, wide),
         column(features, wide, parts), column(features, wide, 2 * parts), lower(wide, features),
         whole(cosine.shape), whole(sine.shape)],
        (jax.ShapeDtypeStruct((tokens, features), F32), stack, stack),
        (whole((tokens, features)), whole(stack.shape), stacked(3, tokens, wide)),
        [pltpu.VMEM((tokens, wide), BF16)], 8 * tokens * features ** 2)


def attention_back(active, lengths, grad_mid, x, qkv, w_qkv, w_out, cosine, sine, parts=2):
    tokens, features = x.shape
    row_tokens = tokens // lengths.shape[0]
    size = features // HEADS
    low = jax.ShapeDtypeStruct((tokens, features), BF16)
    stack = jax.ShapeDtypeStruct((3, tokens, features), BF16)
    full = jax.ShapeDtypeStruct((tokens, features), F32)
    vectors = jax.ShapeDtypeStruct((8, features), F32)
    outs = (low, stack, full, low, vectors)
    hbm, smem, dma = pl.BlockSpec(memory_space=pl.ANY), pl.BlockSpec(memory_space=pltpu.SMEM), pltpu.SemaphoreType.DMA
    held = [grad_mid, x, qkv, w_qkv, w_out, cosine, sine, low, stack, low, vectors]
    return pl.pallas_call(
        functools.partial(attention_back_kernel, size, row_tokens, parts),
        out_shape=outs,
        in_specs=[smem, smem] + [hbm] * 7,
        out_specs=[hbm] * len(outs),
        scratch_shapes=[pltpu.VMEM(item.shape, item.dtype) for item in held] + [
            pltpu.VMEM((tokens, features // parts), BF16), pltpu.VMEM((tokens, features), F32),
            dma((4,)), dma((parts, 5)), dma((4 + parts,))],
        name="attention_back",
        cost_estimate=pl.CostEstimate(
            flops=20 * tokens * features ** 2, bytes_accessed=40 * 2 ** 20, transcendentals=0),
        compiler_params=pltpu.CompilerParams(vmem_limit_bytes=56 * 1024 * 1024),
    )(active, lengths, grad_mid, x, qkv, w_qkv, w_out, cosine, sine)


def third(tokens, features):
    return pl.BlockSpec((1, tokens, features), lambda part, *_: (2, 0, 0))


def meeting_call(kernel, name, parts, args, in_specs, outs, out_specs, scratch, flops, collective_id):
    return pl.pallas_call(
        kernel,
        grid=(parts,),
        in_specs=in_specs,
        out_specs=out_specs,
        out_shape=outs,
        scratch_shapes=scratch,
        name=name,
        cost_estimate=pl.CostEstimate(flops=flops, bytes_accessed=40 * 2 ** 20, transcendentals=0),
        compiler_params=pltpu.CompilerParams(
            dimension_semantics=("arbitrary",), vmem_limit_bytes=56 * 1024 * 1024, collective_id=collective_id,
            has_side_effects=True),
    )(*args)


def feed(mid, lefts, rows, w_gate_up, w_down, unit_rows, collective_id, parts=8):
    tokens, features = mid.shape
    wide = w_down.shape[0] // parts
    hbm = pl.BlockSpec(memory_space=pl.ANY)
    low = jax.ShapeDtypeStruct((tokens, features), BF16)
    return meeting_call(
        functools.partial(feed_kernel, unit_rows), "feed", parts,
        (mid, lefts, w_gate_up, w_gate_up, w_down, lefts, rows),
        [whole((tokens, features)), third(tokens, features), column(features, wide), column(features, wide, parts),
         lower(wide, features), hbm, hbm],
        (low, jax.ShapeDtypeStruct((tokens, w_down.shape[0] // 2), BF16), low,
         jax.ShapeDtypeStruct((2, tokens, features), BF16), low),
        (whole((tokens, features)), column(tokens, wide // 2), hbm, hbm, hbm),
        [pltpu.VMEM((tokens, features), F32), pltpu.SemaphoreType.DMA((2, 2))],
        6 * tokens * features * w_down.shape[0], collective_id)


def feed_both(active, mid, lefts, grad, gain, gain_a, w_gate_up, w_down, sends, lands, collective_id, parts=8):
    tokens, features = mid.shape
    hidden = w_down.shape[0]
    wide = hidden // parts
    hbm = pl.BlockSpec(memory_space=pl.ANY)
    return meeting_call(
        functools.partial(feed_both_kernel, active), "feed_both", parts,
        (mid, lefts, grad, gain, gain_a, w_gate_up, w_gate_up, w_down, *sends),
        [whole((tokens, features)), third(tokens, features), whole((tokens, features)), whole((1, features)),
         whole((1, features)), column(features, wide), column(features, wide, parts), lower(wide, features)]
        + [hbm] * len(sends),
        (jax.ShapeDtypeStruct((tokens, features), F32), jax.ShapeDtypeStruct((tokens, hidden), BF16),
         jax.ShapeDtypeStruct((2, tokens, hidden), BF16), jax.ShapeDtypeStruct((tokens + 8, features), F32),
         jax.ShapeDtypeStruct((8, features), F32), *lands),
        (whole((tokens, features)), column(tokens, wide), stacked(2, tokens, wide),
         whole((tokens + 8, features)), whole((8, features))) + (hbm,) * len(lands),
        [pltpu.VMEM((tokens, features), F32), pltpu.SemaphoreType.DMA((2, 10))],
        12 * tokens * features * hidden, collective_id)


def tables(lengths, row_tokens, size):
    index = jnp.arange(row_tokens, dtype=jnp.int32)[None]
    end, before = 0, 0
    for window in range(lengths.shape[1]):
        length = lengths[:, window:window + 1]
        end = end + length
        before = before + jnp.where(index >= end, length, 0)
    position = (index - before).astype(F32).reshape(-1, 1)
    half = jnp.arange(2 * size, dtype=jnp.int32) % (size // 2)
    frequency = 10000.0 ** (-2.0 * half.astype(F32) / size)
    angles = position * frequency
    return jnp.cos(angles), jnp.sin(angles)


def exchange_kernel(cfg, *refs):
    shards, bits, seats, unit_rows, width, section, aliased, late, layers, other_layers, lag, supply, order = cfg
    arrays = len(seats)
    refs = list(refs)

    def take(count):
        taken = refs[:count]
        del refs[:count]
        return taken

    lefts, rights = take(arrays), take(arrays)
    left_others, right_others = take(arrays - (1 if late else 0)), take(1)
    lefts = [ref if at is None else ref.at[at] for ref, at in zip(lefts, layers)]
    left_others = [ref if at is None else ref.at[at] for ref, at in zip(left_others, other_layers)]
    (vector,) = take(1)
    vector_given = take(1) if supply else []
    take(arrays + 1 if aliased else 0)
    outs, (vector_out,) = take(arrays), take(1)
    if late:
        left_others = left_others + take(1)
    given = [rights[index] for index in supply]
    for index in supply:
        rights[index] = take(1)[0]
    (given_send, given_recv, vector_far, vector_full, vector_land, vector_sum, vector_send, vector_recv, vector_store, left, right, left_sem, right_sem, other_sem,
     right_send, right_recv, late_send, late_recv, mine, side_land, side, side_send, side_recv, chain_a, chain_b,
     chain_send, chain_recv, rest_send, rest_land, rest_keep, rest_ssem, rest_rsem, piece, store_sem, gather_send,
     gather_recv) = refs
    units = sum(seat[0] for seat in seats)
    by_column = units - seats[-1][0]
    others = bits - 1
    final_rows = unit_rows >> others
    tokens = left.shape[1] // 2
    chains = (chain_a, chain_b)
    chain_rows = (final_rows, unit_rows)
    depth = chain_a.shape[1] - 1
    ring = mine.shape[1]
    slots, right_slots = piece.shape[1], right.shape[0]
    sec = lax.axis_index("section")
    here = lax.axis_index("shard")
    seat = lax.axis_index("group")
    group = 1 << bits
    peers = shards * group
    me = here * group + seat
    part = vector_out.shape[1]

    def bit_of(index):
        return lax.rem(lax.div(seat, 1 << order[index]), 2)

    def across(index):
        return (sec, here, seat + (1 - 2 * bit_of(index)) * (1 << order[index]))

    above = (sec, jnp.minimum(here + 1, shards - 1), seat)
    below = (sec, jnp.maximum(here - 1, 0), seat)
    half = bit_of(0)

    def remote(source, target, send, recv, device):
        return pltpu.make_async_remote_copy(
            src_ref=source, dst_ref=target, send_sem=send, recv_sem=recv,
            device_id=device, device_id_type=MESH,
        )

    def aligned(start, size):
        return pl.ds(pl.multiple_of(start, size), size)

    def peer(step):
        index = lax.rem(me + step, peers)
        return index, (sec, lax.div(index, group), lax.rem(index, group))

    def vector_copy(index, device):
        return remote(vector_full.at[:, aligned(device[1] * part, part)], vector_land.at[me], vector_send.at[index],
                      vector_recv.at[me], device)

    def vector_finish():
        vector_full[...] = vector[...]
        if supply:
            vector_full[...] += vector_far[...]

        @pl.loop(1, peers)
        def _(step):
            vector_copy(*peer(step)).start()
        vector_sum[...] = vector_full[:, aligned(here * part, part)]

        @pl.loop(1, peers)
        def _(step):
            index, device = peer(step)
            vector_copy(index, device).wait_send()
            remote(vector_land.at[index], vector_land.at[index], vector_send.at[index], vector_recv.at[index],
                   device).wait_recv()
            vector_sum[...] += vector_land[index]
        copy = pltpu.make_async_copy(vector_sum, vector_out, vector_store)
        copy.start()
        copy.wait()

    def valid(chunk):
        return (chunk >= 0) & (chunk < units)

    def on(condition, run):
        pl.when(condition)(run)

    def by_rows(rows, run, tall=64):
        step = min(rows, tall)

        @pl.loop(0, rows // step)
        def _(index):
            run(aligned(index * step, step))

    def shifted(rows, offset):
        return aligned(rows.start + offset, rows.size)

    pace = min(by_column // seats[-1][0], 2)
    lead = by_column - pace * seats[-1][0]

    def seat_of(chunk):
        behind = jnp.maximum(chunk - lead, 0)
        period = lax.div(behind, pace + 1)
        step = behind - period * (pace + 1)
        last = (chunk >= lead) & (step == 0)
        return last, jnp.where(last, period, jnp.where(chunk < lead, chunk, lead + period * pace + step - 1))

    def each_array(chunk, run):
        last, index = seat_of(chunk)
        start = 0
        for which, (count, blocks, _, _) in enumerate(seats):
            begin = 0 if split_rows(which) else start

            def launch(which=which, begin=begin, blocks=blocks):
                local = index - begin
                row = lax.div(local, blocks)
                run(which, row, local - row * blocks)
            here_it_is = last if split_rows(which) else jnp.logical_not(last) & (index >= start) & (index < start + count)
            on((chunk < units) & here_it_is, launch)
            start += count

    def split_rows(which):
        return which == arrays - 1

    def right_columns(which, block, bit):
        inner = seats[which][2]
        if split_rows(which):
            return 0, aligned(block * (2 * width), 2 * width)
        outer = lax.div(block, inner)
        return outer, aligned((block - outer * inner) * (4 * width) + bit * (2 * width), 2 * width)

    def loads(chunk, run):
        slot = lax.rem(chunk, right_slots)

        def each(which, row, block):
            outer, columns = right_columns(which, block, half)
            run(pltpu.make_async_copy(
                rights[which].at[outer, :, columns], right.at[slot, :tokens], right_sem.at[slot]))
            if split_rows(which):
                run(pltpu.make_async_copy(
                    right_others[0].at[:, columns], right.at[slot, tokens:], other_sem.at[slot]))
        each_array(chunk, each)

    def load_left(chunk):
        def each(which, row, block):
            rows = seats[which][3]
            kind = int(split_rows(which))
            copies = []
            for shard in range(shards):
                if split_rows(which):
                    offsets = (shard * rows + (2 * row + half) * unit_rows, shard * (rows // 2) + row * unit_rows)
                else:
                    offsets = (shard * rows + row * unit_rows,) * 2
                for side, source in enumerate((lefts[which], left_others[which])):
                    copies.append(pltpu.make_async_copy(
                        source.at[:, aligned(offsets[side], unit_rows)],
                        left.at[kind, side * tokens:(side + 1) * tokens, shard * unit_rows:(shard + 1) * unit_rows],
                        left_sem.at[kind, side, shard]))

            def fetch():
                for copy in copies:
                    copy.start()
                for copy in copies:
                    copy.wait()
            on(block == 0, fetch)
        each_array(chunk, each)

    def right_copy(chunk, source):
        four = lax.rem(chunk, right_slots)
        return remote(source, right.at[four, tokens:], right_send.at[four], right_recv.at[four], across(0))

    def send_right(chunk):
        def each(which, row, block):
            if not split_rows(which):
                outer, columns = right_columns(which, block, 1 - half)
                right_copy(chunk, rights[which].at[outer, :, columns]).start()
        each_array(chunk, each)

    late_rows = seats[-1][3] // (2 * unit_rows)

    def late_copy(row, shard):
        source = aligned(shard * seats[-1][3] + (2 * row + 1 - half) * unit_rows, unit_rows)
        target = aligned(shard * (seats[-1][3] // 2) + row * unit_rows, unit_rows)
        return remote(lefts[-1].at[:, source], left_others[-1].at[:, target], late_send.at[row, shard],
                      late_recv.at[row, shard], across(0))

    def late_turn(turn):
        begin = 0
        for row in range(late_rows):
            need = max(lead + row * seats[-1][1] * (pace + 1) - 1, 0)
            at_once = -(-shards // max(need - begin, 1))
            for index in range(at_once):
                shard = (turn - begin) * at_once + index
                on((turn >= begin) & (shard < shards), lambda row=row, shard=shard: late_copy(row, shard).start())

            def finish(row=row):
                @pl.loop(0, shards)
                def _(shard):
                    late_copy(row, shard).wait_send()
                    late_copy(row, shard).wait_recv()
            on(turn == need, finish)
            begin = need

    def multiply(chunk):
        four, slot = lax.rem(chunk, right_slots), lax.rem(chunk, ring)
        load_left(chunk)
        loads(chunk, lambda copy: copy.wait())
        last = seat_of(chunk)[0]

        def arrived():
            copy = right_copy(chunk, right.at[four, tokens:])
            copy.wait_recv()
            copy.wait_send()
        on(jnp.logical_not(last), arrived)
        result = lax.dot_general(left[last.astype(jnp.int32)], right[four], (((0,), (0,)), ((), ())), preferred_element_type=F32)
        for shard in range(shards):
            for path in range(2):
                mine[path, slot, shard] = result[
                    shard * unit_rows:(shard + 1) * unit_rows, path * width:(path + 1) * width].astype(BF16)

    def side_copy(step, chunk):
        slot, four = lax.rem(chunk, ring), lax.rem(chunk, slots)
        rows = unit_rows >> (step + 1)
        away = aligned((1 - bit_of(step + 1)) * rows, rows)
        source = mine.at[0, slot, :, away] if step == 0 else side.at[step - 1, slot, :, away]
        return remote(source, side_land.at[step, four, :, :rows], side_send.at[step, four], side_recv.at[step, four],
                      across(step + 1))

    def side_sum(step, chunk):
        slot, four = lax.rem(chunk, ring), lax.rem(chunk, slots)
        rows = unit_rows >> (step + 1)
        kept = bit_of(step + 1) * rows
        copy = side_copy(step, chunk)
        copy.wait_recv()
        copy.wait_send()

        @pl.loop(0, shards)
        def _(shard):
            def add(part):
                source = mine[0, slot, shard, shifted(part, kept)] if step == 0 else side[
                    step - 1, slot, shard, shifted(part, kept)]
                side[step, slot, shard, part] = (
                    source.astype(F32) + side_land[step, four, shard, part].astype(F32)).astype(BF16)
            by_rows(rows, add)
        if step + 1 < others:
            side_copy(step + 1, chunk).start()

    def base(path, slot, shard, rows):
        return (side[others - 1, slot, shard, rows] if path == 0 else mine[1, slot, shard, rows]).astype(F32)

    def hop(path, way, chunk, shard):
        slot = lax.rem(chunk, depth)
        ref = chains[path].at[way, slot, shard]
        return remote(ref, ref, chain_send.at[path, way, slot, shard], chain_recv.at[path, way, slot, shard],
                      above if way == 0 else below)

    def onward(path, way, chunk):
        slot, from_base = lax.rem(chunk, depth), lax.rem(chunk, ring)
        arrives = here > 0 if way == 0 else here < shards - 1

        @pl.loop(0, shards - 1 - here if way == 0 else here)
        def _(index):
            shard = shards - 1 - index if way == 0 else index
            copy = hop(path, way, chunk, shard)
            on(arrives, lambda: copy.wait_recv())
            source = jnp.where(arrives, slot, depth)

            def add(rows):
                chains[path][way, slot, shard, rows] = (
                    chains[path][way, source, shard, rows].astype(F32) + base(path, from_base, shard, rows)
                ).astype(BF16)
            by_rows(chain_rows[path], add)
            copy.start()

    def sent(path, way, chunk):
        @pl.loop(0, shards - 1 - here if way == 0 else here)
        def _(index):
            hop(path, way, chunk, shards - 1 - index if way == 0 else index).wait_send()

    def last_hop(path, chunk):
        from_base, slot = lax.rem(chunk, ring), lax.rem(chunk, depth)
        on(here > 0, lambda: hop(path, 0, chunk, here).wait_recv())
        on(here < shards - 1, lambda: hop(path, 1, chunk, here).wait_recv())
        from_below = jnp.where(here > 0, slot, depth)
        from_above = jnp.where(here < shards - 1, slot, depth)

        def total(rows, offset):
            rows = shifted(rows, offset)
            return (
                base(path, from_base, here, rows)
                + chains[path][0, from_below, here, rows].astype(F32)
                + chains[path][1, from_above, here, rows].astype(F32)
            )
        if path == 0:
            finish(path, chunk, total)
        else:
            share(0, chunk, total)

    def rest_copy(step, chunk):
        slot, rows = lax.rem(chunk, slots), pl.ds(0, unit_rows >> (step + 1))
        return remote(rest_send.at[step, slot, rows], rest_land.at[step, slot, rows], rest_ssem.at[step, slot],
                      rest_rsem.at[step, slot], across(step + 1))

    def share(step, chunk, total):
        slot, rows = lax.rem(chunk, slots), unit_rows >> (step + 1)
        bit = bit_of(step + 1)

        def give(part):
            rest_send[step, slot, part] = total(part, (1 - bit) * rows).astype(BF16)
        by_rows(rows, give)
        rest_copy(step, chunk).start()

        def keep(part):
            rest_keep[step, slot, part] = total(part, bit * rows)
        by_rows(rows, keep)

    def rest_sum(step, chunk):
        slot = lax.rem(chunk, slots)
        copy = rest_copy(step, chunk)
        copy.wait_recv()
        copy.wait_send()

        def total(part, offset):
            part = shifted(part, offset)
            return rest_keep[step, slot, part] + rest_land[step, slot, part].astype(F32)
        if step + 1 < others:
            share(step + 1, chunk, total)
        else:
            finish(1, chunk, total)

    def finish(path, chunk, total):
        def put(part):
            piece[path, lax.rem(chunk, slots), part] = total(part, 0).astype(BF16)
        by_rows(final_rows, put)
        spread(path, 0, chunk)

    def place(which, row, block, path, bit, offset, rows):
        if split_rows(which):
            row0, column = (2 * row + bit) * unit_rows, block * (2 * width) + path * width
        else:
            row0, column = row * unit_rows, block * (4 * width) + bit * (2 * width) + path * width
        return outs[which].at[aligned(row0 + offset, rows), aligned(column, width)]

    def seat_row(steps):
        row = 0
        for step in range(steps):
            row = row + bit_of(step + 1) * (unit_rows >> (step + 1))
        return row

    def store(path, chunk, target):
        slot = lax.rem(chunk, slots)
        return pltpu.make_async_copy(piece.at[path, slot], target, store_sem.at[path, slot])

    def gather(path, step, other, chunk, target):
        slot = lax.rem(chunk, slots)
        source = piece.at[path, slot] if step == 0 else target
        return remote(source, target, gather_send.at[path, step, other, slot], gather_recv.at[path, step, other, slot],
                      across(0 if step == 0 else bits - step))

    def spread(path, step, chunk):
        steps = others - max(step - 1, 0)
        rows = unit_rows >> steps

        def each(which, row, block):
            for other in range(1 if step == 0 else 2):
                bit = half if other == 0 else 1 - half
                target = place(which, row, block, path, bit, seat_row(steps), rows)
                if step == 0:
                    store(path, chunk, target).start()
                gather(path, step, other, chunk, target).start()
        each_array(chunk, each)

    def gathered(path, step, chunk):
        rows = unit_rows >> (others - max(step - 1, 0))
        target = outs[0].at[pl.ds(0, rows), pl.ds(0, width)]
        for other in range(1 if step == 0 else 2):
            copy = gather(path, step, other, chunk, target)
            copy.wait_recv()
            copy.wait_send()
        if step == 0:
            store(path, chunk, target).wait()
        if step + 1 < bits:
            spread(path, step + 1, chunk)

    def given_copies():
        device = (section, here, seat)
        targets = [rights[index] for index in supply] + [vector_far]
        return [remote(source, target, given_send.at[index], given_recv.at[index], device)
                for index, (source, target) in enumerate(zip(given + vector_given, targets))]

    def hand_over():
        pl.semaphore_wait(pltpu.get_barrier_semaphore(), 1)
        for copy in given_copies():
            copy.start()
        for copy in given_copies():
            copy.wait_send()

    def take_over():
        for copy in given_copies():
            copy.wait_recv()

    def unit_of(index):
        return index if index < lead else lead + (index - lead) // pace * (pace + 1) + 1 + (index - lead) % pace

    def work():
        barrier = pltpu.get_barrier_semaphore()
        if supply:
            pl.semaphore_signal(barrier, inc=1, device_id=(1 - section, here, seat), device_id_type=MESH)

        @pl.loop(1, peers)
        def _(step):
            pl.semaphore_signal(barrier, inc=1, device_id=peer(step)[1], device_id_type=MESH)
        pl.semaphore_wait(barrier, peers - 1)
        for chunk in range(lag):
            send_right(chunk)
        loads(0, lambda copy: copy.start())

        for path in range(2):
            for way in range(2):
                @pl.loop(0, shards)
                def _(shard):
                    def clear(rows):
                        chains[path][way, depth, shard, rows] = jnp.zeros((rows.size, width), BF16)
                    by_rows(chain_rows[path], clear)

        line = shards - 1

        @pl.loop(0, units + lag * (line + others + bits) + 2)
        def _(turn):
            if supply:
                on(turn == unit_of(sum(seat[0] for seat in seats[:supply[0]])) - lag, take_over)
            on(turn + lag < units, lambda: send_right(turn + lag))
            if late:
                late_turn(turn)
            on(turn + 1 < units, lambda: loads(turn + 1, lambda copy: copy.start()))

            def opening():
                multiply(turn)
                side_copy(0, turn).start()
            on(turn < units, opening)
            for step in range(others):
                chunk = turn - lag * (1 + step)
                on(valid(chunk), lambda step=step, chunk=chunk: side_sum(step, chunk))
            for path in range(2):
                for way in range(2):
                    chunk = turn - lag * ((others if path == 0 else 0) + (here if way == 0 else line - here))
                    on(valid(chunk - 2), lambda path=path, way=way, chunk=chunk: sent(path, way, chunk - 2))
                    on(valid(chunk), lambda path=path, way=way, chunk=chunk: onward(path, way, chunk))
            on(valid(turn - lag * line), lambda: last_hop(1, turn - lag * line))
            on(valid(turn - lag * (line + others)), lambda: last_hop(0, turn - lag * (line + others)))
            for step in range(others):
                chunk = turn - lag * (line + 1 + step)
                on(valid(chunk), lambda step=step, chunk=chunk: rest_sum(step, chunk))
            for step in range(bits):
                for path in range(2):
                    chunk = turn - lag * (line + others + 1 + step)
                    on(valid(chunk), lambda path=path, step=step, chunk=chunk: gathered(path, step, chunk))

        vector_finish()

    if section is None:
        work()
    else:
        pl.when(sec == section)(work)
        if supply:
            pl.when(sec != section)(hand_over)


def exchange(pairs, vector, shards, group, section, collective_id, unit_width, previous=None, lag=2, supply=(), vector_given=None, first_bit=0, unit_rows_max=256,
             name="exchange"):
    bits = group.bit_length() - 1
    arrays = len(pairs)
    order = (first_bit,) + tuple(bit for bit in range(bits) if bit != first_bit)
    lefts, rights = [pair[0][0] for pair in pairs], [pair[1] for pair in pairs]
    layers = tuple(pair[0][1] for pair in pairs)
    left_others = [pair[2] and pair[2][0] for pair in pairs]
    other_layers = tuple(pair[2] and pair[2][1] for pair in pairs)
    late = pairs[-1][2] is None
    if late:
        left_others = left_others[:-1]
    tokens = lefts[0].shape[-2]
    rows_of = [left.shape[-1] // shards for left in lefts]
    unit_rows = min([unit_rows_max] + rows_of[:-1])
    width = unit_width // 4
    seats = []
    for index, (rows, right) in enumerate(zip(rows_of, rights)):
        tall, wide = (2 * unit_rows, 2 * width) if index == arrays - 1 else (unit_rows, 4 * width)
        inner = right.shape[2] // wide
        seats.append((rows // tall * right.shape[0] * inner, right.shape[0] * inner, inner, rows))
    units = sum(seat[0] for seat in seats)
    others = bits - 1
    final_rows = unit_rows >> others
    slots, right_slots = 2 * lag + 2, 2 * lag + 3
    depth, ring = lag * shards + 3, lag * (shards - 1) + 2
    late_rows = rows_of[-1] // (2 * unit_rows)
    peers, lanes = shards * group, vector.shape[1] // shards
    dma = pltpu.SemaphoreType.DMA
    scratch = [
        dma((len(supply) + 1,)), dma((len(supply) + 1,)),
        pltpu.VMEM(vector.shape, F32), pltpu.VMEM(vector.shape, F32),
        pltpu.VMEM((peers, vector.shape[0], lanes), F32),
        pltpu.VMEM((vector.shape[0], lanes), F32),
        dma((peers,)), dma((peers,)), dma,
        pltpu.VMEM((2, 2 * tokens, shards * unit_rows), BF16),
        pltpu.VMEM((right_slots, 2 * tokens, 2 * width), BF16),
        dma((2, 2, shards)), dma((right_slots,)), dma((right_slots,)),
        dma((right_slots,)), dma((right_slots,)),
        dma((late_rows, shards)), dma((late_rows, shards)),
        pltpu.VMEM((2, ring, shards, unit_rows, width), BF16),
        pltpu.VMEM((others, slots, shards, unit_rows // 2, width), BF16),
        pltpu.VMEM((others, ring, shards, unit_rows // 2, width), BF16),
        dma((others, slots)), dma((others, slots)),
        pltpu.VMEM((2, depth + 1, shards, final_rows, width), BF16),
        pltpu.VMEM((2, depth + 1, shards, unit_rows, width), BF16),
        dma((2, 2, depth, shards)), dma((2, 2, depth, shards)),
        pltpu.VMEM((others, slots, unit_rows // 2, width), BF16),
        pltpu.VMEM((others, slots, unit_rows // 2, width), BF16),
        pltpu.VMEM((others, slots, unit_rows // 2, width), F32),
        dma((others, slots)), dma((others, slots)),
        pltpu.VMEM((2, slots, final_rows, width), BF16),
        dma((2, slots)),
        dma((2, bits, 2, slots)), dma((2, bits, 2, slots)),
    ]
    cfg = (shards, bits, tuple(seats), unit_rows, width, section, previous is not None, late, layers, other_layers, lag, supply, order)
    vectors = [vector] + ([vector_given] if supply else [])
    operands = lefts + rights + left_others + [pairs[-1][3]] + vectors + list(previous or [])
    first = len(operands) - len(previous or [])
    results = [jax.ShapeDtypeStruct((r, g.shape[0] * g.shape[2]), BF16) for r, g in zip(rows_of, rights)]
    results.append(jax.ShapeDtypeStruct((vector.shape[0], lanes), F32))
    if late:
        results.append(jax.ShapeDtypeStruct((tokens, lefts[-1].shape[-1] // 2), BF16))
    results.extend(jax.ShapeDtypeStruct(rights[index].shape, BF16) for index in supply)
    hbm, vmem = pl.BlockSpec(memory_space=pl.ANY), pl.BlockSpec(memory_space=pltpu.VMEM)
    in_specs = [vmem if first - len(vectors) <= index < first else hbm for index in range(len(operands))]
    return pl.pallas_call(
        functools.partial(exchange_kernel, cfg),
        out_shape=results,
        in_specs=in_specs,
        out_specs=[hbm] * len(results),
        scratch_shapes=scratch,
        input_output_aliases={first + index: index for index in range(len(previous or []))},
        name=name,
        cost_estimate=pl.CostEstimate(
            flops=4 * tokens * units * shards * unit_rows * 2 * width, bytes_accessed=100 * 2 ** 20,
            transcendentals=0),
        compiler_params=pltpu.CompilerParams(
            collective_id=collective_id, has_side_effects=True, vmem_limit_bytes=56 * 1024 * 1024),
    )(*operands)[:arrays + 1]


UNIT_WIDTH = 512


def body(
    ends_in,
    lengths,
    norm_gain_a,
    norm_bias_a,
    w_qkv,
    w_out,
    norm_gain_f,
    norm_bias_f,
    w_gate_up,
    w_down,
):
    section = lax.axis_index("section")
    shards, group = lax.axis_size("shard"), lax.axis_size("group")
    is_first = section == 0
    first, second = ((section == which).astype(jnp.int32).reshape(1) for which in range(2))
    tokens, features = ends_in.shape[1:]
    size = features // HEADS
    rows = ends_in[0]
    weight_qkv, weight_out, weight_gu, weight_down = w_qkv[0], w_out[0], w_gate_up[0], w_down[0]
    cosine, sine = tables(lengths, tokens // lengths.shape[0], size)
    unit_rows = min(256, features // shards)
    low = jax.ShapeDtypeStruct((tokens, features), BF16)
    stack = jax.ShapeDtypeStruct((3, tokens, features), BF16)

    def like(array):
        return jax.ShapeDtypeStruct(array.shape, array.dtype)

    def attend(active, values):
        return attention(active, lengths, values, norm_gain_a, norm_bias_a, norm_gain_f, norm_bias_f, weight_qkv,
                         weight_out, cosine, sine)

    def feed_back(active, middle, lefts, grad, sends, lands, collective_id):
        return feed_both(active, middle, lefts, grad, norm_gain_f, norm_gain_a, weight_gu, weight_down, sends, lands,
                         collective_id)

    def attend_back(grad_middle, values, qkv, weight_qkv, weight_out):
        return attention_back(first, lengths, grad_middle, values, qkv, weight_qkv, weight_out, cosine, sine)

    def sum_all(which, lefts, lefts_beside, hidden, hidden_beside, rights, right_beside, vectors, **more):
        pairs = [((lefts, at), right, other) for at, right, other in zip((2, 1, 0), rights, lefts_beside)]
        pairs.append(((hidden, None), rights[3], hidden_beside, right_beside))
        return exchange(pairs, vectors, shards, group, which, which + 1, UNIT_WIDTH * features // 1024,
                        first_bit=1 - which, **more)

    middle_0, lefts_0, qkv_0 = attend(first, rows)
    passed, hidden_half_0, arrived, early_beside, rows_beside = feed(
        middle_0, lefts_0, rows, weight_gu, weight_down, unit_rows, 3)
    middle_1, lefts_1, qkv_1 = attend(second, arrived)
    result, hidden_1, grad_gu_1, _, vectors_1, lefts_beside, qkv_there, qkv_weight, out_weight, hidden_beside, \
        grad_middle = feed_back(
            1, middle_1, lefts_1, rows,
            (lefts_1, qkv_1, weight_qkv, weight_out, lefts_0, hidden_half_0),
            (stack, stack, like(weight_qkv), like(weight_out), like(hidden_half_0), jax.ShapeDtypeStruct((tokens + 8, features), F32)), 4)
    branch, grad_qkv, _, returned, vectors_far = attend_back(grad_middle, passed, qkv_there, qkv_weight, out_weight)
    sums = sum_all(1, lefts_1, [(lefts_beside, at) for at in (2, 1, 0)], hidden_1, None,
                   (grad_gu_1, branch[None], grad_qkv, rows[None]), rows_beside, vectors_1, vector_given=vectors_far,
                   lag=1, supply=(1, 2), name="exchange_second")
    returned, _ = lax.optimization_barrier((returned, sums[4]))
    _, hidden_0, grad_gu_0, grad_middle, vectors_0, returned_beside = feed_back(
        0, middle_0, lefts_0, returned, (returned,), (low,), 5)
    branch, grad_qkv, grad_in, _, vectors_near = attend_back(grad_middle, rows, qkv_0, weight_qkv, weight_out)
    sums = sum_all(0, lefts_0, [(lefts_beside, 2), (early_beside, 1), (early_beside, 0)], hidden_0,
                   (hidden_beside, None), (grad_gu_0, branch[None], grad_qkv, returned[None]), returned_beside,
                   vectors_0 + vectors_near, previous=sums, lag=2, name="exchange_first")
    ends_out = jnp.where(is_first, grad_in, result)[None]
    grad_gate_up, grad_out, grad_qkv, grad_down = (item.astype(F32)[None] for item in sums[:4])
    vectors = sums[4]
    return (
        ends_out,
        vectors[0:1],
        vectors[1:2],
        grad_qkv,
        grad_out,
        vectors[2:3],
        vectors[3:4],
        grad_gate_up,
        grad_down,
    )


def solution(mesh):
    placed = (
        P("section", ("shard", "group"), None),
        P(("shard", "group"), None),
        P("section", None),
        P("section", None),
        P("section", None, None),
        P("section", None, None),
        P("section", None),
        P("section", None),
        P("section", None, None),
        P("section", None, None),
    )
    return jax.shard_map(
        body,
        mesh=mesh,
        in_specs=placed,
        out_specs=(
            P("section", ("shard", "group"), None),
            P("section", "shard"),
            P("section", "shard"),
            P("section", "shard", None),
            P("section", "shard", None),
            P("section", "shard"),
            P("section", "shard"),
            P("section", "shard", None),
            P("section", "shard", None),
        ),
        check_vma=False,
    )
```

```python
import functools

import jax
import jax.numpy as jnp
from jax import lax
from jax.experimental import pallas as pl
from jax.experimental.pallas import tpu as pltpu
from jax.sharding import PartitionSpec as P

MESH = pl.DeviceIdType.MESH
F32, BF16 = jnp.float32, jnp.bfloat16
HEADS = 16
EPSILON = 1e-05


def dot(a, b):
    return jnp.dot(a, b, preferred_element_type=F32)


def dot_cols(a, b):
    return lax.dot_general(a, b, (((1,), (1,)), ((), ())), preferred_element_type=F32)


def dot_rows(a, b):
    return lax.dot_general(a, b, (((0,), (0,)), ((), ())), preferred_element_type=F32)


def in_rows(total, step, run):
    @pl.loop(0, total // step)
    def _(index):
        run(pl.ds(pl.multiple_of(index * step, step), step))


def normalized(values):
    average = jnp.mean(values, axis=-1, keepdims=True)
    centered = values - average
    variance = jnp.mean(centered * centered, axis=-1, keepdims=True)
    spread = lax.rsqrt(variance + EPSILON)
    return centered * spread, spread


def norm_back(grad, values, gain):
    unit, spread = normalized(values)
    scaled = grad * gain
    return spread * (
        scaled
        - jnp.mean(scaled, axis=-1, keepdims=True)
        - unit * jnp.mean(scaled * unit, axis=-1, keepdims=True)
    ), grad * unit


def lanes_of(shape):
    return lax.broadcasted_iota(jnp.int32, shape, len(shape) - 1)


def turn(values, half, size):
    wide = values.shape[-1]
    early = lax.rem(lanes_of(values.shape), size) < half
    return jnp.where(early, pltpu.roll(values, wide - half, 1), pltpu.roll(values, half, 1)), early


def rotated(values, cosine, sine, size):
    other, early = turn(values, size // 2, size)
    return values * cosine + jnp.where(early, -other, other) * sine


def unrotated(values, cosine, sine, size):
    other, early = turn(values * sine, size // 2, size)
    return values * cosine + jnp.where(early, other, -other)


def window_of(index, lengths_ref, row):
    windows = lengths_ref.shape[1]
    end = lengths_ref[row, 0]
    segment = (index >= end).astype(jnp.int32)
    for window in range(1, windows):
        end = end + lengths_ref[row, window]
        segment = segment + (index >= end).astype(jnp.int32)
    return segment


def same_window(lengths_ref, row, tokens):
    queries = window_of(lax.broadcasted_iota(jnp.int32, (tokens, 1), 0), lengths_ref, row)
    keys = window_of(lax.broadcasted_iota(jnp.int32, (1, tokens), 1), lengths_ref, row)
    return queries == keys


def softmax(scores, allowed):
    scores = jnp.where(allowed, scores, -1e30)
    weights = jnp.exp(scores - jnp.max(scores, axis=-1, keepdims=True))
    return weights * (1.0 / jnp.sum(weights, axis=-1, keepdims=True))


def attention_kernel(size, row_tokens, act_ref, lengths_ref, x_ref, gain_ref, bias_ref, gain_f_ref, bias_f_ref,
                     wq_ref, wk_ref, wv_ref, wo_ref, cos_ref, sin_ref, mid_ref, lefts_ref, qkv_ref, mix_ref):
    tokens = x_ref.shape[0]
    part = pl.program_id(0)
    block = wq_ref.shape[1]
    pair = 2 * size

    @pl.when(act_ref[0] == 1)
    def _():
        @pl.when(part == 0)
        def _():
            def begin(rows):
                values = x_ref[rows].astype(F32)
                unit, _ = normalized(values)
                lefts_ref[0, rows] = (unit * gain_ref[...] + bias_ref[...]).astype(BF16)
                mid_ref[rows] = values
            in_rows(tokens, 64, begin)

        for which, weight in enumerate((wq_ref, wk_ref, wv_ref)):
            projected = dot(lefts_ref[0], weight[...])
            for at in range(block // pair):
                lanes = slice(at * pair, (at + 1) * pair)
                values = projected[:, lanes]
                if which < 2:
                    values = rotated(values, cos_ref[...], sin_ref[...], size)
                qkv_ref[which, :, lanes] = values.astype(BF16)

        first = lanes_of((row_tokens, pair)) < size
        @pl.loop(0, tokens // row_tokens)
        def _(row):
            rows = pl.ds(pl.multiple_of(row * row_tokens, row_tokens), row_tokens)
            allowed = same_window(lengths_ref, row, row_tokens)
            for start in range(0, block // pair, 2):
                work = []
                for at in range(start, start + 2):
                    lanes = pl.ds(at * pair, pair)
                    query, key, value = (qkv_ref[which, rows, lanes] for which in range(3))
                    query = query * (size ** -0.5)
                    for head in range(2):
                        own = jnp.where(first if head == 0 else jnp.logical_not(first), query, jnp.zeros_like(query))
                        work.append((dot_cols(own, key), value))
                work = [(softmax(scores, allowed).astype(BF16), value) for scores, value in work]
                work = [dot(probs, value) for probs, value in work]
                for at in range(2):
                    lanes = pl.ds((start + at) * pair, pair)
                    mix_ref[rows, lanes] = jnp.where(first, work[2 * at], work[2 * at + 1]).astype(BF16)

        mixture = mix_ref[...]
        lefts_ref[1, :, pl.ds(pl.multiple_of(part * block, block), block)] = mixture
        mid_ref[...] += dot(mixture, wo_ref[...])

        @pl.when(part == pl.num_programs(0) - 1)
        def _():
            def close(rows):
                unit, _ = normalized(mid_ref[rows])
                lefts_ref[2, rows] = (unit * gain_f_ref[...] + bias_f_ref[...]).astype(BF16)
            in_rows(tokens, 64, close)


def places():
    section, shard, seat = (lax.axis_index(name) for name in ("section", "shard", "group"))
    stride = 2 - section
    bit = lax.rem(lax.div(seat, stride), 2)
    return section, bit, (section, shard, seat + (1 - 2 * bit) * stride), (1 - section, shard, seat)


def remote(source, target, sems, index, device):
    return pltpu.make_async_remote_copy(
        src_ref=source, dst_ref=target, send_sem=sems.at[0, index], recv_sem=sems.at[1, index], device_id=device,
        device_id_type=pl.DeviceIdType.MESH)


def meet(*devices):
    barrier = pltpu.get_barrier_semaphore()
    for device in devices:
        pl.semaphore_signal(barrier, inc=1, device_id=device, device_id_type=pl.DeviceIdType.MESH)
    pl.semaphore_wait(barrier, len(devices))


def feed_kernel(unit_rows, mid_ref, low_ref, wg_ref, wu_ref, wd_ref, lefts_ref, rows_ref, out_ref, half_ref,
                arrived_ref, lefts_land, rows_land, total_ref, sems):
    part = pl.program_id(0)
    section, bit, beside, above = places()
    lefts_copy = remote(lefts_ref.at[0:2], lefts_land, sems, 0, beside)
    rows_copy = remote(rows_ref, rows_land, sems, 0, beside)
    out_copy = remote(out_ref, arrived_ref, sems, 1, above)

    @pl.when(part == 0)
    def _():
        meet(beside, above)
        pl.when(section == 0)(lefts_copy.start)
        pl.when(section == 1)(rows_copy.start)

    @pl.when(section == 0)
    def _():
        @pl.when(part == 0)
        def _():
            total_ref[...] = mid_ref[...]

        low = low_ref[0]
        gate = dot(low, wg_ref[...])
        up = dot(low, wu_ref[...])
        hidden = (gate / (1.0 + jnp.exp(-gate)) * up).astype(BF16)
        for at in range(half_ref.shape[1] // unit_rows):
            rows = [hidden[:, (2 * at + side) * unit_rows:(2 * at + side + 1) * unit_rows] for side in range(2)]
            half_ref[:, at * unit_rows:(at + 1) * unit_rows] = jnp.where(bit == 0, rows[1], rows[0])
        total_ref[...] += dot(hidden, wd_ref[...])

    @pl.when(part == pl.num_programs(0) - 1)
    def _():
        @pl.when(section == 0)
        def _():
            out_ref[...] = total_ref[...].astype(BF16)
            out_copy.start()
            out_copy.wait_send()
            lefts_copy.wait()

        @pl.when(section == 1)
        def _():
            out_copy.wait_recv()
            rows_copy.wait()


def feed_both_kernel(active, mid_ref, low_ref, grad_ref, gain_ref, gain_a_ref, wg_ref, wu_ref, wd_ref, *refs):
    sends, refs = refs[:6 if active else 1], refs[6 if active else 1:]
    out_ref, hidden_ref, ggu_ref, grad_mid_ref, vectors_ref = refs[:5]
    lands = refs[5:5 + (6 if active else 1)]
    total_ref, sems = refs[-2:]
    tokens = mid_ref.shape[0]
    part = pl.program_id(0)
    section, _, beside, other = places()
    pieces = 4
    step = tokens // pieces
    if active:
        lefts_ref, qkv_ref, wqkv_ref, wo_ref, lefts_first, hidden_first = sends
        lefts_land, qkv_land, wqkv_land, wo_land, hidden_land, grad_land = lands
        working = [
            remote(lefts_ref, lefts_land, sems, 0, beside), remote(qkv_ref, qkv_land, sems, 1, other),
            remote(wqkv_ref, wqkv_land, sems, 2, other), remote(wo_ref, wo_land, sems, 3, other)]
        waiting = [
            remote(lefts_first.at[2], lefts_land.at[2], sems, 4, beside),
            remote(hidden_first, hidden_land, sems, 5, beside)]

        def grad_copy(piece):
            rows = pl.ds(piece * step, step + (8 if piece == pieces - 1 else 0))
            return remote(grad_mid_ref.at[rows], grad_land.at[rows], sems, 6 + piece, other)
    else:
        working = [remote(sends[0], lands[0], sems, 0, beside)]

    @pl.when(part == 0)
    def _():
        if active:
            meet(beside, other)

            @pl.when(section != active)
            def _():
                for copy in waiting:
                    copy.start()

        @pl.when(section == active)
        def _():
            if not active:
                meet(beside)
            for copy in working:
                copy.start()

    @pl.when(section == active)
    def _():
        @pl.when(part == 0)
        def _():
            out_ref[...] = mid_ref[...]

        low = low_ref[0]
        gate = dot(low, wg_ref[...])
        up = dot(low, wu_ref[...])
        grad_hidden = dot_cols(grad_ref[...], wd_ref[...])
        sig = 1.0 / (1.0 + jnp.exp(-gate))
        silu = gate * sig
        hidden_ref[...] = (silu * up).astype(BF16)
        ggu_ref[0] = (grad_hidden * up * (sig * (1.0 + gate * (1.0 - sig)))).astype(BF16)
        ggu_ref[1] = (grad_hidden * silu).astype(BF16)
        out_ref[...] += dot(hidden_ref[...], wd_ref[...])
        added = dot_cols(ggu_ref[0], wg_ref[...]) + dot_cols(ggu_ref[1], wu_ref[...])
        total_ref[...] = jnp.where(part == 0, added, total_ref[...] + added)

    @pl.when(part == pl.num_programs(0) - 1)
    def _():
        @pl.when(section == active)
        def _():
            vectors_ref[...] = jnp.zeros_like(vectors_ref)
            grad_mid_ref[pl.ds(tokens, 8)] = jnp.broadcast_to(gain_a_ref[...], (8, gain_a_ref.shape[1]))

            def finish(rows):
                grad = total_ref[rows]
                through, by_gain = norm_back(grad, mid_ref[rows], gain_ref[...])
                grad_mid_ref[rows] = grad_ref[rows].astype(F32) + through
                vectors_ref[2:3] += jnp.sum(by_gain, axis=0, keepdims=True)
                vectors_ref[3:4] += jnp.sum(grad, axis=0, keepdims=True)
            for piece in range(pieces):
                for at in range(2):
                    finish(pl.ds(piece * step + at * (step // 2), step // 2))
                if active:
                    grad_copy(piece).start()
            if active:
                for piece in range(pieces):
                    grad_copy(piece).wait_send()
                for copy in working[1:]:
                    copy.wait_send()
            working[0].wait()

        if active:
            @pl.when(section != active)
            def _():
                for piece in range(pieces):
                    grad_copy(piece).wait_recv()
                for copy in working[1:]:
                    copy.wait_recv()
                for copy in waiting:
                    copy.wait()


def whole(shape):
    return pl.BlockSpec(shape, lambda part, *_: (0,) * len(shape))


def column(rows, wide, offset=0):
    return pl.BlockSpec((rows, wide), lambda part, *act: (0, (part + offset) * (act[0][0] if act else 1)))


def stacked(count, rows, wide):
    return pl.BlockSpec((count, rows, wide), lambda part, *act: (0, 0, part * (act[0][0] if act else 1)))


def lower(rows, wide):
    return pl.BlockSpec((rows, wide), lambda part, *act: (part * (act[0][0] if act else 1), 0))


def local_call(kernel, name, grid, scalars, args, in_specs, outs, out_specs, scratch, flops, limit=56):
    return pl.pallas_call(
        kernel,
        grid_spec=pltpu.PrefetchScalarGridSpec(
            num_scalar_prefetch=len(scalars), grid=(grid,), in_specs=in_specs, out_specs=out_specs,
            scratch_shapes=scratch),
        out_shape=outs,
        name=name,
        cost_estimate=pl.CostEstimate(flops=flops, bytes_accessed=40 * 2 ** 20, transcendentals=0),
        compiler_params=pltpu.CompilerParams(
            dimension_semantics=("arbitrary",), vmem_limit_bytes=limit * 1024 * 1024),
    )(*scalars, *args)


def attention(active, lengths, x, gain, bias, gain_f, bias_f, w_qkv, w_out, cosine, sine, parts=2):
    tokens, features = x.shape
    row_tokens = tokens // lengths.shape[0]
    size = features // HEADS
    wide = features // parts
    stack = jax.ShapeDtypeStruct((3, tokens, features), BF16)
    return local_call(
        functools.partial(attention_kernel, size, row_tokens), "attention", parts, (active, lengths),
        (x, gain, bias, gain_f, bias_f, w_qkv, w_qkv, w_qkv, w_out, cosine, sine),
        [whole((tokens, features))] + [whole((1, features))] * 4 + [column(features, wide),
         column(features, wide, parts), column(features, wide, 2 * parts), lower(wide, features),
         whole(cosine.shape), whole(sine.shape)],
        (jax.ShapeDtypeStruct((tokens, features), F32), stack, stack),
        (whole((tokens, features)), whole(stack.shape), stacked(3, tokens, wide)),
        [pltpu.VMEM((tokens, wide), BF16)], 8 * tokens * features ** 2)


def third(tokens, features):
    return pl.BlockSpec((1, tokens, features), lambda part, *_: (2, 0, 0))


def meeting_call(kernel, name, parts, args, in_specs, outs, out_specs, scratch, flops, collective_id):
    return pl.pallas_call(
        kernel,
        grid=(parts,),
        in_specs=in_specs,
        out_specs=out_specs,
        out_shape=outs,
        scratch_shapes=scratch,
        name=name,
        cost_estimate=pl.CostEstimate(flops=flops, bytes_accessed=40 * 2 ** 20, transcendentals=0),
        compiler_params=pltpu.CompilerParams(
            dimension_semantics=("arbitrary",), vmem_limit_bytes=56 * 1024 * 1024, collective_id=collective_id,
            has_side_effects=True),
    )(*args)


def feed(mid, lefts, rows, w_gate_up, w_down, unit_rows, collective_id, parts=8):
    tokens, features = mid.shape
    wide = w_down.shape[0] // parts
    hbm = pl.BlockSpec(memory_space=pl.ANY)
    low = jax.ShapeDtypeStruct((tokens, features), BF16)
    return meeting_call(
        functools.partial(feed_kernel, unit_rows), "feed", parts,
        (mid, lefts, w_gate_up, w_gate_up, w_down, lefts, rows),
        [whole((tokens, features)), third(tokens, features), column(features, wide), column(features, wide, parts),
         lower(wide, features), hbm, hbm],
        (low, jax.ShapeDtypeStruct((tokens, w_down.shape[0] // 2), BF16), low,
         jax.ShapeDtypeStruct((2, tokens, features), BF16), low),
        (whole((tokens, features)), column(tokens, wide // 2), hbm, hbm, hbm),
        [pltpu.VMEM((tokens, features), F32), pltpu.SemaphoreType.DMA((2, 2))],
        6 * tokens * features * w_down.shape[0], collective_id)


def feed_both(active, mid, lefts, grad, gain, gain_a, w_gate_up, w_down, sends, lands, collective_id, parts=8):
    tokens, features = mid.shape
    hidden = w_down.shape[0]
    wide = hidden // parts
    hbm = pl.BlockSpec(memory_space=pl.ANY)
    return meeting_call(
        functools.partial(feed_both_kernel, active), "feed_both", parts,
        (mid, lefts, grad, gain, gain_a, w_gate_up, w_gate_up, w_down, *sends),
        [whole((tokens, features)), third(tokens, features), whole((tokens, features)), whole((1, features)),
         whole((1, features)), column(features, wide), column(features, wide, parts), lower(wide, features)]
        + [hbm] * len(sends),
        (jax.ShapeDtypeStruct((tokens, features), F32), jax.ShapeDtypeStruct((tokens, hidden), BF16),
         jax.ShapeDtypeStruct((2, tokens, hidden), BF16), jax.ShapeDtypeStruct((tokens + 8, features), F32),
         jax.ShapeDtypeStruct((8, features), F32), *lands),
        (whole((tokens, features)), column(tokens, wide), stacked(2, tokens, wide),
         whole((tokens + 8, features)), whole((8, features))) + (hbm,) * len(lands),
        [pltpu.VMEM((tokens, features), F32), pltpu.SemaphoreType.DMA((2, 10))],
        12 * tokens * features * hidden, collective_id)


def tables(lengths, row_tokens, size):
    index = jnp.arange(row_tokens, dtype=jnp.int32)[None]
    end, before = 0, 0
    for window in range(lengths.shape[1]):
        length = lengths[:, window:window + 1]
        end = end + length
        before = before + jnp.where(index >= end, length, 0)
    position = (index - before).astype(F32).reshape(-1, 1)
    half = jnp.arange(2 * size, dtype=jnp.int32) % (size // 2)
    frequency = 10000.0 ** (-2.0 * half.astype(F32) / size)
    angles = position * frequency
    return jnp.cos(angles), jnp.sin(angles)


def exchange_kernel(cfg, back_sizes, *refs):
    shards, bits, seats, unit_rows, width, section, aliased, late, layers, other_layers, lag, supply, order, backs = cfg
    arrays = len(seats)
    refs = list(refs)

    def take(count):
        taken = refs[:count]
        del refs[:count]
        return taken

    lefts, rights = take(arrays), take(arrays - len(supply))
    for index in supply:
        rights.insert(index, None)
    left_others, right_others = take(arrays - (1 if late else 0)), take(1)
    lefts = [ref if at is None else ref.at[at] for ref, at in zip(lefts, layers)]
    left_others = [ref if at is None else ref.at[at] for ref, at in zip(left_others, other_layers)]
    (vector,) = take(1)
    back_in = take(7)
    (lengths_ref,) = take(1)
    take(arrays + 2 if aliased else 0)
    outs, (vector_out,) = take(arrays), take(1)
    if late:
        left_others = left_others + take(1)
    for index in supply:
        rights[index] = take(1)[0]
    (back_out,) = take(1)
    back_refs, (back_load, back_store) = take(12), take(2)
    (grad_ref, x_ref, qkv_ref, wqkv_ref, wo_ref, cos_ref, sin_ref, branch_ref, proj_ref, vectors_ref, gm_ref,
     total_ref) = back_refs
    (given_send, given_recv, vector_far, vector_full, vector_land, vector_sum, vector_send, vector_recv, vector_store, left, right, left_sem, right_sem, other_sem,
     right_send, right_recv, late_send, late_recv, mine, side_land, side, side_send, side_recv, chain_a, chain_b,
     chain_send, chain_recv, rest_send, rest_land, rest_keep, rest_ssem, rest_rsem, piece, store_sem, gather_send,
     gather_recv) = refs
    units = sum(seat[0] for seat in seats)
    by_column = units - seats[-1][0]
    others = bits - 1
    final_rows = unit_rows >> others
    tokens = left.shape[1] // 2
    chains = (chain_a, chain_b)
    chain_rows = (final_rows, unit_rows)
    depth = chain_a.shape[1] - 1
    ring = mine.shape[1]
    slots, right_slots = piece.shape[1], right.shape[0]
    sec = lax.axis_index("section")
    here = lax.axis_index("shard")
    seat = lax.axis_index("group")
    group = 1 << bits
    peers = shards * group
    me = here * group + seat
    part = vector_out.shape[1]

    def bit_of(index):
        return lax.rem(lax.div(seat, 1 << order[index]), 2)

    def across(index):
        return (sec, here, seat + (1 - 2 * bit_of(index)) * (1 << order[index]))

    above = (sec, jnp.minimum(here + 1, shards - 1), seat)
    below = (sec, jnp.maximum(here - 1, 0), seat)
    half = bit_of(0)

    def remote(source, target, send, recv, device):
        return pltpu.make_async_remote_copy(
            src_ref=source, dst_ref=target, send_sem=send, recv_sem=recv,
            device_id=device, device_id_type=MESH,
        )

    def aligned(start, size):
        return pl.ds(pl.multiple_of(start, size), size)

    def peer(step):
        index = lax.rem(me + step, peers)
        return index, (sec, lax.div(index, group), lax.rem(index, group))

    def vector_copy(index, device):
        return remote(vector_full.at[:, aligned(device[1] * part, part)], vector_land.at[me], vector_send.at[index],
                      vector_recv.at[me], device)

    def vector_finish():
        vector_full[...] = vector[...] + (vectors_ref[...] if backs else vector_far[...])

        @pl.loop(1, peers)
        def _(step):
            vector_copy(*peer(step)).start()
        vector_sum[...] = vector_full[:, aligned(here * part, part)]

        @pl.loop(1, peers)
        def _(step):
            index, device = peer(step)
            vector_copy(index, device).wait_send()
            remote(vector_land.at[index], vector_land.at[index], vector_send.at[index], vector_recv.at[index],
                   device).wait_recv()
            vector_sum[...] += vector_land[index]
        copy = pltpu.make_async_copy(vector_sum, vector_out, vector_store)
        copy.start()
        copy.wait()

    def valid(chunk):
        return (chunk >= 0) & (chunk < units)

    def on(condition, run):
        pl.when(condition)(run)

    def by_rows(rows, run, tall=64):
        step = min(rows, tall)

        @pl.loop(0, rows // step)
        def _(index):
            run(aligned(index * step, step))

    def shifted(rows, offset):
        return aligned(rows.start + offset, rows.size)

    pace = min(by_column // seats[-1][0], 2)
    lead = by_column - pace * seats[-1][0]

    def seat_of(chunk):
        behind = jnp.maximum(chunk - lead, 0)
        period = lax.div(behind, pace + 1)
        step = behind - period * (pace + 1)
        last = (chunk >= lead) & (step == 0)
        return last, jnp.where(last, period, jnp.where(chunk < lead, chunk, lead + period * pace + step - 1))

    def each_array(chunk, run):
        last, index = seat_of(chunk)
        start = 0
        for which, (count, blocks, _, _) in enumerate(seats):
            begin = 0 if split_rows(which) else start

            def launch(which=which, begin=begin, blocks=blocks):
                local = index - begin
                row = lax.div(local, blocks)
                run(which, row, local - row * blocks)
            here_it_is = last if split_rows(which) else jnp.logical_not(last) & (index >= start) & (index < start + count)
            on((chunk < units) & here_it_is, launch)
            start += count

    def split_rows(which):
        return which == arrays - 1

    def right_columns(which, block, bit):
        inner = seats[which][2]
        if split_rows(which):
            return 0, aligned(block * (2 * width), 2 * width)
        outer = lax.div(block, inner)
        return outer, aligned((block - outer * inner) * (4 * width) + bit * (2 * width), 2 * width)

    def loads(chunk, run):
        slot = lax.rem(chunk, right_slots)

        def each(which, row, block):
            outer, columns = right_columns(which, block, half)
            run(pltpu.make_async_copy(
                rights[which].at[outer, :, columns], right.at[slot, :tokens], right_sem.at[slot]))
            if split_rows(which):
                run(pltpu.make_async_copy(
                    right_others[0].at[:, columns], right.at[slot, tokens:], other_sem.at[slot]))
        each_array(chunk, each)

    def load_left(chunk):
        def each(which, row, block):
            rows = seats[which][3]
            kind = int(split_rows(which))
            copies = []
            for shard in range(shards):
                if split_rows(which):
                    offsets = (shard * rows + (2 * row + half) * unit_rows, shard * (rows // 2) + row * unit_rows)
                else:
                    offsets = (shard * rows + row * unit_rows,) * 2
                for side, source in enumerate((lefts[which], left_others[which])):
                    copies.append(pltpu.make_async_copy(
                        source.at[:, aligned(offsets[side], unit_rows)],
                        left.at[kind, side * tokens:(side + 1) * tokens, shard * unit_rows:(shard + 1) * unit_rows],
                        left_sem.at[kind, side, shard]))

            def fetch():
                for copy in copies:
                    copy.start()
                for copy in copies:
                    copy.wait()
            on(block == 0, fetch)
        each_array(chunk, each)

    def right_copy(chunk, source):
        four = lax.rem(chunk, right_slots)
        return remote(source, right.at[four, tokens:], right_send.at[four], right_recv.at[four], across(0))

    def send_right(chunk):
        def each(which, row, block):
            if not split_rows(which):
                outer, columns = right_columns(which, block, 1 - half)
                right_copy(chunk, rights[which].at[outer, :, columns]).start()
        each_array(chunk, each)

    late_rows = seats[-1][3] // (2 * unit_rows)

    def late_copy(row, shard):
        source = aligned(shard * seats[-1][3] + (2 * row + 1 - half) * unit_rows, unit_rows)
        target = aligned(shard * (seats[-1][3] // 2) + row * unit_rows, unit_rows)
        return remote(lefts[-1].at[:, source], left_others[-1].at[:, target], late_send.at[row, shard],
                      late_recv.at[row, shard], across(0))

    def late_turn(turn):
        begin = 0
        for row in range(late_rows):
            need = max(lead + row * seats[-1][1] * (pace + 1) - 1, 0)
            at_once = -(-shards // max(need - begin, 1))
            for index in range(at_once):
                shard = (turn - begin) * at_once + index
                on((turn >= begin) & (shard < shards), lambda row=row, shard=shard: late_copy(row, shard).start())

            def finish(row=row):
                @pl.loop(0, shards)
                def _(shard):
                    late_copy(row, shard).wait_send()
                    late_copy(row, shard).wait_recv()
            on(turn == need, finish)
            begin = need

    def multiply(chunk):
        four, slot = lax.rem(chunk, right_slots), lax.rem(chunk, ring)
        load_left(chunk)
        loads(chunk, lambda copy: copy.wait())
        last = seat_of(chunk)[0]

        def arrived():
            copy = right_copy(chunk, right.at[four, tokens:])
            copy.wait_recv()
            copy.wait_send()
        on(jnp.logical_not(last), arrived)
        result = lax.dot_general(left[last.astype(jnp.int32)], right[four], (((0,), (0,)), ((), ())), preferred_element_type=F32)
        for shard in range(shards):
            for path in range(2):
                mine[path, slot, shard] = result[
                    shard * unit_rows:(shard + 1) * unit_rows, path * width:(path + 1) * width].astype(BF16)

    def side_copy(step, chunk):
        slot, four = lax.rem(chunk, ring), lax.rem(chunk, slots)
        rows = unit_rows >> (step + 1)
        away = aligned((1 - bit_of(step + 1)) * rows, rows)
        source = mine.at[0, slot, :, away] if step == 0 else side.at[step - 1, slot, :, away]
        return remote(source, side_land.at[step, four, :, :rows], side_send.at[step, four], side_recv.at[step, four],
                      across(step + 1))

    def side_sum(step, chunk):
        slot, four = lax.rem(chunk, ring), lax.rem(chunk, slots)
        rows = unit_rows >> (step + 1)
        kept = bit_of(step + 1) * rows
        copy = side_copy(step, chunk)
        copy.wait_recv()
        copy.wait_send()

        @pl.loop(0, shards)
        def _(shard):
            def add(part):
                source = mine[0, slot, shard, shifted(part, kept)] if step == 0 else side[
                    step - 1, slot, shard, shifted(part, kept)]
                side[step, slot, shard, part] = (
                    source.astype(F32) + side_land[step, four, shard, part].astype(F32)).astype(BF16)
            by_rows(rows, add)
        if step + 1 < others:
            side_copy(step + 1, chunk).start()

    def base(path, slot, shard, rows):
        return (side[others - 1, slot, shard, rows] if path == 0 else mine[1, slot, shard, rows]).astype(F32)

    def hop(path, way, chunk, shard):
        slot = lax.rem(chunk, depth)
        ref = chains[path].at[way, slot, shard]
        return remote(ref, ref, chain_send.at[path, way, slot, shard], chain_recv.at[path, way, slot, shard],
                      above if way == 0 else below)

    def onward(path, way, chunk):
        slot, from_base = lax.rem(chunk, depth), lax.rem(chunk, ring)
        arrives = here > 0 if way == 0 else here < shards - 1

        @pl.loop(0, shards - 1 - here if way == 0 else here)
        def _(index):
            shard = shards - 1 - index if way == 0 else index
            copy = hop(path, way, chunk, shard)
            on(arrives, lambda: copy.wait_recv())
            source = jnp.where(arrives, slot, depth)

            def add(rows):
                chains[path][way, slot, shard, rows] = (
                    chains[path][way, source, shard, rows].astype(F32) + base(path, from_base, shard, rows)
                ).astype(BF16)
            by_rows(chain_rows[path], add)
            copy.start()

    def sent(path, way, chunk):
        @pl.loop(0, shards - 1 - here if way == 0 else here)
        def _(index):
            hop(path, way, chunk, shards - 1 - index if way == 0 else index).wait_send()

    def last_hop(path, chunk):
        from_base, slot = lax.rem(chunk, ring), lax.rem(chunk, depth)
        on(here > 0, lambda: hop(path, 0, chunk, here).wait_recv())
        on(here < shards - 1, lambda: hop(path, 1, chunk, here).wait_recv())
        from_below = jnp.where(here > 0, slot, depth)
        from_above = jnp.where(here < shards - 1, slot, depth)

        def total(rows, offset):
            rows = shifted(rows, offset)
            return (
                base(path, from_base, here, rows)
                + chains[path][0, from_below, here, rows].astype(F32)
                + chains[path][1, from_above, here, rows].astype(F32)
            )
        if path == 0:
            finish(path, chunk, total)
        else:
            share(0, chunk, total)

    def rest_copy(step, chunk):
        slot, rows = lax.rem(chunk, slots), pl.ds(0, unit_rows >> (step + 1))
        return remote(rest_send.at[step, slot, rows], rest_land.at[step, slot, rows], rest_ssem.at[step, slot],
                      rest_rsem.at[step, slot], across(step + 1))

    def share(step, chunk, total):
        slot, rows = lax.rem(chunk, slots), unit_rows >> (step + 1)
        bit = bit_of(step + 1)

        def give(part):
            rest_send[step, slot, part] = total(part, (1 - bit) * rows).astype(BF16)
        by_rows(rows, give)
        rest_copy(step, chunk).start()

        def keep(part):
            rest_keep[step, slot, part] = total(part, bit * rows)
        by_rows(rows, keep)

    def rest_sum(step, chunk):
        slot = lax.rem(chunk, slots)
        copy = rest_copy(step, chunk)
        copy.wait_recv()
        copy.wait_send()

        def total(part, offset):
            part = shifted(part, offset)
            return rest_keep[step, slot, part] + rest_land[step, slot, part].astype(F32)
        if step + 1 < others:
            share(step + 1, chunk, total)
        else:
            finish(1, chunk, total)

    def finish(path, chunk, total):
        def put(part):
            piece[path, lax.rem(chunk, slots), part] = total(part, 0).astype(BF16)
        by_rows(final_rows, put)
        spread(path, 0, chunk)

    def place(which, row, block, path, bit, offset, rows):
        if split_rows(which):
            row0, column = (2 * row + bit) * unit_rows, block * (2 * width) + path * width
        else:
            row0, column = row * unit_rows, block * (4 * width) + bit * (2 * width) + path * width
        return outs[which].at[aligned(row0 + offset, rows), aligned(column, width)]

    def seat_row(steps):
        row = 0
        for step in range(steps):
            row = row + bit_of(step + 1) * (unit_rows >> (step + 1))
        return row

    def store(path, chunk, target):
        slot = lax.rem(chunk, slots)
        return pltpu.make_async_copy(piece.at[path, slot], target, store_sem.at[path, slot])

    def gather(path, step, other, chunk, target):
        slot = lax.rem(chunk, slots)
        source = piece.at[path, slot] if step == 0 else target
        return remote(source, target, gather_send.at[path, step, other, slot], gather_recv.at[path, step, other, slot],
                      across(0 if step == 0 else bits - step))

    def spread(path, step, chunk):
        steps = others - max(step - 1, 0)
        rows = unit_rows >> steps

        def each(which, row, block):
            for other in range(1 if step == 0 else 2):
                bit = half if other == 0 else 1 - half
                target = place(which, row, block, path, bit, seat_row(steps), rows)
                if step == 0:
                    store(path, chunk, target).start()
                gather(path, step, other, chunk, target).start()
        each_array(chunk, each)

    def gathered(path, step, chunk):
        rows = unit_rows >> (others - max(step - 1, 0))
        target = outs[0].at[pl.ds(0, rows), pl.ds(0, width)]
        for other in range(1 if step == 0 else 2):
            copy = gather(path, step, other, chunk, target)
            copy.wait_recv()
            copy.wait_send()
        if step == 0:
            store(path, chunk, target).wait()
        if step + 1 < bits:
            spread(path, step + 1, chunk)

    size, row_tokens, parts = back_sizes
    features = x_ref.shape[1]
    block, pair, scale = features // parts, 2 * size, size ** -0.5
    groups = block // pair // 2
    part_steps = 2 + tokens // row_tokens * groups
    back_steps = 2 + parts * part_steps

    def back_loads():
        return [pltpu.make_async_copy(source, target, back_load.at[index])
                for index, (source, target) in enumerate(zip(back_in, back_refs))]

    def back_start():
        copies = back_loads()
        for index in (0, 4, 2, 5, 6, 3, 1):
            copies[index].start()

    def back_lanes(part):
        return aligned(part * block, block)

    def deliver(index, source, target):
        if backs:
            return pltpu.make_async_copy(source, target, back_store.at[index])
        return remote(source, target, given_send.at[index], given_recv.at[index], (section, here, seat))

    def deliver_branch():
        return deliver(0, branch_ref, rights[supply[0]].at[0])

    def deliver_part(part):
        lanes = back_lanes(part)
        return deliver(1 + part, proj_ref.at[:, :, lanes], rights[supply[1]].at[:, :, lanes])

    def deliver_vectors():
        return deliver(1 + parts, vectors_ref, vector_far)

    def back_store_last():
        return pltpu.make_async_copy(total_ref if backs else branch_ref, back_out, back_store.at[1 + parts])

    def back_begin():
        back_loads()[0].wait()

        def put(rows):
            branch_ref[rows] = grad_ref[rows].astype(BF16)
        by_rows(tokens, put)
        deliver_branch().start()

    def back_open(part):
        @pl.when(part == 0)
        def _():
            for index in (4, 2, 5, 6):
                back_loads()[index].wait()
        gm_ref[...] = dot_cols(branch_ref[...], wo_ref[back_lanes(part)]).astype(BF16)

    def back_heads(part, row, group):
        rows = aligned(row * row_tokens, row_tokens)
        first = lanes_of((row_tokens, pair)) < size
        allowed = same_window(lengths_ref, row, row_tokens)
        cosine, sine = cos_ref[rows], sin_ref[rows]
        lanes = [aligned(part * block + (2 * group + at) * pair, pair) for at in range(2)]
        work = []
        for at in range(2):
            query, key, value = (qkv_ref[which, rows, lanes[at]] for which in range(3))
            grad_mix = gm_ref[rows, aligned((2 * group + at) * pair, pair)]
            scaled = query * scale
            for head in range(2):
                own = first if head == 0 else jnp.logical_not(first)
                work.append((
                    query, key, grad_mix,
                    dot_cols(jnp.where(own, scaled, jnp.zeros_like(scaled)), key),
                    dot_cols(jnp.where(own, grad_mix, jnp.zeros_like(grad_mix)), value)))
        results = []
        for query, key, grad_mix, scores, grad_probs in work:
            probs = softmax(scores, allowed)
            weighted = probs * grad_probs
            grad_scores = (weighted - probs * jnp.sum(weighted, axis=-1, keepdims=True)).astype(BF16)
            results.append((query, key, grad_mix, grad_scores, probs.astype(BF16)))
        results = [
            (dot(grad_scores, key), dot_rows(grad_scores, query), dot_rows(probs, grad_mix))
            for query, key, grad_mix, grad_scores, probs in results]
        for at in range(2):
            grad_query, grad_key, grad_value = (
                jnp.where(first, a, b) for a, b in zip(results[2 * at], results[2 * at + 1]))
            proj_ref[0, rows, lanes[at]] = unrotated(grad_query * scale, cosine, sine, size).astype(BF16)
            proj_ref[1, rows, lanes[at]] = unrotated(grad_key * scale, cosine, sine, size).astype(BF16)
            proj_ref[2, rows, lanes[at]] = grad_value.astype(BF16)

    def back_close(part):
        deliver_part(part).start()

        @pl.when(part == 0)
        def _():
            back_loads()[3].wait()
        added = 0.0
        for which in range(3):
            added = added + dot_cols(
                proj_ref[which, :, back_lanes(part)], wqkv_ref[:, aligned(which * features + part * block, block)])
        total_ref[...] = jnp.where(part == 0, added, total_ref[...] + added)

    def back_end():
        back_loads()[1].wait()
        vectors_ref[...] = jnp.zeros_like(vectors_ref)
        if not backs:
            deliver_branch().wait_send()

        def end(rows):
            grad = total_ref[rows]
            through, by_gain = norm_back(grad, x_ref[rows].astype(F32), grad_ref[tokens:tokens + 1])
            result = grad_ref[rows] + through
            if backs:
                total_ref[rows] = result
            else:
                branch_ref[rows] = result.astype(BF16)
            vectors_ref[0:1] += jnp.sum(by_gain, axis=0, keepdims=True)
            vectors_ref[1:2] += jnp.sum(grad, axis=0, keepdims=True)
        by_rows(tokens, end)
        back_store_last().start()
        if backs:
            deliver_branch().wait()
        else:
            deliver_vectors().start()
            deliver_vectors().wait_send()
        for part in range(parts):
            if backs:
                deliver_part(part).wait()
            else:
                deliver_part(part).wait_send()
        back_store_last().wait()

    def back_step(step):
        on(step == 0, back_begin)
        inner = jnp.maximum(step - 1, 0)
        part = lax.div(inner, part_steps)
        at = inner - part * part_steps
        within = (step > 0) & (step < back_steps - 1)
        on(within & (at == 0), lambda: back_open(part))
        head = at - 1
        row = lax.div(jnp.maximum(head, 0), groups)
        on(within & (at > 0) & (at < part_steps - 1), lambda: back_heads(part, row, head - row * groups))
        on(within & (at == part_steps - 1), lambda: back_close(part))
        on(step == back_steps - 1, back_end)

    def hand_over():
        back_start()
        pl.semaphore_wait(pltpu.get_barrier_semaphore(), 1)

        @pl.loop(0, back_steps)
        def _(step):
            back_step(step)

    def take_over():
        deliver_branch().wait_recv()
        for part in range(parts):
            deliver_part(part).wait_recv()
        deliver_vectors().wait_recv()

    def unit_of(index):
        return index if index < lead else lead + (index - lead) // pace * (pace + 1) + 1 + (index - lead) % pace

    def work():
        barrier = pltpu.get_barrier_semaphore()
        if not backs:
            pl.semaphore_signal(barrier, inc=1, device_id=(1 - section, here, seat), device_id_type=MESH)

        @pl.loop(1, peers)
        def _(step):
            pl.semaphore_signal(barrier, inc=1, device_id=peer(step)[1], device_id_type=MESH)
        pl.semaphore_wait(barrier, peers - 1)
        for chunk in range(lag):
            send_right(chunk)
        loads(0, lambda copy: copy.start())
        if backs:
            back_start()

        for path in range(2):
            for way in range(2):
                @pl.loop(0, shards)
                def _(shard):
                    def clear(rows):
                        chains[path][way, depth, shard, rows] = jnp.zeros((rows.size, width), BF16)
                    by_rows(chain_rows[path], clear)

        line = shards - 1

        @pl.loop(0, units + lag * (line + others + bits) + 2)
        def _(turn):
            if backs:
                back_step(turn - 1)
            else:
                on(turn == unit_of(sum(seat[0] for seat in seats[:supply[0]])) - lag, take_over)
            on(turn + lag < units, lambda: send_right(turn + lag))
            if late:
                late_turn(turn)
            on(turn + 1 < units, lambda: loads(turn + 1, lambda copy: copy.start()))

            def opening():
                multiply(turn)
                side_copy(0, turn).start()
            on(turn < units, opening)
            for step in range(others):
                chunk = turn - lag * (1 + step)
                on(valid(chunk), lambda step=step, chunk=chunk: side_sum(step, chunk))
            for path in range(2):
                for way in range(2):
                    chunk = turn - lag * ((others if path == 0 else 0) + (here if way == 0 else line - here))
                    on(valid(chunk - 2), lambda path=path, way=way, chunk=chunk: sent(path, way, chunk - 2))
                    on(valid(chunk), lambda path=path, way=way, chunk=chunk: onward(path, way, chunk))
            on(valid(turn - lag * line), lambda: last_hop(1, turn - lag * line))
            on(valid(turn - lag * (line + others)), lambda: last_hop(0, turn - lag * (line + others)))
            for step in range(others):
                chunk = turn - lag * (line + 1 + step)
                on(valid(chunk), lambda step=step, chunk=chunk: rest_sum(step, chunk))
            for step in range(bits):
                for path in range(2):
                    chunk = turn - lag * (line + others + 1 + step)
                    on(valid(chunk), lambda path=path, step=step, chunk=chunk: gathered(path, step, chunk))

        vector_finish()

    if section is None:
        work()
    else:
        pl.when(sec == section)(work)
        if not backs:
            pl.when(sec != section)(hand_over)


def exchange(pairs, vector, shards, group, section, collective_id, unit_width, previous=None, lag=None, first_bit=0, supply=(1, 2), back=(), backs=False, parts=2, unit_rows_max=256,
             name="exchange"):
    bits = group.bit_length() - 1
    arrays = len(pairs)
    order = (first_bit,) + tuple(bit for bit in range(bits) if bit != first_bit)
    lefts, rights = [pair[0][0] for pair in pairs], [pair[1] for pair in pairs]
    layers = tuple(pair[0][1] for pair in pairs)
    left_others = [pair[2] and pair[2][0] for pair in pairs]
    other_layers = tuple(pair[2] and pair[2][1] for pair in pairs)
    late = pairs[-1][2] is None
    if late:
        left_others = left_others[:-1]
    tokens = lefts[0].shape[-2]
    rows_of = [left.shape[-1] // shards for left in lefts]
    unit_rows = min([unit_rows_max] + rows_of[:-1])
    width = unit_width // 4
    seats = []
    for index, (rows, right) in enumerate(zip(rows_of, rights)):
        tall, wide = (2 * unit_rows, 2 * width) if index == arrays - 1 else (unit_rows, 4 * width)
        inner = right.shape[2] // wide
        seats.append((rows // tall * right.shape[0] * inner, right.shape[0] * inner, inner, rows))
    units = sum(seat[0] for seat in seats)
    others = bits - 1
    final_rows = unit_rows >> others
    lag = lag or (2 if shards <= 4 else 1)
    slots, right_slots = 2 * lag + 2, 2 * lag + 3
    depth, ring = lag * shards + 3, lag * (shards - 1) + 2
    late_rows = rows_of[-1] // (2 * unit_rows)
    peers, lanes = shards * group, vector.shape[1] // shards
    dma = pltpu.SemaphoreType.DMA
    *back, lengths = back
    x = back[1]
    previous = list(previous or [])
    scratch = [
        *(pltpu.VMEM(item.shape, item.dtype) for item in back),
        pltpu.VMEM(x.shape, BF16), pltpu.VMEM((3,) + x.shape, BF16), pltpu.VMEM(vector.shape, F32),
        pltpu.VMEM((tokens, x.shape[1] // parts), BF16), pltpu.VMEM(x.shape, F32),
        dma((len(back),)), dma((2 + parts,)),
        dma((2 + parts,)), dma((2 + parts,)),
        pltpu.VMEM(vector.shape, F32), pltpu.VMEM(vector.shape, F32),
        pltpu.VMEM((peers, vector.shape[0], lanes), F32),
        pltpu.VMEM((vector.shape[0], lanes), F32),
        dma((peers,)), dma((peers,)), dma,
        pltpu.VMEM((2, 2 * tokens, shards * unit_rows), BF16),
        pltpu.VMEM((right_slots, 2 * tokens, 2 * width), BF16),
        dma((2, 2, shards)), dma((right_slots,)), dma((right_slots,)),
        dma((right_slots,)), dma((right_slots,)),
        dma((late_rows, shards)), dma((late_rows, shards)),
        pltpu.VMEM((2, ring, shards, unit_rows, width), BF16),
        pltpu.VMEM((others, slots, shards, unit_rows // 2, width), BF16),
        pltpu.VMEM((others, ring, shards, unit_rows // 2, width), BF16),
        dma((others, slots)), dma((others, slots)),
        pltpu.VMEM((2, depth + 1, shards, final_rows, width), BF16),
        pltpu.VMEM((2, depth + 1, shards, unit_rows, width), BF16),
        dma((2, 2, depth, shards)), dma((2, 2, depth, shards)),
        pltpu.VMEM((others, slots, unit_rows // 2, width), BF16),
        pltpu.VMEM((others, slots, unit_rows // 2, width), BF16),
        pltpu.VMEM((others, slots, unit_rows // 2, width), F32),
        dma((others, slots)), dma((others, slots)),
        pltpu.VMEM((2, slots, final_rows, width), BF16),
        dma((2, slots)),
        dma((2, bits, 2, slots)), dma((2, bits, 2, slots)),
    ]
    cfg = (shards, bits, tuple(seats), unit_rows, width, section, len(previous) > 0, late, layers, other_layers, lag, supply, order, backs)
    operands = lefts + [r for n, r in enumerate(rights) if n not in supply] + left_others + [
        pairs[-1][3], vector] + back + [lengths] + previous
    first = len(operands) - len(previous)
    results = [jax.ShapeDtypeStruct((r, g.shape[0] * g.shape[2]), BF16) for r, g in zip(rows_of, rights)]
    results.append(jax.ShapeDtypeStruct((vector.shape[0], lanes), F32))
    if late:
        results.append(jax.ShapeDtypeStruct((tokens, lefts[-1].shape[-1] // 2), BF16))
    results.extend(jax.ShapeDtypeStruct(rights[index].shape, BF16) for index in supply)
    results.append(jax.ShapeDtypeStruct(x.shape, F32 if backs else BF16))
    aliases = {first + index: index for index in range(len(previous))}
    if previous:
        aliases[len(operands) - 1] = len(results) - 1
    hbm, vmem = pl.BlockSpec(memory_space=pl.ANY), pl.BlockSpec(memory_space=pltpu.VMEM)
    in_specs = [hbm] * len(operands)
    in_specs[first - 1] = pl.BlockSpec(memory_space=pltpu.SMEM)
    in_specs[first - 2 - len(back)] = vmem
    return pl.pallas_call(
        functools.partial(exchange_kernel, cfg, (x.shape[1] // HEADS, tokens // lengths.shape[0], parts)),
        out_shape=results,
        in_specs=in_specs,
        out_specs=[hbm] * len(results),
        scratch_shapes=scratch,
        input_output_aliases=aliases,
        name=name,
        cost_estimate=pl.CostEstimate(
            flops=4 * tokens * units * shards * unit_rows * 2 * width, bytes_accessed=100 * 2 ** 20,
            transcendentals=0),
        compiler_params=pltpu.CompilerParams(
            collective_id=collective_id, has_side_effects=True, vmem_limit_bytes=56 * 1024 * 1024),
    )(*operands)


UNIT_WIDTH = 512


def body(
    ends_in,
    lengths,
    norm_gain_a,
    norm_bias_a,
    w_qkv,
    w_out,
    norm_gain_f,
    norm_bias_f,
    w_gate_up,
    w_down,
):
    section = lax.axis_index("section")
    shards, group = lax.axis_size("shard"), lax.axis_size("group")
    first, second = ((section == which).astype(jnp.int32).reshape(1) for which in range(2))
    tokens, features = ends_in.shape[1:]
    size = features // HEADS
    rows = ends_in[0]
    weight_qkv, weight_out, weight_gu, weight_down = w_qkv[0], w_out[0], w_gate_up[0], w_down[0]
    cosine, sine = tables(lengths, tokens // lengths.shape[0], size)
    unit_rows = min(256, features // shards)
    low = jax.ShapeDtypeStruct((tokens, features), BF16)
    stack = jax.ShapeDtypeStruct((3, tokens, features), BF16)

    def like(array):
        return jax.ShapeDtypeStruct(array.shape, array.dtype)

    def attend(active, values):
        return attention(active, lengths, values, norm_gain_a, norm_bias_a, norm_gain_f, norm_bias_f, weight_qkv,
                         weight_out, cosine, sine)

    def feed_back(active, middle, lefts, grad, sends, lands, collective_id):
        return feed_both(active, middle, lefts, grad, norm_gain_f, norm_gain_a, weight_gu, weight_down, sends, lands,
                         collective_id)

    def sum_all(which, lefts, lefts_beside, hidden, hidden_beside, grad_gu, grad, grad_beside, vectors, back, **more):
        rights = (grad_gu, jax.ShapeDtypeStruct((1, tokens, features), BF16), stack)
        pairs = [((lefts, at), right, other) for at, right, other in zip((2, 1, 0), rights, lefts_beside)]
        pairs.append(((hidden, None), grad[None], hidden_beside, grad_beside))
        return exchange(pairs, vectors, shards, group, which, which + 1, UNIT_WIDTH * features // 1024,
                        first_bit=1 - which, back=back + (cosine, sine, lengths), **more)

    middle_0, lefts_0, qkv_0 = attend(first, rows)
    passed, hidden_half_0, arrived, early_beside, rows_beside = feed(
        middle_0, lefts_0, rows, weight_gu, weight_down, unit_rows, 3)
    middle_1, lefts_1, qkv_1 = attend(second, arrived)
    result, hidden_1, grad_gu_1, _, vectors_1, lefts_beside, qkv_there, qkv_weight, out_weight, hidden_beside, \
        grad_middle = feed_back(
            1, middle_1, lefts_1, rows,
            (lefts_1, qkv_1, weight_qkv, weight_out, lefts_0, hidden_half_0),
            (stack, stack, like(weight_qkv), like(weight_out), like(hidden_half_0), jax.ShapeDtypeStruct((tokens + 8, features), F32)), 4)
    sums = sum_all(1, lefts_1, [(lefts_beside, at) for at in (2, 1, 0)], hidden_1, None, grad_gu_1, rows, rows_beside,
                   vectors_1, (grad_middle, passed, qkv_there, qkv_weight, out_weight), name="exchange_second")
    returned = sums[-1]
    _, hidden_0, grad_gu_0, grad_middle, vectors_0, returned_beside = feed_back(
        0, middle_0, lefts_0, returned, (returned,), (low,), 5)
    sums = sum_all(0, lefts_0, [(lefts_beside, 2), (early_beside, 1), (early_beside, 0)], hidden_0,
                   (hidden_beside, None), grad_gu_0, returned, returned_beside, vectors_0,
                   (grad_middle, rows, qkv_0, weight_qkv, weight_out), backs=True, previous=[*sums[:5], result],
                   name="exchange_first")
    ends_out = sums[-1][None]
    grad_gate_up, grad_out, grad_qkv, grad_down = (item.astype(F32)[None] for item in sums[:4])
    vectors = sums[4]
    return (
        ends_out,
        vectors[0:1],
        vectors[1:2],
        grad_qkv,
        grad_out,
        vectors[2:3],
        vectors[3:4],
        grad_gate_up,
        grad_down,
    )


def solution(mesh):
    placed = (
        P("section", ("shard", "group"), None),
        P(("shard", "group"), None),
        P("section", None),
        P("section", None),
        P("section", None, None),
        P("section", None, None),
        P("section", None),
        P("section", None),
        P("section", None, None),
        P("section", None, None),
    )
    return jax.shard_map(
        body,
        mesh=mesh,
        in_specs=placed,
        out_specs=(
            P("section", ("shard", "group"), None),
            P("section", "shard"),
            P("section", "shard"),
            P("section", "shard", None),
            P("section", "shard", None),
            P("section", "shard"),
            P("section", "shard"),
            P("section", "shard", None),
            P("section", "shard", None),
        ),
        check_vma=False,
    )
```

```python
import functools

import jax
import jax.numpy as jnp
from jax import lax
from jax.experimental import pallas as pl
from jax.experimental.pallas import tpu as pltpu
from jax.sharding import PartitionSpec as P

MESH = pl.DeviceIdType.MESH
F32, BF16 = jnp.float32, jnp.bfloat16
HEADS = 16
EPSILON = 1e-05


def dot(a, b):
    return jnp.dot(a, b, preferred_element_type=F32)


def dot_cols(a, b):
    return lax.dot_general(a, b, (((1,), (1,)), ((), ())), preferred_element_type=F32)


def dot_rows(a, b):
    return lax.dot_general(a, b, (((0,), (0,)), ((), ())), preferred_element_type=F32)


def in_rows(total, step, run):
    @pl.loop(0, total // step)
    def _(index):
        run(pl.ds(pl.multiple_of(index * step, step), step))


def normalized(values):
    average = jnp.mean(values, axis=-1, keepdims=True)
    centered = values - average
    variance = jnp.mean(centered * centered, axis=-1, keepdims=True)
    spread = lax.rsqrt(variance + EPSILON)
    return centered * spread, spread


def norm_back(grad, values, gain):
    unit, spread = normalized(values)
    scaled = grad * gain
    return spread * (
        scaled
        - jnp.mean(scaled, axis=-1, keepdims=True)
        - unit * jnp.mean(scaled * unit, axis=-1, keepdims=True)
    ), grad * unit


def lanes_of(shape):
    return lax.broadcasted_iota(jnp.int32, shape, len(shape) - 1)


def turn(values, half, size):
    wide = values.shape[-1]
    early = lax.rem(lanes_of(values.shape), size) < half
    return jnp.where(early, pltpu.roll(values, wide - half, 1), pltpu.roll(values, half, 1)), early


def rotated(values, cosine, sine, size):
    other, early = turn(values, size // 2, size)
    return values * cosine + jnp.where(early, -other, other) * sine


def unrotated(values, cosine, sine, size):
    other, early = turn(values * sine, size // 2, size)
    return values * cosine + jnp.where(early, other, -other)


def window_of(index, lengths_ref, row):
    windows = lengths_ref.shape[1]
    end = lengths_ref[row, 0]
    segment = (index >= end).astype(jnp.int32)
    for window in range(1, windows):
        end = end + lengths_ref[row, window]
        segment = segment + (index >= end).astype(jnp.int32)
    return segment


def same_window(lengths_ref, row, tokens):
    queries = window_of(lax.broadcasted_iota(jnp.int32, (tokens, 1), 0), lengths_ref, row)
    keys = window_of(lax.broadcasted_iota(jnp.int32, (1, tokens), 1), lengths_ref, row)
    return queries == keys


def softmax(scores, allowed):
    scores = jnp.where(allowed, scores, -1e30)
    weights = jnp.exp(scores - jnp.max(scores, axis=-1, keepdims=True))
    return weights * (1.0 / jnp.sum(weights, axis=-1, keepdims=True))


def attention_kernel(size, row_tokens, active, x_ref, gain_ref, bias_ref, gain_f_ref, bias_f_ref, wq_ref, wk_ref,
                     wv_ref, wo_ref, cos_ref, sin_ref, lengths_ref, mid_ref, lefts_ref, qkv_ref, low_land, mix_ref, sems):
    tokens = x_ref.shape[0]
    part = pl.program_id(0)
    block = wq_ref.shape[1]
    pair = 2 * size

    section, _, beside, _ = places()
    low_copy = remote(lefts_ref.at[0], low_land, sems, 0, beside)

    @pl.when(section == active)
    def _():
        @pl.when(part == 0)
        def _():
            if active:
                greet(beside)

            def begin(rows):
                values = x_ref[rows].astype(F32)
                unit, _ = normalized(values)
                lefts_ref[0, rows] = (unit * gain_ref[...] + bias_ref[...]).astype(BF16)
                mid_ref[rows] = values
            in_rows(tokens, 64, begin)
            if active:
                await_greetings(1)
                low_copy.start()

        for which, weight in enumerate((wq_ref, wk_ref, wv_ref)):
            projected = dot(lefts_ref[0], weight[...])
            for at in range(block // pair):
                lanes = slice(at * pair, (at + 1) * pair)
                values = projected[:, lanes]
                if which < 2:
                    values = rotated(values, cos_ref[...], sin_ref[...], size)
                qkv_ref[which, :, lanes] = values.astype(BF16)

        first = lanes_of((row_tokens, pair)) < size
        @pl.loop(0, tokens // row_tokens)
        def _(row):
            rows = pl.ds(pl.multiple_of(row * row_tokens, row_tokens), row_tokens)
            allowed = same_window(lengths_ref, row, row_tokens)
            for start in range(0, block // pair, 2):
                work = []
                for at in range(start, start + 2):
                    lanes = pl.ds(at * pair, pair)
                    query, key, value = (qkv_ref[which, rows, lanes] for which in range(3))
                    query = query * (size ** -0.5)
                    for head in range(2):
                        own = jnp.where(first if head == 0 else jnp.logical_not(first), query, jnp.zeros_like(query))
                        work.append((dot_cols(own, key), value))
                work = [(softmax(scores, allowed).astype(BF16), value) for scores, value in work]
                work = [dot(probs, value) for probs, value in work]
                for at in range(2):
                    lanes = pl.ds((start + at) * pair, pair)
                    mix_ref[rows, lanes] = jnp.where(first, work[2 * at], work[2 * at + 1]).astype(BF16)

        mixture = mix_ref[...]
        lefts_ref[1, :, pl.ds(pl.multiple_of(part * block, block), block)] = mixture
        mid_ref[...] += dot(mixture, wo_ref[...])

        @pl.when(part == pl.num_programs(0) - 1)
        def _():
            def close(rows):
                unit, _ = normalized(mid_ref[rows])
                lefts_ref[2, rows] = (unit * gain_f_ref[...] + bias_f_ref[...]).astype(BF16)
            in_rows(tokens, 64, close)
            if active:
                low_copy.wait()


def places():
    section, shard, seat = (lax.axis_index(name) for name in ("section", "shard", "group"))
    stride = 2 - section
    bit = lax.rem(lax.div(seat, stride), 2)
    return section, bit, (section, shard, seat + (1 - 2 * bit) * stride), (1 - section, shard, seat)


def remote(source, target, sems, index, device):
    return pltpu.make_async_remote_copy(
        src_ref=source, dst_ref=target, send_sem=sems.at[0, index], recv_sem=sems.at[1, index], device_id=device,
        device_id_type=pl.DeviceIdType.MESH)


def greet(*devices):
    for device in devices:
        pl.semaphore_signal(
            pltpu.get_barrier_semaphore(), inc=1, device_id=device, device_id_type=pl.DeviceIdType.MESH)


def await_greetings(count):
    pl.semaphore_wait(pltpu.get_barrier_semaphore(), count)


def feed_kernel(unit_rows, mid_ref, low_ref, wg_ref, wu_ref, wd_ref, lefts_ref, rows_ref, out_ref, half_ref,
                arrived_ref, lefts_land, rows_land, total_ref, sems):
    part = pl.program_id(0)
    section, bit, beside, above = places()
    lefts_copy = remote(lefts_ref.at[0:2], lefts_land, sems, 0, beside)
    rows_copy = remote(rows_ref, rows_land, sems, 0, beside)
    out_copy = remote(out_ref, arrived_ref, sems, 1, above)

    pl.when(part == 0)(lambda: greet(beside, above))

    @pl.when(part == 1)
    def _():
        await_greetings(2)
        pl.when(section == 0)(lefts_copy.start)
        pl.when(section == 1)(rows_copy.start)

    @pl.when(section == 0)
    def _():
        @pl.when(part == 0)
        def _():
            total_ref[...] = mid_ref[...]

        low = low_ref[0]
        gate = dot(low, wg_ref[...])
        up = dot(low, wu_ref[...])
        hidden = (gate / (1.0 + jnp.exp(-gate)) * up).astype(BF16)
        for at in range(half_ref.shape[1] // unit_rows):
            rows = [hidden[:, (2 * at + side) * unit_rows:(2 * at + side + 1) * unit_rows] for side in range(2)]
            half_ref[:, at * unit_rows:(at + 1) * unit_rows] = jnp.where(bit == 0, rows[1], rows[0])
        total_ref[...] += dot(hidden, wd_ref[...])

    @pl.when(part == pl.num_programs(0) - 1)
    def _():
        @pl.when(section == 0)
        def _():
            out_ref[...] = total_ref[...].astype(BF16)
            out_copy.start()
            out_copy.wait_send()
            lefts_copy.wait()

        @pl.when(section == 1)
        def _():
            out_copy.wait_recv()
            rows_copy.wait()


def feed_both_kernel(active, mid_ref, low_ref, grad_ref, gain_ref, gain_a_ref, wg_ref, wu_ref, wd_ref, *refs):
    sends, refs = refs[:6 if active else 1], refs[6 if active else 1:]
    hidden_ref, ggu_ref, grad_mid_ref, vectors_ref = refs[:4]
    lands = refs[4:4 + (6 if active else 1)]
    total_ref, sems = refs[-2:]
    tokens = mid_ref.shape[0]
    part = pl.program_id(0)
    section, _, beside, other = places()
    pieces = 4
    step = tokens // pieces
    if active:
        lefts_ref, qkv_ref, wqkv_ref, wo_ref, lefts_first, hidden_first = sends
        lefts_land, qkv_land, wqkv_land, wo_land, hidden_land, grad_land = lands
        working = [
            remote(lefts_ref.at[1:3], lefts_land.at[1:3], sems, 0, beside), remote(qkv_ref, qkv_land, sems, 1, other),
            remote(wqkv_ref, wqkv_land, sems, 2, other), remote(wo_ref, wo_land, sems, 3, other)]
        waiting = [
            remote(lefts_first.at[2], lefts_land.at[2], sems, 4, beside),
            remote(hidden_first, hidden_land, sems, 5, beside)]

        def grad_copy(piece):
            rows = pl.ds(piece * step, step + (8 if piece == pieces - 1 else 0))
            return remote(grad_mid_ref.at[rows], grad_land.at[rows], sems, 6 + piece, other)
    else:
        working = [remote(sends[0], lands[0], sems, 0, beside)]

    @pl.when(part == 0)
    def _():
        if active:
            greet(beside, other)
        else:
            pl.when(section == active)(lambda: greet(beside))

    @pl.when(part == 1)
    def _():
        if active:
            await_greetings(2)

            @pl.when(section != active)
            def _():
                for copy in waiting:
                    copy.start()

        @pl.when(section == active)
        def _():
            if not active:
                await_greetings(1)
            for copy in working:
                copy.start()

    @pl.when(section == active)
    def _():
        low = low_ref[0]
        gate = dot(low, wg_ref[...])
        up = dot(low, wu_ref[...])
        grad_hidden = dot_cols(grad_ref[...], wd_ref[...])
        sig = 1.0 / (1.0 + jnp.exp(-gate))
        silu = gate * sig
        hidden_ref[...] = (silu * up).astype(BF16)
        ggu_ref[0] = (grad_hidden * up * (sig * (1.0 + gate * (1.0 - sig)))).astype(BF16)
        ggu_ref[1] = (grad_hidden * silu).astype(BF16)
        added = dot_cols(ggu_ref[0], wg_ref[...]) + dot_cols(ggu_ref[1], wu_ref[...])
        total_ref[...] = jnp.where(part == 0, added, total_ref[...] + added)

    @pl.when(part == pl.num_programs(0) - 1)
    def _():
        @pl.when(section == active)
        def _():
            vectors_ref[...] = jnp.zeros_like(vectors_ref)
            grad_mid_ref[pl.ds(tokens, 8)] = jnp.broadcast_to(gain_a_ref[...], (8, gain_a_ref.shape[1]))

            def finish(rows):
                grad = total_ref[rows]
                through, by_gain = norm_back(grad, mid_ref[rows], gain_ref[...])
                grad_mid_ref[rows] = grad_ref[rows].astype(F32) + through
                vectors_ref[2:3] += jnp.sum(by_gain, axis=0, keepdims=True)
                vectors_ref[3:4] += jnp.sum(grad, axis=0, keepdims=True)
            for piece in range(pieces):
                for at in range(2):
                    finish(pl.ds(piece * step + at * (step // 2), step // 2))
                if active:
                    grad_copy(piece).start()
            if active:
                for piece in range(pieces):
                    grad_copy(piece).wait_send()
                for copy in working[1:]:
                    copy.wait_send()
            working[0].wait()

        if active:
            @pl.when(section != active)
            def _():
                for piece in range(pieces):
                    grad_copy(piece).wait_recv()
                for copy in working[1:]:
                    copy.wait_recv()
                for copy in waiting:
                    copy.wait()


def whole(shape):
    return pl.BlockSpec(shape, lambda part: (0,) * len(shape))


def column(rows, wide, offset=0):
    return pl.BlockSpec((rows, wide), lambda part: (0, part + offset))


def stacked(count, rows, wide):
    return pl.BlockSpec((count, rows, wide), lambda part: (0, 0, part))


def lower(rows, wide):
    return pl.BlockSpec((rows, wide), lambda part: (part, 0))


def third(tokens, features):
    return pl.BlockSpec((1, tokens, features), lambda part: (2, 0, 0))


def meeting_call(kernel, name, parts, args, in_specs, outs, out_specs, scratch, flops, collective_id):
    return pl.pallas_call(
        kernel,
        grid=(parts,),
        in_specs=in_specs,
        out_specs=out_specs,
        out_shape=outs,
        scratch_shapes=scratch,
        name=name,
        cost_estimate=pl.CostEstimate(flops=flops, bytes_accessed=40 * 2 ** 20, transcendentals=0),
        compiler_params=pltpu.CompilerParams(
            dimension_semantics=("arbitrary",), vmem_limit_bytes=56 * 1024 * 1024, collective_id=collective_id,
            has_side_effects=collective_id is not None),
    )(*args)


def attention(active, lengths, x, gain, bias, gain_f, bias_f, w_qkv, w_out, cosine, sine, collective_id, parts=2):
    tokens, features = x.shape
    row_tokens = tokens // lengths.shape[0]
    size = features // HEADS
    wide = features // parts
    stack = jax.ShapeDtypeStruct((3, tokens, features), BF16)
    hbm = pl.BlockSpec(memory_space=pl.ANY)
    return meeting_call(
        functools.partial(attention_kernel, size, row_tokens, active), "attention", parts,
        (x, gain, bias, gain_f, bias_f, w_qkv, w_qkv, w_qkv, w_out, cosine, sine, lengths),
        [whole((tokens, features))] + [whole((1, features))] * 4 + [column(features, wide),
         column(features, wide, parts), column(features, wide, 2 * parts), lower(wide, features),
         whole(cosine.shape), whole(sine.shape), pl.BlockSpec(memory_space=pltpu.SMEM)],
        (jax.ShapeDtypeStruct((tokens, features), F32), stack, stack, jax.ShapeDtypeStruct((tokens, features), BF16)),
        (whole((tokens, features)), whole(stack.shape), stacked(3, tokens, wide), hbm),
        [pltpu.VMEM((tokens, wide), BF16), pltpu.SemaphoreType.DMA((2, 1))], 8 * tokens * features ** 2, collective_id)


def feed(mid, lefts, rows, w_gate_up, w_down, unit_rows, collective_id, parts=8):
    tokens, features = mid.shape
    wide = w_down.shape[0] // parts
    hbm = pl.BlockSpec(memory_space=pl.ANY)
    low = jax.ShapeDtypeStruct((tokens, features), BF16)
    return meeting_call(
        functools.partial(feed_kernel, unit_rows), "feed", parts,
        (mid, lefts, w_gate_up, w_gate_up, w_down, lefts, rows),
        [whole((tokens, features)), third(tokens, features), column(features, wide), column(features, wide, parts),
         lower(wide, features), hbm, hbm],
        (low, jax.ShapeDtypeStruct((tokens, w_down.shape[0] // 2), BF16), low,
         jax.ShapeDtypeStruct((2, tokens, features), BF16), low),
        (whole((tokens, features)), column(tokens, wide // 2), hbm, hbm, hbm),
        [pltpu.VMEM((tokens, features), F32), pltpu.SemaphoreType.DMA((2, 2))],
        6 * tokens * features * w_down.shape[0], collective_id)


def feed_both(active, mid, lefts, grad, gain, gain_a, w_gate_up, w_down, sends, lands, collective_id, parts=8):
    tokens, features = mid.shape
    hidden = w_down.shape[0]
    wide = hidden // parts
    hbm = pl.BlockSpec(memory_space=pl.ANY)
    return meeting_call(
        functools.partial(feed_both_kernel, active), "feed_both", parts,
        (mid, lefts, grad, gain, gain_a, w_gate_up, w_gate_up, w_down, *sends),
        [whole((tokens, features)), third(tokens, features), whole((tokens, features)), whole((1, features)),
         whole((1, features)), column(features, wide), column(features, wide, parts), lower(wide, features)]
        + [hbm] * len(sends),
        (jax.ShapeDtypeStruct((tokens, hidden), BF16), jax.ShapeDtypeStruct((2, tokens, hidden), BF16), jax.ShapeDtypeStruct((tokens + 8, features), F32),
         jax.ShapeDtypeStruct((8, features), F32), *lands),
        (column(tokens, wide), stacked(2, tokens, wide), whole((tokens + 8, features)), whole((8, features))) + (hbm,) * len(lands),
        [pltpu.VMEM((tokens, features), F32), pltpu.SemaphoreType.DMA((2, 10))],
        10 * tokens * features * hidden, collective_id)


def feed_out_kernel(parts, mid_in, hidden_in, weight_in, out, total_ref, hidden_ref, weight_ref, load_sem, store_sem):
    wide = hidden_ref.shape[1] // parts
    first = pltpu.make_async_copy(mid_in, total_ref, store_sem)
    loads = []
    for part in range(parts):
        at = pl.ds(part * wide, wide)
        loads.append((pltpu.make_async_copy(hidden_in.at[:, at], hidden_ref.at[:, at], load_sem.at[0, part]),
                      pltpu.make_async_copy(weight_in.at[at], weight_ref.at[at], load_sem.at[1, part])))

    @pl.when(lax.axis_index("section") == 1)
    def _():
        first.start()
        for copies in loads:
            for copy in copies:
                copy.start()
        first.wait()
        for part, copies in enumerate(loads):
            for copy in copies:
                copy.wait()
            at = slice(part * wide, (part + 1) * wide)
            total_ref[...] += dot(hidden_ref[:, at], weight_ref[at])
        last = pltpu.make_async_copy(total_ref, out, store_sem)
        last.start()
        last.wait()


def feed_out(mid, hidden, w_down, parts=4):
    hbm = pl.BlockSpec(memory_space=pl.ANY)
    return pl.pallas_call(
        functools.partial(feed_out_kernel, parts),
        out_shape=jax.ShapeDtypeStruct(mid.shape, F32),
        in_specs=[hbm] * 3,
        out_specs=hbm,
        scratch_shapes=[pltpu.VMEM(mid.shape, F32), pltpu.VMEM(hidden.shape, BF16), pltpu.VMEM(w_down.shape, BF16),
                        pltpu.SemaphoreType.DMA((2, parts)), pltpu.SemaphoreType.DMA],
        name="feed_out",
        cost_estimate=pl.CostEstimate(
            flops=2 * mid.shape[0] * w_down.size, bytes_accessed=16 * 2 ** 20, transcendentals=0),
        compiler_params=pltpu.CompilerParams(vmem_limit_bytes=56 * 1024 * 1024),
    )(mid, hidden, w_down)


def tables(lengths, row_tokens, size):
    index = jnp.arange(row_tokens, dtype=jnp.int32)[None]
    end, before = 0, 0
    for window in range(lengths.shape[1]):
        length = lengths[:, window:window + 1]
        end = end + length
        before = before + jnp.where(index >= end, length, 0)
    position = (index - before).astype(F32).reshape(-1, 1)
    half = jnp.arange(2 * size, dtype=jnp.int32) % (size // 2)
    frequency = 10000.0 ** (-2.0 * half.astype(F32) / size)
    angles = position * frequency
    return jnp.cos(angles), jnp.sin(angles)


def exchange_kernel(cfg, back_sizes, *refs):
    shards, bits, seats, unit_rows, width, section, aliased, late, layers, other_layers, lag, supply, order, backs, swapped = cfg
    arrays = len(seats)
    refs = list(refs)

    def take(count):
        taken = refs[:count]
        del refs[:count]
        return taken

    lefts, rights = take(arrays), take(arrays - len(supply))
    for index in supply:
        rights.insert(index, None)
    left_others, right_others = take(arrays - (1 if late else 0)), take(1)
    lefts = [ref if at is None else ref.at[at] for ref, at in zip(lefts, layers)]
    left_others = [ref if at is None else ref.at[at] for ref, at in zip(left_others, other_layers)]
    (vector,) = take(1)
    back_in = take(7)
    (lengths_ref,) = take(1)
    take(arrays + 2 if aliased else 0)
    outs, (vector_out,) = take(arrays), take(1)
    if late:
        left_others = left_others + take(1)
    for index in supply:
        rights[index] = take(1)[0]
    (back_out,) = take(1)
    back_refs, (back_load, back_store) = take(12), take(2)
    (grad_ref, x_ref, qkv_ref, wqkv_ref, wo_ref, cos_ref, sin_ref, branch_ref, proj_ref, vectors_ref, gm_ref,
     total_ref) = back_refs
    (given_send, given_recv, vector_far, vector_full, vector_land, vector_sum, vector_send, vector_recv, vector_store, left, right, left_sem, right_sem, other_sem,
     right_send, right_recv, late_send, late_recv, mine, side_land, side, side_send, side_recv, chain_a, chain_b,
     chain_send, chain_recv, rest_send, rest_land, rest_keep, rest_ssem, rest_rsem, piece, store_sem, gather_send,
     gather_recv) = refs
    units = sum(seat[0] for seat in seats)
    by_column = units - seats[-1][0]
    others = bits - 1
    final_rows = unit_rows >> others
    tokens = left.shape[1] // 2
    chains = (chain_a, chain_b)
    chain_rows = (final_rows, unit_rows)
    depth = chain_a.shape[1] - 1
    ring = mine.shape[1]
    slots, right_slots = piece.shape[1], right.shape[0]
    sec = lax.axis_index("section")
    here = lax.axis_index("shard")
    seat = lax.axis_index("group")
    group = 1 << bits
    peers = shards * group
    me = here * group + seat
    part = vector_out.shape[1]

    def bit_of(index):
        return lax.rem(lax.div(seat, 1 << order[index]), 2)

    def across(index):
        return (sec, here, seat + (1 - 2 * bit_of(index)) * (1 << order[index]))

    above = (sec, jnp.minimum(here + 1, shards - 1), seat)
    below = (sec, jnp.maximum(here - 1, 0), seat)
    half = bit_of(0)

    def remote(source, target, send, recv, device):
        return pltpu.make_async_remote_copy(
            src_ref=source, dst_ref=target, send_sem=send, recv_sem=recv,
            device_id=device, device_id_type=MESH,
        )

    def aligned(start, size):
        return pl.ds(pl.multiple_of(start, size), size)

    def peer(step):
        index = lax.rem(me + step, peers)
        return index, (sec, lax.div(index, group), lax.rem(index, group))

    def vector_copy(index, device):
        return remote(vector_full.at[:, aligned(device[1] * part, part)], vector_land.at[me], vector_send.at[index],
                      vector_recv.at[me], device)

    def vector_finish():
        vector_full[...] = vector[...] + (vectors_ref[...] if backs else vector_far[...])

        @pl.loop(1, peers)
        def _(step):
            vector_copy(*peer(step)).start()
        vector_sum[...] = vector_full[:, aligned(here * part, part)]

        @pl.loop(1, peers)
        def _(step):
            index, device = peer(step)
            vector_copy(index, device).wait_send()
            remote(vector_land.at[index], vector_land.at[index], vector_send.at[index], vector_recv.at[index],
                   device).wait_recv()
            vector_sum[...] += vector_land[index]
        copy = pltpu.make_async_copy(vector_sum, vector_out, vector_store)
        copy.start()
        copy.wait()

    def valid(chunk):
        return (chunk >= 0) & (chunk < units)

    def on(condition, run):
        pl.when(condition)(run)

    def by_rows(rows, run, tall=64):
        step = min(rows, tall)

        @pl.loop(0, rows // step)
        def _(index):
            run(aligned(index * step, step))

    def shifted(rows, offset):
        return aligned(rows.start + offset, rows.size)

    pace = min(by_column // seats[-1][0], 2)
    lead = by_column - pace * seats[-1][0]

    def seat_of(chunk):
        behind = jnp.maximum(chunk - lead, 0)
        period = lax.div(behind, pace + 1)
        step = behind - period * (pace + 1)
        last = (chunk >= lead) & (step == 0)
        return last, jnp.where(last, period, jnp.where(chunk < lead, chunk, lead + period * pace + step - 1))

    def each_array(chunk, run):
        last, index = seat_of(chunk)
        start = 0
        for which, (count, blocks, _, _) in enumerate(seats):
            begin = 0 if split_rows(which) else start

            def launch(which=which, begin=begin, blocks=blocks):
                local = index - begin
                row = lax.div(local, blocks)
                run(which, row, local - row * blocks)
            here_it_is = last if split_rows(which) else jnp.logical_not(last) & (index >= start) & (index < start + count)
            on((chunk < units) & here_it_is, launch)
            start += count

    def split_rows(which):
        return which == arrays - 1

    def right_columns(which, block, bit):
        inner = seats[which][2]
        if split_rows(which):
            return 0, aligned(block * (2 * width), 2 * width)
        outer = lax.div(block, inner)
        return outer, aligned((block - outer * inner) * (4 * width) + bit * (2 * width), 2 * width)

    def loads(chunk, run):
        slot = lax.rem(chunk, right_slots)

        def each(which, row, block):
            outer, columns = right_columns(which, block, half)
            run(pltpu.make_async_copy(
                rights[which].at[outer, :, columns], right.at[slot, :tokens], right_sem.at[slot]))
            if split_rows(which):
                run(pltpu.make_async_copy(
                    right_others[0].at[:, columns], right.at[slot, tokens:], other_sem.at[slot]))
        each_array(chunk, each)

    def load_left(chunk):
        def each(which, row, block):
            rows = seats[which][3]
            kind = int(split_rows(which))
            copies = []
            for shard in range(shards):
                if split_rows(which):
                    offsets = (shard * rows + (2 * row + half) * unit_rows, shard * (rows // 2) + row * unit_rows)
                else:
                    offsets = (shard * rows + row * unit_rows,) * 2
                for side, source in enumerate((lefts[which], left_others[which])):
                    copies.append(pltpu.make_async_copy(
                        source.at[:, aligned(offsets[side], unit_rows)],
                        left.at[kind, side * tokens:(side + 1) * tokens, shard * unit_rows:(shard + 1) * unit_rows],
                        left_sem.at[kind, side, shard]))

            def fetch():
                for copy in copies:
                    copy.start()
                for copy in copies:
                    copy.wait()
            on(block == 0, fetch)
        each_array(chunk, each)

    def right_copy(chunk, source):
        four = lax.rem(chunk, right_slots)
        return remote(source, right.at[four, tokens:], right_send.at[four], right_recv.at[four], across(0))

    def send_right(chunk):
        def each(which, row, block):
            if not split_rows(which):
                outer, columns = right_columns(which, block, 1 - half)
                right_copy(chunk, rights[which].at[outer, :, columns]).start()
        each_array(chunk, each)

    late_rows = seats[-1][3] // (2 * unit_rows)

    def late_copy(row, shard):
        source = aligned(shard * seats[-1][3] + (2 * row + 1 - half) * unit_rows, unit_rows)
        target = aligned(shard * (seats[-1][3] // 2) + row * unit_rows, unit_rows)
        return remote(lefts[-1].at[:, source], left_others[-1].at[:, target], late_send.at[row, shard],
                      late_recv.at[row, shard], across(0))

    def late_turn(turn):
        begin = 0
        for row in range(late_rows):
            need = max(lead + row * seats[-1][1] * (pace + 1) - 1, 0)
            stride = max((need - begin) // shards, 1)
            at_once = -(-shards // max(need - begin, 1))
            for index in range(at_once):
                passed = turn - begin
                shard = lax.div(jnp.maximum(passed, 0), stride) * at_once + index
                on((passed >= 0) & (passed - lax.div(jnp.maximum(passed, 0), stride) * stride == 0) & (shard < shards),
                   lambda row=row, shard=shard: late_copy(row, shard).start())

            def finish(row=row):
                @pl.loop(0, shards)
                def _(shard):
                    late_copy(row, shard).wait_send()
                    late_copy(row, shard).wait_recv()
            on(turn == need, finish)
            begin = need

    def multiply(chunk):
        four, slot = lax.rem(chunk, right_slots), lax.rem(chunk, ring)
        load_left(chunk)
        loads(chunk, lambda copy: copy.wait())
        last = seat_of(chunk)[0]

        def arrived():
            copy = right_copy(chunk, right.at[four, tokens:])
            copy.wait_recv()
            copy.wait_send()
        on(jnp.logical_not(last), arrived)
        result = lax.dot_general(left[last.astype(jnp.int32)], right[four], (((0,), (0,)), ((), ())), preferred_element_type=F32)
        for shard in range(shards):
            for path in range(2):
                mine[path, slot, shard] = result[
                    shard * unit_rows:(shard + 1) * unit_rows, path * width:(path + 1) * width].astype(BF16)

    def side_copy(step, chunk):
        slot, four = lax.rem(chunk, ring), lax.rem(chunk, slots)
        rows = unit_rows >> (step + 1)
        away = aligned((1 - bit_of(step + 1)) * rows, rows)
        source = mine.at[0, slot, :, away] if step == 0 else side.at[step - 1, slot, :, away]
        return remote(source, side_land.at[step, four, :, :rows], side_send.at[step, four], side_recv.at[step, four],
                      across(step + 1))

    def side_sum(step, chunk):
        slot, four = lax.rem(chunk, ring), lax.rem(chunk, slots)
        rows = unit_rows >> (step + 1)
        kept = bit_of(step + 1) * rows
        copy = side_copy(step, chunk)
        copy.wait_recv()
        copy.wait_send()

        @pl.loop(0, shards)
        def _(shard):
            def add(part):
                source = mine[0, slot, shard, shifted(part, kept)] if step == 0 else side[
                    step - 1, slot, shard, shifted(part, kept)]
                side[step, slot, shard, part] = (
                    source.astype(F32) + side_land[step, four, shard, part].astype(F32)).astype(BF16)
            by_rows(rows, add)
        if step + 1 < others:
            side_copy(step + 1, chunk).start()

    def base(path, slot, shard, rows):
        return (side[others - 1, slot, shard, rows] if path == 0 else mine[1, slot, shard, rows]).astype(F32)

    def hop(path, way, chunk, at):
        begin, end = (at + 1, shards) if way == 0 else (0, at)
        ref = chains[path].at[way, lax.rem(chunk, depth), begin:end]
        return remote(ref, ref, chain_send.at[path, way, lax.rem(chunk, 3)],
                      chain_recv.at[path, way, lax.rem(chunk, depth)], above if way == 0 else below)

    def at_each(run):
        for at in range(shards):
            on(here == at, lambda at=at: run(at))

    def onward(path, way, chunk):
        slot, from_base = lax.rem(chunk, depth), lax.rem(chunk, ring)

        def from_here(at):
            first, last = (at == 0, at == shards - 1) if way == 0 else (at == shards - 1, at == 0)
            if not first:
                hop(path, way, chunk, at - 1 if way == 0 else at + 1).wait_recv()
            if not last:
                begin, count = (at + 1, shards - 1 - at) if way == 0 else (0, at)

                @pl.loop(begin, begin + count)
                def _(shard):
                    def add(rows):
                        value = base(path, from_base, shard, rows)
                        if not first:
                            value = value + chains[path][way, slot, shard, rows].astype(F32)
                        chains[path][way, slot, shard, rows] = value.astype(BF16)
                    by_rows(chain_rows[path], add)
                hop(path, way, chunk, at).start()
        at_each(from_here)

    def sent(path, way, chunk):
        def from_here(at):
            if at != (shards - 1 if way == 0 else 0):
                hop(path, way, chunk, at).wait_send()
        at_each(from_here)

    def last_hop(path, chunk):
        from_base, slot = lax.rem(chunk, ring), lax.rem(chunk, depth)
        from_below = jnp.where(here > 0, slot, depth)
        from_above = jnp.where(here < shards - 1, slot, depth)

        def total(rows, offset):
            rows = shifted(rows, offset)
            return (
                base(path, from_base, here, rows)
                + chains[path][0, from_below, here, rows].astype(F32)
                + chains[path][1, from_above, here, rows].astype(F32)
            )
        if path == 0:
            finish(path, chunk, total)
        else:
            share(0, chunk, total)

    def rest_copy(step, chunk):
        slot, rows = lax.rem(chunk, slots), pl.ds(0, unit_rows >> (step + 1))
        return remote(rest_send.at[step, slot, rows], rest_land.at[step, slot, rows], rest_ssem.at[step, slot],
                      rest_rsem.at[step, slot], across(step + 1))

    def share(step, chunk, total):
        slot, rows = lax.rem(chunk, slots), unit_rows >> (step + 1)
        bit = bit_of(step + 1)

        def give(part):
            rest_send[step, slot, part] = total(part, (1 - bit) * rows).astype(BF16)
        by_rows(rows, give)
        rest_copy(step, chunk).start()

        def keep(part):
            rest_keep[step, slot, part] = total(part, bit * rows)
        by_rows(rows, keep)

    def rest_sum(step, chunk):
        slot = lax.rem(chunk, slots)
        copy = rest_copy(step, chunk)
        copy.wait_recv()
        copy.wait_send()

        def total(part, offset):
            part = shifted(part, offset)
            return rest_keep[step, slot, part] + rest_land[step, slot, part].astype(F32)
        if step + 1 < others:
            share(step + 1, chunk, total)
        else:
            finish(1, chunk, total)

    def finish(path, chunk, total):
        def put(part):
            piece[path, lax.rem(chunk, slots), part] = total(part, 0).astype(BF16)
        by_rows(final_rows, put)
        spread(path, 0, chunk)

    def place(which, row, block, path, bit, offset, rows):
        if split_rows(which):
            row0, column = (2 * row + bit) * unit_rows, block * (2 * width) + path * width
        else:
            row0, column = row * unit_rows, block * (4 * width) + bit * (2 * width) + path * width
        return outs[which].at[aligned(row0 + offset, rows), aligned(column, width)]

    def seat_row(steps):
        row = 0
        for step in range(steps):
            row = row + bit_of(step + 1) * (unit_rows >> (step + 1))
        return row

    def store(path, chunk, target):
        slot = lax.rem(chunk, slots)
        return pltpu.make_async_copy(piece.at[path, slot], target, store_sem.at[path, slot])

    def gather(path, step, other, chunk, target):
        slot = lax.rem(chunk, slots)
        source = piece.at[path, slot] if step == 0 else target
        if swapped[path]:
            index = bits - 1 - step
        else:
            index = 0 if step == 0 else bits - step
        return remote(source, target, gather_send.at[path, step, other, slot], gather_recv.at[path, step, other, slot],
                      across(index))

    def gather_size(path, step):
        if swapped[path]:
            return others - step, 1
        return others - max(step - 1, 0), 1 if step == 0 else 2

    def spread(path, step, chunk):
        steps, copies = gather_size(path, step)
        rows = unit_rows >> steps

        def each(which, row, block):
            for other in range(copies):
                bit = half if other == 0 else 1 - half
                target = place(which, row, block, path, bit, seat_row(steps), rows)
                if step == 0:
                    store(path, chunk, target).start()
                gather(path, step, other, chunk, target).start()
        each_array(chunk, each)

    def gathered(path, step, chunk):
        steps, copies = gather_size(path, step)
        target = outs[0].at[pl.ds(0, unit_rows >> steps), pl.ds(0, width)]
        for other in range(copies):
            copy = gather(path, step, other, chunk, target)
            copy.wait_recv()
            copy.wait_send()
        if step == 0:
            store(path, chunk, target).wait()
        if step + 1 < bits:
            spread(path, step + 1, chunk)

    size, row_tokens, parts = back_sizes
    features = x_ref.shape[1]
    block, pair, scale = features // parts, 2 * size, size ** -0.5
    groups = block // pair // 2
    part_steps = 2 + tokens // row_tokens * groups
    back_steps = 2 + parts * part_steps

    def back_loads():
        return [pltpu.make_async_copy(source, target, back_load.at[index])
                for index, (source, target) in enumerate(zip(back_in, back_refs))]

    def back_start():
        copies = back_loads()
        for index in (0, 4, 2, 5, 6, 3, 1):
            copies[index].start()

    def back_lanes(part):
        return aligned(part * block, block)

    def deliver(index, source, target):
        if backs:
            return pltpu.make_async_copy(source, target, back_store.at[index])
        return remote(source, target, given_send.at[index], given_recv.at[index], (section, here, seat))

    def deliver_branch():
        return deliver(0, branch_ref, rights[supply[0]].at[0])

    def deliver_part(part):
        lanes = back_lanes(part)
        return deliver(1 + part, proj_ref.at[:, :, lanes], rights[supply[1]].at[:, :, lanes])

    def deliver_vectors():
        return deliver(1 + parts, vectors_ref, vector_far)

    def back_store_last():
        return pltpu.make_async_copy(total_ref if backs else branch_ref, back_out, back_store.at[1 + parts])

    def back_begin():
        back_loads()[0].wait()

        def put(rows):
            branch_ref[rows] = grad_ref[rows].astype(BF16)
        by_rows(tokens, put)
        deliver_branch().start()

    def back_open(part):
        @pl.when(part == 0)
        def _():
            for index in (4, 2, 5, 6):
                back_loads()[index].wait()
        gm_ref[...] = dot_cols(branch_ref[...], wo_ref[back_lanes(part)]).astype(BF16)

    def back_heads(part, row, group):
        rows = aligned(row * row_tokens, row_tokens)
        first = lanes_of((row_tokens, pair)) < size
        allowed = same_window(lengths_ref, row, row_tokens)
        cosine, sine = cos_ref[rows], sin_ref[rows]
        lanes = [aligned(part * block + (2 * group + at) * pair, pair) for at in range(2)]
        work = []
        for at in range(2):
            query, key, value = (qkv_ref[which, rows, lanes[at]] for which in range(3))
            grad_mix = gm_ref[rows, aligned((2 * group + at) * pair, pair)]
            scaled = query * scale
            for head in range(2):
                own = first if head == 0 else jnp.logical_not(first)
                work.append((
                    query, key, grad_mix,
                    dot_cols(jnp.where(own, scaled, jnp.zeros_like(scaled)), key),
                    dot_cols(jnp.where(own, grad_mix, jnp.zeros_like(grad_mix)), value)))
        results = []
        for query, key, grad_mix, scores, grad_probs in work:
            probs = softmax(scores, allowed)
            weighted = probs * grad_probs
            grad_scores = (weighted - probs * jnp.sum(weighted, axis=-1, keepdims=True)).astype(BF16)
            results.append((query, key, grad_mix, grad_scores, probs.astype(BF16)))
        results = [
            (dot(grad_scores, key), dot_rows(grad_scores, query), dot_rows(probs, grad_mix))
            for query, key, grad_mix, grad_scores, probs in results]
        for at in range(2):
            grad_query, grad_key, grad_value = (
                jnp.where(first, a, b) for a, b in zip(results[2 * at], results[2 * at + 1]))
            proj_ref[0, rows, lanes[at]] = unrotated(grad_query * scale, cosine, sine, size).astype(BF16)
            proj_ref[1, rows, lanes[at]] = unrotated(grad_key * scale, cosine, sine, size).astype(BF16)
            proj_ref[2, rows, lanes[at]] = grad_value.astype(BF16)

    def back_close(part):
        deliver_part(part).start()

        @pl.when(part == 0)
        def _():
            back_loads()[3].wait()
        added = 0.0
        for which in range(3):
            added = added + dot_cols(
                proj_ref[which, :, back_lanes(part)], wqkv_ref[:, aligned(which * features + part * block, block)])
        total_ref[...] = jnp.where(part == 0, added, total_ref[...] + added)

    def back_end():
        back_loads()[1].wait()
        vectors_ref[...] = jnp.zeros_like(vectors_ref)
        if not backs:
            deliver_branch().wait_send()

        def end(rows):
            grad = total_ref[rows]
            through, by_gain = norm_back(grad, x_ref[rows].astype(F32), grad_ref[tokens:tokens + 1])
            result = grad_ref[rows] + through
            if backs:
                total_ref[rows] = result
            else:
                branch_ref[rows] = result.astype(BF16)
            vectors_ref[0:1] += jnp.sum(by_gain, axis=0, keepdims=True)
            vectors_ref[1:2] += jnp.sum(grad, axis=0, keepdims=True)
        by_rows(tokens, end)
        back_store_last().start()
        if backs:
            deliver_branch().wait()
        else:
            deliver_vectors().start()
            deliver_vectors().wait_send()
        for part in range(parts):
            if backs:
                deliver_part(part).wait()
            else:
                deliver_part(part).wait_send()
        back_store_last().wait()

    def back_step(step):
        on(step == 0, back_begin)
        inner = jnp.maximum(step - 1, 0)
        part = lax.div(inner, part_steps)
        at = inner - part * part_steps
        within = (step > 0) & (step < back_steps - 1)
        on(within & (at == 0), lambda: back_open(part))
        head = at - 1
        row = lax.div(jnp.maximum(head, 0), groups)
        on(within & (at > 0) & (at < part_steps - 1), lambda: back_heads(part, row, head - row * groups))
        on(within & (at == part_steps - 1), lambda: back_close(part))
        on(step == back_steps - 1, back_end)

    def hand_over():
        back_start()
        pl.semaphore_wait(pltpu.get_barrier_semaphore(), 1)

        @pl.loop(0, back_steps)
        def _(step):
            back_step(step)

    def take_over():
        deliver_branch().wait_recv()
        for part in range(parts):
            deliver_part(part).wait_recv()
        deliver_vectors().wait_recv()

    def unit_of(index):
        return index if index < lead else lead + (index - lead) // pace * (pace + 1) + 1 + (index - lead) % pace

    def work():
        barrier = pltpu.get_barrier_semaphore()
        if not backs:
            pl.semaphore_signal(barrier, inc=1, device_id=(1 - section, here, seat), device_id_type=MESH)

        @pl.loop(1, peers)
        def _(step):
            pl.semaphore_signal(barrier, inc=1, device_id=peer(step)[1], device_id_type=MESH)
        loads(0, lambda copy: copy.start())
        if backs:
            back_start()

        for path in range(2):
            for way in range(2):
                @pl.loop(0, shards)
                def _(shard):
                    def clear(rows):
                        chains[path][way, depth, shard, rows] = jnp.zeros((rows.size, width), BF16)
                    by_rows(chain_rows[path], clear)
        pl.semaphore_wait(barrier, peers - 1)
        for chunk in range(lag):
            send_right(chunk)

        line = shards - 1

        @pl.loop(0, units + lag * (line + others + bits) + 2)
        def _(turn):
            if backs:
                back_step(turn - 1)
            else:
                on(turn == unit_of(sum(seat[0] for seat in seats[:supply[0]])) - lag, take_over)
            on(turn + lag < units, lambda: send_right(turn + lag))
            if late:
                late_turn(turn)
            on(turn + 1 < units, lambda: loads(turn + 1, lambda copy: copy.start()))

            def opening():
                multiply(turn)
                side_copy(0, turn).start()
            on(turn < units, opening)
            for step in range(others):
                chunk = turn - lag * (1 + step)
                on(valid(chunk), lambda step=step, chunk=chunk: side_sum(step, chunk))
            for path in range(2):
                for way in range(2):
                    chunk = turn - lag * ((others if path == 0 else 0) + (here if way == 0 else line - here))
                    on(valid(chunk - 2), lambda path=path, way=way, chunk=chunk: sent(path, way, chunk - 2))
                    on(valid(chunk), lambda path=path, way=way, chunk=chunk: onward(path, way, chunk))
            on(valid(turn - lag * line), lambda: last_hop(1, turn - lag * line))
            on(valid(turn - lag * (line + others)), lambda: last_hop(0, turn - lag * (line + others)))
            for step in range(others):
                chunk = turn - lag * (line + 1 + step)
                on(valid(chunk), lambda step=step, chunk=chunk: rest_sum(step, chunk))
            for step in range(bits):
                for path in range(2):
                    chunk = turn - lag * (line + others + 1 + step)
                    on(valid(chunk), lambda path=path, step=step, chunk=chunk: gathered(path, step, chunk))

        vector_finish()

    if section is None:
        work()
    else:
        pl.when(sec == section)(work)
        if not backs:
            pl.when(sec != section)(hand_over)


def exchange(pairs, vector, shards, group, section, collective_id, unit_width, previous=None, lag=None, first_bit=0, supply=(1, 2), back=(), backs=False, swapped=(False, False), parts=2, unit_rows_max=256,
             name="exchange"):
    bits = group.bit_length() - 1
    arrays = len(pairs)
    order = (first_bit,) + tuple(bit for bit in range(bits) if bit != first_bit)
    lefts, rights = [pair[0][0] for pair in pairs], [pair[1] for pair in pairs]
    layers = tuple(pair[0][1] for pair in pairs)
    left_others = [pair[2] and pair[2][0] for pair in pairs]
    other_layers = tuple(pair[2] and pair[2][1] for pair in pairs)
    late = pairs[-1][2] is None
    if late:
        left_others = left_others[:-1]
    tokens = lefts[0].shape[-2]
    rows_of = [left.shape[-1] // shards for left in lefts]
    unit_rows = min([unit_rows_max] + rows_of[:-1])
    width = unit_width // 4
    seats = []
    for index, (rows, right) in enumerate(zip(rows_of, rights)):
        tall, wide = (2 * unit_rows, 2 * width) if index == arrays - 1 else (unit_rows, 4 * width)
        inner = right.shape[2] // wide
        seats.append((rows // tall * right.shape[0] * inner, right.shape[0] * inner, inner, rows))
    units = sum(seat[0] for seat in seats)
    others = bits - 1
    final_rows = unit_rows >> others
    lag = lag or (2 if shards <= 4 else 1)
    slots, right_slots = 2 * lag + 2, 2 * lag + 3
    depth, ring = lag * shards + 3, lag * (shards - 1) + 2
    late_rows = rows_of[-1] // (2 * unit_rows)
    peers, lanes = shards * group, vector.shape[1] // shards
    dma = pltpu.SemaphoreType.DMA
    *back, lengths = back
    x = back[1]
    previous = list(previous or [])
    scratch = [
        *(pltpu.VMEM(item.shape, item.dtype) for item in back),
        pltpu.VMEM(x.shape, BF16), pltpu.VMEM((3,) + x.shape, BF16), pltpu.VMEM(vector.shape, F32),
        pltpu.VMEM((tokens, x.shape[1] // parts), BF16), pltpu.VMEM(x.shape, F32),
        dma((len(back),)), dma((2 + parts,)),
        dma((2 + parts,)), dma((2 + parts,)),
        pltpu.VMEM(vector.shape, F32), pltpu.VMEM(vector.shape, F32),
        pltpu.VMEM((peers, vector.shape[0], lanes), F32),
        pltpu.VMEM((vector.shape[0], lanes), F32),
        dma((peers,)), dma((peers,)), dma,
        pltpu.VMEM((2, 2 * tokens, shards * unit_rows), BF16),
        pltpu.VMEM((right_slots, 2 * tokens, 2 * width), BF16),
        dma((2, 2, shards)), dma((right_slots,)), dma((right_slots,)),
        dma((right_slots,)), dma((right_slots,)),
        dma((late_rows, shards)), dma((late_rows, shards)),
        pltpu.VMEM((2, ring, shards, unit_rows, width), BF16),
        pltpu.VMEM((others, slots, shards, unit_rows // 2, width), BF16),
        pltpu.VMEM((others, ring, shards, unit_rows // 2, width), BF16),
        dma((others, slots)), dma((others, slots)),
        pltpu.VMEM((2, depth + 1, shards, final_rows, width), BF16),
        pltpu.VMEM((2, depth + 1, shards, unit_rows, width), BF16),
        dma((2, 2, 3)), dma((2, 2, depth)),
        pltpu.VMEM((others, slots, unit_rows // 2, width), BF16),
        pltpu.VMEM((others, slots, unit_rows // 2, width), BF16),
        pltpu.VMEM((others, slots, unit_rows // 2, width), F32),
        dma((others, slots)), dma((others, slots)),
        pltpu.VMEM((2, slots, final_rows, width), BF16),
        dma((2, slots)),
        dma((2, bits, 2, slots)), dma((2, bits, 2, slots)),
    ]
    cfg = (shards, bits, tuple(seats), unit_rows, width, section, len(previous) > 0, late, layers, other_layers, lag, supply, order, backs, swapped)
    operands = lefts + [r for n, r in enumerate(rights) if n not in supply] + left_others + [
        pairs[-1][3], vector] + back + [lengths] + previous
    first = len(operands) - len(previous)
    results = [jax.ShapeDtypeStruct((r, g.shape[0] * g.shape[2]), BF16) for r, g in zip(rows_of, rights)]
    results.append(jax.ShapeDtypeStruct((vector.shape[0], lanes), F32))
    if late:
        results.append(jax.ShapeDtypeStruct((tokens, lefts[-1].shape[-1] // 2), BF16))
    results.extend(jax.ShapeDtypeStruct(rights[index].shape, BF16) for index in supply)
    results.append(jax.ShapeDtypeStruct(x.shape, F32 if backs else BF16))
    aliases = {first + index: index for index in range(len(previous))}
    if previous:
        aliases[len(operands) - 1] = len(results) - 1
    hbm, vmem = pl.BlockSpec(memory_space=pl.ANY), pl.BlockSpec(memory_space=pltpu.VMEM)
    in_specs = [hbm] * len(operands)
    in_specs[first - 1] = pl.BlockSpec(memory_space=pltpu.SMEM)
    in_specs[first - 2 - len(back)] = vmem
    return pl.pallas_call(
        functools.partial(exchange_kernel, cfg, (x.shape[1] // HEADS, tokens // lengths.shape[0], parts)),
        out_shape=results,
        in_specs=in_specs,
        out_specs=[hbm] * len(results),
        scratch_shapes=scratch,
        input_output_aliases=aliases,
        name=name,
        cost_estimate=pl.CostEstimate(
            flops=4 * tokens * units * shards * unit_rows * 2 * width, bytes_accessed=100 * 2 ** 20,
            transcendentals=0),
        compiler_params=pltpu.CompilerParams(
            collective_id=collective_id, has_side_effects=True, vmem_limit_bytes=56 * 1024 * 1024),
    )(*operands)


UNIT_WIDTH = 512


def body(
    ends_in,
    lengths,
    norm_gain_a,
    norm_bias_a,
    w_qkv,
    w_out,
    norm_gain_f,
    norm_bias_f,
    w_gate_up,
    w_down,
):
    shards, group = lax.axis_size("shard"), lax.axis_size("group")
    tokens, features = ends_in.shape[1:]
    size = features // HEADS
    rows = ends_in[0]
    weight_qkv, weight_out, weight_gu, weight_down = w_qkv[0], w_out[0], w_gate_up[0], w_down[0]
    cosine, sine = tables(lengths, tokens // lengths.shape[0], size)
    unit_rows = min(256, features // shards)
    low = jax.ShapeDtypeStruct((tokens, features), BF16)
    stack = jax.ShapeDtypeStruct((3, tokens, features), BF16)

    def like(array):
        return jax.ShapeDtypeStruct(array.shape, array.dtype)

    def attend(active, values, collective_id):
        return attention(active, lengths, values, norm_gain_a, norm_bias_a, norm_gain_f, norm_bias_f, weight_qkv,
                         weight_out, cosine, sine, collective_id)

    def feed_back(active, middle, lefts, grad, sends, lands, collective_id):
        return feed_both(active, middle, lefts, grad, norm_gain_f, norm_gain_a, weight_gu, weight_down, sends, lands,
                         collective_id)

    def sum_all(which, lefts, lefts_beside, hidden, hidden_beside, grad_gu, grad, grad_beside, vectors, back, **more):
        rights = (grad_gu, jax.ShapeDtypeStruct((1, tokens, features), BF16), stack)
        pairs = [((lefts, at), right, other) for at, right, other in zip((2, 1, 0), rights, lefts_beside)]
        pairs.append(((hidden, None), grad[None], hidden_beside, grad_beside))
        return exchange(pairs, vectors, shards, group, which, which + 1, UNIT_WIDTH * features // 1024,
                        first_bit=1 - which, back=back + (cosine, sine, lengths), **more)

    middle_0, lefts_0, qkv_0, _ = attend(0, rows, None)
    passed, hidden_half_0, arrived, early_beside, rows_beside = feed(
        middle_0, lefts_0, rows, weight_gu, weight_down, unit_rows, 3)
    middle_1, lefts_1, qkv_1, low_beside = attend(1, arrived, 6)
    hidden_1, grad_gu_1, _, vectors_1, lefts_beside, qkv_there, qkv_weight, out_weight, hidden_beside, \
        grad_middle = feed_back(
            1, middle_1, lefts_1, rows,
            (lefts_1, qkv_1, weight_qkv, weight_out, lefts_0, hidden_half_0),
            (stack, stack, like(weight_qkv), like(weight_out), like(hidden_half_0), jax.ShapeDtypeStruct((tokens + 8, features), F32)), 4)
    sums = sum_all(1, lefts_1, [(lefts_beside, 2), (lefts_beside, 1), (low_beside, None)], hidden_1, None, grad_gu_1, rows, rows_beside,
                   vectors_1, (grad_middle, passed, qkv_there, qkv_weight, out_weight), name="exchange_second")
    returned = sums[-1]
    hidden_later, _ = lax.optimization_barrier((hidden_1, sums[4]))
    result = feed_out(middle_1, hidden_later, weight_down)
    hidden_0, grad_gu_0, grad_middle, vectors_0, returned_beside = feed_back(
        0, middle_0, lefts_0, returned, (returned,), (low,), 5)
    sums = sum_all(0, lefts_0, [(lefts_beside, 2), (early_beside, 1), (early_beside, 0)], hidden_0,
                   (hidden_beside, None), grad_gu_0, returned, returned_beside, vectors_0,
                   (grad_middle, rows, qkv_0, weight_qkv, weight_out), backs=True, previous=[*sums[:5], result], swapped=(False, True),
                   name="exchange_first")
    ends_out = sums[-1][None]
    grad_gate_up, grad_out, grad_qkv, grad_down = (item.astype(F32)[None] for item in sums[:4])
    gain_a, bias_a, gain_f, bias_f = (sums[4][row:row + 1] for row in range(4))
    return (ends_out, gain_a, bias_a, grad_qkv, grad_out, gain_f, bias_f, grad_gate_up, grad_down)


def solution(mesh):
    placed = (
        P("section", ("shard", "group"), None),
        P(("shard", "group"), None),
        P("section", None),
        P("section", None),
        P("section", None, None),
        P("section", None, None),
        P("section", None),
        P("section", None),
        P("section", None, None),
        P("section", None, None),
    )
    return jax.shard_map(
        body,
        mesh=mesh,
        in_specs=placed,
        out_specs=(
            P("section", ("shard", "group"), None),
            P("section", "shard"),
            P("section", "shard"),
            P("section", "shard", None),
            P("section", "shard", None),
            P("section", "shard"),
            P("section", "shard"),
            P("section", "shard", None),
            P("section", "shard", None),
        ),
        check_vma=False,
    )
```

```python
import functools

import jax
import jax.numpy as jnp
from jax import lax
from jax.experimental import pallas as pl
from jax.experimental.pallas import tpu as pltpu
from jax.sharding import PartitionSpec as P

MESH = pl.DeviceIdType.MESH
F32, BF16 = jnp.float32, jnp.bfloat16
HEADS = 16
EPSILON = 1e-05


def dot(a, b):
    return jnp.dot(a, b, preferred_element_type=F32)


def dot_cols(a, b):
    return lax.dot_general(a, b, (((1,), (1,)), ((), ())), preferred_element_type=F32)


def dot_rows(a, b):
    return lax.dot_general(a, b, (((0,), (0,)), ((), ())), preferred_element_type=F32)


def in_rows(total, step, run):
    @pl.loop(0, total // step)
    def _(index):
        run(pl.ds(pl.multiple_of(index * step, step), step))


def normalized(values):
    average = jnp.mean(values, axis=-1, keepdims=True)
    centered = values - average
    variance = jnp.mean(centered * centered, axis=-1, keepdims=True)
    spread = lax.rsqrt(variance + EPSILON)
    return centered * spread, spread


def norm_back(grad, values, gain):
    unit, spread = normalized(values)
    scaled = grad * gain
    return spread * (
        scaled
        - jnp.mean(scaled, axis=-1, keepdims=True)
        - unit * jnp.mean(scaled * unit, axis=-1, keepdims=True)
    ), grad * unit


def lanes_of(shape):
    return lax.broadcasted_iota(jnp.int32, shape, len(shape) - 1)


def turn(values, half, size):
    wide = values.shape[-1]
    early = lax.rem(lanes_of(values.shape), size) < half
    return jnp.where(early, pltpu.roll(values, wide - half, 1), pltpu.roll(values, half, 1)), early


def rotated(values, cosine, sine, size):
    other, early = turn(values, size // 2, size)
    return values * cosine + jnp.where(early, -other, other) * sine


def unrotated(values, cosine, sine, size):
    other, early = turn(values * sine, size // 2, size)
    return values * cosine + jnp.where(early, other, -other)


def window_of(index, lengths_ref, row):
    windows = lengths_ref.shape[1]
    end = lengths_ref[row, 0]
    segment = (index >= end).astype(jnp.int32)
    for window in range(1, windows):
        end = end + lengths_ref[row, window]
        segment = segment + (index >= end).astype(jnp.int32)
    return segment


def same_window(lengths_ref, row, tokens):
    queries = window_of(lax.broadcasted_iota(jnp.int32, (tokens, 1), 0), lengths_ref, row)
    keys = window_of(lax.broadcasted_iota(jnp.int32, (1, tokens), 1), lengths_ref, row)
    return queries == keys


def softmax(scores, allowed):
    scores = jnp.where(allowed, scores, -1e30)
    weights = jnp.exp(scores - jnp.max(scores, axis=-1, keepdims=True))
    return weights * (1.0 / jnp.sum(weights, axis=-1, keepdims=True))


def attention_kernel(size, row_tokens, active, x_ref, gain_ref, bias_ref, gain_f_ref, bias_f_ref, wq_ref, wk_ref,
                     wv_ref, wo_ref, cos_ref, sin_ref, lengths_ref, mid_ref, lefts_ref, qkv_ref, low_land, mix_ref, sems):
    tokens = x_ref.shape[0]
    part = pl.program_id(0)
    block = wq_ref.shape[1]
    pair = 2 * size

    section, _, beside, _ = places()
    low_copy = remote(lefts_ref.at[0], low_land, sems, 0, beside)

    @pl.when(section == active)
    def _():
        @pl.when(part == 0)
        def _():
            if active:
                greet(beside)

            def begin(rows):
                values = x_ref[rows].astype(F32)
                unit, _ = normalized(values)
                lefts_ref[0, rows] = (unit * gain_ref[...] + bias_ref[...]).astype(BF16)
                mid_ref[rows] = values
            in_rows(tokens, 64, begin)
            if active:
                await_greetings(1)
                low_copy.start()

        for which, weight in enumerate((wq_ref, wk_ref, wv_ref)):
            projected = dot(lefts_ref[0], weight[...])
            for at in range(block // pair):
                lanes = slice(at * pair, (at + 1) * pair)
                values = projected[:, lanes]
                if which < 2:
                    values = rotated(values, cos_ref[...], sin_ref[...], size)
                qkv_ref[which, :, lanes] = values.astype(BF16)

        first = lanes_of((row_tokens, pair)) < size
        @pl.loop(0, tokens // row_tokens)
        def _(row):
            rows = pl.ds(pl.multiple_of(row * row_tokens, row_tokens), row_tokens)
            allowed = same_window(lengths_ref, row, row_tokens)
            for start in range(0, block // pair, 2):
                work = []
                for at in range(start, start + 2):
                    lanes = pl.ds(at * pair, pair)
                    query, key, value = (qkv_ref[which, rows, lanes] for which in range(3))
                    query = query * (size ** -0.5)
                    for head in range(2):
                        own = jnp.where(first if head == 0 else jnp.logical_not(first), query, jnp.zeros_like(query))
                        work.append((dot_cols(own, key), value))
                work = [(softmax(scores, allowed).astype(BF16), value) for scores, value in work]
                work = [dot(probs, value) for probs, value in work]
                for at in range(2):
                    lanes = pl.ds((start + at) * pair, pair)
                    mix_ref[rows, lanes] = jnp.where(first, work[2 * at], work[2 * at + 1]).astype(BF16)

        mixture = mix_ref[...]
        lefts_ref[1, :, pl.ds(pl.multiple_of(part * block, block), block)] = mixture
        mid_ref[...] += dot(mixture, wo_ref[...])

        @pl.when(part == pl.num_programs(0) - 1)
        def _():
            def close(rows):
                unit, _ = normalized(mid_ref[rows])
                lefts_ref[2, rows] = (unit * gain_f_ref[...] + bias_f_ref[...]).astype(BF16)
            in_rows(tokens, 64, close)
            if active:
                low_copy.wait()


def places():
    section, shard, seat = (lax.axis_index(name) for name in ("section", "shard", "group"))
    stride = 2 - section
    bit = lax.rem(lax.div(seat, stride), 2)
    return section, bit, (section, shard, seat + (1 - 2 * bit) * stride), (1 - section, shard, seat)


def remote(source, target, sems, index, device):
    return pltpu.make_async_remote_copy(
        src_ref=source, dst_ref=target, send_sem=sems.at[0, index], recv_sem=sems.at[1, index], device_id=device,
        device_id_type=pl.DeviceIdType.MESH)


def greet(*devices):
    for device in devices:
        pl.semaphore_signal(
            pltpu.get_barrier_semaphore(), inc=1, device_id=device, device_id_type=pl.DeviceIdType.MESH)


def await_greetings(count):
    pl.semaphore_wait(pltpu.get_barrier_semaphore(), count)


def feed_kernel(unit_rows, mid_ref, low_ref, wg_ref, wu_ref, wd_ref, lefts_ref, rows_ref, out_ref, half_ref,
                arrived_ref, lefts_land, rows_land, total_ref, sems):
    part = pl.program_id(0)
    section, bit, beside, above = places()
    lefts_copy = remote(lefts_ref.at[0:2], lefts_land, sems, 0, beside)
    rows_copy = remote(rows_ref, rows_land, sems, 0, beside)
    out_copy = remote(out_ref, arrived_ref, sems, 1, above)

    pl.when(part == 0)(lambda: greet(beside, above))

    @pl.when(part == 1)
    def _():
        await_greetings(2)
        pl.when(section == 0)(lefts_copy.start)
        pl.when(section == 1)(rows_copy.start)

    @pl.when(section == 0)
    def _():
        @pl.when(part == 0)
        def _():
            total_ref[...] = mid_ref[...]

        low = low_ref[0]
        gate = dot(low, wg_ref[...])
        up = dot(low, wu_ref[...])
        hidden = (gate / (1.0 + jnp.exp(-gate)) * up).astype(BF16)
        for at in range(half_ref.shape[1] // unit_rows):
            rows = [hidden[:, (2 * at + side) * unit_rows:(2 * at + side + 1) * unit_rows] for side in range(2)]
            half_ref[:, at * unit_rows:(at + 1) * unit_rows] = jnp.where(bit == 0, rows[1], rows[0])
        total_ref[...] += dot(hidden, wd_ref[...])

    @pl.when(part == pl.num_programs(0) - 1)
    def _():
        @pl.when(section == 0)
        def _():
            out_ref[...] = total_ref[...].astype(BF16)
            out_copy.start()
            out_copy.wait_send()
            lefts_copy.wait()

        @pl.when(section == 1)
        def _():
            out_copy.wait_recv()
            rows_copy.wait()


def feed_both_kernel(active, mid_ref, low_ref, grad_ref, gain_ref, gain_a_ref, wg_ref, wu_ref, wd_ref, *refs):
    sends, refs = refs[:6 if active else 1], refs[6 if active else 1:]
    hidden_ref, ggu_ref, grad_mid_ref, vectors_ref = refs[:4]
    lands = refs[4:4 + (6 if active else 1)]
    total_ref, sems = refs[-2:]
    tokens = mid_ref.shape[0]
    part = pl.program_id(0)
    section, _, beside, other = places()
    pieces = 4
    step = tokens // pieces
    if active:
        lefts_ref, qkv_ref, wqkv_ref, wo_ref, lefts_first, hidden_first = sends
        lefts_land, qkv_land, wqkv_land, wo_land, hidden_land, grad_land = lands
        working = [
            remote(lefts_ref.at[1:3], lefts_land.at[1:3], sems, 0, beside), remote(qkv_ref, qkv_land, sems, 1, other),
            remote(wqkv_ref, wqkv_land, sems, 2, other), remote(wo_ref, wo_land, sems, 3, other)]
        waiting = [
            remote(lefts_first.at[2], lefts_land.at[2], sems, 4, beside),
            remote(hidden_first, hidden_land, sems, 5, beside)]

        def grad_copy(piece):
            rows = pl.ds(piece * step, step + (8 if piece == pieces - 1 else 0))
            return remote(grad_mid_ref.at[rows], grad_land.at[rows], sems, 6 + piece, other)
    else:
        working = [remote(sends[0], lands[0], sems, 0, beside)]

    @pl.when(part == 0)
    def _():
        if active:
            greet(beside, other)
        else:
            pl.when(section == active)(lambda: greet(beside))

    @pl.when(part == 1)
    def _():
        if active:
            await_greetings(2)

            @pl.when(section != active)
            def _():
                for copy in waiting:
                    copy.start()

        @pl.when(section == active)
        def _():
            if not active:
                await_greetings(1)
            for copy in working:
                copy.start()

    @pl.when(section == active)
    def _():
        low = low_ref[0]
        gate = dot(low, wg_ref[...])
        up = dot(low, wu_ref[...])
        grad_hidden = dot_cols(grad_ref[...], wd_ref[...])
        sig = 1.0 / (1.0 + jnp.exp(-gate))
        silu = gate * sig
        hidden_ref[...] = (silu * up).astype(BF16)
        ggu_ref[0] = (grad_hidden * up * (sig * (1.0 + gate * (1.0 - sig)))).astype(BF16)
        ggu_ref[1] = (grad_hidden * silu).astype(BF16)
        added = dot_cols(ggu_ref[0], wg_ref[...]) + dot_cols(ggu_ref[1], wu_ref[...])
        total_ref[...] = jnp.where(part == 0, added, total_ref[...] + added)

    @pl.when(part == pl.num_programs(0) - 1)
    def _():
        @pl.when(section == active)
        def _():
            vectors_ref[...] = jnp.zeros_like(vectors_ref)
            grad_mid_ref[pl.ds(tokens, 8)] = jnp.broadcast_to(gain_a_ref[...], (8, gain_a_ref.shape[1]))

            def finish(rows):
                grad = total_ref[rows]
                through, by_gain = norm_back(grad, mid_ref[rows], gain_ref[...])
                grad_mid_ref[rows] = grad_ref[rows].astype(F32) + through
                vectors_ref[2:3] += jnp.sum(by_gain, axis=0, keepdims=True)
                vectors_ref[3:4] += jnp.sum(grad, axis=0, keepdims=True)
            for piece in range(pieces):
                for at in range(2):
                    finish(pl.ds(piece * step + at * (step // 2), step // 2))
                if active:
                    grad_copy(piece).start()
            if active:
                for piece in range(pieces):
                    grad_copy(piece).wait_send()
                for copy in working[1:]:
                    copy.wait_send()
            working[0].wait()

        if active:
            @pl.when(section != active)
            def _():
                for piece in range(pieces):
                    grad_copy(piece).wait_recv()
                for copy in working[1:]:
                    copy.wait_recv()
                for copy in waiting:
                    copy.wait()


def whole(shape):
    return pl.BlockSpec(shape, lambda part: (0,) * len(shape))


def column(rows, wide, offset=0):
    return pl.BlockSpec((rows, wide), lambda part: (0, part + offset))


def stacked(count, rows, wide):
    return pl.BlockSpec((count, rows, wide), lambda part: (0, 0, part))


def lower(rows, wide):
    return pl.BlockSpec((rows, wide), lambda part: (part, 0))


def third(tokens, features):
    return pl.BlockSpec((1, tokens, features), lambda part: (2, 0, 0))


def meeting_call(kernel, name, parts, args, in_specs, outs, out_specs, scratch, flops, collective_id):
    return pl.pallas_call(
        kernel,
        grid=(parts,),
        in_specs=in_specs,
        out_specs=out_specs,
        out_shape=outs,
        scratch_shapes=scratch,
        name=name,
        cost_estimate=pl.CostEstimate(flops=flops, bytes_accessed=40 * 2 ** 20, transcendentals=0),
        compiler_params=pltpu.CompilerParams(
            dimension_semantics=("arbitrary",), vmem_limit_bytes=56 * 1024 * 1024, collective_id=collective_id,
            has_side_effects=collective_id is not None),
    )(*args)


def attention(active, lengths, x, gain, bias, gain_f, bias_f, w_qkv, w_out, cosine, sine, collective_id, parts=2):
    tokens, features = x.shape
    row_tokens = tokens // lengths.shape[0]
    size = features // HEADS
    wide = features // parts
    stack = jax.ShapeDtypeStruct((3, tokens, features), BF16)
    hbm = pl.BlockSpec(memory_space=pl.ANY)
    return meeting_call(
        functools.partial(attention_kernel, size, row_tokens, active), "attention", parts,
        (x, gain, bias, gain_f, bias_f, w_qkv, w_qkv, w_qkv, w_out, cosine, sine, lengths),
        [whole((tokens, features))] + [whole((1, features))] * 4 + [column(features, wide),
         column(features, wide, parts), column(features, wide, 2 * parts), lower(wide, features),
         whole(cosine.shape), whole(sine.shape), pl.BlockSpec(memory_space=pltpu.SMEM)],
        (jax.ShapeDtypeStruct((tokens, features), F32), stack, stack, jax.ShapeDtypeStruct((tokens, features), BF16)),
        (whole((tokens, features)), whole(stack.shape), stacked(3, tokens, wide), hbm),
        [pltpu.VMEM((tokens, wide), BF16), pltpu.SemaphoreType.DMA((2, 1))], 8 * tokens * features ** 2, collective_id)


def feed(mid, lefts, rows, w_gate_up, w_down, unit_rows, collective_id, parts=8):
    tokens, features = mid.shape
    wide = w_down.shape[0] // parts
    hbm = pl.BlockSpec(memory_space=pl.ANY)
    low = jax.ShapeDtypeStruct((tokens, features), BF16)
    return meeting_call(
        functools.partial(feed_kernel, unit_rows), "feed", parts,
        (mid, lefts, w_gate_up, w_gate_up, w_down, lefts, rows),
        [whole((tokens, features)), third(tokens, features), column(features, wide), column(features, wide, parts),
         lower(wide, features), hbm, hbm],
        (low, jax.ShapeDtypeStruct((tokens, w_down.shape[0] // 2), BF16), low,
         jax.ShapeDtypeStruct((2, tokens, features), BF16), low),
        (whole((tokens, features)), column(tokens, wide // 2), hbm, hbm, hbm),
        [pltpu.VMEM((tokens, features), F32), pltpu.SemaphoreType.DMA((2, 2))],
        6 * tokens * features * w_down.shape[0], collective_id)


def feed_both(active, mid, lefts, grad, gain, gain_a, w_gate_up, w_down, sends, lands, collective_id, parts=8):
    tokens, features = mid.shape
    hidden = w_down.shape[0]
    wide = hidden // parts
    hbm = pl.BlockSpec(memory_space=pl.ANY)
    return meeting_call(
        functools.partial(feed_both_kernel, active), "feed_both", parts,
        (mid, lefts, grad, gain, gain_a, w_gate_up, w_gate_up, w_down, *sends),
        [whole((tokens, features)), third(tokens, features), whole((tokens, features)), whole((1, features)),
         whole((1, features)), column(features, wide), column(features, wide, parts), lower(wide, features)]
        + [hbm] * len(sends),
        (jax.ShapeDtypeStruct((tokens, hidden), BF16), jax.ShapeDtypeStruct((2, tokens, hidden), BF16), jax.ShapeDtypeStruct((tokens + 8, features), F32),
         jax.ShapeDtypeStruct((8, features), F32), *lands),
        (column(tokens, wide), stacked(2, tokens, wide), whole((tokens + 8, features)), whole((8, features))) + (hbm,) * len(lands),
        [pltpu.VMEM((tokens, features), F32), pltpu.SemaphoreType.DMA((2, 10))],
        10 * tokens * features * hidden, collective_id)


def feed_out_kernel(parts, mid_in, hidden_in, weight_in, out, total_ref, hidden_ref, weight_ref, load_sem, store_sem):
    wide = hidden_ref.shape[1] // parts
    first = pltpu.make_async_copy(mid_in, total_ref, store_sem)
    loads = []
    for part in range(parts):
        at = pl.ds(part * wide, wide)
        loads.append((pltpu.make_async_copy(hidden_in.at[:, at], hidden_ref.at[:, at], load_sem.at[0, part]),
                      pltpu.make_async_copy(weight_in.at[at], weight_ref.at[at], load_sem.at[1, part])))

    @pl.when(lax.axis_index("section") == 1)
    def _():
        first.start()
        for copies in loads:
            for copy in copies:
                copy.start()
        first.wait()
        for part, copies in enumerate(loads):
            for copy in copies:
                copy.wait()
            at = slice(part * wide, (part + 1) * wide)
            total_ref[...] += dot(hidden_ref[:, at], weight_ref[at])
        last = pltpu.make_async_copy(total_ref, out, store_sem)
        last.start()
        last.wait()


def feed_out(mid, hidden, w_down, parts=4):
    hbm = pl.BlockSpec(memory_space=pl.ANY)
    return pl.pallas_call(
        functools.partial(feed_out_kernel, parts),
        out_shape=jax.ShapeDtypeStruct(mid.shape, F32),
        in_specs=[hbm] * 3,
        out_specs=hbm,
        scratch_shapes=[pltpu.VMEM(mid.shape, F32), pltpu.VMEM(hidden.shape, BF16), pltpu.VMEM(w_down.shape, BF16),
                        pltpu.SemaphoreType.DMA((2, parts)), pltpu.SemaphoreType.DMA],
        name="feed_out",
        cost_estimate=pl.CostEstimate(
            flops=2 * mid.shape[0] * w_down.size, bytes_accessed=16 * 2 ** 20, transcendentals=0),
        compiler_params=pltpu.CompilerParams(vmem_limit_bytes=56 * 1024 * 1024),
    )(mid, hidden, w_down)


def tables(lengths, row_tokens, size):
    index = jnp.arange(row_tokens, dtype=jnp.int32)[None]
    end, before = 0, 0
    for window in range(lengths.shape[1]):
        length = lengths[:, window:window + 1]
        end = end + length
        before = before + jnp.where(index >= end, length, 0)
    position = (index - before).astype(F32).reshape(-1, 1)
    half = jnp.arange(2 * size, dtype=jnp.int32) % (size // 2)
    frequency = 10000.0 ** (-2.0 * half.astype(F32) / size)
    angles = position * frequency
    return jnp.cos(angles), jnp.sin(angles)


def exchange_kernel(cfg, back_sizes, *refs):
    shards, bits, seats, unit_rows, width, section, aliased, late, layers, other_layers, lag, supply, order, backs, swapped = cfg
    arrays = len(seats)
    refs = list(refs)

    def take(count):
        taken = refs[:count]
        del refs[:count]
        return taken

    lefts, rights = take(arrays), take(arrays - len(supply))
    for index in supply:
        rights.insert(index, None)
    left_others, right_others = take(arrays - (1 if late else 0)), take(1)
    lefts = [ref if at is None else ref.at[at] for ref, at in zip(lefts, layers)]
    left_others = [ref if at is None else ref.at[at] for ref, at in zip(left_others, other_layers)]
    (vector,) = take(1)
    back_in = take(7)
    (lengths_ref,) = take(1)
    take(arrays + 2 if aliased else 0)
    outs, (vector_out,) = take(arrays), take(1)
    if late:
        left_others = left_others + take(1)
    for index in supply:
        rights[index] = take(1)[0]
    (back_out,) = take(1)
    back_refs, (back_load, back_store) = take(12), take(2)
    (grad_ref, x_ref, qkv_ref, wqkv_ref, wo_ref, cos_ref, sin_ref, branch_ref, proj_ref, vectors_ref, gm_ref,
     total_ref) = back_refs
    (given_send, given_recv, vector_far, vector_full, vector_land, vector_sum, vector_send, vector_recv, vector_store, left, right, left_sem, right_sem, other_sem,
     right_send, right_recv, late_send, late_recv, mine, side_land, side, side_send, side_recv, chain_a, chain_b,
     chain_send, chain_recv, rest_send, rest_land, rest_keep, rest_ssem, rest_rsem, piece, store_sem, gather_send,
     gather_recv) = refs
    units = sum(seat[0] for seat in seats)
    by_column = units - seats[-1][0]
    others = bits - 1
    final_rows = unit_rows >> others
    tokens = left.shape[1] // 2
    chains = (chain_a, chain_b)
    chain_rows = (final_rows, unit_rows)
    depth = chain_a.shape[1] - 1
    ring = mine.shape[1]
    slots, right_slots = piece.shape[1], right.shape[0]
    sec = lax.axis_index("section")
    here = lax.axis_index("shard")
    seat = lax.axis_index("group")
    group = 1 << bits
    peers = shards * group
    me = here * group + seat
    part = vector_out.shape[1]

    def bit_of(index):
        return lax.rem(lax.div(seat, 1 << order[index]), 2)

    def across(index):
        return (sec, here, seat + (1 - 2 * bit_of(index)) * (1 << order[index]))

    above = (sec, jnp.minimum(here + 1, shards - 1), seat)
    below = (sec, jnp.maximum(here - 1, 0), seat)
    half = bit_of(0)

    def remote(source, target, send, recv, device):
        return pltpu.make_async_remote_copy(
            src_ref=source, dst_ref=target, send_sem=send, recv_sem=recv,
            device_id=device, device_id_type=MESH,
        )

    def aligned(start, size):
        return pl.ds(pl.multiple_of(start, size), size)

    def peer(step):
        index = lax.rem(me + step, peers)
        return index, (sec, lax.div(index, group), lax.rem(index, group))

    def vector_copy(index, device):
        return remote(vector_full.at[:, aligned(device[1] * part, part)], vector_land.at[me], vector_send.at[index],
                      vector_recv.at[me], device)

    def vector_finish():
        vector_full[...] = vector[...] + (vectors_ref[...] if backs else vector_far[...])

        @pl.loop(1, peers)
        def _(step):
            vector_copy(*peer(step)).start()
        vector_sum[...] = vector_full[:, aligned(here * part, part)]

        @pl.loop(1, peers)
        def _(step):
            index, device = peer(step)
            vector_copy(index, device).wait_send()
            remote(vector_land.at[index], vector_land.at[index], vector_send.at[index], vector_recv.at[index],
                   device).wait_recv()
            vector_sum[...] += vector_land[index]
        copy = pltpu.make_async_copy(vector_sum, vector_out, vector_store)
        copy.start()
        copy.wait()

    def valid(chunk):
        return (chunk >= 0) & (chunk < units)

    def on(condition, run):
        pl.when(condition)(run)

    def by_rows(rows, run, tall=128):
        step = min(rows, tall)

        @pl.loop(0, rows // step)
        def _(index):
            run(aligned(index * step, step))

    def shifted(rows, offset):
        return aligned(rows.start + offset, rows.size)

    pace = min(by_column // seats[-1][0], 2)
    lead = by_column - pace * seats[-1][0]

    def seat_of(chunk):
        behind = jnp.maximum(chunk - lead, 0)
        period = lax.div(behind, pace + 1)
        step = behind - period * (pace + 1)
        last = (chunk >= lead) & (step == 0)
        return last, jnp.where(last, period, jnp.where(chunk < lead, chunk, lead + period * pace + step - 1))

    def each_array(chunk, run):
        last, index = seat_of(chunk)
        start = 0
        for which, (count, blocks, _, _) in enumerate(seats):
            begin = 0 if split_rows(which) else start

            def launch(which=which, begin=begin, blocks=blocks):
                local = index - begin
                row = lax.div(local, blocks)
                run(which, row, local - row * blocks)
            here_it_is = last if split_rows(which) else jnp.logical_not(last) & (index >= start) & (index < start + count)
            on((chunk < units) & here_it_is, launch)
            start += count

    def split_rows(which):
        return which == arrays - 1

    def right_columns(which, block, bit):
        inner = seats[which][2]
        if split_rows(which):
            return 0, aligned(block * (2 * width), 2 * width)
        outer = lax.div(block, inner)
        return outer, aligned((block - outer * inner) * (4 * width) + bit * (2 * width), 2 * width)

    def loads(chunk, run):
        slot = lax.rem(chunk, right_slots)

        def each(which, row, block):
            outer, columns = right_columns(which, block, half)
            run(pltpu.make_async_copy(
                rights[which].at[outer, :, columns], right.at[slot, :tokens], right_sem.at[slot]))
            if split_rows(which):
                run(pltpu.make_async_copy(
                    right_others[0].at[:, columns], right.at[slot, tokens:], other_sem.at[slot]))
        each_array(chunk, each)

    def load_left(chunk, wanted):
        def each(which, row, block):
            rows = seats[which][3]
            kind = int(split_rows(which))
            copies = []
            for shard in range(shards):
                if split_rows(which):
                    offsets = (shard * rows + (2 * row + half) * unit_rows, shard * (rows // 2) + row * unit_rows)
                else:
                    offsets = (shard * rows + row * unit_rows,) * 2
                for side, source in enumerate((lefts[which], left_others[which])):
                    copies.append(pltpu.make_async_copy(
                        source.at[:, aligned(offsets[side], unit_rows)],
                        left.at[kind, side * tokens:(side + 1) * tokens, shard * unit_rows:(shard + 1) * unit_rows],
                        left_sem.at[kind, side, shard]))

            def fetch():
                for copy in copies:
                    copy.start()
                for copy in copies:
                    copy.wait()
            on((block == 0) & wanted, fetch)
        each_array(chunk, each)

    def right_copy(chunk, source):
        four = lax.rem(chunk, right_slots)
        return remote(source, right.at[four, tokens:], right_send.at[four], right_recv.at[four], across(0))

    def send_right(chunk):
        def each(which, row, block):
            if not split_rows(which):
                outer, columns = right_columns(which, block, 1 - half)
                right_copy(chunk, rights[which].at[outer, :, columns]).start()
        each_array(chunk, each)

    late_rows = seats[-1][3] // (2 * unit_rows)

    def late_copy(row, shard):
        source = aligned(shard * seats[-1][3] + (2 * row + 1 - half) * unit_rows, unit_rows)
        target = aligned(shard * (seats[-1][3] // 2) + row * unit_rows, unit_rows)
        return remote(lefts[-1].at[:, source], left_others[-1].at[:, target], late_send.at[row, shard],
                      late_recv.at[row, shard], across(0))

    def late_turn(turn):
        begin = 0
        for row in range(late_rows):
            need = max(lead + row * seats[-1][1] * (pace + 1) - 1, 0)
            stride = max((need - begin) // shards, 1)
            at_once = -(-shards // max(need - begin, 1))
            for index in range(at_once):
                passed = turn - begin
                shard = lax.div(jnp.maximum(passed, 0), stride) * at_once + index
                on((passed >= 0) & (passed - lax.div(jnp.maximum(passed, 0), stride) * stride == 0) & (shard < shards),
                   lambda row=row, shard=shard: late_copy(row, shard).start())

            def finish(row=row):
                @pl.loop(0, shards)
                def _(shard):
                    late_copy(row, shard).wait_send()
                    late_copy(row, shard).wait_recv()
            on(turn == need, finish)
            begin = need

    def multiply(chunk):
        four, slot = lax.rem(chunk, right_slots), lax.rem(chunk, ring)
        load_left(chunk, chunk > 0)
        loads(chunk, lambda copy: copy.wait())
        last = seat_of(chunk)[0]

        def arrived():
            copy = right_copy(chunk, right.at[four, tokens:])
            copy.wait_recv()
            copy.wait_send()
        on(jnp.logical_not(last), arrived)
        result = lax.dot_general(left[last.astype(jnp.int32)], right[four], (((0,), (0,)), ((), ())), preferred_element_type=F32)
        for shard in range(shards):
            for path in range(2):
                mine[path, slot, shard] = result[
                    shard * unit_rows:(shard + 1) * unit_rows, path * width:(path + 1) * width].astype(BF16)

    def side_copy(step, chunk):
        slot, four = lax.rem(chunk, ring), lax.rem(chunk, slots)
        rows = unit_rows >> (step + 1)
        away = aligned((1 - bit_of(step + 1)) * rows, rows)
        source = mine.at[0, slot, :, away] if step == 0 else side.at[step - 1, slot, :, away]
        return remote(source, side_land.at[step, four, :, :rows], side_send.at[step, four], side_recv.at[step, four],
                      across(step + 1))

    def side_sum(step, chunk):
        slot, four = lax.rem(chunk, ring), lax.rem(chunk, slots)
        rows = unit_rows >> (step + 1)
        kept = bit_of(step + 1) * rows
        copy = side_copy(step, chunk)
        copy.wait_recv()
        copy.wait_send()

        @pl.loop(0, shards)
        def _(shard):
            def add(part):
                source = mine[0, slot, shard, shifted(part, kept)] if step == 0 else side[
                    step - 1, slot, shard, shifted(part, kept)]
                side[step, slot, shard, part] = (
                    source.astype(F32) + side_land[step, four, shard, part].astype(F32)).astype(BF16)
            by_rows(rows, add)
        if step + 1 < others:
            side_copy(step + 1, chunk).start()

    def base(path, slot, shard, rows):
        return (side[others - 1, slot, shard, rows] if path == 0 else mine[1, slot, shard, rows]).astype(F32)

    def hop(path, way, chunk, at):
        begin, end = (at + 1, shards) if way == 0 else (0, at)
        ref = chains[path].at[way, lax.rem(chunk, depth), begin:end]
        return remote(ref, ref, chain_send.at[path, way, lax.rem(chunk, 3)],
                      chain_recv.at[path, way, lax.rem(chunk, depth)], above if way == 0 else below)

    def at_each(run):
        for at in range(shards):
            on(here == at, lambda at=at: run(at))

    def onward(path, way, chunk):
        slot, from_base = lax.rem(chunk, depth), lax.rem(chunk, ring)

        def from_here(at):
            first, last = (at == 0, at == shards - 1) if way == 0 else (at == shards - 1, at == 0)
            if not first:
                hop(path, way, chunk, at - 1 if way == 0 else at + 1).wait_recv()
            if not last:
                begin, count = (at + 1, shards - 1 - at) if way == 0 else (0, at)

                @pl.loop(begin, begin + count)
                def _(shard):
                    def add(rows):
                        value = base(path, from_base, shard, rows)
                        if not first:
                            value = value + chains[path][way, slot, shard, rows].astype(F32)
                        chains[path][way, slot, shard, rows] = value.astype(BF16)
                    by_rows(chain_rows[path], add)
                hop(path, way, chunk, at).start()
        at_each(from_here)

    def sent(path, way, chunk):
        def from_here(at):
            if at != (shards - 1 if way == 0 else 0):
                hop(path, way, chunk, at).wait_send()
        at_each(from_here)

    def last_hop(path, chunk):
        from_base, slot = lax.rem(chunk, ring), lax.rem(chunk, depth)
        from_below = jnp.where(here > 0, slot, depth)
        from_above = jnp.where(here < shards - 1, slot, depth)

        def total(rows, offset):
            rows = shifted(rows, offset)
            return (
                base(path, from_base, here, rows)
                + chains[path][0, from_below, here, rows].astype(F32)
                + chains[path][1, from_above, here, rows].astype(F32)
            )
        if path == 0:
            finish(path, chunk, total)
        else:
            share(0, chunk, total)

    def rest_copy(step, chunk):
        slot, rows = lax.rem(chunk, slots), pl.ds(0, unit_rows >> (step + 1))
        return remote(rest_send.at[step, slot, rows], rest_land.at[step, slot, rows], rest_ssem.at[step, slot],
                      rest_rsem.at[step, slot], across(step + 1))

    def share(step, chunk, total):
        slot, rows = lax.rem(chunk, slots), unit_rows >> (step + 1)
        bit = bit_of(step + 1)

        def give(part):
            rest_send[step, slot, part] = total(part, (1 - bit) * rows).astype(BF16)
        by_rows(rows, give)
        rest_copy(step, chunk).start()

        def keep(part):
            rest_keep[step, slot, part] = total(part, bit * rows)
        by_rows(rows, keep)

    def rest_sum(step, chunk):
        slot = lax.rem(chunk, slots)
        copy = rest_copy(step, chunk)
        copy.wait_recv()
        copy.wait_send()

        def total(part, offset):
            part = shifted(part, offset)
            return rest_keep[step, slot, part] + rest_land[step, slot, part].astype(F32)
        if step + 1 < others:
            share(step + 1, chunk, total)
        else:
            finish(1, chunk, total)

    def finish(path, chunk, total):
        def put(part):
            piece[path, lax.rem(chunk, slots), part] = total(part, 0).astype(BF16)
        by_rows(final_rows, put)
        spread(path, 0, chunk)

    def place(which, row, block, path, bit, offset, rows):
        if split_rows(which):
            row0, column = (2 * row + bit) * unit_rows, block * (2 * width) + path * width
        else:
            row0, column = row * unit_rows, block * (4 * width) + bit * (2 * width) + path * width
        return outs[which].at[aligned(row0 + offset, rows), aligned(column, width)]

    def seat_row(steps):
        row = 0
        for step in range(steps):
            row = row + bit_of(step + 1) * (unit_rows >> (step + 1))
        return row

    def store(path, chunk, target):
        slot = lax.rem(chunk, slots)
        return pltpu.make_async_copy(piece.at[path, slot], target, store_sem.at[path, slot])

    def gather(path, step, other, chunk, target):
        slot = lax.rem(chunk, slots)
        source = piece.at[path, slot] if step == 0 else target
        if swapped[path]:
            index = bits - 1 - step
        else:
            index = 0 if step == 0 else bits - step
        return remote(source, target, gather_send.at[path, step, other, slot], gather_recv.at[path, step, other, slot],
                      across(index))

    def gather_size(path, step):
        if swapped[path]:
            return others - step, 1
        return others - max(step - 1, 0), 1 if step == 0 else 2

    def spread(path, step, chunk):
        steps, copies = gather_size(path, step)
        rows = unit_rows >> steps

        def each(which, row, block):
            for other in range(copies):
                bit = half if other == 0 else 1 - half
                target = place(which, row, block, path, bit, seat_row(steps), rows)
                if step == 0:
                    store(path, chunk, target).start()
                gather(path, step, other, chunk, target).start()
        each_array(chunk, each)

    def gathered(path, step, chunk):
        steps, copies = gather_size(path, step)
        target = outs[0].at[pl.ds(0, unit_rows >> steps), pl.ds(0, width)]
        for other in range(copies):
            copy = gather(path, step, other, chunk, target)
            copy.wait_recv()
            copy.wait_send()
        if step == 0:
            store(path, chunk, target).wait()
        if step + 1 < bits:
            spread(path, step + 1, chunk)

    size, row_tokens, parts = back_sizes
    features = x_ref.shape[1]
    block, pair, scale = features // parts, 2 * size, size ** -0.5
    groups = block // pair // 2
    part_steps = 2 + tokens // row_tokens * groups
    back_steps = 2 + parts * part_steps

    def back_loads():
        return [pltpu.make_async_copy(source, target, back_load.at[index])
                for index, (source, target) in enumerate(zip(back_in, back_refs))]

    def back_start():
        copies = back_loads()
        for index in (0, 4, 2, 5, 6, 3, 1):
            copies[index].start()

    def back_lanes(part):
        return aligned(part * block, block)

    def deliver(index, source, target):
        if backs:
            return pltpu.make_async_copy(source, target, back_store.at[index])
        return remote(source, target, given_send.at[index], given_recv.at[index], (section, here, seat))

    def deliver_branch():
        return deliver(0, branch_ref, rights[supply[0]].at[0])

    def deliver_part(part):
        lanes = back_lanes(part)
        return deliver(1 + part, proj_ref.at[:, :, lanes], rights[supply[1]].at[:, :, lanes])

    def deliver_vectors():
        return deliver(1 + parts, vectors_ref, vector_far)

    def back_store_last():
        return pltpu.make_async_copy(total_ref if backs else branch_ref, back_out, back_store.at[1 + parts])

    def back_begin():
        back_loads()[0].wait()

        def put(rows):
            branch_ref[rows] = grad_ref[rows].astype(BF16)
        by_rows(tokens, put)
        deliver_branch().start()

    def back_open(part):
        @pl.when(part == 0)
        def _():
            for index in (4, 2, 5, 6):
                back_loads()[index].wait()
        gm_ref[...] = dot_cols(branch_ref[...], wo_ref[back_lanes(part)]).astype(BF16)

    def back_heads(part, row, group):
        rows = aligned(row * row_tokens, row_tokens)
        first = lanes_of((row_tokens, pair)) < size
        allowed = same_window(lengths_ref, row, row_tokens)
        cosine, sine = cos_ref[rows], sin_ref[rows]
        lanes = [aligned(part * block + (2 * group + at) * pair, pair) for at in range(2)]
        work = []
        for at in range(2):
            query, key, value = (qkv_ref[which, rows, lanes[at]] for which in range(3))
            grad_mix = gm_ref[rows, aligned((2 * group + at) * pair, pair)]
            scaled = query * scale
            for head in range(2):
                own = first if head == 0 else jnp.logical_not(first)
                work.append((
                    query, key, grad_mix,
                    dot_cols(jnp.where(own, scaled, jnp.zeros_like(scaled)), key),
                    dot_cols(jnp.where(own, grad_mix, jnp.zeros_like(grad_mix)), value)))
        results = []
        for query, key, grad_mix, scores, grad_probs in work:
            probs = softmax(scores, allowed)
            weighted = probs * grad_probs
            grad_scores = (weighted - probs * jnp.sum(weighted, axis=-1, keepdims=True)).astype(BF16)
            results.append((query, key, grad_mix, grad_scores, probs.astype(BF16)))
        results = [
            (dot(grad_scores, key), dot_rows(grad_scores, query), dot_rows(probs, grad_mix))
            for query, key, grad_mix, grad_scores, probs in results]
        for at in range(2):
            grad_query, grad_key, grad_value = (
                jnp.where(first, a, b) for a, b in zip(results[2 * at], results[2 * at + 1]))
            proj_ref[0, rows, lanes[at]] = unrotated(grad_query * scale, cosine, sine, size).astype(BF16)
            proj_ref[1, rows, lanes[at]] = unrotated(grad_key * scale, cosine, sine, size).astype(BF16)
            proj_ref[2, rows, lanes[at]] = grad_value.astype(BF16)

    def back_close(part):
        deliver_part(part).start()

        @pl.when(part == 0)
        def _():
            back_loads()[3].wait()
        added = 0.0
        for which in range(3):
            added = added + dot_cols(
                proj_ref[which, :, back_lanes(part)], wqkv_ref[:, aligned(which * features + part * block, block)])
        total_ref[...] = jnp.where(part == 0, added, total_ref[...] + added)

    def back_end():
        back_loads()[1].wait()
        vectors_ref[...] = jnp.zeros_like(vectors_ref)
        if not backs:
            deliver_branch().wait_send()

        def end(rows):
            grad = total_ref[rows]
            through, by_gain = norm_back(grad, x_ref[rows].astype(F32), grad_ref[tokens:tokens + 1])
            result = grad_ref[rows] + through
            if backs:
                total_ref[rows] = result
            else:
                branch_ref[rows] = result.astype(BF16)
            vectors_ref[0:1] += jnp.sum(by_gain, axis=0, keepdims=True)
            vectors_ref[1:2] += jnp.sum(grad, axis=0, keepdims=True)
        by_rows(tokens, end)
        back_store_last().start()
        if backs:
            deliver_branch().wait()
        else:
            deliver_vectors().start()
            deliver_vectors().wait_send()
        for part in range(parts):
            if backs:
                deliver_part(part).wait()
            else:
                deliver_part(part).wait_send()
        back_store_last().wait()

    def back_step(step):
        on(step == 0, back_begin)
        inner = jnp.maximum(step - 1, 0)
        part = lax.div(inner, part_steps)
        at = inner - part * part_steps
        within = (step > 0) & (step < back_steps - 1)
        on(within & (at == 0), lambda: back_open(part))
        head = at - 1
        row = lax.div(jnp.maximum(head, 0), groups)
        on(within & (at > 0) & (at < part_steps - 1), lambda: back_heads(part, row, head - row * groups))
        on(within & (at == part_steps - 1), lambda: back_close(part))
        on(step == back_steps - 1, back_end)

    def hand_over():
        back_start()
        pl.semaphore_wait(pltpu.get_barrier_semaphore(), 1)

        @pl.loop(0, back_steps)
        def _(step):
            back_step(step)

    def take_over():
        deliver_branch().wait_recv()
        for part in range(parts):
            deliver_part(part).wait_recv()
        deliver_vectors().wait_recv()

    def unit_of(index):
        return index if index < lead else lead + (index - lead) // pace * (pace + 1) + 1 + (index - lead) % pace

    def work():
        barrier = pltpu.get_barrier_semaphore()
        if not backs:
            pl.semaphore_signal(barrier, inc=1, device_id=(1 - section, here, seat), device_id_type=MESH)

        @pl.loop(1, peers)
        def _(step):
            pl.semaphore_signal(barrier, inc=1, device_id=peer(step)[1], device_id_type=MESH)
        loads(0, lambda copy: copy.start())
        if backs:
            back_start()

        for path in range(2):
            for way in range(2):
                @pl.loop(0, shards)
                def _(shard):
                    def clear(rows):
                        chains[path][way, depth, shard, rows] = jnp.zeros((rows.size, width), BF16)
                    by_rows(chain_rows[path], clear)
        load_left(0, True)
        pl.semaphore_wait(barrier, peers - 1)
        for chunk in range(lag):
            send_right(chunk)

        line = shards - 1

        @pl.loop(0, units + lag * (line + others + bits) + 2)
        def _(turn):
            if backs:
                back_step(turn - 1)
            else:
                on(turn == unit_of(sum(seat[0] for seat in seats[:supply[0]])) - lag, take_over)
            on(turn + lag < units, lambda: send_right(turn + lag))
            if late:
                late_turn(turn)
            on(turn + 1 < units, lambda: loads(turn + 1, lambda copy: copy.start()))

            def opening():
                multiply(turn)
                side_copy(0, turn).start()
            on(turn < units, opening)
            for step in range(others):
                chunk = turn - lag * (1 + step)
                on(valid(chunk), lambda step=step, chunk=chunk: side_sum(step, chunk))
            for path in range(2):
                for way in range(2):
                    chunk = turn - lag * ((others if path == 0 else 0) + (here if way == 0 else line - here))
                    on(valid(chunk - 2), lambda path=path, way=way, chunk=chunk: sent(path, way, chunk - 2))
                    on(valid(chunk), lambda path=path, way=way, chunk=chunk: onward(path, way, chunk))
            on(valid(turn - lag * line), lambda: last_hop(1, turn - lag * line))
            on(valid(turn - lag * (line + others)), lambda: last_hop(0, turn - lag * (line + others)))
            for step in range(others):
                chunk = turn - lag * (line + 1 + step)
                on(valid(chunk), lambda step=step, chunk=chunk: rest_sum(step, chunk))
            for step in range(bits):
                for path in range(2):
                    chunk = turn - lag * (line + others + 1 + step)
                    on(valid(chunk), lambda path=path, step=step, chunk=chunk: gathered(path, step, chunk))

        vector_finish()

    if section is None:
        work()
    else:
        pl.when(sec == section)(work)
        if not backs:
            pl.when(sec != section)(hand_over)


def exchange(pairs, vector, shards, group, section, collective_id, unit_width, previous=None, lag=None, first_bit=0, supply=(1, 2), back=(), backs=False, swapped=(False, False), parts=2, unit_rows_max=256,
             name="exchange"):
    bits = group.bit_length() - 1
    arrays = len(pairs)
    order = (first_bit,) + tuple(bit for bit in range(bits) if bit != first_bit)
    lefts, rights = [pair[0][0] for pair in pairs], [pair[1] for pair in pairs]
    layers = tuple(pair[0][1] for pair in pairs)
    left_others = [pair[2] and pair[2][0] for pair in pairs]
    other_layers = tuple(pair[2] and pair[2][1] for pair in pairs)
    late = pairs[-1][2] is None
    if late:
        left_others = left_others[:-1]
    tokens = lefts[0].shape[-2]
    rows_of = [left.shape[-1] // shards for left in lefts]
    unit_rows = min([unit_rows_max] + rows_of[:-1])
    width = unit_width // 4
    seats = []
    for index, (rows, right) in enumerate(zip(rows_of, rights)):
        tall, wide = (2 * unit_rows, 2 * width) if index == arrays - 1 else (unit_rows, 4 * width)
        inner = right.shape[2] // wide
        seats.append((rows // tall * right.shape[0] * inner, right.shape[0] * inner, inner, rows))
    units = sum(seat[0] for seat in seats)
    others = bits - 1
    final_rows = unit_rows >> others
    lag = lag or (2 if shards <= 4 else 1)
    slots, right_slots = 2 * lag + 2, 2 * lag + 3
    depth, ring = lag * shards + 3, lag * (shards - 1) + 2
    late_rows = rows_of[-1] // (2 * unit_rows)
    peers, lanes = shards * group, vector.shape[1] // shards
    dma = pltpu.SemaphoreType.DMA
    *back, lengths = back
    x = back[1]
    previous = list(previous or [])
    scratch = [
        *(pltpu.VMEM(item.shape, item.dtype) for item in back),
        pltpu.VMEM(x.shape, BF16), pltpu.VMEM((3,) + x.shape, BF16), pltpu.VMEM(vector.shape, F32),
        pltpu.VMEM((tokens, x.shape[1] // parts), BF16), pltpu.VMEM(x.shape, F32),
        dma((len(back),)), dma((2 + parts,)),
        dma((2 + parts,)), dma((2 + parts,)),
        pltpu.VMEM(vector.shape, F32), pltpu.VMEM(vector.shape, F32),
        pltpu.VMEM((peers, vector.shape[0], lanes), F32),
        pltpu.VMEM((vector.shape[0], lanes), F32),
        dma((peers,)), dma((peers,)), dma,
        pltpu.VMEM((2, 2 * tokens, shards * unit_rows), BF16),
        pltpu.VMEM((right_slots, 2 * tokens, 2 * width), BF16),
        dma((2, 2, shards)), dma((right_slots,)), dma((right_slots,)),
        dma((right_slots,)), dma((right_slots,)),
        dma((late_rows, shards)), dma((late_rows, shards)),
        pltpu.VMEM((2, ring, shards, unit_rows, width), BF16),
        pltpu.VMEM((others, slots, shards, unit_rows // 2, width), BF16),
        pltpu.VMEM((others, ring, shards, unit_rows // 2, width), BF16),
        dma((others, slots)), dma((others, slots)),
        pltpu.VMEM((2, depth + 1, shards, final_rows, width), BF16),
        pltpu.VMEM((2, depth + 1, shards, unit_rows, width), BF16),
        dma((2, 2, 3)), dma((2, 2, depth)),
        pltpu.VMEM((others, slots, unit_rows // 2, width), BF16),
        pltpu.VMEM((others, slots, unit_rows // 2, width), BF16),
        pltpu.VMEM((others, slots, unit_rows // 2, width), F32),
        dma((others, slots)), dma((others, slots)),
        pltpu.VMEM((2, slots, final_rows, width), BF16),
        dma((2, slots)),
        dma((2, bits, 2, slots)), dma((2, bits, 2, slots)),
    ]
    cfg = (shards, bits, tuple(seats), unit_rows, width, section, len(previous) > 0, late, layers, other_layers, lag, supply, order, backs, swapped)
    operands = lefts + [r for n, r in enumerate(rights) if n not in supply] + left_others + [
        pairs[-1][3], vector] + back + [lengths] + previous
    first = len(operands) - len(previous)
    results = [jax.ShapeDtypeStruct((r, g.shape[0] * g.shape[2]), BF16) for r, g in zip(rows_of, rights)]
    results.append(jax.ShapeDtypeStruct((vector.shape[0], lanes), F32))
    if late:
        results.append(jax.ShapeDtypeStruct((tokens, lefts[-1].shape[-1] // 2), BF16))
    results.extend(jax.ShapeDtypeStruct(rights[index].shape, BF16) for index in supply)
    results.append(jax.ShapeDtypeStruct(x.shape, F32 if backs else BF16))
    aliases = {first + index: index for index in range(len(previous))}
    if previous:
        aliases[len(operands) - 1] = len(results) - 1
    hbm, vmem = pl.BlockSpec(memory_space=pl.ANY), pl.BlockSpec(memory_space=pltpu.VMEM)
    in_specs = [hbm] * len(operands)
    in_specs[first - 1] = pl.BlockSpec(memory_space=pltpu.SMEM)
    in_specs[first - 2 - len(back)] = vmem
    return pl.pallas_call(
        functools.partial(exchange_kernel, cfg, (x.shape[1] // HEADS, tokens // lengths.shape[0], parts)),
        out_shape=results,
        in_specs=in_specs,
        out_specs=[hbm] * len(results),
        scratch_shapes=scratch,
        input_output_aliases=aliases,
        name=name,
        cost_estimate=pl.CostEstimate(
            flops=4 * tokens * units * shards * unit_rows * 2 * width, bytes_accessed=100 * 2 ** 20,
            transcendentals=0),
        compiler_params=pltpu.CompilerParams(
            collective_id=collective_id, has_side_effects=True, vmem_limit_bytes=56 * 1024 * 1024),
    )(*operands)


UNIT_WIDTH = 512


def body(
    ends_in,
    lengths,
    norm_gain_a,
    norm_bias_a,
    w_qkv,
    w_out,
    norm_gain_f,
    norm_bias_f,
    w_gate_up,
    w_down,
):
    shards, group = lax.axis_size("shard"), lax.axis_size("group")
    tokens, features = ends_in.shape[1:]
    size = features // HEADS
    rows = ends_in[0]
    weight_qkv, weight_out, weight_gu, weight_down = w_qkv[0], w_out[0], w_gate_up[0], w_down[0]
    cosine, sine = tables(lengths, tokens // lengths.shape[0], size)
    unit_rows = min(256, features // shards)
    low = jax.ShapeDtypeStruct((tokens, features), BF16)
    stack = jax.ShapeDtypeStruct((3, tokens, features), BF16)

    def like(array):
        return jax.ShapeDtypeStruct(array.shape, array.dtype)

    def attend(active, values, collective_id):
        return attention(active, lengths, values, norm_gain_a, norm_bias_a, norm_gain_f, norm_bias_f, weight_qkv,
                         weight_out, cosine, sine, collective_id)

    def feed_back(active, middle, lefts, grad, sends, lands, collective_id):
        return feed_both(active, middle, lefts, grad, norm_gain_f, norm_gain_a, weight_gu, weight_down, sends, lands,
                         collective_id)

    def sum_all(which, lefts, lefts_beside, hidden, hidden_beside, grad_gu, grad, grad_beside, vectors, back, **more):
        rights = (grad_gu, jax.ShapeDtypeStruct((1, tokens, features), BF16), stack)
        pairs = [((lefts, at), right, other) for at, right, other in zip((2, 1, 0), rights, lefts_beside)]
        pairs.append(((hidden, None), grad[None], hidden_beside, grad_beside))
        return exchange(pairs, vectors, shards, group, which, which + 1, UNIT_WIDTH * features // 1024,
                        first_bit=1 - which, back=back + (cosine, sine, lengths), **more)

    middle_0, lefts_0, qkv_0, _ = attend(0, rows, None)
    passed, hidden_half_0, arrived, early_beside, rows_beside = feed(
        middle_0, lefts_0, rows, weight_gu, weight_down, unit_rows, 3)
    middle_1, lefts_1, qkv_1, low_beside = attend(1, arrived, 6)
    hidden_1, grad_gu_1, _, vectors_1, lefts_beside, qkv_there, qkv_weight, out_weight, hidden_beside, \
        grad_middle = feed_back(
            1, middle_1, lefts_1, rows,
            (lefts_1, qkv_1, weight_qkv, weight_out, lefts_0, hidden_half_0),
            (stack, stack, like(weight_qkv), like(weight_out), like(hidden_half_0), jax.ShapeDtypeStruct((tokens + 8, features), F32)), 4)
    sums = sum_all(1, lefts_1, [(lefts_beside, 2), (lefts_beside, 1), (low_beside, None)], hidden_1, None, grad_gu_1, rows, rows_beside,
                   vectors_1, (grad_middle, passed, qkv_there, qkv_weight, out_weight), name="exchange_second")
    returned = sums[-1]
    hidden_later, _ = lax.optimization_barrier((hidden_1, sums[4]))
    result = feed_out(middle_1, hidden_later, weight_down)
    hidden_0, grad_gu_0, grad_middle, vectors_0, returned_beside = feed_back(
        0, middle_0, lefts_0, returned, (returned,), (low,), 5)
    sums = sum_all(0, lefts_0, [(lefts_beside, 2), (early_beside, 1), (early_beside, 0)], hidden_0,
                   (hidden_beside, None), grad_gu_0, returned, returned_beside, vectors_0,
                   (grad_middle, rows, qkv_0, weight_qkv, weight_out), backs=True, previous=[*sums[:5], result],
                   name="exchange_first")
    ends_out = sums[-1][None]
    grad_gate_up, grad_out, grad_qkv, grad_down = (item.astype(F32)[None] for item in sums[:4])
    gain_a, bias_a, gain_f, bias_f = (sums[4][row:row + 1] for row in range(4))
    return (ends_out, gain_a, bias_a, grad_qkv, grad_out, gain_f, bias_f, grad_gate_up, grad_down)


def solution(mesh):
    placed = (
        P("section", ("shard", "group"), None),
        P(("shard", "group"), None),
        P("section", None),
        P("section", None),
        P("section", None, None),
        P("section", None, None),
        P("section", None),
        P("section", None),
        P("section", None, None),
        P("section", None, None),
    )
    return jax.shard_map(
        body,
        mesh=mesh,
        in_specs=placed,
        out_specs=(
            P("section", ("shard", "group"), None),
            P("section", "shard"),
            P("section", "shard"),
            P("section", "shard", None),
            P("section", "shard", None),
            P("section", "shard"),
            P("section", "shard"),
            P("section", "shard", None),
            P("section", "shard", None),
        ),
        check_vma=False,
    )
```
